128 devices in a mesh: gx: 8 (over x, core), gy: 4 (over y), gz: 4 (over z).
Axes of the slice: x: 4, y: 4, z: 4, core: 2. Of those that a mesh axis runs over, the one named last changes fastest.
Arguments:
- normals: bfloat16 [2, 512, 512, 512], P(None, 'gx', 'gy', 'gz'), may hold values from -6 to 6
- spectrum: float32 [512, 512, 512], P('gx', 'gy', 'gz'), may hold values from 1e-05 to 0.0001
- block_owner: int32 [131072, 1], P(('gx', 'gy', 'gz')), may hold values from 0 to 127; in each aligned block of 1024 rows (0 to 1023, 1024 to 2047, ...) at most 16 rows name the same one
Outputs:
- owned: float32 [128, 128, 16, 2, 128], P(('gx', 'gy', 'gz'))
The draws below stay inside these ranges and needn't reach their ends.
Inputs may be any that keep to these rules, and one draw needn't show every extreme that they name: `block_owner`: among the 1024 blocks of one source device no owner is named more than 16 times, and in every draw some owner is named exactly 16 times by some device.
All inputs are finite; a program needn't handle non-finite values.
Results may differ from the reference program's by a relative error of at most 0.0003.
Values sent between devices are 32-bit elements; how exact they have to be, the bound alone decides.
No kernel may reach another device: no remote copies, remote signals or barrier semaphores. Data moves between devices by JAX's collectives and lax.ppermute only.
A program may use at most 128 MiB of HBM per device.

```python
import math
import jax
import jax.numpy as jnp
import numpy as np
from jax import lax

EX = 512
EY = 512
EZ = 512
BW = 128
XP = 256
ZP = 256
YL = 2
BLOCKS_DEV = 1024
BLOCKS = 131072
CAP = 16
DEVICES = 128


def level_of(rng, extent, split, least, top_value):
    gain = 1.0
    for position, blocks in split:
        steps = jax.random.uniform(jax.random.fold_in(jax.random.fold_in(rng, 6), position), (blocks,), jnp.float32, least / len(split), top_value / len(split))
        gain = gain * jnp.repeat(jnp.exp(steps), extent[position] // blocks).reshape((-1,) + (1,) * (len(extent) - 1 - position))
    return gain


def assign_block(rng, own, number, rows, count, top, bound, skew):
    sequence = jax.random.permutation(rng, count)
    heavy_load, usual = load_shares(count, rows * top, bound, skew, True), load_shares(count, rows * top, bound, skew, False)
    places = jnp.arange(count)

    def named(lengths, rotation):
        used = int((lengths > 0).sum())
        fixed = max(1, used // 4)
        shifted = fixed + (places - fixed + rotation * (used - fixed)) % max(1, count - fixed)
        return jnp.zeros((count,), jnp.int32).at[sequence[jnp.where(places < fixed, places, shifted)]].set(jnp.asarray(lengths, jnp.int32))

    lengths = jnp.where(number % 4 == 0, named(heavy_load, number // 4), named(usual, number - number // 4 - 1))
    mixed = jax.random.permutation(jax.random.fold_in(own, 3), count)
    giver, receiver = mixed[0:count // 2 * 2:2], mixed[1:count // 2 * 2:2]
    room = jnp.minimum(lengths[giver] - 1, bound - lengths[receiver]) // 2
    room = jnp.where((giver == sequence[0]) | (receiver == sequence[0]) | (lengths[receiver] == 0), 0, jnp.maximum(room, 0))
    shifted = jax.random.randint(jax.random.fold_in(own, 4), (count // 2,), 0, 1 << 20) % (room + 1)
    lengths = lengths.at[giver].add(-shifted).at[receiver].add(shifted)
    members = jnp.searchsorted(jnp.cumsum(lengths), jnp.arange(rows * top), side="right").astype(jnp.int32)
    listing = members.reshape(top, rows).T
    listing = listing[jax.random.permutation(jax.random.fold_in(own, 1), rows)]
    rotation = jax.random.randint(jax.random.fold_in(own, 2), (rows, 1), 0, top)
    return jnp.take_along_axis(listing, (jnp.arange(top)[None, :] + rotation) % top, axis=1)


def load_shares(count, total, bound, lean, full):
    portions = [(1 << 20) // math.isqrt(standing ** lean) + 1 for standing in range(1, count + 1)]
    largest = bound if full else min(bound, max(-(-total // count), total * portions[0] // sum(portions)))
    least = 1 if total - largest >= count - 1 else 0
    given, spare = [largest] + [least] * (count - 1), total - largest - least * (count - 1)
    while spare > 0:
        candidates = [i for i in range(1, count) if given[i] < largest] or [i for i in range(1, count) if given[i] < bound]
        mass, remaining = sum([portions[i] for i in candidates]), spare
        for i in candidates:
            addition = min(bound - given[i], max(1, remaining * portions[i] // mass), spare)
            given[i] = given[i] + addition
            spare = spare - addition
    return np.array(given)


def gaussian(rng, dims, scale, reach, cuts=(), kind=jnp.bfloat16):
    factor_of = level_of(rng, dims, cuts, -0.22, 0.18) if cuts else 1.0
    entries = jax.random.normal(rng, dims, jnp.float32) * scale * factor_of
    return jnp.minimum(jnp.maximum(entries, -reach), reach).astype(kind)


def setup_inputs(seed: int = 0) -> dict:
    splits = jax.random.split(jax.random.key(seed), 4)
    normals = gaussian(splits[0], (2, EX, EY, EZ), 1.0, 6.0, ((1, 8), (2, 4), (3, 4)))
    spectrum = jnp.clip(jnp.exp(math.log(0.0001) - 2.3025851 * jax.random.uniform(splits[1], (EX, EY, EZ), jnp.float32) ** level_of(splits[1], (EX, EY, EZ), ((0, 8), (1, 4), (2, 4)), -0.2, 0.2)), 9.999999747378752e-06, 0.0001)
    block_owner_keys = jax.random.split(jax.random.fold_in(splits[2], 1), BLOCKS // BLOCKS_DEV)
    block_owner_turns = jax.random.permutation(jax.random.fold_in(splits[2], 3), BLOCKS // BLOCKS_DEV)
    block_owner = jax.vmap(lambda own, number: assign_block(jax.random.fold_in(splits[2], 2), own, number, BLOCKS_DEV, DEVICES, 1, CAP, 2))(block_owner_keys, block_owner_turns).reshape((BLOCKS, 1))
    return dict(normals=normals, spectrum=spectrum, block_owner=block_owner)


def reference(normals, spectrum, block_owner):
    real_part = spectrum * normals[0].astype(jnp.float32)
    imag_part = spectrum * normals[1].astype(jnp.float32)
    values = lax.complex(real_part, imag_part)
    values = jnp.fft.fft(values, axis=1)[:, : EY // 2, :]
    values = jnp.fft.fft(values, axis=2)[:, :, : EZ // 2]
    values = jnp.fft.fft(values, axis=0)[: EX // 2]
    field_pair = jnp.stack([jnp.real(values), jnp.imag(values)])
    coefficient = jnp.exp(field_pair)
    blocks = coefficient.reshape(2, XP, DEVICES, YL, ZP // BW, BW)
    blocks = blocks.transpose(2, 1, 3, 4, 0, 5).reshape(DEVICES, BLOCKS_DEV, 2, BW)
    destination = block_owner[:, 0].reshape(DEVICES, BLOCKS_DEV)
    one_hot = (destination[:, :, None] == jnp.arange(DEVICES, dtype=jnp.int32)[None, None, :]).astype(jnp.int32)
    earlier = jnp.cumsum(one_hot, axis=1) - one_hot
    slot_index = jnp.sum(earlier * one_hot, axis=2).astype(jnp.int32)
    source = jnp.broadcast_to(jnp.arange(DEVICES, dtype=jnp.int32)[:, None], destination.shape)
    owned = jnp.zeros((DEVICES, DEVICES, CAP, 2, BW), jnp.float32)
    owned = owned.at[destination, source, slot_index].set(blocks)
    return owned
```

```python
import functools

import jax
import jax.numpy as jnp
import ml_dtypes
import numpy as np
from jax import lax
from jax.experimental import pallas as pl
from jax.experimental.pallas import tpu as pltpu
from jax.sharding import PartitionSpec as P

N = 512
KEPT = 256
BW = 128
CAP = 16
ALL = ("gx", "gy", "gz")
MIB = 1 << 20


def split_table(table):
    high = table.astype(np.float32).astype(ml_dtypes.bfloat16)
    low = (table - high.astype(np.float64)).astype(np.float32).astype(ml_dtypes.bfloat16)
    return np.stack([high, low])


def cos_sin(positions, kept):
    angles = (positions[:, None] * kept[None, :] % N) * (2.0 * np.pi / N)
    return np.cos(angles), np.sin(angles)


@functools.cache
def tables():
    cosine, sine = cos_sin(np.arange(N), np.arange(KEPT))
    real_rows = np.concatenate([cosine, -sine], 1).reshape(4, 1, 128, 2 * KEPT)
    imag_rows = np.concatenate([sine, cosine], 1).reshape(4, 1, 128, 2 * KEPT)
    table_z = np.concatenate([real_rows, imag_rows], 1).reshape(4, 256, 2 * KEPT)
    order = np.arange(KEPT).reshape(KEPT // 2, 2).T.reshape(-1)
    cosine, sine = cos_sin(np.arange(N), order)
    cosine, sine = cosine.reshape(4, 128, KEPT), sine.reshape(4, 128, KEPT)
    top = np.concatenate([cosine, sine], 1)
    bottom = np.concatenate([-sine, cosine], 1)
    table_y = np.concatenate([top, bottom], 2).transpose(0, 2, 1)
    gx, gy, gz = np.meshgrid(np.arange(8), np.arange(4), np.arange(4), indexing="ij")
    first = 64 * gx + 8 * gz + 2 * gy
    second = 64 * gx + 32 + 8 * gy + 2 * gz
    cells = np.stack([first, first + 1, second, second + 1], -1).reshape(128, 4)
    cosine, sine = cos_sin(cells.reshape(-1), np.arange(KEPT))
    cosine = cosine.T.reshape(KEPT, 128, 1, 4)
    sine = sine.T.reshape(KEPT, 128, 1, 4)
    top = np.concatenate([cosine, sine], 2).reshape(KEPT, 1024)
    bottom = np.concatenate([-sine, cosine], 2).reshape(KEPT, 1024)
    table_x = np.concatenate([top, bottom], 0)
    return split_table(table_x), split_table(table_y), split_table(table_z)


def halves(values):
    high = values.astype(jnp.bfloat16)
    low = (values - high.astype(jnp.float32)).astype(jnp.bfloat16)
    return high, low


def product(left, right):
    def dot(a, b):
        return jnp.dot(a, b, preferred_element_type=jnp.float32)

    return dot(left[0], right[0]) + (dot(left[0], right[1]) + dot(left[1], right[0]))


def params(mib):
    return pltpu.CompilerParams(vmem_limit_bytes=mib * MIB)


def cost(multiplies, moved):
    return pl.CostEstimate(flops=6 * multiplies, bytes_accessed=moved, transcendentals=0)


def first_z_kernel(place_ref, in_ref, table_ref, out_ref):
    total = None
    for g in range(4):
        rows = jnp.concatenate(
            [in_ref[g, plane].reshape(256, 128) for plane in range(2)], axis=1
        )
        term = product(halves(rows), (table_ref[0, g], table_ref[1, g]))
        total = term if total is None else total + term
    for plane in range(2):
        out_ref[plane] = total[:, plane * KEPT : (plane + 1) * KEPT].reshape(2, 128, KEPT)


def first_z(place, arrived, table_z):
    return pl.pallas_call(
        first_z_kernel,
        grid_spec=pltpu.PrefetchScalarGridSpec(
            num_scalar_prefetch=1,
            grid=(1,),
            in_specs=[
                pl.BlockSpec((4, 2, 2, 128, 128), lambda i, place: (0, 0, place[0], 0, 0)),
                pl.BlockSpec((2, 4, 256, 512), lambda i, place: (0, 0, 0, 0)),
            ],
            out_specs=pl.BlockSpec((2, 2, 128, KEPT), lambda i, place: (0, 0, 0, 0)),
        ),
        out_shape=jax.ShapeDtypeStruct((2, 2, 128, KEPT), jnp.float32),
        compiler_params=params(24),
        cost_estimate=cost(256 * 1024 * 512, 4 * MIB),
        name="first_z",
    )(place, arrived, table_z)


def first_y_kernel(place_ref, p0, p1, p2, p3, table_ref, out_ref):
    total = None
    for shift, piece in enumerate((p0, p1, p2, p3)):
        g = lax.rem(place_ref[0] + (4 - shift), 4)
        columns = jnp.concatenate([piece[:, x].reshape(256, 128) for x in range(2)], axis=1)
        term = product((table_ref[0, g], table_ref[1, g]), halves(columns))
        total = term if total is None else total + term
    for plane in range(2):
        for x in range(2):
            out_ref[0, plane, x] = total[
                plane * KEPT : (plane + 1) * KEPT, x * 128 : (x + 1) * 128
            ]


def first_y(place, pieces, table_y):
    return pl.pallas_call(
        first_y_kernel,
        grid_spec=pltpu.PrefetchScalarGridSpec(
            num_scalar_prefetch=1,
            grid=(4,),
            in_specs=[pl.BlockSpec((2, 2, 128, 128), lambda i, place: (0, i, 0, 0))] * 4
            + [pl.BlockSpec((2, 4, 512, 256), lambda i, place: (0, 0, 0, 0))],
            out_specs=pl.BlockSpec((1, 2, 2, KEPT, 128), lambda i, place: (i, 0, 0, 0, 0)),
        ),
        out_shape=jax.ShapeDtypeStruct((4, 2, 2, KEPT, 128), jnp.float32),
        compiler_params=params(24),
        cost_estimate=cost(1024 * 1024 * 512, 8 * MIB),
        name="first_y",
    )(place, *pieces, table_y)


def second_kernel(place_ref, p0, p1, p2, p3, b_ref, table_y_ref, table_z_ref, out_ref):
    def put(values, row):
        for parity in range(2):
            for half in range(2):
                out_ref[pl.ds(parity * 16 + half * 8 + row, 128, stride=32), :] = values[
                    parity * 128 : (parity + 1) * 128, half * 128 : (half + 1) * 128
                ]

    for x in range(2):
        total = None
        for shift, piece in enumerate((p0, p1, p2, p3)):
            g = lax.rem(place_ref[0] + (4 - shift), 4)
            columns = piece[:, x].reshape(256, KEPT)
            term = product((table_y_ref[0, g], table_y_ref[1, g]), halves(columns))
            total = term if total is None else total + term
        for plane in range(2):
            put(total[plane * KEPT : (plane + 1) * KEPT], plane * 4 + x)
    for x in range(2):
        total = None
        for g in range(4):
            rows = jnp.concatenate([b_ref[g, plane, x] for plane in range(2)], axis=1)
            term = product(halves(rows), (table_z_ref[0, g], table_z_ref[1, g]))
            total = term if total is None else total + term
        for plane in range(2):
            put(total[:, plane * KEPT : (plane + 1) * KEPT], plane * 4 + 2 + x)


def second(place, pieces, arrived, table_y, table_z):
    whole = pl.BlockSpec(memory_space=pltpu.VMEM)
    return pl.pallas_call(
        second_kernel,
        in_specs=[pl.BlockSpec(memory_space=pltpu.SMEM)] + [whole] * 7,
        out_specs=whole,
        out_shape=jax.ShapeDtypeStruct((4096, 128), jnp.float32),
        compiler_params=params(40),
        cost_estimate=cost(1024 * 1024 * 512, 10 * MIB),
        name="second",
    )(place, *pieces, arrived, table_y, table_z)


def third_kernel(slot_ref, in_ref, table_ref, out_ref, held):
    parity = pl.program_id(0)

    @pl.when(parity == 0)
    def _():
        out_ref[...] = jnp.zeros_like(out_ref)

    columns = jnp.concatenate(
        [in_ref[:, 0, half].reshape(1024, 128) for half in range(2)], axis=1
    )
    values = jnp.exp(product((table_ref[0], table_ref[1]), halves(columns)))
    for plane in range(2):
        for half in range(2):
            held[plane, half] = values[
                plane * KEPT : (plane + 1) * KEPT, half * 128 : (half + 1) * 128
            ]

    def place_rows(group, carry):
        for offset in range(8):
            x = group * 8 + offset
            for half in range(2):
                slot = slot_ref[x * 4 + parity * 2 + half]
                for plane in range(2):
                    out_ref[pl.ds(slot * 2 + plane, 1), :] = held[plane, half, pl.ds(x, 1), :]
        return carry

    lax.fori_loop(0, KEPT // 8, place_rows, 0)


def third(slots, arrived, table_x):
    return pl.pallas_call(
        third_kernel,
        grid_spec=pltpu.PrefetchScalarGridSpec(
            num_scalar_prefetch=1,
            grid=(2,),
            in_specs=[
                pl.BlockSpec((128, 1, 2, 8, 128), lambda i, slots: (0, i, 0, 0, 0)),
                pl.BlockSpec((2, 512, 1024), lambda i, slots: (0, 0, 0)),
            ],
            out_specs=pl.BlockSpec((4096, 128), lambda i, slots: (0, 0)),
            scratch_shapes=[pltpu.VMEM((2, 2, KEPT, 128), jnp.float32)],
        ),
        out_shape=jax.ShapeDtypeStruct((4096, 128), jnp.float32),
        compiler_params=params(32),
        cost_estimate=cost(512 * 1024 * 512, 6 * MIB),
        name="third",
    )(slots, arrived, table_x)


def shifted(piece, axis, shift):
    size = lax.axis_size(axis)
    return lax.ppermute(piece, axis, [(i, (i + shift) % size) for i in range(size)])


def exchange(pieces, axis):
    return [pieces[0]] + [shifted(pieces[s], axis, s) for s in range(1, 4)]


def slots_of(block_owner):
    destination = block_owner[:, 0]
    one_hot = (destination[:, None] == jnp.arange(128, dtype=jnp.int32)[None, :]).astype(jnp.int32)
    earlier = jnp.cumsum(one_hot, axis=0) - one_hot
    return destination * CAP + jnp.sum(earlier * one_hot, axis=1)


def per_device(normals, spectrum, block_owner):
    table_x, table_y, table_z = (jnp.asarray(table) for table in tables())
    gy = lax.axis_index("gy").astype(jnp.int32)
    place = gy.reshape(1)

    first = spectrum[:32].reshape(4, 1, 8, 128, 128) * normals[:, :32].astype(
        jnp.float32
    ).reshape(2, 4, 8, 128, 128).transpose(1, 0, 2, 3, 4)
    arrived_a = lax.all_to_all(first, "gz", split_axis=0, concat_axis=0, tiled=True)

    def chunk_b(shift):
        start = 32 + 8 * lax.rem(gy + shift, 4)
        return lax.dynamic_slice_in_dim(spectrum, start, 8, 0)[None] * lax.dynamic_slice_in_dim(
            normals, start, 8, 1
        ).astype(jnp.float32)

    pieces_b = exchange([chunk_b(s) for s in range(4)], "gy")

    pieces_a = exchange(
        [first_z(lax.rem(place + s, 4), arrived_a, table_z) for s in range(4)], "gy"
    )
    sent_b = first_y(place, pieces_b, table_y)
    arrived_b = lax.all_to_all(sent_b, "gz", split_axis=0, concat_axis=0, tiled=True)

    planes = second(place, pieces_a, arrived_b, table_y, table_z)
    lines = lax.all_to_all(
        planes.reshape(128, 2, 2, 8, 128), ALL, split_axis=0, concat_axis=0, tiled=True
    )
    outgoing = third(slots_of(block_owner), lines, table_x)
    return lax.all_to_all(
        outgoing.reshape(128, 1, CAP, 2, BW), ALL, split_axis=0, concat_axis=1, tiled=True
    )


def solution(mesh):
    placed = (P(None, "gx", "gy", "gz"), P("gx", "gy", "gz"), P(ALL, None))
    return jax.shard_map(
        per_device,
        mesh=mesh,
        in_specs=placed,
        out_specs=P(ALL, None, None, None, None),
        check_vma=False,
    )
```

```python
import functools

import jax
import jax.numpy as jnp
import ml_dtypes
import numpy as np
from jax import lax
from jax.experimental import pallas as pl
from jax.experimental.pallas import tpu as pltpu
from jax.sharding import PartitionSpec as P

N = 512
KEPT = 256
BW = 128
CAP = 16
ALL = ("gx", "gy", "gz")
MIB = 1 << 20
VMEM = 40


def split_table(table):
    high = table.astype(np.float32).astype(ml_dtypes.bfloat16)
    low = (table - high.astype(np.float64)).astype(np.float32).astype(ml_dtypes.bfloat16)
    return np.stack([high, low])


def cos_sin(positions, kept):
    angles = (positions[:, None] * kept[None, :] % N) * (2.0 * np.pi / N)
    return np.cos(angles), np.sin(angles)


@functools.cache
def tables():
    cosine, sine = cos_sin(np.arange(N), np.arange(KEPT))
    real_rows = np.concatenate([cosine, -sine], 1).reshape(4, 1, 128, 2 * KEPT)
    imag_rows = np.concatenate([sine, cosine], 1).reshape(4, 1, 128, 2 * KEPT)
    table_z = np.concatenate([real_rows, imag_rows], 1).reshape(4, 256, 2 * KEPT)
    order = np.arange(KEPT).reshape(KEPT // 2, 2).T.reshape(-1)
    cosine, sine = cos_sin(np.arange(N), order)
    cosine, sine = cosine.reshape(4, 128, KEPT), sine.reshape(4, 128, KEPT)
    top = np.concatenate([cosine, sine], 1)
    bottom = np.concatenate([-sine, cosine], 1)
    table_y = np.concatenate([top, bottom], 2).transpose(0, 2, 1)
    gx, gy, gz = np.meshgrid(np.arange(8), np.arange(4), np.arange(4), indexing="ij")
    first = 64 * gx + 8 * gz + 2 * gy
    second = 64 * gx + 32 + 8 * gy + 2 * gz
    cells = np.stack([first, first + 1, second, second + 1], -1).reshape(128, 4)
    cosine, sine = cos_sin(cells.reshape(-1), np.arange(KEPT))
    cosine = cosine.T.reshape(KEPT, 128, 1, 4)
    sine = sine.T.reshape(KEPT, 128, 1, 4)
    top = np.concatenate([cosine, sine], 2).reshape(KEPT, 1024)
    bottom = np.concatenate([-sine, cosine], 2).reshape(KEPT, 1024)
    table_x = np.concatenate([top, bottom], 0)
    return split_table(table_x), split_table(table_y), split_table(table_z)


def halves(values):
    high = values.astype(jnp.bfloat16)
    low = (values - high.astype(jnp.float32)).astype(jnp.bfloat16)
    return high, low


def product(left, right):
    def dot(a, b):
        return jnp.dot(a, b, preferred_element_type=jnp.float32)

    return dot(left[0], right[0]) + (dot(left[0], right[1]) + dot(left[1], right[0]))


def params(mib):
    return pltpu.CompilerParams(vmem_limit_bytes=mib * MIB)


def cost(multiplies, moved):
    return pl.CostEstimate(flops=6 * multiplies, bytes_accessed=moved, transcendentals=0)


def scale_kernel(place_ref, normals_ref, spectrum_ref, out_ref):
    out_ref[...] = normals_ref[...].astype(jnp.float32) * spectrum_ref[...][None]


def scale(chunk, normals, spectrum):
    return pl.pallas_call(
        scale_kernel,
        grid_spec=pltpu.PrefetchScalarGridSpec(
            num_scalar_prefetch=1,
            grid=(2,),
            in_specs=[
                pl.BlockSpec((2, 4, 128, 128), lambda i, chunk: (0, 2 * chunk[0] + i, 0, 0)),
                pl.BlockSpec((4, 128, 128), lambda i, chunk: (2 * chunk[0] + i, 0, 0)),
            ],
            out_specs=pl.BlockSpec((2, 4, 128, 128), lambda i, chunk: (0, i, 0, 0)),
        ),
        out_shape=jax.ShapeDtypeStruct((2, 8, 128, 128), jnp.float32),
        compiler_params=params(VMEM),
        cost_estimate=cost(1 << 18, 2 * MIB),
        name="scale",
    )(chunk, normals, spectrum)


def rows_z(piece):
    return halves(jnp.concatenate([piece[plane].reshape(-1, 128) for plane in range(2)], axis=1))


def columns_y(piece):
    planes, cells = piece.shape[:2]
    return halves(
        jnp.concatenate([piece[:, x].reshape(256, piece.shape[3]) for x in range(cells)], axis=1)
    )


def source(place, shift):
    return lax.rem(place + (4 - shift), 4)


def first_part_kernel(along_z, place_ref, p0, p1, p3, table_ref, out_ref):
    total = None
    for shift, piece in ((0, p0), (1, p1), (3, p3)):
        g = source(place_ref[0], shift)
        table = (table_ref[0, g], table_ref[1, g])
        if along_z:
            term = product(rows_z(piece[...]), table)
        else:
            term = product(table, columns_y(piece[...]))
        total = term if total is None else total + term
    out_ref[0] = total


def first_part(along_z, place, pieces, table):
    shape = (256, 512) if along_z else (512, 256)
    return pl.pallas_call(
        functools.partial(first_part_kernel, along_z),
        grid_spec=pltpu.PrefetchScalarGridSpec(
            num_scalar_prefetch=1,
            grid=(4,),
            in_specs=[pl.BlockSpec((2, 2, 128, 128), lambda i, place: (0, i, 0, 0))] * 3
            + [pl.BlockSpec((2, 4) + table.shape[2:], lambda i, place: (0, 0, 0, 0))],
            out_specs=pl.BlockSpec((1,) + shape, lambda i, place: (i, 0, 0)),
        ),
        out_shape=jax.ShapeDtypeStruct((4,) + shape, jnp.float32),
        compiler_params=params(VMEM),
        cost_estimate=cost(768 * 1024 * 512, 8 * MIB),
        name="first_part_z" if along_z else "first_part_y",
    )(place, *pieces, table)


def first_last_kernel(along_z, shifts, place_ref, to_ref, part_ref, p2, table_ref, *out_refs):
    table = (table_ref[0, 0], table_ref[1, 0])
    if along_z:
        total = part_ref[0] + product(rows_z(p2[...]), table)
    else:
        total = part_ref[0] + product(table, columns_y(p2[...]))
    for step, out_ref in enumerate(out_refs):

        @pl.when(pl.program_id(0) == step)
        def _():
            for plane in range(2):
                if along_z:
                    out_ref[plane] = total[:, plane * KEPT : (plane + 1) * KEPT].reshape(
                        2, 128, KEPT
                    )
                else:
                    for x in range(2):
                        out_ref[plane, x] = total[
                            plane * KEPT : (plane + 1) * KEPT, x * 128 : (x + 1) * 128
                        ]


def first_last(along_z, shifts, place, to, part, piece, table):
    def pair(i, to):
        shift = shifts[0]
        for step in range(1, len(shifts)):
            shift = jnp.where(i == step, shifts[step], shift)
        return lax.rem(to[0] + shift, 4)

    shape = (2, 2, 128, KEPT) if along_z else (2, 2, KEPT, 128)
    return pl.pallas_call(
        functools.partial(first_last_kernel, along_z, shifts),
        grid_spec=pltpu.PrefetchScalarGridSpec(
            num_scalar_prefetch=2,
            grid=(len(shifts),),
            in_specs=[
                pl.BlockSpec((1,) + part.shape[1:], lambda i, place, to: (pair(i, to), 0, 0)),
                pl.BlockSpec((2, 2, 128, 128), lambda i, place, to: (0, pair(i, to), 0, 0)),
                pl.BlockSpec(
                    (2, 1) + table.shape[2:],
                    lambda i, place, to: (0, lax.rem(place[0] + 2, 4), 0, 0),
                ),
            ],
            out_specs=[pl.BlockSpec(shape, lambda i, place, to: (0, 0, 0, 0))] * len(shifts),
        ),
        out_shape=[jax.ShapeDtypeStruct(shape, jnp.float32)] * len(shifts),
        compiler_params=params(VMEM),
        cost_estimate=cost(len(shifts) * 256 * 256 * 512, 2 * len(shifts) * MIB),
        name="first_last_z" if along_z else "first_last_y",
    )(place, to, part, piece, table)


def second_part_kernel(along_z, place_ref, p0, p1, p3, table_ref, out_ref):
    total = None
    for shift, piece in ((0, p0), (1, p1), (3, p3)):
        g = source(place_ref[0], shift)
        table = (table_ref[0, g], table_ref[1, g])
        if along_z:
            term = product(rows_z(piece[...]), table)
        else:
            term = product(table, columns_y(piece[...]))
        total = term if total is None else total + term
    out_ref[0] = total


def second_part(along_z, place, pieces, table):
    shape = (256, 512) if along_z else (512, 256)
    return pl.pallas_call(
        functools.partial(second_part_kernel, along_z),
        grid_spec=pltpu.PrefetchScalarGridSpec(
            num_scalar_prefetch=1,
            grid=(2,),
            in_specs=[
                pl.BlockSpec((2, 1) + pieces[0].shape[2:], lambda i, place: (0, i, 0, 0))
            ]
            * 3
            + [pl.BlockSpec((2, 4) + table.shape[2:], lambda i, place: (0, 0, 0, 0))],
            out_specs=pl.BlockSpec((1,) + shape, lambda i, place: (i, 0, 0)),
        ),
        out_shape=jax.ShapeDtypeStruct((2,) + shape, jnp.float32),
        compiler_params=params(VMEM),
        cost_estimate=cost(384 * 1024 * 512, 5 * MIB),
        name="second_part_z" if along_z else "second_part_y",
    )(place, *pieces, table)


def second_last_kernel(
    gy_ref, gz_ref, part_y, last_y, table_y_ref, part_z, last_z, table_z_ref, out_ref, held
):
    def put(values, row):
        for half in range(2):
            held[pl.ds(half * 8 + row, 128, stride=16), :] = values[
                :, half * 128 : (half + 1) * 128
            ]

    table = tuple(table_y_ref[i, 0].reshape(256, 256) for i in range(2))
    for x in range(2):
        total = part_y[x].reshape(256, KEPT) + product(table, columns_y(last_y[:, x : x + 1]))
        for plane in range(2):
            put(total[plane * 128 : (plane + 1) * 128], plane * 4 + x)
    table = (table_z_ref[0, 0], table_z_ref[1, 0])
    total = part_z[...].reshape(256, 512) + product(rows_z(last_z[...]), table)
    for x in range(2):
        for plane in range(2):
            put(
                total[x * 128 : (x + 1) * 128, plane * KEPT : (plane + 1) * KEPT],
                plane * 4 + 2 + x,
            )
    out_ref[...] = held[...].reshape(128, 1, 2, 8, 128)


def second_last(gy, gz, part_y, last_y, table_y, part_z, last_z, table_z):
    return pl.pallas_call(
        second_last_kernel,
        grid_spec=pltpu.PrefetchScalarGridSpec(
            num_scalar_prefetch=2,
            grid=(2,),
            in_specs=[
                pl.BlockSpec((2, 2, 128, KEPT), lambda i, gy, gz: (0, 0, i, 0)),
                pl.BlockSpec((2, 2, 128, KEPT), lambda i, gy, gz: (0, 0, 0, 0)),
                pl.BlockSpec(
                    (2, 1, 2, 128, 256), lambda i, gy, gz: (0, lax.rem(gy[0] + 2, 4), 0, i, 0)
                ),
                pl.BlockSpec((2, 128, 512), lambda i, gy, gz: (0, i, 0)),
                pl.BlockSpec((2, 2, 128, 128), lambda i, gy, gz: (0, 0, i, 0)),
                pl.BlockSpec(
                    (2, 1, 256, 512), lambda i, gy, gz: (0, lax.rem(gz[0] + 2, 4), 0, 0)
                ),
            ],
            out_specs=pl.BlockSpec((128, 1, 2, 8, 128), lambda i, gy, gz: (0, i, 0, 0, 0)),
            scratch_shapes=[pltpu.VMEM((2048, 128), jnp.float32)],
        ),
        out_shape=jax.ShapeDtypeStruct((128, 2, 2, 8, 128), jnp.float32),
        compiler_params=params(VMEM),
        cost_estimate=cost(256 * 1024 * 512, 6 * MIB),
        name="second_last",
    )(
        gy,
        gz,
        part_y.reshape(2, 2, KEPT, KEPT),
        last_y,
        table_y.reshape(2, 4, 2, KEPT, 256),
        part_z,
        last_z,
        table_z,
    )


def third_kernel(slot_ref, in_ref, table_ref, out_ref, held):
    parity = pl.program_id(0)

    @pl.when(parity == 0)
    def _():
        out_ref[...] = jnp.zeros_like(out_ref)

    columns = jnp.concatenate(
        [in_ref[:, 0, half].reshape(1024, 128) for half in range(2)], axis=1
    )
    values = jnp.exp(product((table_ref[0], table_ref[1]), halves(columns)))
    for plane in range(2):
        for half in range(2):
            held[plane, half] = values[
                plane * KEPT : (plane + 1) * KEPT, half * 128 : (half + 1) * 128
            ]

    def place_rows(group, carry):
        for offset in range(8):
            x = group * 8 + offset
            for half in range(2):
                slot = slot_ref[x * 4 + parity * 2 + half]
                for plane in range(2):
                    out_ref[pl.ds(slot * 2 + plane, 1), :] = held[plane, half, pl.ds(x, 1), :]
        return carry

    lax.fori_loop(0, KEPT // 8, place_rows, 0)


def third(slots, arrived, table_x):
    return pl.pallas_call(
        third_kernel,
        grid_spec=pltpu.PrefetchScalarGridSpec(
            num_scalar_prefetch=1,
            grid=(2,),
            in_specs=[
                pl.BlockSpec((128, 1, 2, 8, 128), lambda i, slots: (0, i, 0, 0, 0)),
                pl.BlockSpec((2, 512, 1024), lambda i, slots: (0, 0, 0)),
            ],
            out_specs=pl.BlockSpec((4096, 128), lambda i, slots: (0, 0)),
            scratch_shapes=[pltpu.VMEM((2, 2, KEPT, 128), jnp.float32)],
        ),
        out_shape=jax.ShapeDtypeStruct((4096, 128), jnp.float32),
        compiler_params=params(VMEM),
        cost_estimate=cost(512 * 1024 * 512, 6 * MIB),
        name="third",
    )(slots, arrived, table_x)


def shifted(piece, axis, shift):
    size = lax.axis_size(axis)
    return lax.ppermute(piece, axis, [(i, (i + shift) % size) for i in range(size)])


def slots_of(block_owner):
    destination = block_owner[:, 0]
    one_hot = (destination[:, None] == jnp.arange(128, dtype=jnp.int32)[None, :]).astype(jnp.int32)
    earlier = jnp.cumsum(one_hot, axis=0) - one_hot
    return destination * CAP + jnp.sum(earlier * one_hot, axis=1)


def per_device(normals, spectrum, block_owner):
    table_x, table_y, table_z = (jnp.asarray(table) for table in tables())
    gy = lax.axis_index("gy").astype(jnp.int32).reshape(1)
    gz = lax.axis_index("gz").astype(jnp.int32).reshape(1)

    a, b = {}, {}
    for s in (1, 3, 2):
        a[s] = shifted(scale(lax.rem(gz + s, 4), normals, spectrum), "gz", s)
        b[s] = shifted(scale(4 + lax.rem(gy + s, 4), normals, spectrum), "gy", s)
    a[0] = scale(gz, normals, spectrum)
    b[0] = scale(4 + gy, normals, spectrum)

    part_a = first_part(True, gz, (a[0], a[1], a[3]), table_z)
    part_b = first_part(False, gy, (b[0], b[1], b[3]), table_y)
    a1, a3 = first_last(True, (1, 3), gz, gy, part_a, a[2], table_z)
    b1, b3 = first_last(False, (1, 3), gy, gz, part_b, b[2], table_y)
    a2, a0 = first_last(True, (2, 0), gz, gy, part_a, a[2], table_z)
    b2, b0 = first_last(False, (2, 0), gy, gz, part_b, b[2], table_y)
    a1, b1 = shifted(a1, "gy", 1), shifted(b1, "gz", 1)
    a3, b3 = shifted(a3, "gy", 3), shifted(b3, "gz", 3)
    a2, b2 = shifted(a2, "gy", 2), shifted(b2, "gz", 2)

    part_a = second_part(False, gy, (a0, a1, a3), table_y)
    part_b = second_part(True, gz, (b0, b1, b3), table_z)
    planes = second_last(gy, gz, part_a, a2, table_y, part_b, b2, table_z)
    planes, slots = lax.optimization_barrier((planes, slots_of(block_owner)))
    lines = lax.all_to_all(planes, ALL, split_axis=0, concat_axis=0, tiled=True)
    outgoing = third(slots, lines, table_x)
    return lax.all_to_all(
        outgoing.reshape(128, 1, CAP, 2, BW), ALL, split_axis=0, concat_axis=1, tiled=True
    )


def solution(mesh):
    placed = (P(None, "gx", "gy", "gz"), P("gx", "gy", "gz"), P(ALL, None))
    return jax.shard_map(
        per_device,
        mesh=mesh,
        in_specs=placed,
        out_specs=P(ALL, None, None, None, None),
        check_vma=False,
    )
```

```python
import functools

import jax
import jax.numpy as jnp
import ml_dtypes
import numpy as np
from jax import lax
from jax.experimental import pallas as pl
from jax.experimental.pallas import tpu as pltpu
from jax.sharding import PartitionSpec as P

N = 512
KEPT = 256
BW = 128
CAP = 16
ALL = ("gx", "gy", "gz")
MIB = 1 << 20
VMEM = 60


def split_table(table):
    high = table.astype(np.float32).astype(ml_dtypes.bfloat16)
    low = (table - high.astype(np.float64)).astype(np.float32).astype(ml_dtypes.bfloat16)
    return np.stack([high, low])


def cos_sin(positions, kept):
    angles = (positions[:, None] * kept[None, :] % N) * (2.0 * np.pi / N)
    return np.cos(angles), np.sin(angles)


@functools.cache
def tables():
    cosine, sine = cos_sin(np.arange(N), np.arange(KEPT))
    real_rows = np.concatenate([cosine, -sine], 1).reshape(4, 1, 128, 2 * KEPT)
    imag_rows = np.concatenate([sine, cosine], 1).reshape(4, 1, 128, 2 * KEPT)
    table_z = np.concatenate([real_rows, imag_rows], 1).reshape(4, 256, 2 * KEPT)
    order = np.arange(KEPT).reshape(KEPT // 2, 2).T.reshape(-1)
    cosine, sine = cos_sin(np.arange(N), order)
    cosine, sine = cosine.reshape(4, 128, KEPT), sine.reshape(4, 128, KEPT)
    top = np.concatenate([cosine, sine], 1)
    bottom = np.concatenate([-sine, cosine], 1)
    table_y = np.concatenate([top, bottom], 2).transpose(0, 2, 1)
    gx, gy, gz = np.meshgrid(np.arange(8), np.arange(4), np.arange(4), indexing="ij")
    first = 64 * gx + 8 * gz + 2 * gy
    second = 64 * gx + 32 + 8 * gy + 2 * gz
    cells = np.stack([first, first + 1, second, second + 1], -1).reshape(128, 4)
    cosine, sine = cos_sin(cells.reshape(-1), np.arange(KEPT))
    cosine = cosine.T.reshape(KEPT, 128, 1, 4)
    sine = sine.T.reshape(KEPT, 128, 1, 4)
    top = np.concatenate([cosine, sine], 2).reshape(KEPT, 1024)
    bottom = np.concatenate([-sine, cosine], 2).reshape(KEPT, 1024)
    table_x = np.concatenate([top, bottom], 0)
    return split_table(table_x), split_table(table_y), split_table(table_z)


def halves(values):
    high = values.astype(jnp.bfloat16)
    low = (values - high.astype(jnp.float32)).astype(jnp.bfloat16)
    return high, low


def product(left, right):
    def dot(a, b):
        return jnp.dot(a, b, preferred_element_type=jnp.float32)

    return dot(left[0], right[0]) + (dot(left[0], right[1]) + dot(left[1], right[0]))


def params(mib):
    return pltpu.CompilerParams(vmem_limit_bytes=mib * MIB)


def cost(multiplies, moved):
    return pl.CostEstimate(flops=6 * multiplies, bytes_accessed=moved, transcendentals=0)


def scale_kernel(place_ref, normals_ref, spectrum_ref, out_ref):
    out_ref[...] = normals_ref[...].astype(jnp.float32) * spectrum_ref[...][None]


def scale(chunk, normals, spectrum):
    return pl.pallas_call(
        scale_kernel,
        grid_spec=pltpu.PrefetchScalarGridSpec(
            num_scalar_prefetch=1,
            grid=(2,),
            in_specs=[
                pl.BlockSpec((2, 4, 128, 128), lambda i, chunk: (0, 2 * chunk[0] + i, 0, 0)),
                pl.BlockSpec((4, 128, 128), lambda i, chunk: (2 * chunk[0] + i, 0, 0)),
            ],
            out_specs=pl.BlockSpec((2, 4, 128, 128), lambda i, chunk: (0, i, 0, 0)),
        ),
        out_shape=jax.ShapeDtypeStruct((2, 8, 128, 128), jnp.float32),
        compiler_params=params(VMEM),
        cost_estimate=cost(1 << 18, 2 * MIB),
        name="scale",
    )(chunk, normals, spectrum)


def rows_z(piece):
    return halves(jnp.concatenate([piece[plane].reshape(-1, 128) for plane in range(2)], axis=1))


def columns_y(piece):
    planes, cells = piece.shape[:2]
    return halves(
        jnp.concatenate([piece[:, x].reshape(256, piece.shape[3]) for x in range(cells)], axis=1)
    )


def source(place, shift):
    return lax.rem(place + (4 - shift), 4)


def first_part_kernel(along_z, place_ref, p0, p1, p3, table_ref, out_ref):
    total = None
    for shift, piece in ((0, p0), (1, p1), (3, p3)):
        g = source(place_ref[0], shift)
        table = (table_ref[0, g], table_ref[1, g])
        if along_z:
            term = product(rows_z(piece[...]), table)
        else:
            term = product(table, columns_y(piece[...]))
        total = term if total is None else total + term
    out_ref[0] = total


def first_part(along_z, place, pieces, table):
    shape = (256, 512) if along_z else (512, 256)
    return pl.pallas_call(
        functools.partial(first_part_kernel, along_z),
        grid_spec=pltpu.PrefetchScalarGridSpec(
            num_scalar_prefetch=1,
            grid=(4,),
            in_specs=[pl.BlockSpec((2, 2, 128, 128), lambda i, place: (0, i, 0, 0))] * 3
            + [pl.BlockSpec((2, 4) + table.shape[2:], lambda i, place: (0, 0, 0, 0))],
            out_specs=pl.BlockSpec((1,) + shape, lambda i, place: (i, 0, 0)),
        ),
        out_shape=jax.ShapeDtypeStruct((4,) + shape, jnp.float32),
        compiler_params=params(VMEM),
        cost_estimate=cost(768 * 1024 * 512, 8 * MIB),
        name="first_part_z" if along_z else "first_part_y",
    )(place, *pieces, table)


def first_last_kernel(along_z, shifts, place_ref, to_ref, part_ref, p2, table_ref, *out_refs):
    table = (table_ref[0, 0], table_ref[1, 0])
    if along_z:
        total = part_ref[0] + product(rows_z(p2[...]), table)
    else:
        total = part_ref[0] + product(table, columns_y(p2[...]))
    for step, out_ref in enumerate(out_refs):

        @pl.when(pl.program_id(0) == step)
        def _():
            for plane in range(2):
                if along_z:
                    out_ref[plane] = total[:, plane * KEPT : (plane + 1) * KEPT].reshape(
                        2, 128, KEPT
                    )
                else:
                    for x in range(2):
                        out_ref[plane, x] = total[
                            plane * KEPT : (plane + 1) * KEPT, x * 128 : (x + 1) * 128
                        ]


def first_last(along_z, shifts, place, to, part, piece, table):
    def pair(i, to):
        shift = shifts[0]
        for step in range(1, len(shifts)):
            shift = jnp.where(i == step, shifts[step], shift)
        return lax.rem(to[0] + shift, 4)

    shape = (2, 2, 128, KEPT) if along_z else (2, 2, KEPT, 128)
    return pl.pallas_call(
        functools.partial(first_last_kernel, along_z, shifts),
        grid_spec=pltpu.PrefetchScalarGridSpec(
            num_scalar_prefetch=2,
            grid=(len(shifts),),
            in_specs=[
                pl.BlockSpec((1,) + part.shape[1:], lambda i, place, to: (pair(i, to), 0, 0)),
                pl.BlockSpec((2, 2, 128, 128), lambda i, place, to: (0, pair(i, to), 0, 0)),
                pl.BlockSpec(
                    (2, 1) + table.shape[2:],
                    lambda i, place, to: (0, lax.rem(place[0] + 2, 4), 0, 0),
                ),
            ],
            out_specs=[pl.BlockSpec(shape, lambda i, place, to: (0, 0, 0, 0))] * len(shifts),
        ),
        out_shape=[jax.ShapeDtypeStruct(shape, jnp.float32)] * len(shifts),
        compiler_params=params(VMEM),
        cost_estimate=cost(len(shifts) * 256 * 256 * 512, 2 * len(shifts) * MIB),
        name="first_last_z" if along_z else "first_last_y",
    )(place, to, part, piece, table)


def second_part_kernel(along_z, place_ref, p0, p1, p3, table_ref, out_ref):
    total = None
    for shift, piece in ((0, p0), (1, p1), (3, p3)):
        g = source(place_ref[0], shift)
        table = (table_ref[0, g], table_ref[1, g])
        if along_z:
            term = product(rows_z(piece[...]), table)
        else:
            term = product(table, columns_y(piece[...]))
        total = term if total is None else total + term
    out_ref[0] = total


def second_part(along_z, place, pieces, table):
    shape = (256, 512) if along_z else (512, 256)
    return pl.pallas_call(
        functools.partial(second_part_kernel, along_z),
        grid_spec=pltpu.PrefetchScalarGridSpec(
            num_scalar_prefetch=1,
            grid=(2,),
            in_specs=[
                pl.BlockSpec((2, 1) + pieces[0].shape[2:], lambda i, place: (0, i, 0, 0))
            ]
            * 3
            + [pl.BlockSpec((2, 4) + table.shape[2:], lambda i, place: (0, 0, 0, 0))],
            out_specs=pl.BlockSpec((1,) + shape, lambda i, place: (i, 0, 0)),
        ),
        out_shape=jax.ShapeDtypeStruct((2,) + shape, jnp.float32),
        compiler_params=params(VMEM),
        cost_estimate=cost(384 * 1024 * 512, 5 * MIB),
        name="second_part_z" if along_z else "second_part_y",
    )(place, *pieces, table)


def second_last_kernel(
    gy_ref, gz_ref, part_y, last_y, table_y_ref, part_z, last_z, table_z_ref, out_ref, held
):
    def put(values, row):
        for half in range(2):
            held[pl.ds(half * 8 + row, 128, stride=16), :] = values[
                :, half * 128 : (half + 1) * 128
            ]

    table = tuple(table_y_ref[i, 0].reshape(256, 256) for i in range(2))
    for x in range(2):
        total = part_y[x].reshape(256, KEPT) + product(table, columns_y(last_y[:, x : x + 1]))
        for plane in range(2):
            put(total[plane * 128 : (plane + 1) * 128], plane * 4 + x)
    table = (table_z_ref[0, 0], table_z_ref[1, 0])
    total = part_z[...].reshape(256, 512) + product(rows_z(last_z[...]), table)
    for x in range(2):
        for plane in range(2):
            put(
                total[x * 128 : (x + 1) * 128, plane * KEPT : (plane + 1) * KEPT],
                plane * 4 + 2 + x,
            )
    out_ref[...] = held[...].reshape(128, 1, 2, 8, 128)


def second_last(gy, gz, part_y, last_y, table_y, part_z, last_z, table_z):
    return pl.pallas_call(
        second_last_kernel,
        grid_spec=pltpu.PrefetchScalarGridSpec(
            num_scalar_prefetch=2,
            grid=(2,),
            in_specs=[
                pl.BlockSpec((2, 2, 128, KEPT), lambda i, gy, gz: (0, 0, i, 0)),
                pl.BlockSpec((2, 2, 128, KEPT), lambda i, gy, gz: (0, 0, 0, 0)),
                pl.BlockSpec(
                    (2, 1, 2, 128, 256), lambda i, gy, gz: (0, lax.rem(gy[0] + 2, 4), 0, i, 0)
                ),
                pl.BlockSpec((2, 128, 512), lambda i, gy, gz: (0, i, 0)),
                pl.BlockSpec((2, 2, 128, 128), lambda i, gy, gz: (0, 0, i, 0)),
                pl.BlockSpec(
                    (2, 1, 256, 512), lambda i, gy, gz: (0, lax.rem(gz[0] + 2, 4), 0, 0)
                ),
            ],
            out_specs=pl.BlockSpec((128, 1, 2, 8, 128), lambda i, gy, gz: (0, i, 0, 0, 0)),
            scratch_shapes=[pltpu.VMEM((2048, 128), jnp.float32)],
        ),
        out_shape=jax.ShapeDtypeStruct((128, 2, 2, 8, 128), jnp.float32),
        compiler_params=params(VMEM),
        cost_estimate=cost(256 * 1024 * 512, 6 * MIB),
        name="second_last",
    )(
        gy,
        gz,
        part_y.reshape(2, 2, KEPT, KEPT),
        last_y,
        table_y.reshape(2, 4, 2, KEPT, 256),
        part_z,
        last_z,
        table_z,
    )


def third_kernel(slot_ref, in_ref, table_ref, out_ref, held):
    parity = pl.program_id(0)

    @pl.when(parity == 0)
    def _():
        out_ref[...] = jnp.zeros_like(out_ref)

    columns = jnp.concatenate(
        [in_ref[:, 0, half].reshape(1024, 128) for half in range(2)], axis=1
    )
    values = jnp.exp(product((table_ref[0], table_ref[1]), halves(columns)))
    for plane in range(2):
        for half in range(2):
            held[plane, half] = values[
                plane * KEPT : (plane + 1) * KEPT, half * 128 : (half + 1) * 128
            ]

    def place_rows(group, carry):
        for offset in range(8):
            x = group * 8 + offset
            for half in range(2):
                slot = slot_ref[x * 4 + parity * 2 + half]
                for plane in range(2):
                    out_ref[pl.ds(slot * 2 + plane, 1), :] = held[plane, half, pl.ds(x, 1), :]
        return carry

    lax.fori_loop(0, KEPT // 8, place_rows, 0)


def third(slots, arrived, table_x):
    return pl.pallas_call(
        third_kernel,
        grid_spec=pltpu.PrefetchScalarGridSpec(
            num_scalar_prefetch=1,
            grid=(2,),
            in_specs=[
                pl.BlockSpec((128, 1, 2, 8, 128), lambda i, slots: (0, i, 0, 0, 0)),
                pl.BlockSpec((2, 512, 1024), lambda i, slots: (0, 0, 0)),
            ],
            out_specs=pl.BlockSpec((4096, 128), lambda i, slots: (0, 0)),
            scratch_shapes=[pltpu.VMEM((2, 2, KEPT, 128), jnp.float32)],
        ),
        out_shape=jax.ShapeDtypeStruct((4096, 128), jnp.float32),
        compiler_params=params(VMEM),
        cost_estimate=cost(512 * 1024 * 512, 6 * MIB),
        name="third",
    )(slots, arrived, table_x)


def shifted(piece, axis, shift):
    size = lax.axis_size(axis)
    return lax.ppermute(piece, axis, [(i, (i + shift) % size) for i in range(size)])


def slots_of(block_owner):
    destination = block_owner[:, 0]
    one_hot = (destination[:, None] == jnp.arange(128, dtype=jnp.int32)[None, :]).astype(jnp.int32)
    earlier = jnp.cumsum(one_hot, axis=0) - one_hot
    return destination * CAP + jnp.sum(earlier * one_hot, axis=1)


def per_device(normals, spectrum, block_owner):
    table_x, table_y, table_z = (jnp.asarray(table) for table in tables())
    gy = lax.axis_index("gy").astype(jnp.int32).reshape(1)
    gz = lax.axis_index("gz").astype(jnp.int32).reshape(1)

    a, b = {}, {}
    for s in (1, 3, 2):
        a[s] = shifted(scale(lax.rem(gz + s, 4), normals, spectrum), "gz", s)
        b[s] = shifted(scale(4 + lax.rem(gy + s, 4), normals, spectrum), "gy", s)
    a[0] = scale(gz, normals, spectrum)
    b[0] = scale(4 + gy, normals, spectrum)

    part_a = first_part(True, gz, (a[0], a[1], a[3]), table_z)
    part_b = first_part(False, gy, (b[0], b[1], b[3]), table_y)
    part_a, part_b = lax.optimization_barrier((part_a, part_b))
    a1, a3 = first_last(True, (1, 3), gz, gy, part_a, a[2], table_z)
    b1, b3 = first_last(False, (1, 3), gy, gz, part_b, b[2], table_y)
    a2, a0 = first_last(True, (2, 0), gz, gy, part_a, a[2], table_z)
    b2, b0 = first_last(False, (2, 0), gy, gz, part_b, b[2], table_y)
    a1, b1 = shifted(a1, "gy", 1), shifted(b1, "gz", 1)
    a3, b3 = shifted(a3, "gy", 3), shifted(b3, "gz", 3)
    a2, b2 = shifted(a2, "gy", 2), shifted(b2, "gz", 2)

    part_a = second_part(False, gy, (a0, a1, a3), table_y)
    part_b = second_part(True, gz, (b0, b1, b3), table_z)
    planes = second_last(gy, gz, part_a, a2, table_y, part_b, b2, table_z)
    planes, slots = lax.optimization_barrier((planes, slots_of(block_owner)))
    lines = lax.all_to_all(planes, ALL, split_axis=0, concat_axis=0, tiled=True)
    outgoing = third(slots, lines, table_x)
    return lax.all_to_all(
        outgoing.reshape(128, 1, CAP, 2, BW), ALL, split_axis=0, concat_axis=1, tiled=True
    )


def solution(mesh):
    placed = (P(None, "gx", "gy", "gz"), P("gx", "gy", "gz"), P(ALL, None))
    return jax.shard_map(
        per_device,
        mesh=mesh,
        in_specs=placed,
        out_specs=P(ALL, None, None, None, None),
        check_vma=False,
    )
```

```python
import functools

import jax
import jax.numpy as jnp
import ml_dtypes
import numpy as np
from jax import lax
from jax.experimental import pallas as pl
from jax.experimental.pallas import tpu as pltpu
from jax.sharding import PartitionSpec as P

N = 512
KEPT = 256
BW = 128
CAP = 16
ALL = ("gx", "gy", "gz")
MIB = 1 << 20
VMEM = 40


def split_table(table):
    high = table.astype(np.float32).astype(ml_dtypes.bfloat16)
    low = (table - high.astype(np.float64)).astype(np.float32).astype(ml_dtypes.bfloat16)
    return np.stack([high, low])


def cos_sin(positions, kept):
    angles = (positions[:, None] * kept[None, :] % N) * (2.0 * np.pi / N)
    return np.cos(angles), np.sin(angles)


@functools.cache
def tables():
    cosine, sine = cos_sin(np.arange(N), np.arange(KEPT))
    real_rows = np.concatenate([cosine, -sine], 1).reshape(4, 1, 128, 2 * KEPT)
    imag_rows = np.concatenate([sine, cosine], 1).reshape(4, 1, 128, 2 * KEPT)
    table_z = np.concatenate([real_rows, imag_rows], 1).reshape(4, 256, 2 * KEPT)
    order = np.arange(KEPT).reshape(KEPT // 2, 2).T.reshape(-1)
    cosine, sine = cos_sin(np.arange(N), order)
    cosine, sine = cosine.reshape(4, 128, KEPT), sine.reshape(4, 128, KEPT)
    top = np.concatenate([cosine, sine], 1)
    bottom = np.concatenate([-sine, cosine], 1)
    table_y = np.concatenate([top, bottom], 2).transpose(0, 2, 1)
    gx, gy, gz = np.meshgrid(np.arange(8), np.arange(4), np.arange(4), indexing="ij")
    first = 64 * gx + 8 * gz + 2 * gy
    second = 64 * gx + 32 + 8 * gy + 2 * gz
    cells = np.stack([first, first + 1, second, second + 1], -1).reshape(128, 4)
    cosine, sine = cos_sin(cells.reshape(-1), np.arange(KEPT))
    cosine = cosine.T.reshape(KEPT, 128, 1, 4)
    sine = sine.T.reshape(KEPT, 128, 1, 4)
    top = np.concatenate([cosine, sine], 2).reshape(KEPT, 1024)
    bottom = np.concatenate([-sine, cosine], 2).reshape(KEPT, 1024)
    table_x = np.concatenate([top, bottom], 0)
    return split_table(table_x), split_table(table_y), split_table(table_z)


def halves(values):
    high = values.astype(jnp.bfloat16)
    low = (values - high.astype(jnp.float32)).astype(jnp.bfloat16)
    return high, low


def product(left, right):
    def dot(a, b):
        return jnp.dot(a, b, preferred_element_type=jnp.float32)

    return dot(left[0], right[0]) + (dot(left[0], right[1]) + dot(left[1], right[0]))


def params(mib):
    return pltpu.CompilerParams(vmem_limit_bytes=mib * MIB)


def cost(multiplies, moved):
    return pl.CostEstimate(flops=6 * multiplies, bytes_accessed=moved, transcendentals=0)


def scale_kernel(rotated, place_ref, normals_ref, spectrum_ref, *out_refs):
    for shift, out_ref in enumerate(out_refs if rotated else range(4)):
        chunk = lax.rem(place_ref[0] + shift, 4) if rotated else shift
        values = normals_ref[:, chunk].astype(jnp.float32) * spectrum_ref[chunk][None]
        if rotated:
            out_ref[...] = values
        else:
            out_refs[0][shift] = values


def scale(half, rotated, place, normals, spectrum):
    if rotated:
        out_specs = [pl.BlockSpec((2, 1, 128, 128), lambda i, place: (0, i, 0, 0))] * 4
        out_shape = [jax.ShapeDtypeStruct((2, 8, 128, 128), jnp.float32)] * 4
    else:
        out_specs = pl.BlockSpec((4, 2, 1, 128, 128), lambda i, place: (0, 0, i, 0, 0))
        out_shape = jax.ShapeDtypeStruct((4, 2, 8, 128, 128), jnp.float32)
    return pl.pallas_call(
        functools.partial(scale_kernel, rotated),
        grid_spec=pltpu.PrefetchScalarGridSpec(
            num_scalar_prefetch=1,
            grid=(8,),
            in_specs=[
                pl.BlockSpec((2, 4, 1, 128, 128), lambda i, place: (0, half, i, 0, 0)),
                pl.BlockSpec((4, 1, 128, 128), lambda i, place: (half, i, 0, 0)),
            ],
            out_specs=out_specs,
        ),
        out_shape=out_shape,
        compiler_params=params(60),
        cost_estimate=cost(1 << 20, 8 * MIB),
        name="scale_b" if rotated else "scale_a",
    )(place, normals.reshape(2, 8, 8, 128, 128), spectrum.reshape(8, 8, 128, 128))


def rows_z(piece):
    return halves(jnp.concatenate([piece[plane].reshape(-1, 128) for plane in range(2)], axis=1))


def columns_y(piece):
    planes, cells = piece.shape[:2]
    return halves(
        jnp.concatenate([piece[:, x].reshape(256, piece.shape[3]) for x in range(cells)], axis=1)
    )


def source(place, shift):
    return lax.rem(place + (4 - shift), 4)


def part_kernel(place_ref, p0, p1, p3, table_ref, out_ref):
    total = None
    for shift, piece in ((0, p0), (1, p1), (3, p3)):
        g = source(place_ref[0], shift)
        term = product((table_ref[0, g], table_ref[1, g]), columns_y(piece[...]))
        total = term if total is None else total + term
    out_ref[0] = total


def part_y(place, pieces, cells, table):
    count, columns = pieces[0].shape[1], pieces[0].shape[3]
    return pl.pallas_call(
        part_kernel,
        grid_spec=pltpu.PrefetchScalarGridSpec(
            num_scalar_prefetch=1,
            grid=(count // cells,),
            in_specs=[
                pl.BlockSpec((2, cells, 128, columns), lambda i, place: (0, i, 0, 0))
            ]
            * 3
            + [pl.BlockSpec((2, 4, 512, 256), lambda i, place: (0, 0, 0, 0))],
            out_specs=pl.BlockSpec((1, 512, cells * columns), lambda i, place: (i, 0, 0)),
        ),
        out_shape=jax.ShapeDtypeStruct((count // cells, 512, cells * columns), jnp.float32),
        compiler_params=params(VMEM),
        cost_estimate=cost(count * columns * 768 * 512, 8 * MIB),
        name="part_y",
    )(place, *pieces, table)


def first_y_kernel(place_ref, part_ref, p2, table_ref, out_ref):
    table = (table_ref[0, 0], table_ref[1, 0])
    total = part_ref[0] + product(table, columns_y(p2[...]))
    for plane in range(2):
        for x in range(2):
            out_ref[0, plane, x] = total[
                plane * KEPT : (plane + 1) * KEPT, x * 128 : (x + 1) * 128
            ]


def first_y(place, part, piece, table):
    return pl.pallas_call(
        first_y_kernel,
        grid_spec=pltpu.PrefetchScalarGridSpec(
            num_scalar_prefetch=1,
            grid=(4,),
            in_specs=[
                pl.BlockSpec((1, 512, 256), lambda i, place: (i, 0, 0)),
                pl.BlockSpec((2, 2, 128, 128), lambda i, place: (0, i, 0, 0)),
                pl.BlockSpec(
                    (2, 1, 512, 256), lambda i, place: (0, lax.rem(place[0] + 2, 4), 0, 0)
                ),
            ],
            out_specs=pl.BlockSpec((1, 2, 2, KEPT, 128), lambda i, place: (i, 0, 0, 0, 0)),
        ),
        out_shape=jax.ShapeDtypeStruct((4, 2, 2, KEPT, 128), jnp.float32),
        compiler_params=params(VMEM),
        cost_estimate=cost(1024 * 256 * 512, 6 * MIB),
        name="first_y",
    )(place, part, piece, table)


def first_z_kernel(to_ref, in_ref, table_ref, *out_refs):
    total = None
    for g in range(4):
        term = product(rows_z(in_ref[g]), (table_ref[0, g], table_ref[1, g]))
        total = term if total is None else total + term
    for step, out_ref in enumerate(out_refs):

        @pl.when(pl.program_id(0) == step)
        def _():
            for plane in range(2):
                out_ref[plane] = total[:, plane * KEPT : (plane + 1) * KEPT].reshape(2, 128, KEPT)


def first_z(shifts, to, arrived, table):
    def pair(i, to):
        shift = shifts[0]
        for step in range(1, len(shifts)):
            shift = jnp.where(i == step, shifts[step], shift)
        return lax.rem(to[0] + shift, 4)

    shape = (2, 2, 128, KEPT)
    return pl.pallas_call(
        first_z_kernel,
        grid_spec=pltpu.PrefetchScalarGridSpec(
            num_scalar_prefetch=1,
            grid=(len(shifts),),
            in_specs=[
                pl.BlockSpec((4, 2, 2, 128, 128), lambda i, to: (0, 0, pair(i, to), 0, 0)),
                pl.BlockSpec((2, 4, 256, 512), lambda i, to: (0, 0, 0, 0)),
            ],
            out_specs=[pl.BlockSpec(shape, lambda i, to: (0, 0, 0, 0))] * len(shifts),
        ),
        out_shape=[jax.ShapeDtypeStruct(shape, jnp.float32)] * len(shifts),
        compiler_params=params(VMEM),
        cost_estimate=cost(len(shifts) * 256 * 1024 * 512, 2 * len(shifts) * MIB),
        name="first_z",
    )(to, arrived, table)


def second_kernel(gy_ref, part_ref, last_y, table_y_ref, in_z, table_z_ref, out_ref, held):
    def put(values, row):
        for half in range(2):
            held[pl.ds(half * 8 + row, 128, stride=16), :] = values[
                :, half * 128 : (half + 1) * 128
            ]

    total = None
    for g in range(4):
        term = product(rows_z(in_z[g]), (table_z_ref[0, g], table_z_ref[1, g]))
        total = term if total is None else total + term
    for x in range(2):
        for plane in range(2):
            put(
                total[x * 128 : (x + 1) * 128, plane * KEPT : (plane + 1) * KEPT],
                plane * 4 + 2 + x,
            )
    table = tuple(table_y_ref[i, 0].reshape(256, 256) for i in range(2))
    for x in range(2):
        total = part_ref[x].reshape(256, KEPT) + product(table, columns_y(last_y[:, x : x + 1]))
        for plane in range(2):
            put(total[plane * 128 : (plane + 1) * 128], plane * 4 + x)
    out_ref[...] = held[...].reshape(128, 1, 2, 8, 128)


def second(gy, part, last_y, table_y, arrived, table_z):
    return pl.pallas_call(
        second_kernel,
        grid_spec=pltpu.PrefetchScalarGridSpec(
            num_scalar_prefetch=1,
            grid=(2,),
            in_specs=[
                pl.BlockSpec((2, 2, 128, KEPT), lambda i, gy: (0, 0, i, 0)),
                pl.BlockSpec((2, 2, 128, KEPT), lambda i, gy: (0, 0, 0, 0)),
                pl.BlockSpec(
                    (2, 1, 2, 128, 256), lambda i, gy: (0, lax.rem(gy[0] + 2, 4), 0, i, 0)
                ),
                pl.BlockSpec((4, 2, 2, 128, 128), lambda i, gy: (0, 0, 0, i, 0)),
                pl.BlockSpec((2, 4, 256, 512), lambda i, gy: (0, 0, 0, 0)),
            ],
            out_specs=pl.BlockSpec((128, 1, 2, 8, 128), lambda i, gy: (0, i, 0, 0, 0)),
            scratch_shapes=[pltpu.VMEM((2048, 128), jnp.float32)],
        ),
        out_shape=jax.ShapeDtypeStruct((128, 2, 2, 8, 128), jnp.float32),
        compiler_params=params(VMEM),
        cost_estimate=cost(640 * 1024 * 512, 8 * MIB),
        name="second",
    )(
        gy,
        part.reshape(2, 2, KEPT, KEPT),
        last_y,
        table_y.reshape(2, 4, 2, KEPT, 256),
        arrived,
        table_z,
    )


def third_kernel(slot_ref, in_ref, table_ref, out_ref, held):
    parity = pl.program_id(0)

    @pl.when(parity == 0)
    def _():
        out_ref[...] = jnp.zeros_like(out_ref)

    columns = jnp.concatenate(
        [in_ref[:, 0, half].reshape(1024, 128) for half in range(2)], axis=1
    )
    values = jnp.exp(product((table_ref[0], table_ref[1]), halves(columns)))
    for plane in range(2):
        for half in range(2):
            held[plane, half] = values[
                plane * KEPT : (plane + 1) * KEPT, half * 128 : (half + 1) * 128
            ]

    def place_rows(group, carry):
        for offset in range(8):
            x = group * 8 + offset
            for half in range(2):
                slot = slot_ref[x * 4 + parity * 2 + half]
                for plane in range(2):
                    out_ref[pl.ds(slot * 2 + plane, 1), :] = held[plane, half, pl.ds(x, 1), :]
        return carry

    lax.fori_loop(0, KEPT // 8, place_rows, 0)


def third(slots, arrived, table_x):
    return pl.pallas_call(
        third_kernel,
        grid_spec=pltpu.PrefetchScalarGridSpec(
            num_scalar_prefetch=1,
            grid=(2,),
            in_specs=[
                pl.BlockSpec((128, 1, 2, 8, 128), lambda i, slots: (0, i, 0, 0, 0)),
                pl.BlockSpec((2, 512, 1024), lambda i, slots: (0, 0, 0)),
            ],
            out_specs=pl.BlockSpec((4096, 128), lambda i, slots: (0, 0)),
            scratch_shapes=[pltpu.VMEM((2, 2, KEPT, 128), jnp.float32)],
        ),
        out_shape=jax.ShapeDtypeStruct((4096, 128), jnp.float32),
        compiler_params=params(VMEM),
        cost_estimate=cost(512 * 1024 * 512, 6 * MIB),
        name="third",
    )(slots, arrived, table_x)


def shifted(piece, axis, shift):
    size = lax.axis_size(axis)
    return lax.ppermute(piece, axis, [(i, (i + shift) % size) for i in range(size)])


def slots_of(block_owner):
    destination = block_owner[:, 0]
    one_hot = (destination[:, None] == jnp.arange(128, dtype=jnp.int32)[None, :]).astype(jnp.int32)
    earlier = jnp.cumsum(one_hot, axis=0) - one_hot
    return destination * CAP + jnp.sum(earlier * one_hot, axis=1)


def per_device(normals, spectrum, block_owner):
    table_x, table_y, table_z = (jnp.asarray(table) for table in tables())
    gy = lax.axis_index("gy").astype(jnp.int32).reshape(1)
    gz = lax.axis_index("gz").astype(jnp.int32).reshape(1)

    a = scale(0, False, gz, normals, spectrum)
    a = lax.all_to_all(a, "gz", split_axis=0, concat_axis=0, tiled=True)
    b0, b1, b2, b3 = scale(1, True, gy, normals, spectrum)
    b1, b3, b2 = shifted(b1, "gy", 1), shifted(b3, "gy", 3), shifted(b2, "gy", 2)

    part_b = part_y(gy, (b0, b1, b3), 2, table_y)
    b = first_y(gy, part_b, b2, table_y)
    b = lax.all_to_all(b, "gz", split_axis=0, concat_axis=0, tiled=True)
    a1, a3 = first_z((1, 3), gy, a, table_z)
    a2, a0 = first_z((2, 0), gy, a, table_z)
    a1, a3, a2 = shifted(a1, "gy", 1), shifted(a3, "gy", 3), shifted(a2, "gy", 2)

    part_a = part_y(gy, (a0, a1, a3), 1, table_y)
    planes = second(gy, part_a, a2, table_y, b, table_z)
    planes, slots = lax.optimization_barrier((planes, slots_of(block_owner)))
    lines = lax.all_to_all(planes, ALL, split_axis=0, concat_axis=0, tiled=True)
    outgoing = third(slots, lines, table_x)
    return lax.all_to_all(
        outgoing.reshape(128, 1, CAP, 2, BW), ALL, split_axis=0, concat_axis=1, tiled=True
    )


def solution(mesh):
    placed = (P(None, "gx", "gy", "gz"), P("gx", "gy", "gz"), P(ALL, None))
    return jax.shard_map(
        per_device,
        mesh=mesh,
        in_specs=placed,
        out_specs=P(ALL, None, None, None, None),
        check_vma=False,
    )
```

```python
import functools

import jax
import jax.numpy as jnp
import ml_dtypes
import numpy as np
from jax import lax
from jax.experimental import pallas as pl
from jax.experimental.pallas import tpu as pltpu
from jax.sharding import PartitionSpec as P

N = 512
KEPT = 256
BW = 128
CAP = 16
ALL = ("gx", "gy", "gz")
MIB = 1 << 20
VMEM = 40


def split_table(table):
    high = table.astype(np.float32).astype(ml_dtypes.bfloat16)
    low = (table - high.astype(np.float64)).astype(np.float32).astype(ml_dtypes.bfloat16)
    return np.stack([high, low])


def cos_sin(positions, kept):
    angles = (positions[:, None] * kept[None, :] % N) * (2.0 * np.pi / N)
    return np.cos(angles), np.sin(angles)


@functools.cache
def tables():
    cosine, sine = cos_sin(np.arange(N), np.arange(KEPT))
    real_rows = np.concatenate([cosine, -sine], 1).reshape(4, 1, 128, 2 * KEPT)
    imag_rows = np.concatenate([sine, cosine], 1).reshape(4, 1, 128, 2 * KEPT)
    table_z = np.concatenate([real_rows, imag_rows], 1).reshape(4, 256, 2 * KEPT)
    order = np.arange(KEPT).reshape(KEPT // 2, 2).T.reshape(-1)
    cosine, sine = cos_sin(np.arange(N), order)
    cosine, sine = cosine.reshape(4, 128, KEPT), sine.reshape(4, 128, KEPT)
    top = np.concatenate([cosine, sine], 1)
    bottom = np.concatenate([-sine, cosine], 1)
    table_y = np.concatenate([top, bottom], 2).transpose(0, 2, 1)
    gx, gy, gz = np.meshgrid(np.arange(8), np.arange(4), np.arange(4), indexing="ij")
    first = 64 * gx + 8 * gz + 2 * gy
    second = 64 * gx + 32 + 8 * gy + 2 * gz
    cells = np.stack([first, first + 1, second, second + 1], -1).reshape(128, 4)
    cosine, sine = cos_sin(cells.reshape(-1), np.arange(KEPT))
    cosine = cosine.T.reshape(KEPT, 128, 1, 4)
    sine = sine.T.reshape(KEPT, 128, 1, 4)
    top = np.concatenate([cosine, sine], 2).reshape(KEPT, 1024)
    bottom = np.concatenate([-sine, cosine], 2).reshape(KEPT, 1024)
    table_x = np.concatenate([top, bottom], 0)
    return split_table(table_x), split_table(table_y), split_table(table_z)


def halves(values):
    high = values.astype(jnp.bfloat16)
    low = (values - high.astype(jnp.float32)).astype(jnp.bfloat16)
    return high, low


def product(left, right):
    def dot(a, b):
        return jnp.dot(a, b, preferred_element_type=jnp.float32)

    return dot(left[0], right[0]) + (dot(left[0], right[1]) + dot(left[1], right[0]))


def params(mib):
    return pltpu.CompilerParams(vmem_limit_bytes=mib * MIB)


def cost(multiplies, moved):
    return pl.CostEstimate(flops=6 * multiplies, bytes_accessed=moved, transcendentals=0)


def rows_z(piece):
    return halves(jnp.concatenate([piece[plane].reshape(-1, 128) for plane in range(2)], axis=1))


def columns_y(piece):
    planes, cells = piece.shape[:2]
    return halves(
        jnp.concatenate([piece[:, x].reshape(256, piece.shape[3]) for x in range(cells)], axis=1)
    )


def source(place, shift):
    return lax.rem(place + (4 - shift), 4)


def part_kernel(place_ref, p0, p1, p3, table_ref, out_ref):
    total = None
    for shift, piece in ((0, p0), (1, p1), (3, p3)):
        g = source(place_ref[0], shift)
        term = product((table_ref[0, g], table_ref[1, g]), columns_y(piece[...]))
        total = term if total is None else total + term
    out_ref[0] = total


def part_y(place, pieces, cells, table):
    count, columns = pieces[0].shape[1], pieces[0].shape[3]
    return pl.pallas_call(
        part_kernel,
        grid_spec=pltpu.PrefetchScalarGridSpec(
            num_scalar_prefetch=1,
            grid=(count // cells,),
            in_specs=[
                pl.BlockSpec((2, cells, 128, columns), lambda i, place: (0, i, 0, 0))
            ]
            * 3
            + [pl.BlockSpec((2, 4, 512, 256), lambda i, place: (0, 0, 0, 0))],
            out_specs=pl.BlockSpec((1, 512, cells * columns), lambda i, place: (i, 0, 0)),
        ),
        out_shape=jax.ShapeDtypeStruct((count // cells, 512, cells * columns), jnp.float32),
        compiler_params=params(VMEM),
        cost_estimate=cost(count * columns * 768 * 512, 8 * MIB),
        name="part_y",
    )(place, *pieces, table)


def first_y_kernel(place_ref, part_ref, p2, table_ref, out_ref):
    table = (table_ref[0, 0], table_ref[1, 0])
    total = part_ref[0] + product(table, columns_y(p2[...]))
    for plane in range(2):
        for x in range(2):
            out_ref[0, plane, x] = total[
                plane * KEPT : (plane + 1) * KEPT, x * 128 : (x + 1) * 128
            ]


def first_y(place, part, piece, table):
    return pl.pallas_call(
        first_y_kernel,
        grid_spec=pltpu.PrefetchScalarGridSpec(
            num_scalar_prefetch=1,
            grid=(4,),
            in_specs=[
                pl.BlockSpec((1, 512, 256), lambda i, place: (i, 0, 0)),
                pl.BlockSpec((2, 2, 128, 128), lambda i, place: (0, i, 0, 0)),
                pl.BlockSpec(
                    (2, 1, 512, 256), lambda i, place: (0, lax.rem(place[0] + 2, 4), 0, 0)
                ),
            ],
            out_specs=pl.BlockSpec((1, 2, 2, KEPT, 128), lambda i, place: (i, 0, 0, 0, 0)),
        ),
        out_shape=pltpu.HBM((4, 2, 2, KEPT, 128), jnp.float32),
        compiler_params=params(VMEM),
        cost_estimate=cost(1024 * 256 * 512, 6 * MIB),
        name="first_y",
    )(place, part, piece, table)


def first_z_kernel(to_ref, in_ref, table_ref, *out_refs):
    total = None
    for g in range(4):
        term = product(rows_z(in_ref[g]), (table_ref[0, g], table_ref[1, g]))
        total = term if total is None else total + term
    for step, out_ref in enumerate(out_refs):

        @pl.when(pl.program_id(0) == step)
        def _():
            for plane in range(2):
                out_ref[plane] = total[:, plane * KEPT : (plane + 1) * KEPT].reshape(2, 128, KEPT)


def first_z(shifts, to, arrived, table):
    def pair(i, to):
        shift = shifts[0]
        for step in range(1, len(shifts)):
            shift = jnp.where(i == step, shifts[step], shift)
        return lax.rem(to[0] + shift, 4)

    shape = (2, 2, 128, KEPT)
    return pl.pallas_call(
        first_z_kernel,
        grid_spec=pltpu.PrefetchScalarGridSpec(
            num_scalar_prefetch=1,
            grid=(len(shifts),),
            in_specs=[
                pl.BlockSpec((4, 2, 2, 128, 128), lambda i, to: (0, 0, pair(i, to), 0, 0)),
                pl.BlockSpec((2, 4, 256, 512), lambda i, to: (0, 0, 0, 0)),
            ],
            out_specs=[pl.BlockSpec(shape, lambda i, to: (0, 0, 0, 0))] * len(shifts),
        ),
        out_shape=[jax.ShapeDtypeStruct(shape, jnp.float32)] * len(shifts),
        compiler_params=params(VMEM),
        cost_estimate=cost(len(shifts) * 256 * 1024 * 512, 2 * len(shifts) * MIB),
        name="first_z",
    )(to, arrived, table)


def second_z_kernel(in_ref, table_ref, out_ref):
    total = None
    for g in range(4):
        term = product(rows_z(in_ref[g]), (table_ref[0, g], table_ref[1, g]))
        total = term if total is None else total + term
    out_ref[0] = total


def second_z(arrived, table):
    return pl.pallas_call(
        second_z_kernel,
        grid=(2,),
        in_specs=[
            pl.BlockSpec((4, 2, 1, KEPT, 128), lambda i: (0, 0, i, 0, 0)),
            pl.BlockSpec((2, 4, 256, 512), lambda i: (0, 0, 0, 0)),
        ],
        out_specs=pl.BlockSpec((1, KEPT, 512), lambda i: (i, 0, 0)),
        out_shape=jax.ShapeDtypeStruct((2, KEPT, 512), jnp.float32),
        compiler_params=params(VMEM),
        cost_estimate=cost(512 * 1024 * 512, 5 * MIB),
        name="second_z",
    )(arrived, table)


def second_kernel(gy_ref, part_ref, last_y, table_y_ref, in_z, out_ref, held):
    def put(values, row):
        for half in range(2):
            held[pl.ds(half * 8 + row, 128, stride=16), :] = values[
                :, half * 128 : (half + 1) * 128
            ]

    for x in range(2):
        for plane in range(2):
            put(in_z[x, :, plane * KEPT : (plane + 1) * KEPT], plane * 4 + 2 + x)
    table = tuple(table_y_ref[i, 0].reshape(256, 256) for i in range(2))
    for x in range(2):
        total = part_ref[x].reshape(256, KEPT) + product(table, columns_y(last_y[:, x : x + 1]))
        for plane in range(2):
            put(total[plane * 128 : (plane + 1) * 128], plane * 4 + x)
    out_ref[...] = held[...].reshape(128, 1, 2, 8, 128)


def second(gy, part, last_y, table_y, done_z):
    return pl.pallas_call(
        second_kernel,
        grid_spec=pltpu.PrefetchScalarGridSpec(
            num_scalar_prefetch=1,
            grid=(2,),
            in_specs=[
                pl.BlockSpec((2, 2, 128, KEPT), lambda i, gy: (0, 0, i, 0)),
                pl.BlockSpec((2, 2, 128, KEPT), lambda i, gy: (0, 0, 0, 0)),
                pl.BlockSpec(
                    (2, 1, 2, 128, 256), lambda i, gy: (0, lax.rem(gy[0] + 2, 4), 0, i, 0)
                ),
                pl.BlockSpec((2, 128, 512), lambda i, gy: (0, i, 0)),
            ],
            out_specs=pl.BlockSpec((128, 1, 2, 8, 128), lambda i, gy: (0, i, 0, 0, 0)),
            scratch_shapes=[pltpu.VMEM((2048, 128), jnp.float32)],
        ),
        out_shape=pltpu.HBM((128, 2, 2, 8, 128), jnp.float32),
        compiler_params=params(VMEM),
        cost_estimate=cost(128 * 1024 * 512, 8 * MIB),
        name="second",
    )(gy, part.reshape(2, 2, KEPT, KEPT), last_y, table_y.reshape(2, 4, 2, KEPT, 256), done_z)


def third_kernel(slot_ref, in_ref, table_ref, out_ref, held):
    parity = pl.program_id(0)

    @pl.when(parity == 0)
    def _():
        out_ref[...] = jnp.zeros_like(out_ref)

    columns = jnp.concatenate(
        [in_ref[:, 0, half].reshape(1024, 128) for half in range(2)], axis=1
    )
    values = jnp.exp(product((table_ref[0], table_ref[1]), halves(columns)))
    for plane in range(2):
        for half in range(2):
            held[plane, half] = values[
                plane * KEPT : (plane + 1) * KEPT, half * 128 : (half + 1) * 128
            ]

    def place_rows(group, carry):
        for offset in range(8):
            x = group * 8 + offset
            for half in range(2):
                slot = slot_ref[x * 4 + parity * 2 + half]
                for plane in range(2):
                    out_ref[pl.ds(slot * 2 + plane, 1), :] = held[plane, half, pl.ds(x, 1), :]
        return carry

    lax.fori_loop(0, KEPT // 8, place_rows, 0)


def third(slots, arrived, table_x):
    return pl.pallas_call(
        third_kernel,
        grid_spec=pltpu.PrefetchScalarGridSpec(
            num_scalar_prefetch=1,
            grid=(2,),
            in_specs=[
                pl.BlockSpec((128, 1, 2, 8, 128), lambda i, slots: (0, i, 0, 0, 0)),
                pl.BlockSpec((2, 512, 1024), lambda i, slots: (0, 0, 0)),
            ],
            out_specs=pl.BlockSpec((4096, 128), lambda i, slots: (0, 0)),
            scratch_shapes=[pltpu.VMEM((2, 2, KEPT, 128), jnp.float32)],
        ),
        out_shape=pltpu.HBM((4096, 128), jnp.float32),
        compiler_params=params(VMEM),
        cost_estimate=cost(512 * 1024 * 512, 6 * MIB),
        name="third",
    )(slots, arrived, table_x)


def shifted(piece, axis, shift):
    size = lax.axis_size(axis)
    return lax.ppermute(piece, axis, [(i, (i + shift) % size) for i in range(size)])


def slots_of(block_owner):
    destination = block_owner[:, 0]
    one_hot = (destination[:, None] == jnp.arange(128, dtype=jnp.int32)[None, :]).astype(jnp.int32)
    earlier = jnp.cumsum(one_hot, axis=0) - one_hot
    return destination * CAP + jnp.sum(earlier * one_hot, axis=1)


def per_device(normals, spectrum, block_owner):
    table_x, table_y, table_z = (jnp.asarray(table) for table in tables())
    gy = lax.axis_index("gy").astype(jnp.int32).reshape(1)
    gz = lax.axis_index("gz").astype(jnp.int32).reshape(1)

    def chunk_b(shift):
        start = 32 + 8 * lax.rem(gy[0] + shift, 4)
        return lax.dynamic_slice_in_dim(spectrum, start, 8, 0)[None] * lax.dynamic_slice_in_dim(
            normals, start, 8, 1
        ).astype(jnp.float32)

    b1, b3 = chunk_b(1), chunk_b(3)
    b1, b3, normals, spectrum = lax.optimization_barrier((b1, b3, normals, spectrum))
    b1, b3 = shifted(b1, "gy", 1), shifted(b3, "gy", 3)
    a = spectrum[:32].reshape(4, 1, 8, 128, 128) * normals[:, :32].astype(jnp.float32).reshape(
        2, 4, 8, 128, 128
    ).transpose(1, 0, 2, 3, 4)
    a, normals, spectrum = lax.optimization_barrier((a, normals, spectrum))
    a = lax.all_to_all(a, "gz", split_axis=0, concat_axis=0, tiled=True)
    b2, b0 = shifted(chunk_b(2), "gy", 2), chunk_b(0)

    part_b = part_y(gy, (b0, b1, b3), 2, table_y)
    b = first_y(gy, part_b, b2, table_y)
    b = lax.all_to_all(b, "gz", split_axis=0, concat_axis=0, tiled=True)
    a1, a3 = first_z((1, 3), gy, a, table_z)
    a2, a0 = first_z((2, 0), gy, a, table_z)
    a1, a3, a2 = shifted(a1, "gy", 1), shifted(a3, "gy", 3), shifted(a2, "gy", 2)

    part_a = part_y(gy, (a0, a1, a3), 1, table_y)
    done_b = second_z(b, table_z)
    done_b, part_a, a2 = lax.optimization_barrier((done_b, part_a, a2))
    planes = second(gy, part_a, a2, table_y, done_b)
    planes, slots = lax.optimization_barrier((planes, slots_of(block_owner)))
    lines = lax.all_to_all(planes, ALL, split_axis=0, concat_axis=0, tiled=True)
    outgoing = third(slots, lines, table_x)
    return lax.all_to_all(
        outgoing.reshape(128, 1, CAP, 2, BW), ALL, split_axis=0, concat_axis=1, tiled=True
    )


def solution(mesh):
    placed = (P(None, "gx", "gy", "gz"), P("gx", "gy", "gz"), P(ALL, None))
    return jax.shard_map(
        per_device,
        mesh=mesh,
        in_specs=placed,
        out_specs=P(ALL, None, None, None, None),
        check_vma=False,
    )
```

```python
import functools

import jax
import jax.numpy as jnp
import ml_dtypes
import numpy as np
from jax import lax
from jax.experimental import pallas as pl
from jax.experimental.pallas import tpu as pltpu
from jax.sharding import PartitionSpec as P

N = 512
KEPT = 256
BW = 128
CAP = 16
ALL = ("gx", "gy", "gz")
MIB = 1 << 20
VMEM = 40


def split_table(table):
    high = table.astype(np.float32).astype(ml_dtypes.bfloat16)
    low = (table - high.astype(np.float64)).astype(np.float32).astype(ml_dtypes.bfloat16)
    return np.stack([high, low])


def cos_sin(positions, kept):
    angles = (positions[:, None] * kept[None, :] % N) * (2.0 * np.pi / N)
    return np.cos(angles), np.sin(angles)


@functools.cache
def tables():
    cosine, sine = cos_sin(np.arange(N), np.arange(KEPT))
    real_rows = np.concatenate([cosine, -sine], 1).reshape(4, 1, 128, 2 * KEPT)
    imag_rows = np.concatenate([sine, cosine], 1).reshape(4, 1, 128, 2 * KEPT)
    table_z = np.concatenate([real_rows, imag_rows], 1).reshape(4, 256, 2 * KEPT)
    order = np.arange(KEPT).reshape(KEPT // 2, 2).T.reshape(-1)
    cosine, sine = cos_sin(np.arange(N), order)
    cosine, sine = cosine.reshape(4, 128, KEPT), sine.reshape(4, 128, KEPT)
    top = np.concatenate([cosine, sine], 1)
    bottom = np.concatenate([-sine, cosine], 1)
    table_y = np.concatenate([top, bottom], 2).transpose(0, 2, 1)
    gx, gy, gz = np.meshgrid(np.arange(8), np.arange(4), np.arange(4), indexing="ij")
    first = 64 * gx + 8 * gz + 2 * gy
    second = 64 * gx + 32 + 8 * gy + 2 * gz
    cells = np.stack([first, first + 1, second, second + 1], -1).reshape(128, 4)
    cosine, sine = cos_sin(cells.reshape(-1), np.arange(KEPT))
    cosine = cosine.T.reshape(KEPT, 128, 1, 4)
    sine = sine.T.reshape(KEPT, 128, 1, 4)
    top = np.concatenate([cosine, sine], 2).reshape(KEPT, 1024)
    bottom = np.concatenate([-sine, cosine], 2).reshape(KEPT, 1024)
    table_x = np.concatenate([top, bottom], 0)
    return split_table(table_x), split_table(table_y), split_table(table_z)


def halves(values):
    high = values.astype(jnp.bfloat16)
    low = (values - high.astype(jnp.float32)).astype(jnp.bfloat16)
    return high, low


def product(left, right):
    def dot(a, b):
        return jnp.dot(a, b, preferred_element_type=jnp.float32)

    return dot(left[0], right[0]) + (dot(left[0], right[1]) + dot(left[1], right[0]))


def params(mib):
    return pltpu.CompilerParams(vmem_limit_bytes=mib * MIB)


def cost(multiplies, moved):
    return pl.CostEstimate(flops=6 * multiplies, bytes_accessed=moved, transcendentals=0)


def rows_z(piece):
    return halves(jnp.concatenate([piece[plane].reshape(-1, 128) for plane in range(2)], axis=1))


def columns_y(piece):
    planes, cells = piece.shape[:2]
    return halves(
        jnp.concatenate([piece[:, x].reshape(256, piece.shape[3]) for x in range(cells)], axis=1)
    )


def term_of(along_z, piece, table_ref, g):
    table = (table_ref[0, g], table_ref[1, g])
    if along_z:
        return product(rows_z(piece), table)
    return product(table, columns_y(piece))


def sum_kernel(along_z, place_ref, *refs):
    *pieces, table_ref, out_ref = refs
    total = None
    for shift, piece in zip((0, 1, 3), pieces):
        g = lax.rem(place_ref[0] + (4 - shift), 4)
        term = term_of(along_z, piece[...], table_ref, g)
        total = term if total is None else total + term
    out_ref[0] = total


def part_sum(along_z, place, pieces, cells, table):
    _, count, lines, columns = pieces[0].shape
    shape = (cells * lines, 512) if along_z else (512, cells * columns)
    return pl.pallas_call(
        functools.partial(sum_kernel, along_z),
        grid_spec=pltpu.PrefetchScalarGridSpec(
            num_scalar_prefetch=1,
            grid=(count // cells,),
            in_specs=[
                pl.BlockSpec((2, cells, lines, columns), lambda i, place: (0, i, 0, 0))
            ]
            * 3
            + [pl.BlockSpec(table.shape, lambda i, place: (0, 0, 0, 0))],
            out_specs=pl.BlockSpec((1,) + shape, lambda i, place: (i, 0, 0)),
        ),
        out_shape=jax.ShapeDtypeStruct((count // cells,) + shape, jnp.float32),
        compiler_params=params(VMEM),
        cost_estimate=cost(count // cells * shape[0] * shape[1] * 768, 8 * MIB),
        name="part_z" if along_z else "part_y",
    )(place, *pieces, table)


def first_y_kernel(place_ref, to_ref, part_ref, p2, table_ref, *out_refs):
    total = part_ref[0] + term_of(False, p2[...], table_ref, 0)
    for step, out_ref in enumerate(out_refs):

        @pl.when(pl.program_id(0) == step)
        def _():
            for plane in range(2):
                for x in range(2):
                    out_ref[plane, x] = total[
                        plane * KEPT : (plane + 1) * KEPT, x * 128 : (x + 1) * 128
                    ]


def first_y(shifts, place, to, part, piece, table):
    def pair(i, to):
        return lax.rem(to[0] + jnp.where(i == 0, shifts[0], shifts[1]), 4)

    shape = (2, 2, KEPT, 128)
    return pl.pallas_call(
        first_y_kernel,
        grid_spec=pltpu.PrefetchScalarGridSpec(
            num_scalar_prefetch=2,
            grid=(2,),
            in_specs=[
                pl.BlockSpec((1, 512, 256), lambda i, place, to: (pair(i, to), 0, 0)),
                pl.BlockSpec((2, 2, 128, 128), lambda i, place, to: (0, pair(i, to), 0, 0)),
                pl.BlockSpec(
                    (2, 1, 512, 256), lambda i, place, to: (0, lax.rem(place[0] + 2, 4), 0, 0)
                ),
            ],
            out_specs=[pl.BlockSpec(shape, lambda i, place, to: (0, 0, 0, 0))] * 2,
        ),
        out_shape=[jax.ShapeDtypeStruct(shape, jnp.float32)] * 2,
        compiler_params=params(VMEM),
        cost_estimate=cost(512 * 256 * 512, 4 * MIB),
        name="first_y",
    )(place, to, part, piece, table)


def first_z_kernel(in_ref, table_ref, out_ref):
    total = None
    for g in range(4):
        term = term_of(True, in_ref[g], table_ref, g)
        total = term if total is None else total + term
    for plane in range(2):
        out_ref[0, plane] = total[:, plane * KEPT : (plane + 1) * KEPT].reshape(2, 128, KEPT)


def first_z(arrived, table):
    return pl.pallas_call(
        first_z_kernel,
        grid=(4,),
        in_specs=[
            pl.BlockSpec((4, 2, 2, 128, 128), lambda i: (0, 0, i, 0, 0)),
            pl.BlockSpec((2, 4, 256, 512), lambda i: (0, 0, 0, 0)),
        ],
        out_specs=pl.BlockSpec((1, 2, 2, 128, KEPT), lambda i: (i, 0, 0, 0, 0)),
        out_shape=pltpu.HBM((4, 2, 2, 128, KEPT), jnp.float32),
        compiler_params=params(VMEM),
        cost_estimate=cost(1024 * 1024 * 512, 8 * MIB),
        name="first_z",
    )(arrived, table)


def second_y_kernel(in_ref, table_ref, out_ref):
    total = None
    for g in range(4):
        term = term_of(False, in_ref[g], table_ref, g)
        total = term if total is None else total + term
    out_ref[0] = total


def second_y(arrived, table):
    return pl.pallas_call(
        second_y_kernel,
        grid=(2,),
        in_specs=[
            pl.BlockSpec((4, 2, 1, 128, KEPT), lambda i: (0, 0, i, 0, 0)),
            pl.BlockSpec((2, 4, 512, 256), lambda i: (0, 0, 0, 0)),
        ],
        out_specs=pl.BlockSpec((1, 512, KEPT), lambda i: (i, 0, 0)),
        out_shape=jax.ShapeDtypeStruct((2, 512, KEPT), jnp.float32),
        compiler_params=params(VMEM),
        cost_estimate=cost(512 * 1024 * 512, 5 * MIB),
        name="second_y",
    )(arrived, table)


def second_kernel(gz_ref, done_y, part_ref, last_z, table_ref, out_ref, held):
    def put(values, row):
        for half in range(2):
            held[pl.ds(half * 8 + row, 128, stride=16), :] = values[
                :, half * 128 : (half + 1) * 128
            ]

    for x in range(2):
        for plane in range(2):
            put(done_y[x, plane], plane * 4 + x)
    total = part_ref[...].reshape(256, 512) + term_of(True, last_z[...], table_ref, 0)
    for x in range(2):
        for plane in range(2):
            put(
                total[x * 128 : (x + 1) * 128, plane * KEPT : (plane + 1) * KEPT],
                plane * 4 + 2 + x,
            )
    out_ref[...] = held[...].reshape(128, 1, 2, 8, 128)


def second(gz, done_y, part, last_z, table):
    return pl.pallas_call(
        second_kernel,
        grid_spec=pltpu.PrefetchScalarGridSpec(
            num_scalar_prefetch=1,
            grid=(2,),
            in_specs=[
                pl.BlockSpec((2, 2, 128, KEPT), lambda i, gz: (0, 0, i, 0)),
                pl.BlockSpec((2, 128, 512), lambda i, gz: (0, i, 0)),
                pl.BlockSpec((2, 2, 128, 128), lambda i, gz: (0, 0, i, 0)),
                pl.BlockSpec((2, 1, 256, 512), lambda i, gz: (0, lax.rem(gz[0] + 2, 4), 0, 0)),
            ],
            out_specs=pl.BlockSpec((128, 1, 2, 8, 128), lambda i, gz: (0, i, 0, 0, 0)),
            scratch_shapes=[pltpu.VMEM((2048, 128), jnp.float32)],
        ),
        out_shape=jax.ShapeDtypeStruct((128, 2, 2, 8, 128), jnp.float32),
        compiler_params=params(VMEM),
        cost_estimate=cost(128 * 1024 * 512, 8 * MIB),
        name="second",
    )(gz, done_y.reshape(2, 2, KEPT, KEPT), part, last_z, table)


def third_kernel(slot_ref, in_ref, table_ref, out_ref, held):
    parity = pl.program_id(0)

    @pl.when(parity == 0)
    def _():
        out_ref[...] = jnp.zeros_like(out_ref)

    columns = jnp.concatenate(
        [in_ref[:, 0, half].reshape(1024, 128) for half in range(2)], axis=1
    )
    values = jnp.exp(product((table_ref[0], table_ref[1]), halves(columns)))
    for plane in range(2):
        for half in range(2):
            held[plane, half] = values[
                plane * KEPT : (plane + 1) * KEPT, half * 128 : (half + 1) * 128
            ]

    def place_rows(group, carry):
        for offset in range(8):
            x = group * 8 + offset
            for half in range(2):
                slot = slot_ref[x * 4 + parity * 2 + half]
                for plane in range(2):
                    out_ref[pl.ds(slot * 2 + plane, 1), :] = held[plane, half, pl.ds(x, 1), :]
        return carry

    lax.fori_loop(0, KEPT // 8, place_rows, 0)


def third(slots, arrived, table_x):
    return pl.pallas_call(
        third_kernel,
        grid_spec=pltpu.PrefetchScalarGridSpec(
            num_scalar_prefetch=1,
            grid=(2,),
            in_specs=[
                pl.BlockSpec((128, 1, 2, 8, 128), lambda i, slots: (0, i, 0, 0, 0)),
                pl.BlockSpec((2, 512, 1024), lambda i, slots: (0, 0, 0)),
            ],
            out_specs=pl.BlockSpec((4096, 128), lambda i, slots: (0, 0)),
            scratch_shapes=[pltpu.VMEM((2, 2, KEPT, 128), jnp.float32)],
        ),
        out_shape=jax.ShapeDtypeStruct((4096, 128), jnp.float32),
        compiler_params=params(VMEM),
        cost_estimate=cost(512 * 1024 * 512, 6 * MIB),
        name="third",
    )(slots, arrived, table_x)


def shifted(piece, axis, shift):
    size = lax.axis_size(axis)
    return lax.ppermute(piece, axis, [(i, (i + shift) % size) for i in range(size)])


def slots_of(block_owner):
    destination = block_owner[:, 0]
    one_hot = (destination[:, None] == jnp.arange(128, dtype=jnp.int32)[None, :]).astype(jnp.int32)
    earlier = jnp.cumsum(one_hot, axis=0) - one_hot
    return destination * CAP + jnp.sum(earlier * one_hot, axis=1)


def per_device(normals, spectrum, block_owner):
    table_x, table_y, table_z = (jnp.asarray(table) for table in tables())
    gy = lax.axis_index("gy").astype(jnp.int32).reshape(1)
    gz = lax.axis_index("gz").astype(jnp.int32).reshape(1)

    def chunk_b(shift):
        start = 32 + 8 * lax.rem(gy[0] + shift, 4)
        return lax.dynamic_slice_in_dim(spectrum, start, 8, 0)[None] * lax.dynamic_slice_in_dim(
            normals, start, 8, 1
        ).astype(jnp.float32)

    a = spectrum[:32].reshape(4, 1, 8, 128, 128) * normals[:, :32].astype(jnp.float32).reshape(
        2, 4, 8, 128, 128
    ).transpose(1, 0, 2, 3, 4)
    a, normals, spectrum = lax.optimization_barrier((a, normals, spectrum))
    a = lax.all_to_all(a, "gz", split_axis=0, concat_axis=0, tiled=True)
    b1, b3, b2 = shifted(chunk_b(1), "gy", 1), shifted(chunk_b(3), "gy", 3), shifted(chunk_b(2), "gy", 2)
    b0 = chunk_b(0)

    part_b = part_sum(False, gy, (b0, b1, b3), 2, table_y)
    a = first_z(a, table_z)
    a, part_b, b2 = lax.optimization_barrier((a, part_b, b2))
    a = lax.all_to_all(a, "gy", split_axis=0, concat_axis=0, tiled=True)
    b1, b3 = first_y((1, 3), gy, gz, part_b, b2, table_y)
    b1, b3 = shifted(b1, "gz", 1), shifted(b3, "gz", 3)
    b2, b0 = first_y((2, 0), gy, gz, part_b, b2, table_y)
    b2 = shifted(b2, "gz", 2)

    part_b = part_sum(True, gz, (b0, b1, b3), 1, table_z)
    a = second_y(a, table_y)
    a, part_b, b2 = lax.optimization_barrier((a, part_b, b2))
    planes = second(gz, a, part_b, b2, table_z)
    planes, slots = lax.optimization_barrier((planes, slots_of(block_owner)))
    lines = lax.all_to_all(planes, ALL, split_axis=0, concat_axis=0, tiled=True)
    outgoing = third(slots, lines, table_x)
    return lax.all_to_all(
        outgoing.reshape(128, 1, CAP, 2, BW), ALL, split_axis=0, concat_axis=1, tiled=True
    )


def solution(mesh):
    placed = (P(None, "gx", "gy", "gz"), P("gx", "gy", "gz"), P(ALL, None))
    return jax.shard_map(
        per_device,
        mesh=mesh,
        in_specs=placed,
        out_specs=P(ALL, None, None, None, None),
        check_vma=False,
    )
```

```python
import functools

import jax
import jax.numpy as jnp
import ml_dtypes
import numpy as np
from jax import lax
from jax.experimental import pallas as pl
from jax.experimental.pallas import tpu as pltpu
from jax.sharding import PartitionSpec as P

N = 512
KEPT = 256
BW = 128
CAP = 16
ALL = ("gx", "gy", "gz")
MIB = 1 << 20
VMEM = 24


def split_table(table):
    high = table.astype(np.float32).astype(ml_dtypes.bfloat16)
    low = (table - high.astype(np.float64)).astype(np.float32).astype(ml_dtypes.bfloat16)
    return np.stack([high, low])


def cos_sin(positions, kept):
    angles = (positions[:, None] * kept[None, :] % N) * (2.0 * np.pi / N)
    return np.cos(angles), np.sin(angles)


@functools.cache
def tables():
    cosine, sine = cos_sin(np.arange(N), np.arange(KEPT))
    real_rows = np.concatenate([cosine, -sine], 1).reshape(4, 1, 128, 2 * KEPT)
    imag_rows = np.concatenate([sine, cosine], 1).reshape(4, 1, 128, 2 * KEPT)
    table_z = np.concatenate([real_rows, imag_rows], 1).reshape(4, 256, 2 * KEPT)
    order = np.arange(KEPT).reshape(KEPT // 2, 2).T.reshape(-1)
    cosine, sine = cos_sin(np.arange(N), order)
    cosine, sine = cosine.reshape(4, 128, KEPT), sine.reshape(4, 128, KEPT)
    top = np.concatenate([cosine, sine], 1)
    bottom = np.concatenate([-sine, cosine], 1)
    table_y = np.concatenate([top, bottom], 2).transpose(0, 2, 1)
    gx, gy, gz = np.meshgrid(np.arange(8), np.arange(4), np.arange(4), indexing="ij")
    first = 64 * gx + 8 * gz + 2 * gy
    second = 64 * gx + 32 + 8 * gy + 2 * gz
    cells = np.stack([first, first + 1, second, second + 1], -1).reshape(128, 4)
    cosine, sine = cos_sin(cells.reshape(-1), np.arange(KEPT))
    cosine = cosine.T.reshape(KEPT, 128, 1, 4)
    sine = sine.T.reshape(KEPT, 128, 1, 4)
    top = np.concatenate([cosine, sine], 2).reshape(KEPT, 1024)
    bottom = np.concatenate([-sine, cosine], 2).reshape(KEPT, 1024)
    table_x = np.concatenate([top, bottom], 0)
    return split_table(table_x), split_table(table_y), split_table(table_z)


def halves(values):
    high = values.astype(jnp.bfloat16)
    low = (values - high.astype(jnp.float32)).astype(jnp.bfloat16)
    return high, low


def product(left, right):
    def dot(a, b):
        return jnp.dot(a, b, preferred_element_type=jnp.float32)

    return dot(left[0], right[0]) + (dot(left[0], right[1]) + dot(left[1], right[0]))


def params(mib):
    return pltpu.CompilerParams(vmem_limit_bytes=mib * MIB)


def cost(multiplies, moved):
    return pl.CostEstimate(flops=6 * multiplies, bytes_accessed=moved, transcendentals=0)


def rows_z(piece):
    return halves(jnp.concatenate([piece[plane].reshape(-1, 128) for plane in range(2)], axis=1))


def columns_y(piece):
    planes, cells = piece.shape[:2]
    return halves(
        jnp.concatenate([piece[:, x].reshape(256, piece.shape[3]) for x in range(cells)], axis=1)
    )


def term_of(along_z, piece, table_ref, g):
    table = (table_ref[0, g], table_ref[1, g])
    if along_z:
        return product(rows_z(piece), table)
    return product(table, columns_y(piece))


def sum_kernel(along_z, place_ref, *refs):
    *pieces, table_ref, out_ref = refs
    total = None
    for shift, piece in zip((0, 1, 3), pieces):
        g = lax.rem(place_ref[0] + (4 - shift), 4)
        term = term_of(along_z, piece[...], table_ref, g)
        total = term if total is None else total + term
    out_ref[0] = total


def part_sum(along_z, place, pieces, cells, table):
    _, count, lines, columns = pieces[0].shape
    shape = (cells * lines, 512) if along_z else (512, cells * columns)
    return pl.pallas_call(
        functools.partial(sum_kernel, along_z),
        grid_spec=pltpu.PrefetchScalarGridSpec(
            num_scalar_prefetch=1,
            grid=(count // cells,),
            in_specs=[
                pl.BlockSpec((2, cells, lines, columns), lambda i, place: (0, i, 0, 0))
            ]
            * 3
            + [pl.BlockSpec(table.shape, lambda i, place: (0, 0, 0, 0))],
            out_specs=pl.BlockSpec((1,) + shape, lambda i, place: (i, 0, 0)),
        ),
        out_shape=jax.ShapeDtypeStruct((count // cells,) + shape, jnp.float32),
        compiler_params=params(VMEM),
        cost_estimate=cost(count // cells * shape[0] * shape[1] * 768, 8 * MIB),
        name="part_z" if along_z else "part_y",
    )(place, *pieces, table)


def first_y_kernel(place_ref, to_ref, p0, p1, p2, p3, table_ref, *out_refs):
    total = None
    for shift, piece in enumerate((p0, p1, p2, p3)):
        g = lax.rem(place_ref[0] + (4 - shift), 4)
        term = term_of(False, piece[...], table_ref, g)
        total = term if total is None else total + term
    for step, out_ref in enumerate(out_refs):

        @pl.when(pl.program_id(0) == step)
        def _():
            for plane in range(2):
                for x in range(2):
                    out_ref[plane, x] = total[
                        plane * KEPT : (plane + 1) * KEPT, x * 128 : (x + 1) * 128
                    ]


def first_y(shifts, place, to, pieces, table):
    def pair(i, to):
        return lax.rem(to[0] + jnp.where(i == 0, shifts[0], shifts[1]), 4)

    shape = (2, 2, KEPT, 128)
    return pl.pallas_call(
        first_y_kernel,
        grid_spec=pltpu.PrefetchScalarGridSpec(
            num_scalar_prefetch=2,
            grid=(2,),
            in_specs=[
                pl.BlockSpec((2, 2, 128, 128), lambda i, place, to: (0, pair(i, to), 0, 0))
            ]
            * 4
            + [pl.BlockSpec((2, 4, 512, 256), lambda i, place, to: (0, 0, 0, 0))],
            out_specs=[pl.BlockSpec(shape, lambda i, place, to: (0, 0, 0, 0))] * 2,
        ),
        out_shape=[jax.ShapeDtypeStruct(shape, jnp.float32)] * 2,
        compiler_params=params(VMEM),
        cost_estimate=cost(512 * 1024 * 512, 4 * MIB),
        name="first_y",
    )(place, to, *pieces, table)


def first_z_kernel(p0, p1, p2, p3, table_ref, out_ref):
    rows = jnp.concatenate(
        [piece[0, plane].reshape(512, 128) for piece in (p0, p1, p2, p3) for plane in range(2)],
        axis=1,
    )
    table = tuple(table_ref[i].reshape(1024, 512) for i in range(2))
    total = product(halves(rows), table)
    for pair in range(2):
        for plane in range(2):
            out_ref[pair, plane] = total[
                pair * 256 : (pair + 1) * 256, plane * KEPT : (plane + 1) * KEPT
            ].reshape(2, 128, KEPT)


def first_z(arrived, table):
    def from_device(g):
        return pl.BlockSpec((1, 2, 4, 128, 128), lambda i: (g, 0, i, 0, 0))

    return pl.pallas_call(
        first_z_kernel,
        grid=(2,),
        in_specs=[from_device(g) for g in range(4)]
        + [pl.BlockSpec((2, 4, 256, 512), lambda i: (0, 0, 0, 0))],
        out_specs=pl.BlockSpec((2, 2, 2, 128, KEPT), lambda i: (i, 0, 0, 0, 0)),
        out_shape=pltpu.HBM((4, 2, 2, 128, KEPT), jnp.float32),
        compiler_params=params(VMEM),
        cost_estimate=cost(1024 * 1024 * 512, 8 * MIB),
        name="first_z",
    )(arrived, arrived, arrived, arrived, table)


def second_y_kernel(p0, p1, p2, p3, table_ref, out_ref):
    total = None
    for g, piece in enumerate((p0, p1, p2, p3)):
        term = term_of(False, piece[0], table_ref, g)
        total = term if total is None else total + term
    out_ref[0] = total


def second_y(arrived, table):
    def from_device(g):
        return pl.BlockSpec((1, 2, 1, 128, KEPT), lambda i: (g, 0, i, 0, 0))

    return pl.pallas_call(
        second_y_kernel,
        grid=(2,),
        in_specs=[from_device(g) for g in range(4)]
        + [pl.BlockSpec((2, 4, 512, 256), lambda i: (0, 0, 0, 0))],
        out_specs=pl.BlockSpec((1, 512, KEPT), lambda i: (i, 0, 0)),
        out_shape=jax.ShapeDtypeStruct((2, 512, KEPT), jnp.float32),
        compiler_params=params(VMEM),
        cost_estimate=cost(512 * 1024 * 512, 5 * MIB),
        name="second_y",
    )(arrived, arrived, arrived, arrived, table)


def second_kernel(gz_ref, done_y, part_ref, last_z, table_ref, out_ref, held):
    def put(values, row):
        for half in range(2):
            held[pl.ds(half * 8 + row, 128, stride=16), :] = values[
                :, half * 128 : (half + 1) * 128
            ]

    for x in range(2):
        for plane in range(2):
            put(done_y[x, plane], plane * 4 + x)
    total = part_ref[...].reshape(256, 512) + term_of(True, last_z[...], table_ref, 0)
    for x in range(2):
        for plane in range(2):
            put(
                total[x * 128 : (x + 1) * 128, plane * KEPT : (plane + 1) * KEPT],
                plane * 4 + 2 + x,
            )
    out_ref[...] = held[...].reshape(128, 1, 2, 8, 128)


def second(gz, done_y, part, last_z, table):
    return pl.pallas_call(
        second_kernel,
        grid_spec=pltpu.PrefetchScalarGridSpec(
            num_scalar_prefetch=1,
            grid=(2,),
            in_specs=[
                pl.BlockSpec((2, 2, 128, KEPT), lambda i, gz: (0, 0, i, 0)),
                pl.BlockSpec((2, 128, 512), lambda i, gz: (0, i, 0)),
                pl.BlockSpec((2, 2, 128, 128), lambda i, gz: (0, 0, i, 0)),
                pl.BlockSpec((2, 1, 256, 512), lambda i, gz: (0, lax.rem(gz[0] + 2, 4), 0, 0)),
            ],
            out_specs=pl.BlockSpec((128, 1, 2, 8, 128), lambda i, gz: (0, i, 0, 0, 0)),
            scratch_shapes=[pltpu.VMEM((2048, 128), jnp.float32)],
        ),
        out_shape=jax.ShapeDtypeStruct((128, 2, 2, 8, 128), jnp.float32),
        compiler_params=params(VMEM),
        cost_estimate=cost(128 * 1024 * 512, 8 * MIB),
        name="second",
    )(gz, done_y.reshape(2, 2, KEPT, KEPT), part, last_z, table)


def third_kernel(slot_ref, in_ref, table_ref, out_ref, held):
    parity = pl.program_id(0)

    @pl.when(parity == 0)
    def _():
        out_ref[...] = jnp.zeros_like(out_ref)

    columns = jnp.concatenate(
        [in_ref[:, 0, half].reshape(1024, 128) for half in range(2)], axis=1
    )
    values = jnp.exp(product((table_ref[0], table_ref[1]), halves(columns)))
    for plane in range(2):
        for half in range(2):
            held[plane, half] = values[
                plane * KEPT : (plane + 1) * KEPT, half * 128 : (half + 1) * 128
            ]

    def place_rows(group, carry):
        for offset in range(8):
            x = group * 8 + offset
            for half in range(2):
                slot = slot_ref[x * 4 + parity * 2 + half]
                for plane in range(2):
                    out_ref[pl.ds(slot * 2 + plane, 1), :] = held[plane, half, pl.ds(x, 1), :]
        return carry

    lax.fori_loop(0, KEPT // 8, place_rows, 0)


def third(slots, arrived, table_x):
    return pl.pallas_call(
        third_kernel,
        grid_spec=pltpu.PrefetchScalarGridSpec(
            num_scalar_prefetch=1,
            grid=(2,),
            in_specs=[
                pl.BlockSpec((128, 1, 2, 8, 128), lambda i, slots: (0, i, 0, 0, 0)),
                pl.BlockSpec((2, 512, 1024), lambda i, slots: (0, 0, 0)),
            ],
            out_specs=pl.BlockSpec((4096, 128), lambda i, slots: (0, 0)),
            scratch_shapes=[pltpu.VMEM((2, 2, KEPT, 128), jnp.float32)],
        ),
        out_shape=jax.ShapeDtypeStruct((4096, 128), jnp.float32),
        compiler_params=params(VMEM),
        cost_estimate=cost(512 * 1024 * 512, 6 * MIB),
        name="third",
    )(slots, arrived, table_x)


def shifted(piece, axis, shift):
    size = lax.axis_size(axis)
    return lax.ppermute(piece, axis, [(i, (i + shift) % size) for i in range(size)])


def slots_of(block_owner):
    destination = block_owner[:, 0]
    one_hot = (destination[:, None] == jnp.arange(128, dtype=jnp.int32)[None, :]).astype(jnp.int32)
    earlier = jnp.cumsum(one_hot, axis=0) - one_hot
    return destination * CAP + jnp.sum(earlier * one_hot, axis=1)


def per_device(normals, spectrum, block_owner):
    table_x, table_y, table_z = (jnp.asarray(table) for table in tables())
    gy = lax.axis_index("gy").astype(jnp.int32).reshape(1)
    gz = lax.axis_index("gz").astype(jnp.int32).reshape(1)

    def chunk_b(shift):
        start = 32 + 8 * lax.rem(gy[0] + shift, 4)
        return lax.dynamic_slice_in_dim(spectrum, start, 8, 0)[None] * lax.dynamic_slice_in_dim(
            normals, start, 8, 1
        ).astype(jnp.float32)

    zero = lax.optimization_barrier(jnp.int32(0))
    a = lax.dynamic_slice_in_dim(spectrum, zero, 32, 0).reshape(
        4, 1, 8, 128, 128
    ) * lax.dynamic_slice_in_dim(normals, zero, 32, 1).astype(jnp.float32).reshape(
        2, 4, 8, 128, 128
    ).transpose(1, 0, 2, 3, 4)
    a, normals, spectrum = lax.optimization_barrier((a, normals, spectrum))
    a = lax.all_to_all(a, "gz", split_axis=0, concat_axis=0, tiled=True)
    b1, b3, b2 = shifted(chunk_b(1), "gy", 1), shifted(chunk_b(3), "gy", 3), shifted(chunk_b(2), "gy", 2)
    b0 = chunk_b(0)

    a, slots = lax.optimization_barrier((a, slots_of(block_owner)))
    a = first_z(a, table_z)
    b0, b1, b2, b3, _ = lax.optimization_barrier((b0, b1, b2, b3, a))
    a = lax.all_to_all(a, "gy", split_axis=0, concat_axis=0, tiled=True)
    pieces = b0, b1, b2, b3
    b1, b3 = first_y((1, 3), gy, gz, pieces, table_y)
    b1, b3 = shifted(b1, "gz", 1), shifted(b3, "gz", 3)
    b2, b0 = first_y((2, 0), gy, gz, pieces, table_y)
    b2 = shifted(b2, "gz", 2)

    a = second_y(a, table_y)
    a, b1, b3 = lax.optimization_barrier((a, b1, b3))
    part_b = part_sum(True, gz, (b0, b1, b3), 1, table_z)
    part_b, b2 = lax.optimization_barrier((part_b, b2))
    planes = second(gz, a, part_b, b2, table_z)
    lines = lax.all_to_all(planes, ALL, split_axis=0, concat_axis=0, tiled=True)
    outgoing = third(slots, lines, table_x)
    return lax.all_to_all(
        outgoing.reshape(128, 1, CAP, 2, BW), ALL, split_axis=0, concat_axis=1, tiled=True
    )


def solution(mesh):
    placed = (P(None, "gx", "gy", "gz"), P("gx", "gy", "gz"), P(ALL, None))
    return jax.shard_map(
        per_device,
        mesh=mesh,
        in_specs=placed,
        out_specs=P(ALL, None, None, None, None),
        check_vma=False,
    )
```

```python
import functools

import jax
import jax.numpy as jnp
import ml_dtypes
import numpy as np
from jax import lax
from jax.experimental import pallas as pl
from jax.experimental.pallas import tpu as pltpu
from jax.sharding import PartitionSpec as P

N = 512
KEPT = 256
BW = 128
CAP = 16
ALL = ("gx", "gy", "gz")
MIB = 1 << 20
VMEM = 24


def split_table(table):
    high = table.astype(np.float32).astype(ml_dtypes.bfloat16)
    low = (table - high.astype(np.float64)).astype(np.float32).astype(ml_dtypes.bfloat16)
    return np.stack([high, low])


def cos_sin(positions, kept):
    angles = (positions[:, None] * kept[None, :] % N) * (2.0 * np.pi / N)
    return np.cos(angles), np.sin(angles)


@functools.cache
def tables():
    cosine, sine = cos_sin(np.arange(N), np.arange(KEPT))
    real_rows = np.concatenate([cosine, -sine], 1).reshape(4, 1, 128, 2 * KEPT)
    imag_rows = np.concatenate([sine, cosine], 1).reshape(4, 1, 128, 2 * KEPT)
    table_z = np.concatenate([real_rows, imag_rows], 1).reshape(4, 256, 2 * KEPT)
    order = np.arange(KEPT).reshape(KEPT // 2, 2).T.reshape(-1)
    cosine, sine = cos_sin(np.arange(N // 2), order)
    cosine, sine = (t.T.reshape(2, 128, 2, 128).transpose(2, 0, 1, 3) for t in (cosine, sine))
    top = np.concatenate([cosine, sine], 3)
    bottom = np.concatenate([-sine, cosine], 3)
    table_y = np.concatenate([top, bottom], 2)
    gx, gy, gz = np.meshgrid(np.arange(8), np.arange(4), np.arange(4), indexing="ij")
    first = 64 * gx + 8 * gz + 2 * gy
    second = 64 * gx + 32 + 8 * gy + 2 * gz
    cells = np.stack([first, first + 1, second, second + 1], -1).reshape(128, 4)
    cosine, sine = cos_sin(cells.reshape(-1), np.arange(KEPT))
    cosine = cosine.T.reshape(KEPT, 128, 1, 4)
    sine = sine.T.reshape(KEPT, 128, 1, 4)
    top = np.concatenate([cosine, sine], 2).reshape(KEPT, 1024)
    bottom = np.concatenate([-sine, cosine], 2).reshape(KEPT, 1024)
    table_x = np.concatenate([top, bottom], 0)
    return split_table(table_x), split_table(table_y), split_table(table_z)


def halves(values):
    high = values.astype(jnp.bfloat16)
    low = (values - high.astype(jnp.float32)).astype(jnp.bfloat16)
    return high, low


def product(left, right):
    def dot(a, b):
        return jnp.dot(a, b, preferred_element_type=jnp.float32)

    return dot(left[0], right[0]) + (dot(left[0], right[1]) + dot(left[1], right[0]))


def params(mib):
    return pltpu.CompilerParams(vmem_limit_bytes=mib * MIB)


def cost(multiplies, moved):
    return pl.CostEstimate(flops=6 * multiplies, bytes_accessed=moved, transcendentals=0)


def rows_z(piece):
    return halves(jnp.concatenate([piece[plane].reshape(-1, 128) for plane in range(2)], axis=1))


def columns_y(piece):
    planes, cells = piece.shape[:2]
    return halves(
        jnp.concatenate([piece[:, x].reshape(256, piece.shape[3]) for x in range(cells)], axis=1)
    )


def scale_kernel(half, rotated, place_ref, normals_ref, spectrum_ref, *refs):
    *out_refs, held_n, held_s, semaphores = refs

    def copies(shift):
        chunk = 4 * half + (lax.rem(place_ref[0] + shift, 4) if rotated else shift)
        return (
            pltpu.make_async_copy(
                normals_ref.at[:, chunk], held_n.at[shift], semaphores.at[shift, 0]
            ),
            pltpu.make_async_copy(
                spectrum_ref.at[chunk], held_s.at[shift], semaphores.at[shift, 1]
            ),
        )

    for shift in (1, 3, 2, 0):
        for copy in copies(shift):
            copy.start()
    for shift in (1, 3, 2, 0):
        for copy in copies(shift):
            copy.wait()
        for plane in range(2):
            values = held_n[shift, plane].astype(jnp.float32) * held_s[shift]
            if rotated:
                out_refs[shift][plane] = values
            else:
                out_refs[0][shift, plane] = values


def scale(half, rotated, place, normals, spectrum):
    if rotated:
        out_shape = [jax.ShapeDtypeStruct((2, 8, 128, 128), jnp.float32)] * 4
    else:
        out_shape = [jax.ShapeDtypeStruct((4, 2, 8, 128, 128), jnp.float32)]
    return pl.pallas_call(
        functools.partial(scale_kernel, half, rotated),
        in_specs=[pl.BlockSpec(memory_space=pltpu.SMEM)]
        + [pl.BlockSpec(memory_space=pltpu.HBM)] * 2,
        out_specs=[pl.BlockSpec(memory_space=pltpu.VMEM)] * len(out_shape),
        out_shape=out_shape,
        scratch_shapes=[
            pltpu.VMEM((4, 2, 8, 128, 128), jnp.bfloat16),
            pltpu.VMEM((4, 8, 128, 128), jnp.float32),
            pltpu.SemaphoreType.DMA((4, 2)),
        ],
        compiler_params=params(VMEM),
        cost_estimate=cost(1 << 20, 8 * MIB),
        name="scale_b" if rotated else "scale_a",
    )(place, normals.reshape(2, 8, 8, 128, 128), spectrum.reshape(8, 8, 128, 128))


def term_of(piece, table_ref, g):
    return product(rows_z(piece), (table_ref[0, g], table_ref[1, g]))


def transform_y(pairs, table_ref):
    even = odd = None
    for first, second, g in pairs:
        base = lax.rem(g, 2)
        sign = jnp.where(g < 2, 1.0, -1.0).astype(jnp.float32)
        term = product((table_ref[0, base, 0], table_ref[1, base, 0]), columns_y(first + second))
        even = term if even is None else even + term
        term = product(
            (table_ref[0, base, 1], table_ref[1, base, 1]), columns_y((first - second) * sign)
        )
        odd = term if odd is None else odd + term
    return even, odd


def part_z_kernel(place_ref, p0, p1, p3, table_ref, out_ref):
    total = None
    for shift, piece in ((0, p0), (1, p1), (3, p3)):
        term = term_of(piece[...], table_ref, lax.rem(place_ref[0] + (4 - shift), 4))
        total = term if total is None else total + term
    out_ref[0] = total


def part_z(place, pieces, table):
    return pl.pallas_call(
        part_z_kernel,
        grid_spec=pltpu.PrefetchScalarGridSpec(
            num_scalar_prefetch=1,
            grid=(2,),
            in_specs=[pl.BlockSpec((2, 1, KEPT, 128), lambda i, place: (0, i, 0, 0))] * 3
            + [pl.BlockSpec(table.shape, lambda i, place: (0, 0, 0, 0))],
            out_specs=pl.BlockSpec((1, KEPT, 512), lambda i, place: (i, 0, 0)),
        ),
        out_shape=jax.ShapeDtypeStruct((2, KEPT, 512), jnp.float32),
        compiler_params=params(VMEM),
        cost_estimate=cost(512 * 512 * 768, 5 * MIB),
        name="part_z",
    )(place, *pieces, table)


def first_y_kernel(place_ref, to_ref, p0, p1, p2, p3, table_ref, *out_refs):
    g = place_ref[0]
    parts = transform_y(
        [(p0[...], p2[...], g), (p1[...], p3[...], lax.rem(g + 3, 4))], table_ref
    )
    for step, out_ref in enumerate(out_refs):

        @pl.when(pl.program_id(0) == step)
        def _():
            for parity, values in enumerate(parts):
                for plane in range(2):
                    for x in range(2):
                        out_ref[plane, x, parity * 128 : (parity + 1) * 128] = values[
                            plane * 128 : (plane + 1) * 128, x * 128 : (x + 1) * 128
                        ]


def first_y(shifts, place, to, pieces, table):
    def pair(i, to):
        return lax.rem(to[0] + jnp.where(i == 0, shifts[0], shifts[1]), 4)

    shape = (2, 2, KEPT, 128)
    return pl.pallas_call(
        first_y_kernel,
        grid_spec=pltpu.PrefetchScalarGridSpec(
            num_scalar_prefetch=2,
            grid=(2,),
            in_specs=[
                pl.BlockSpec((2, 2, 128, 128), lambda i, place, to: (0, pair(i, to), 0, 0))
            ]
            * 4
            + [pl.BlockSpec(table.shape, lambda i, place, to: (0, 0, 0, 0, 0))],
            out_specs=[pl.BlockSpec(shape, lambda i, place, to: (0, 0, 0, 0))] * 2,
        ),
        out_shape=[jax.ShapeDtypeStruct(shape, jnp.float32)] * 2,
        compiler_params=params(VMEM),
        cost_estimate=cost(512 * 512 * 512, 4 * MIB),
        name="first_y",
    )(place, to, *pieces, table)


def first_z_kernel(p0, p1, p2, p3, table_ref, out_ref):
    rows = jnp.concatenate(
        [piece[0, plane].reshape(512, 128) for piece in (p0, p1, p2, p3) for plane in range(2)],
        axis=1,
    )
    table = tuple(table_ref[i].reshape(1024, 512) for i in range(2))
    total = product(halves(rows), table)
    for pair in range(2):
        for plane in range(2):
            out_ref[pair, plane] = total[
                pair * 256 : (pair + 1) * 256, plane * KEPT : (plane + 1) * KEPT
            ].reshape(2, 128, KEPT)


def first_z(arrived, table):
    def from_device(g):
        return pl.BlockSpec((1, 2, 4, 128, 128), lambda i: (g, 0, i, 0, 0))

    return pl.pallas_call(
        first_z_kernel,
        grid=(2,),
        in_specs=[from_device(g) for g in range(4)]
        + [pl.BlockSpec((2, 4, 256, 512), lambda i: (0, 0, 0, 0))],
        out_specs=pl.BlockSpec((2, 2, 2, 128, KEPT), lambda i: (i, 0, 0, 0, 0)),
        out_shape=pltpu.HBM((4, 2, 2, 128, KEPT), jnp.float32),
        compiler_params=params(VMEM),
        cost_estimate=cost(1024 * 1024 * 512, 8 * MIB),
        name="first_z",
    )(arrived, arrived, arrived, arrived, table)


def second_y_kernel(p0, p1, p2, p3, table_ref, out_ref):
    parts = transform_y([(p0[0], p2[0], 0), (p1[0], p3[0], 1)], table_ref)
    for parity, values in enumerate(parts):
        for plane in range(2):
            out_ref[0, plane, parity * 128 : (parity + 1) * 128] = values[
                plane * 128 : (plane + 1) * 128
            ]


def second_y(arrived, table):
    def from_device(g):
        return pl.BlockSpec((1, 2, 1, 128, KEPT), lambda i: (g, 0, i, 0, 0))

    return pl.pallas_call(
        second_y_kernel,
        grid=(2,),
        in_specs=[from_device(g) for g in range(4)]
        + [pl.BlockSpec(table.shape, lambda i: (0, 0, 0, 0, 0))],
        out_specs=pl.BlockSpec((1, 2, KEPT, KEPT), lambda i: (i, 0, 0, 0)),
        out_shape=jax.ShapeDtypeStruct((2, 2, KEPT, KEPT), jnp.float32),
        compiler_params=params(VMEM),
        cost_estimate=cost(512 * 512 * 512, 5 * MIB),
        name="second_y",
    )(arrived, arrived, arrived, arrived, table)


def second_kernel(gz_ref, done_y, part_ref, last_z, table_ref, out_ref, held):
    def put(values, row):
        for half in range(2):
            held[pl.ds(half * 8 + row, 128, stride=16), :] = values[
                :, half * 128 : (half + 1) * 128
            ]

    for x in range(2):
        for plane in range(2):
            put(done_y[x, plane], plane * 4 + x)
    total = part_ref[...].reshape(256, 512) + term_of(last_z[...], table_ref, 0)
    for x in range(2):
        for plane in range(2):
            put(
                total[x * 128 : (x + 1) * 128, plane * KEPT : (plane + 1) * KEPT],
                plane * 4 + 2 + x,
            )
    out_ref[...] = held[...].reshape(128, 1, 2, 8, 128)


def second(gz, done_y, part, last_z, table):
    return pl.pallas_call(
        second_kernel,
        grid_spec=pltpu.PrefetchScalarGridSpec(
            num_scalar_prefetch=1,
            grid=(2,),
            in_specs=[
                pl.BlockSpec((2, 2, 128, KEPT), lambda i, gz: (0, 0, i, 0)),
                pl.BlockSpec((2, 128, 512), lambda i, gz: (0, i, 0)),
                pl.BlockSpec((2, 2, 128, 128), lambda i, gz: (0, 0, i, 0)),
                pl.BlockSpec((2, 1, 256, 512), lambda i, gz: (0, lax.rem(gz[0] + 2, 4), 0, 0)),
            ],
            out_specs=pl.BlockSpec((128, 1, 2, 8, 128), lambda i, gz: (0, i, 0, 0, 0)),
            scratch_shapes=[pltpu.VMEM((2048, 128), jnp.float32)],
        ),
        out_shape=jax.ShapeDtypeStruct((128, 2, 2, 8, 128), jnp.float32),
        compiler_params=params(VMEM),
        cost_estimate=cost(128 * 1024 * 512, 8 * MIB),
        name="second",
    )(gz, done_y, part, last_z, table)


def third_kernel(slot_ref, in_ref, table_ref, out_ref, held):
    parity = pl.program_id(0)

    @pl.when(parity == 0)
    def _():
        out_ref[...] = jnp.zeros_like(out_ref)

    columns = jnp.concatenate(
        [in_ref[:, 0, half].reshape(1024, 128) for half in range(2)], axis=1
    )
    values = jnp.exp(product((table_ref[0], table_ref[1]), halves(columns)))
    for plane in range(2):
        for half in range(2):
            held[plane, half] = values[
                plane * KEPT : (plane + 1) * KEPT, half * 128 : (half + 1) * 128
            ]

    def place_rows(group, carry):
        for offset in range(8):
            x = group * 8 + offset
            for half in range(2):
                slot = slot_ref[x * 4 + parity * 2 + half]
                for plane in range(2):
                    out_ref[pl.ds(slot * 2 + plane, 1), :] = held[plane, half, pl.ds(x, 1), :]
        return carry

    lax.fori_loop(0, KEPT // 8, place_rows, 0)


def third(slots, arrived, table_x):
    return pl.pallas_call(
        third_kernel,
        grid_spec=pltpu.PrefetchScalarGridSpec(
            num_scalar_prefetch=1,
            grid=(2,),
            in_specs=[
                pl.BlockSpec((128, 1, 2, 8, 128), lambda i, slots: (0, i, 0, 0, 0)),
                pl.BlockSpec((2, 512, 1024), lambda i, slots: (0, 0, 0)),
            ],
            out_specs=pl.BlockSpec((4096, 128), lambda i, slots: (0, 0)),
            scratch_shapes=[pltpu.VMEM((2, 2, KEPT, 128), jnp.float32)],
        ),
        out_shape=jax.ShapeDtypeStruct((4096, 128), jnp.float32),
        compiler_params=params(VMEM),
        cost_estimate=cost(512 * 1024 * 512, 6 * MIB),
        name="third",
    )(slots, arrived, table_x)


def shifted(piece, axis, shift):
    size = lax.axis_size(axis)
    return lax.ppermute(piece, axis, [(i, (i + shift) % size) for i in range(size)])


def slots_of(block_owner):
    destination = block_owner[:, 0]
    one_hot = (destination[:, None] == jnp.arange(128, dtype=jnp.int32)[None, :]).astype(jnp.int32)
    earlier = jnp.cumsum(one_hot, axis=0) - one_hot
    return destination * CAP + jnp.sum(earlier * one_hot, axis=1)


def per_device(normals, spectrum, block_owner):
    table_x, table_y, table_z = (jnp.asarray(table) for table in tables())
    gy = lax.axis_index("gy").astype(jnp.int32).reshape(1)
    gz = lax.axis_index("gz").astype(jnp.int32).reshape(1)

    (a,) = scale(0, False, gz, normals, spectrum)
    a, place = lax.optimization_barrier((a, gy))
    a = lax.all_to_all(a, "gz", split_axis=0, concat_axis=0, tiled=True)
    b0, b1, b2, b3 = scale(1, True, place, normals, spectrum)
    b1, b3, b2 = shifted(b1, "gy", 1), shifted(b3, "gy", 3), shifted(b2, "gy", 2)

    a, slots = lax.optimization_barrier((a, slots_of(block_owner)))
    a = first_z(a, table_z)
    b0, b1, b2, b3, _ = lax.optimization_barrier((b0, b1, b2, b3, a))
    a = lax.all_to_all(a, "gy", split_axis=0, concat_axis=0, tiled=True)
    pieces = b0, b1, b2, b3
    b1, b3 = first_y((1, 3), gy, gz, pieces, table_y)
    b1, b3 = shifted(b1, "gz", 1), shifted(b3, "gz", 3)
    b2, b0 = first_y((2, 0), gy, gz, pieces, table_y)
    b2 = shifted(b2, "gz", 2)

    a = second_y(a, table_y)
    a, b1, b3 = lax.optimization_barrier((a, b1, b3))
    part_b = part_z(gz, (b0, b1, b3), table_z)
    part_b, b2 = lax.optimization_barrier((part_b, b2))
    planes = second(gz, a, part_b, b2, table_z)
    lines = lax.all_to_all(planes, ALL, split_axis=0, concat_axis=0, tiled=True)
    outgoing = third(slots, lines, table_x)
    return lax.all_to_all(
        outgoing.reshape(128, 1, CAP, 2, BW), ALL, split_axis=0, concat_axis=1, tiled=True
    )


def solution(mesh):
    placed = (P(None, "gx", "gy", "gz"), P("gx", "gy", "gz"), P(ALL, None))
    return jax.shard_map(
        per_device,
        mesh=mesh,
        in_specs=placed,
        out_specs=P(ALL, None, None, None, None),
        check_vma=False,
    )
```

```python
import functools

import jax
import jax.numpy as jnp
import ml_dtypes
import numpy as np
from jax import lax
from jax.experimental import pallas as pl
from jax.experimental.pallas import tpu as pltpu
from jax.sharding import PartitionSpec as P

N = 512
KEPT = 256
BW = 128
CAP = 16
ALL = ("gx", "gy", "gz")
MIB = 1 << 20
VMEM = 24


def split_table(table):
    high = table.astype(np.float32).astype(ml_dtypes.bfloat16)
    low = (table - high.astype(np.float64)).astype(np.float32).astype(ml_dtypes.bfloat16)
    return np.stack([high, low])


def cos_sin(positions, kept):
    angles = (positions[:, None] * kept[None, :] % N) * (2.0 * np.pi / N)
    return np.cos(angles), np.sin(angles)


@functools.cache
def tables():
    cosine, sine = cos_sin(np.arange(N), np.arange(KEPT))
    real_rows = np.concatenate([cosine, -sine], 1).reshape(4, 1, 128, 2 * KEPT)
    imag_rows = np.concatenate([sine, cosine], 1).reshape(4, 1, 128, 2 * KEPT)
    table_z = np.concatenate([real_rows, imag_rows], 1).reshape(4, 256, 2 * KEPT)
    order = np.arange(KEPT).reshape(KEPT // 2, 2).T.reshape(-1)
    cosine, sine = cos_sin(np.arange(N // 2), order)
    cosine, sine = (t.T.reshape(2, 128, 2, 128).transpose(2, 0, 1, 3) for t in (cosine, sine))
    top = np.concatenate([cosine, sine], 3)
    bottom = np.concatenate([-sine, cosine], 3)
    table_y = np.concatenate([top, bottom], 2)
    gx, gy, gz = np.meshgrid(np.arange(8), np.arange(4), np.arange(4), indexing="ij")
    first = 64 * gx + 8 * gz + 2 * gy
    second = 64 * gx + 32 + 8 * gy + 2 * gz
    cells = np.stack([first, first + 1, second, second + 1], -1).reshape(128, 4)
    cosine, sine = cos_sin(cells.reshape(-1), np.arange(KEPT))
    cosine = cosine.T.reshape(KEPT, 128, 1, 4)
    sine = sine.T.reshape(KEPT, 128, 1, 4)
    top = np.concatenate([cosine, sine], 2).reshape(KEPT, 1024)
    bottom = np.concatenate([-sine, cosine], 2).reshape(KEPT, 1024)
    table_x = np.concatenate([top, bottom], 0)
    return split_table(table_x), split_table(table_y), split_table(table_z)


def halves(values):
    high = values.astype(jnp.bfloat16)
    low = (values - high.astype(jnp.float32)).astype(jnp.bfloat16)
    return high, low


def product(left, right):
    def dot(a, b):
        return jnp.dot(a, b, preferred_element_type=jnp.float32)

    return dot(left[0], right[0]) + (dot(left[0], right[1]) + dot(left[1], right[0]))


def params(mib):
    return pltpu.CompilerParams(vmem_limit_bytes=mib * MIB)


def cost(multiplies, moved):
    return pl.CostEstimate(flops=6 * multiplies, bytes_accessed=moved, transcendentals=0)


def rows_z(piece):
    return halves(jnp.concatenate([piece[plane].reshape(-1, 128) for plane in range(2)], axis=1))


def columns_y(piece):
    planes, cells = piece.shape[:2]
    return halves(
        jnp.concatenate([piece[:, x].reshape(256, piece.shape[3]) for x in range(cells)], axis=1)
    )


def scale_kernel(half, rotated, place_ref, normals_ref, spectrum_ref, *refs):
    *out_refs, held_n, held_s, held_out, semaphores = refs

    def copies(shift):
        chunk = 4 * half + (lax.rem(place_ref[0] + shift, 4) if rotated else shift)
        return (
            pltpu.make_async_copy(
                normals_ref.at[:, chunk], held_n.at[shift], semaphores.at[shift, 0]
            ),
            pltpu.make_async_copy(
                spectrum_ref.at[chunk], held_s.at[shift], semaphores.at[shift, 1]
            ),
        )

    def result(shift):
        target = out_refs[shift] if rotated else out_refs[0].at[shift]
        return pltpu.make_async_copy(held_out.at[shift], target, semaphores.at[shift, 2])

    for shift in (1, 3, 2, 0):
        for copy in copies(shift):
            copy.start()
    for shift in (1, 3, 2, 0):
        for copy in copies(shift):
            copy.wait()
        for plane in range(2):
            held_out[shift, plane] = held_n[shift, plane].astype(jnp.float32) * held_s[shift]
        result(shift).start()
    for shift in (1, 3, 2, 0):
        result(shift).wait()


def scale(half, rotated, place, normals, spectrum):
    if rotated:
        out_shape = [pltpu.HBM((2, 8, 128, 128), jnp.float32)] * 4
    else:
        out_shape = [pltpu.HBM((4, 2, 8, 128, 128), jnp.float32)]
    return pl.pallas_call(
        functools.partial(scale_kernel, half, rotated),
        in_specs=[pl.BlockSpec(memory_space=pltpu.SMEM)]
        + [pl.BlockSpec(memory_space=pltpu.HBM)] * 2,
        out_specs=[pl.BlockSpec(memory_space=pltpu.HBM)] * len(out_shape),
        out_shape=out_shape,
        scratch_shapes=[
            pltpu.VMEM((4, 2, 8, 128, 128), jnp.bfloat16),
            pltpu.VMEM((4, 8, 128, 128), jnp.float32),
            pltpu.VMEM((4, 2, 8, 128, 128), jnp.float32),
            pltpu.SemaphoreType.DMA((4, 3)),
        ],
        compiler_params=params(60),
        cost_estimate=cost(1 << 20, 8 * MIB),
        name="scale_b" if rotated else "scale_a",
    )(place, normals.reshape(2, 8, 8, 128, 128), spectrum.reshape(8, 8, 128, 128))


def term_of(piece, table_ref, g):
    return product(rows_z(piece), (table_ref[0, g], table_ref[1, g]))


def transform_y(pairs, table_ref):
    even = odd = None
    for first, second, g in pairs:
        base = lax.rem(g, 2)
        sign = jnp.where(g < 2, 1.0, -1.0).astype(jnp.float32)
        term = product((table_ref[0, base, 0], table_ref[1, base, 0]), columns_y(first + second))
        even = term if even is None else even + term
        term = product(
            (table_ref[0, base, 1], table_ref[1, base, 1]), columns_y((first - second) * sign)
        )
        odd = term if odd is None else odd + term
    return even, odd


def part_z_kernel(place_ref, p0, p1, p3, table_ref, out_ref):
    total = None
    for shift, piece in ((0, p0), (1, p1), (3, p3)):
        term = term_of(piece[...], table_ref, lax.rem(place_ref[0] + (4 - shift), 4))
        total = term if total is None else total + term
    out_ref[0] = total


def part_z(place, pieces, table):
    return pl.pallas_call(
        part_z_kernel,
        grid_spec=pltpu.PrefetchScalarGridSpec(
            num_scalar_prefetch=1,
            grid=(2,),
            in_specs=[pl.BlockSpec((2, 1, KEPT, 128), lambda i, place: (0, i, 0, 0))] * 3
            + [pl.BlockSpec(table.shape, lambda i, place: (0, 0, 0, 0))],
            out_specs=pl.BlockSpec((1, KEPT, 512), lambda i, place: (i, 0, 0)),
        ),
        out_shape=jax.ShapeDtypeStruct((2, KEPT, 512), jnp.float32),
        compiler_params=params(VMEM),
        cost_estimate=cost(512 * 512 * 768, 5 * MIB),
        name="part_z",
    )(place, *pieces, table)


def first_y_kernel(place_ref, to_ref, p0, p1, p2, p3, table_ref, *out_refs):
    g = place_ref[0]
    parts = transform_y(
        [(p0[...], p2[...], g), (p1[...], p3[...], lax.rem(g + 3, 4))], table_ref
    )
    for step, out_ref in enumerate(out_refs):

        @pl.when(pl.program_id(0) == step)
        def _():
            for parity, values in enumerate(parts):
                for plane in range(2):
                    for x in range(2):
                        out_ref[plane, x, parity * 128 : (parity + 1) * 128] = values[
                            plane * 128 : (plane + 1) * 128, x * 128 : (x + 1) * 128
                        ]


def first_y(shifts, place, to, pieces, table):
    def pair(i, to):
        return lax.rem(to[0] + jnp.where(i == 0, shifts[0], shifts[1]), 4)

    shape = (2, 2, KEPT, 128)
    return pl.pallas_call(
        first_y_kernel,
        grid_spec=pltpu.PrefetchScalarGridSpec(
            num_scalar_prefetch=2,
            grid=(2,),
            in_specs=[
                pl.BlockSpec((2, 2, 128, 128), lambda i, place, to: (0, pair(i, to), 0, 0))
            ]
            * 4
            + [pl.BlockSpec(table.shape, lambda i, place, to: (0, 0, 0, 0, 0))],
            out_specs=[pl.BlockSpec(shape, lambda i, place, to: (0, 0, 0, 0))] * 2,
        ),
        out_shape=[pltpu.HBM(shape, jnp.float32)] * 2,
        compiler_params=params(VMEM),
        cost_estimate=cost(512 * 512 * 512, 4 * MIB),
        name="first_y",
    )(place, to, *pieces, table)


def first_z_kernel(p0, p1, p2, p3, table_ref, out_ref):
    rows = jnp.concatenate(
        [piece[0, plane].reshape(512, 128) for piece in (p0, p1, p2, p3) for plane in range(2)],
        axis=1,
    )
    table = tuple(table_ref[i].reshape(1024, 512) for i in range(2))
    total = product(halves(rows), table)
    for pair in range(2):
        for plane in range(2):
            out_ref[pair, plane] = total[
                pair * 256 : (pair + 1) * 256, plane * KEPT : (plane + 1) * KEPT
            ].reshape(2, 128, KEPT)


def first_z(arrived, table):
    def from_device(g):
        return pl.BlockSpec((1, 2, 4, 128, 128), lambda i: (g, 0, i, 0, 0))

    return pl.pallas_call(
        first_z_kernel,
        grid=(2,),
        in_specs=[from_device(g) for g in range(4)]
        + [pl.BlockSpec((2, 4, 256, 512), lambda i: (0, 0, 0, 0))],
        out_specs=pl.BlockSpec((2, 2, 2, 128, KEPT), lambda i: (i, 0, 0, 0, 0)),
        out_shape=pltpu.HBM((4, 2, 2, 128, KEPT), jnp.float32),
        compiler_params=params(VMEM),
        cost_estimate=cost(1024 * 1024 * 512, 8 * MIB),
        name="first_z",
    )(arrived, arrived, arrived, arrived, table)


def second_y_kernel(p0, p1, p2, p3, table_ref, out_ref):
    parts = transform_y([(p0[0], p2[0], 0), (p1[0], p3[0], 1)], table_ref)
    for parity, values in enumerate(parts):
        for plane in range(2):
            out_ref[0, plane, parity * 128 : (parity + 1) * 128] = values[
                plane * 128 : (plane + 1) * 128
            ]


def second_y(arrived, table):
    def from_device(g):
        return pl.BlockSpec((1, 2, 1, 128, KEPT), lambda i: (g, 0, i, 0, 0))

    return pl.pallas_call(
        second_y_kernel,
        grid=(2,),
        in_specs=[from_device(g) for g in range(4)]
        + [pl.BlockSpec(table.shape, lambda i: (0, 0, 0, 0, 0))],
        out_specs=pl.BlockSpec((1, 2, KEPT, KEPT), lambda i: (i, 0, 0, 0)),
        out_shape=jax.ShapeDtypeStruct((2, 2, KEPT, KEPT), jnp.float32),
        compiler_params=params(VMEM),
        cost_estimate=cost(512 * 512 * 512, 5 * MIB),
        name="second_y",
    )(arrived, arrived, arrived, arrived, table)


def second_kernel(gz_ref, done_y, part_ref, last_z, table_ref, out_ref, held):
    def put(values, row):
        for half in range(2):
            held[pl.ds(half * 8 + row, 128, stride=16), :] = values[
                :, half * 128 : (half + 1) * 128
            ]

    for x in range(2):
        for plane in range(2):
            put(done_y[x, plane], plane * 4 + x)
    total = part_ref[...].reshape(256, 512) + term_of(last_z[...], table_ref, 0)
    for x in range(2):
        for plane in range(2):
            put(
                total[x * 128 : (x + 1) * 128, plane * KEPT : (plane + 1) * KEPT],
                plane * 4 + 2 + x,
            )
    out_ref[...] = held[...].reshape(128, 1, 2, 8, 128)


def second(gz, done_y, part, last_z, table):
    return pl.pallas_call(
        second_kernel,
        grid_spec=pltpu.PrefetchScalarGridSpec(
            num_scalar_prefetch=1,
            grid=(2,),
            in_specs=[
                pl.BlockSpec((2, 2, 128, KEPT), lambda i, gz: (0, 0, i, 0)),
                pl.BlockSpec((2, 128, 512), lambda i, gz: (0, i, 0)),
                pl.BlockSpec((2, 2, 128, 128), lambda i, gz: (0, 0, i, 0)),
                pl.BlockSpec((2, 1, 256, 512), lambda i, gz: (0, lax.rem(gz[0] + 2, 4), 0, 0)),
            ],
            out_specs=pl.BlockSpec((128, 1, 2, 8, 128), lambda i, gz: (0, i, 0, 0, 0)),
            scratch_shapes=[pltpu.VMEM((2048, 128), jnp.float32)],
        ),
        out_shape=jax.ShapeDtypeStruct((128, 2, 2, 8, 128), jnp.float32),
        compiler_params=params(VMEM),
        cost_estimate=cost(128 * 1024 * 512, 8 * MIB),
        name="second",
    )(gz, done_y, part, last_z, table)


def third_kernel(slot_ref, in_ref, table_ref, out_ref, held):
    parity = pl.program_id(0)

    @pl.when(parity == 0)
    def _():
        out_ref[...] = jnp.zeros_like(out_ref)

    columns = jnp.concatenate(
        [in_ref[:, 0, half].reshape(1024, 128) for half in range(2)], axis=1
    )
    values = jnp.exp(product((table_ref[0], table_ref[1]), halves(columns)))
    for plane in range(2):
        for half in range(2):
            held[plane, half] = values[
                plane * KEPT : (plane + 1) * KEPT, half * 128 : (half + 1) * 128
            ]

    def place_rows(group, carry):
        for offset in range(8):
            x = group * 8 + offset
            for half in range(2):
                slot = slot_ref[x * 4 + parity * 2 + half]
                for plane in range(2):
                    out_ref[pl.ds(slot * 2 + plane, 1), :] = held[plane, half, pl.ds(x, 1), :]
        return carry

    lax.fori_loop(0, KEPT // 8, place_rows, 0)


def third(slots, arrived, table_x):
    return pl.pallas_call(
        third_kernel,
        grid_spec=pltpu.PrefetchScalarGridSpec(
            num_scalar_prefetch=1,
            grid=(2,),
            in_specs=[
                pl.BlockSpec((128, 1, 2, 8, 128), lambda i, slots: (0, i, 0, 0, 0)),
                pl.BlockSpec((2, 512, 1024), lambda i, slots: (0, 0, 0)),
            ],
            out_specs=pl.BlockSpec((4096, 128), lambda i, slots: (0, 0)),
            scratch_shapes=[pltpu.VMEM((2, 2, KEPT, 128), jnp.float32)],
        ),
        out_shape=jax.ShapeDtypeStruct((4096, 128), jnp.float32),
        compiler_params=params(VMEM),
        cost_estimate=cost(512 * 1024 * 512, 6 * MIB),
        name="third",
    )(slots, arrived, table_x)


def shifted(piece, axis, shift):
    size = lax.axis_size(axis)
    return lax.ppermute(piece, axis, [(i, (i + shift) % size) for i in range(size)])


def slots_of(block_owner):
    destination = block_owner[:, 0]
    one_hot = (destination[:, None] == jnp.arange(128, dtype=jnp.int32)[None, :]).astype(jnp.int32)
    earlier = jnp.cumsum(one_hot, axis=0) - one_hot
    return destination * CAP + jnp.sum(earlier * one_hot, axis=1)


def per_device(normals, spectrum, block_owner):
    table_x, table_y, table_z = (jnp.asarray(table) for table in tables())
    gy = lax.axis_index("gy").astype(jnp.int32).reshape(1)
    gz = lax.axis_index("gz").astype(jnp.int32).reshape(1)

    (a,) = scale(0, False, gz, normals, spectrum)
    a, place = lax.optimization_barrier((a, gy))
    a = lax.all_to_all(a, "gz", split_axis=0, concat_axis=0, tiled=True)
    b0, b1, b2, b3 = scale(1, True, place, normals, spectrum)
    b1, b3, b2 = shifted(b1, "gy", 1), shifted(b3, "gy", 3), shifted(b2, "gy", 2)

    a, slots = lax.optimization_barrier((a, slots_of(block_owner)))
    a = first_z(a, table_z)
    b0, b1, b2, b3, _ = lax.optimization_barrier((b0, b1, b2, b3, a))
    a = lax.all_to_all(a, "gy", split_axis=0, concat_axis=0, tiled=True)
    pieces = b0, b1, b2, b3
    b1, b3 = first_y((1, 3), gy, gz, pieces, table_y)
    b1, b3 = shifted(b1, "gz", 1), shifted(b3, "gz", 3)
    b2, b0 = first_y((2, 0), gy, gz, pieces, table_y)
    b2 = shifted(b2, "gz", 2)

    a = second_y(a, table_y)
    a, b1, b3 = lax.optimization_barrier((a, b1, b3))
    part_b = part_z(gz, (b0, b1, b3), table_z)
    part_b, b2 = lax.optimization_barrier((part_b, b2))
    planes = second(gz, a, part_b, b2, table_z)
    lines = lax.all_to_all(planes, ALL, split_axis=0, concat_axis=0, tiled=True)
    outgoing = third(slots, lines, table_x)
    return lax.all_to_all(
        outgoing.reshape(128, 1, CAP, 2, BW), ALL, split_axis=0, concat_axis=1, tiled=True
    )


def solution(mesh):
    placed = (P(None, "gx", "gy", "gz"), P("gx", "gy", "gz"), P(ALL, None))
    return jax.shard_map(
        per_device,
        mesh=mesh,
        in_specs=placed,
        out_specs=P(ALL, None, None, None, None),
        check_vma=False,
    )
```

```python
import functools

import jax
import jax.numpy as jnp
import ml_dtypes
import numpy as np
from jax import lax
from jax.experimental import pallas as pl
from jax.experimental.pallas import tpu as pltpu
from jax.sharding import PartitionSpec as P

N = 512
KEPT = 256
BW = 128
CAP = 16
ALL = ("gx", "gy", "gz")
MIB = 1 << 20
VMEM = 24


def split_table(table):
    high = table.astype(np.float32).astype(ml_dtypes.bfloat16)
    low = (table - high.astype(np.float64)).astype(np.float32).astype(ml_dtypes.bfloat16)
    return np.stack([high, low])


def cos_sin(positions, kept):
    angles = (positions[:, None] * kept[None, :] % N) * (2.0 * np.pi / N)
    return np.cos(angles), np.sin(angles)


@functools.cache
def tables():
    cosine, sine = cos_sin(np.arange(N), np.arange(KEPT))
    real_rows = np.concatenate([cosine, -sine], 1).reshape(4, 1, 128, 2 * KEPT)
    imag_rows = np.concatenate([sine, cosine], 1).reshape(4, 1, 128, 2 * KEPT)
    table_z = np.concatenate([real_rows, imag_rows], 1).reshape(4, 256, 2 * KEPT)
    order = np.arange(KEPT).reshape(KEPT // 2, 2).T.reshape(-1)
    cosine, sine = cos_sin(np.arange(N // 2), order)
    cosine, sine = (t.T.reshape(2, 128, 2, 128).transpose(2, 0, 1, 3) for t in (cosine, sine))
    top = np.concatenate([cosine, sine], 3)
    bottom = np.concatenate([-sine, cosine], 3)
    table_y = np.concatenate([top, bottom], 2)
    gx, gy, gz = np.meshgrid(np.arange(8), np.arange(4), np.arange(4), indexing="ij")
    first = 64 * gx + 8 * gz + 2 * gy
    second = 64 * gx + 32 + 8 * gy + 2 * gz
    cells = np.stack([first, first + 1, second, second + 1], -1).reshape(128, 4)
    order = np.arange(KEPT).reshape(KEPT // 2, 2).T.reshape(-1)
    cosine, sine = cos_sin(cells[:64].reshape(-1), order)
    cosine, sine = (
        t.T.reshape(2, KEPT // 2, 64, 1, 4) for t in (cosine, sine)
    )
    top = np.concatenate([cosine, sine], 3).reshape(2, KEPT // 2, 512)
    bottom = np.concatenate([-sine, cosine], 3).reshape(2, KEPT // 2, 512)
    table_x = np.concatenate([top, bottom], 1)
    return split_table(table_x), split_table(table_y), split_table(table_z)


def halves(values):
    high = values.astype(jnp.bfloat16)
    low = (values - high.astype(jnp.float32)).astype(jnp.bfloat16)
    return high, low


def product(left, right):
    def dot(a, b):
        return jnp.dot(a, b, preferred_element_type=jnp.float32)

    return dot(left[0], right[0]) + (dot(left[0], right[1]) + dot(left[1], right[0]))


def params(mib):
    return pltpu.CompilerParams(vmem_limit_bytes=mib * MIB)


def cost(multiplies, moved):
    return pl.CostEstimate(flops=6 * multiplies, bytes_accessed=moved, transcendentals=0)


def rows_z(piece):
    return halves(jnp.concatenate([piece[plane].reshape(-1, 128) for plane in range(2)], axis=1))


def columns_y(piece):
    planes, cells = piece.shape[:2]
    return halves(
        jnp.concatenate([piece[:, x].reshape(256, piece.shape[3]) for x in range(cells)], axis=1)
    )


def scale_kernel(half, rotated, place_ref, normals_ref, spectrum_ref, *refs):
    *out_refs, held_n, held_s, held_out, semaphores = refs

    def copies(shift):
        chunk = 4 * half + (lax.rem(place_ref[0] + shift, 4) if rotated else shift)
        return (
            pltpu.make_async_copy(
                normals_ref.at[:, chunk], held_n.at[shift], semaphores.at[shift, 0]
            ),
            pltpu.make_async_copy(
                spectrum_ref.at[chunk], held_s.at[shift], semaphores.at[shift, 1]
            ),
        )

    def result(shift):
        target = out_refs[shift] if rotated else out_refs[0].at[shift]
        return pltpu.make_async_copy(held_out.at[shift], target, semaphores.at[shift, 2])

    for shift in (1, 3, 2, 0):
        for copy in copies(shift):
            copy.start()
    for shift in (1, 3, 2, 0):
        for copy in copies(shift):
            copy.wait()
        for plane in range(2):
            held_out[shift, plane] = held_n[shift, plane].astype(jnp.float32) * held_s[shift]
        result(shift).start()
    for shift in (1, 3, 2, 0):
        result(shift).wait()


def scale(half, rotated, place, normals, spectrum):
    if rotated:
        out_shape = [pltpu.HBM((2, 8, 128, 128), jnp.float32)] * 4
    else:
        out_shape = [pltpu.HBM((4, 2, 8, 128, 128), jnp.float32)]
    return pl.pallas_call(
        functools.partial(scale_kernel, half, rotated),
        in_specs=[pl.BlockSpec(memory_space=pltpu.SMEM)]
        + [pl.BlockSpec(memory_space=pltpu.HBM)] * 2,
        out_specs=[pl.BlockSpec(memory_space=pltpu.HBM)] * len(out_shape),
        out_shape=out_shape,
        scratch_shapes=[
            pltpu.VMEM((4, 2, 8, 128, 128), jnp.bfloat16),
            pltpu.VMEM((4, 8, 128, 128), jnp.float32),
            pltpu.VMEM((4, 2, 8, 128, 128), jnp.float32),
            pltpu.SemaphoreType.DMA((4, 3)),
        ],
        compiler_params=params(60),
        cost_estimate=cost(1 << 20, 8 * MIB),
        name="scale_b" if rotated else "scale_a",
    )(place, normals.reshape(2, 8, 8, 128, 128), spectrum.reshape(8, 8, 128, 128))


def term_of(piece, table_ref, g):
    return product(rows_z(piece), (table_ref[0, g], table_ref[1, g]))


def transform_y(pairs, table_ref):
    even = odd = None
    for first, second, g in pairs:
        base = lax.rem(g, 2)
        sign = jnp.where(g < 2, 1.0, -1.0).astype(jnp.float32)
        term = product((table_ref[0, base, 0], table_ref[1, base, 0]), columns_y(first + second))
        even = term if even is None else even + term
        term = product(
            (table_ref[0, base, 1], table_ref[1, base, 1]), columns_y((first - second) * sign)
        )
        odd = term if odd is None else odd + term
    return even, odd


def part_z_kernel(place_ref, p0, p1, p3, table_ref, out_ref):
    total = None
    for shift, piece in ((0, p0), (1, p1), (3, p3)):
        term = term_of(piece[...], table_ref, lax.rem(place_ref[0] + (4 - shift), 4))
        total = term if total is None else total + term
    out_ref[0] = total


def part_z(place, pieces, table):
    return pl.pallas_call(
        part_z_kernel,
        grid_spec=pltpu.PrefetchScalarGridSpec(
            num_scalar_prefetch=1,
            grid=(2,),
            in_specs=[pl.BlockSpec((2, 1, KEPT, 128), lambda i, place: (0, i, 0, 0))] * 3
            + [pl.BlockSpec(table.shape, lambda i, place: (0, 0, 0, 0))],
            out_specs=pl.BlockSpec((1, KEPT, 512), lambda i, place: (i, 0, 0)),
        ),
        out_shape=jax.ShapeDtypeStruct((2, KEPT, 512), jnp.float32),
        compiler_params=params(VMEM),
        cost_estimate=cost(512 * 512 * 768, 5 * MIB),
        name="part_z",
    )(place, *pieces, table)


def first_y_kernel(shifts, place_ref, to_ref, p0, p1, p2, p3, table_ref, *refs):
    *out_refs, pieces, table, held_out, semaphores = refs
    get_table = pltpu.make_async_copy(table_ref, table, semaphores.at[2, 0])

    def gets(step):
        pair = lax.rem(to_ref[0] + shifts[step], 4)
        return [
            pltpu.make_async_copy(
                piece.at[:, pl.ds(2 * pair, 2)], pieces.at[step, shift], semaphores.at[step, shift]
            )
            for shift, piece in enumerate((p0, p1, p2, p3))
        ]

    def put(step):
        return pltpu.make_async_copy(
            held_out.at[step], out_refs[step], semaphores.at[2, 1 + step]
        )

    get_table.start()
    for step in range(2):
        for copy in gets(step):
            copy.start()
    get_table.wait()
    g = place_ref[0]
    for step in range(2):
        for copy in gets(step):
            copy.wait()
        parts = transform_y(
            [
                (pieces[step, 0], pieces[step, 2], g),
                (pieces[step, 1], pieces[step, 3], lax.rem(g + 3, 4)),
            ],
            table,
        )
        for parity, values in enumerate(parts):
            for plane in range(2):
                for x in range(2):
                    held_out[step, plane, x, parity * 128 : (parity + 1) * 128] = values[
                        plane * 128 : (plane + 1) * 128, x * 128 : (x + 1) * 128
                    ]
        put(step).start()
    for step in range(2):
        put(step).wait()


def first_y(shifts, place, to, pieces, table):
    hbm = pl.BlockSpec(memory_space=pltpu.HBM)
    shape = (2, 2, KEPT, 128)
    return pl.pallas_call(
        functools.partial(first_y_kernel, shifts),
        in_specs=[pl.BlockSpec(memory_space=pltpu.SMEM)] * 2 + [hbm] * 5,
        out_specs=[hbm] * 2,
        out_shape=[pltpu.HBM(shape, jnp.float32)] * 2,
        scratch_shapes=[
            pltpu.VMEM((2, 4, 2, 2, 128, 128), jnp.float32),
            pltpu.VMEM(table.shape, table.dtype),
            pltpu.VMEM((2,) + shape, jnp.float32),
            pltpu.SemaphoreType.DMA((3, 4)),
        ],
        compiler_params=params(60),
        cost_estimate=cost(512 * 512 * 512, 4 * MIB),
        name="first_y",
    )(place, to, *pieces, table)


def first_z_kernel(in_ref, table_ref, out_ref, pieces, table, held_out, semaphores):
    get_table = pltpu.make_async_copy(table_ref, table, semaphores.at[2, 0])

    def get(pair):
        return pltpu.make_async_copy(
            in_ref.at[:, :, pl.ds(2 * pair, 2)], pieces.at[pair], semaphores.at[0, pair]
        )

    def put(pair):
        return pltpu.make_async_copy(
            held_out.at[pair], out_ref.at[pair], semaphores.at[1, pair]
        )

    get(0).start()
    get_table.start()
    for pair in range(1, 4):
        get(pair).start()
    for pair in range(4):
        get(pair).wait()
        if pair == 0:
            get_table.wait()
        rows = jnp.concatenate(
            [
                pieces[pair, g, plane].reshape(256, 128)
                for g in range(4)
                for plane in range(2)
            ],
            axis=1,
        )
        total = product(halves(rows), tuple(table[i].reshape(1024, 512) for i in range(2)))
        for plane in range(2):
            held_out[pair, plane] = total[:, plane * KEPT : (plane + 1) * KEPT].reshape(
                2, 128, KEPT
            )
        put(pair).start()
    for pair in range(4):
        put(pair).wait()


def first_z(arrived, table):
    hbm = pl.BlockSpec(memory_space=pltpu.HBM)
    shape = (4, 2, 2, 128, KEPT)
    return pl.pallas_call(
        first_z_kernel,
        in_specs=[hbm] * 2,
        out_specs=hbm,
        out_shape=pltpu.HBM(shape, jnp.float32),
        scratch_shapes=[
            pltpu.VMEM((4, 4, 2, 2, 128, 128), jnp.float32),
            pltpu.VMEM(table.shape, table.dtype),
            pltpu.VMEM(shape, jnp.float32),
            pltpu.SemaphoreType.DMA((3, 4)),
        ],
        compiler_params=params(60),
        cost_estimate=cost(1024 * 1024 * 512, 8 * MIB),
        name="first_z",
    )(arrived, table)


def second_y_kernel(p0, p1, p2, p3, table_ref, out_ref):
    parts = transform_y([(p0[0], p2[0], 0), (p1[0], p3[0], 1)], table_ref)
    for parity, values in enumerate(parts):
        for plane in range(2):
            out_ref[0, plane, parity * 128 : (parity + 1) * 128] = values[
                plane * 128 : (plane + 1) * 128
            ]


def second_y(arrived, table):
    def from_device(g):
        return pl.BlockSpec((1, 2, 1, 128, KEPT), lambda i: (g, 0, i, 0, 0))

    return pl.pallas_call(
        second_y_kernel,
        grid=(2,),
        in_specs=[from_device(g) for g in range(4)]
        + [pl.BlockSpec(table.shape, lambda i: (0, 0, 0, 0, 0))],
        out_specs=pl.BlockSpec((1, 2, KEPT, KEPT), lambda i: (i, 0, 0, 0)),
        out_shape=jax.ShapeDtypeStruct((2, 2, KEPT, KEPT), jnp.float32),
        compiler_params=params(VMEM),
        cost_estimate=cost(512 * 512 * 512, 5 * MIB),
        name="second_y",
    )(arrived, arrived, arrived, arrived, table)


def second_kernel(gz_ref, done_y, part_ref, last_z, table_ref, out_ref, held):
    def put(values, row):
        for half in range(2):
            held[pl.ds(half * 8 + row, 128, stride=16), :] = values[
                :, half * 128 : (half + 1) * 128
            ]

    for x in range(2):
        for plane in range(2):
            put(done_y[x, plane], plane * 4 + x)
    total = part_ref[...].reshape(256, 512) + term_of(last_z[...], table_ref, 0)
    for x in range(2):
        for plane in range(2):
            put(
                total[x * 128 : (x + 1) * 128, plane * KEPT : (plane + 1) * KEPT],
                plane * 4 + 2 + x,
            )
    out_ref[...] = held[...].reshape(128, 1, 2, 8, 128)


def second(gz, done_y, part, last_z, table):
    return pl.pallas_call(
        second_kernel,
        grid_spec=pltpu.PrefetchScalarGridSpec(
            num_scalar_prefetch=1,
            grid=(2,),
            in_specs=[
                pl.BlockSpec((2, 2, 128, KEPT), lambda i, gz: (0, 0, i, 0)),
                pl.BlockSpec((2, 128, 512), lambda i, gz: (0, i, 0)),
                pl.BlockSpec((2, 2, 128, 128), lambda i, gz: (0, 0, i, 0)),
                pl.BlockSpec((2, 1, 256, 512), lambda i, gz: (0, lax.rem(gz[0] + 2, 4), 0, 0)),
            ],
            out_specs=pl.BlockSpec((128, 1, 2, 8, 128), lambda i, gz: (0, i, 0, 0, 0)),
            scratch_shapes=[pltpu.VMEM((2048, 128), jnp.float32)],
        ),
        out_shape=jax.ShapeDtypeStruct((128, 2, 2, 8, 128), jnp.float32),
        compiler_params=params(VMEM),
        cost_estimate=cost(128 * 1024 * 512, 8 * MIB),
        name="second",
    )(gz, done_y, part, last_z, table)


def third_kernel(slot_ref, in_ref, table_ref, out_ref, held):
    parity = pl.program_id(0)

    @pl.when(parity == 0)
    def _():
        out_ref[...] = jnp.zeros_like(out_ref)

    columns = jnp.concatenate(
        [in_ref[:, 0, half].reshape(1024, 128) for half in range(2)], axis=1
    )
    first, second = columns[:512], columns[512:]
    for odd, sides in enumerate((first + second, first - second)):
        values = jnp.exp(product((table_ref[0, odd], table_ref[1, odd]), halves(sides)))
        for plane in range(2):
            for half in range(2):
                held[plane, half, odd * 128 : (odd + 1) * 128] = values[
                    plane * 128 : (plane + 1) * 128, half * 128 : (half + 1) * 128
                ]

    def place_rows(group, carry):
        for offset in range(8):
            x = 2 * (group * 4 + offset // 2) + offset % 2
            row = group * 4 + offset // 2 + 128 * (offset % 2)
            for half in range(2):
                slot = slot_ref[x * 4 + parity * 2 + half]
                for plane in range(2):
                    out_ref[pl.ds(slot * 2 + plane, 1), :] = held[plane, half, pl.ds(row, 1), :]
        return carry

    lax.fori_loop(0, KEPT // 8, place_rows, 0)


def third(slots, arrived, table_x):
    return pl.pallas_call(
        third_kernel,
        grid_spec=pltpu.PrefetchScalarGridSpec(
            num_scalar_prefetch=1,
            grid=(2,),
            in_specs=[
                pl.BlockSpec((128, 1, 2, 8, 128), lambda i, slots: (0, i, 0, 0, 0)),
                pl.BlockSpec((2, 2, 256, 512), lambda i, slots: (0, 0, 0, 0)),
            ],
            out_specs=pl.BlockSpec((4096, 128), lambda i, slots: (0, 0)),
            scratch_shapes=[pltpu.VMEM((2, 2, KEPT, 128), jnp.float32)],
        ),
        out_shape=jax.ShapeDtypeStruct((4096, 128), jnp.float32),
        compiler_params=params(VMEM),
        cost_estimate=cost(512 * 512 * 512, 6 * MIB),
        name="third",
    )(slots, arrived, table_x)


def shifted(piece, axis, shift):
    size = lax.axis_size(axis)
    return lax.ppermute(piece, axis, [(i, (i + shift) % size) for i in range(size)])


def slots_of(block_owner):
    destination = block_owner[:, 0]
    one_hot = (destination[:, None] == jnp.arange(128, dtype=jnp.int32)[None, :]).astype(jnp.int32)
    earlier = jnp.cumsum(one_hot, axis=0) - one_hot
    return destination * CAP + jnp.sum(earlier * one_hot, axis=1)


def per_device(normals, spectrum, block_owner):
    table_x, table_y, table_z = (jnp.asarray(table) for table in tables())
    gy = lax.axis_index("gy").astype(jnp.int32).reshape(1)
    gz = lax.axis_index("gz").astype(jnp.int32).reshape(1)

    (a,) = scale(0, False, gz, normals, spectrum)
    a, place = lax.optimization_barrier((a, gy))
    a = lax.all_to_all(a, "gz", split_axis=0, concat_axis=0, tiled=True)
    b0, b1, b2, b3 = scale(1, True, place, normals, spectrum)
    b1, b3, b2 = shifted(b1, "gy", 1), shifted(b3, "gy", 3), shifted(b2, "gy", 2)

    a, slots = lax.optimization_barrier((a, slots_of(block_owner)))
    a = first_z(a, table_z)
    b0, b1, b2, b3, _ = lax.optimization_barrier((b0, b1, b2, b3, a))
    a = lax.all_to_all(a, "gy", split_axis=0, concat_axis=0, tiled=True)
    pieces = b0, b1, b2, b3
    b1, b3 = first_y((1, 3), gy, gz, pieces, table_y)
    b1, b3 = shifted(b1, "gz", 1), shifted(b3, "gz", 3)
    b2, b0 = first_y((2, 0), gy, gz, pieces, table_y)
    b2 = shifted(b2, "gz", 2)

    a = second_y(a, table_y)
    a, b1, b3 = lax.optimization_barrier((a, b1, b3))
    part_b = part_z(gz, (b0, b1, b3), table_z)
    part_b, b2 = lax.optimization_barrier((part_b, b2))
    planes = second(gz, a, part_b, b2, table_z)
    lines = lax.all_to_all(planes, ALL, split_axis=0, concat_axis=0, tiled=True)
    outgoing = third(slots, lines, table_x)
    return lax.all_to_all(
        outgoing.reshape(128, 1, CAP, 2, BW), ALL, split_axis=0, concat_axis=1, tiled=True
    )


def solution(mesh):
    placed = (P(None, "gx", "gy", "gz"), P("gx", "gy", "gz"), P(ALL, None))
    return jax.shard_map(
        per_device,
        mesh=mesh,
        in_specs=placed,
        out_specs=P(ALL, None, None, None, None),
        check_vma=False,
    )
```

```python
import functools

import jax
import jax.numpy as jnp
import ml_dtypes
import numpy as np
from jax import lax
from jax.experimental import pallas as pl
from jax.experimental.pallas import tpu as pltpu
from jax.sharding import PartitionSpec as P

N = 512
KEPT = 256
BW = 128
CAP = 16
ALL = ("gx", "gy", "gz")
MIB = 1 << 20
VMEM = 16


def split_table(table):
    high = table.astype(np.float32).astype(ml_dtypes.bfloat16)
    low = (table - high.astype(np.float64)).astype(np.float32).astype(ml_dtypes.bfloat16)
    return np.stack([high, low])


def cos_sin(positions, kept):
    angles = (positions[:, None] * kept[None, :] % N) * (2.0 * np.pi / N)
    return np.cos(angles), np.sin(angles)


@functools.cache
def tables():
    cosine, sine = cos_sin(np.arange(N), np.arange(KEPT))
    real_rows = np.concatenate([cosine, -sine], 1).reshape(4, 1, 128, 2 * KEPT)
    imag_rows = np.concatenate([sine, cosine], 1).reshape(4, 1, 128, 2 * KEPT)
    table_z = np.concatenate([real_rows, imag_rows], 1).reshape(4, 256, 2 * KEPT)
    order = np.arange(KEPT).reshape(KEPT // 2, 2).T.reshape(-1)
    cosine, sine = cos_sin(np.arange(N // 2), order)
    cosine, sine = (t.T.reshape(2, 128, 2, 128).transpose(2, 0, 1, 3) for t in (cosine, sine))
    top = np.concatenate([cosine, sine], 3)
    bottom = np.concatenate([-sine, cosine], 3)
    table_y = np.concatenate([top, bottom], 2)
    gx, gy, gz = np.meshgrid(np.arange(8), np.arange(4), np.arange(4), indexing="ij")
    first = 64 * gx + 8 * gz + 2 * gy
    second = 64 * gx + 32 + 8 * gy + 2 * gz
    cells = np.stack([first, first + 1, second, second + 1], -1).reshape(128, 4)
    order = np.arange(KEPT).reshape(KEPT // 2, 2).T.reshape(-1)
    cosine, sine = cos_sin(cells[:64].reshape(-1), order)
    cosine, sine = (
        t.T.reshape(2, KEPT // 2, 64, 1, 4) for t in (cosine, sine)
    )
    top = np.concatenate([cosine, sine], 3).reshape(2, KEPT // 2, 512)
    bottom = np.concatenate([-sine, cosine], 3).reshape(2, KEPT // 2, 512)
    table_x = np.concatenate([top, bottom], 1)
    return split_table(table_x), split_table(table_y), split_table(table_z)


def halves(values):
    high = values.astype(jnp.bfloat16)
    low = (values - high.astype(jnp.float32)).astype(jnp.bfloat16)
    return high, low


def product(left, right):
    def dot(a, b):
        return jnp.dot(a, b, preferred_element_type=jnp.float32)

    return dot(left[0], right[0]) + (dot(left[0], right[1]) + dot(left[1], right[0]))


def params(mib):
    return pltpu.CompilerParams(vmem_limit_bytes=mib * MIB)


def cost(multiplies, moved):
    return pl.CostEstimate(flops=6 * multiplies, bytes_accessed=moved, transcendentals=0)


def rows_z(piece):
    return halves(jnp.concatenate([piece[plane].reshape(-1, 128) for plane in range(2)], axis=1))


def columns_y(piece):
    planes, cells = piece.shape[:2]
    return halves(
        jnp.concatenate([piece[:, x].reshape(256, piece.shape[3]) for x in range(cells)], axis=1)
    )


def scale_kernel(half, rotated, place_ref, normals_ref, spectrum_ref, *refs):
    if rotated:
        *out_refs, held_n, held_s, semaphores = refs
    else:
        out_ref, held_out, held_n, held_s, semaphores = refs
    order = (1, 3, 2, 0)

    def gets(shift):
        chunk = 4 * half + (lax.rem(place_ref[0] + shift, 4) if rotated else shift)
        return (
            pltpu.make_async_copy(
                normals_ref.at[:, chunk], held_n.at[shift], semaphores.at[shift, 0]
            ),
            pltpu.make_async_copy(
                spectrum_ref.at[chunk], held_s.at[shift], semaphores.at[shift, 1]
            ),
        )

    def put(shift):
        return pltpu.make_async_copy(
            held_out.at[shift], out_ref.at[shift], semaphores.at[shift, 2]
        )

    for shift in order:
        for copy in gets(shift):
            copy.start()
    for shift in order:
        for copy in gets(shift):
            copy.wait()
        target = out_refs[shift] if rotated else held_out.at[shift]
        for plane in range(2):
            target[plane] = held_n[shift, plane].astype(jnp.float32) * held_s[shift]
        if not rotated:
            put(shift).start()
    if not rotated:
        for shift in order:
            put(shift).wait()


def scale(half, rotated, place, normals, spectrum):
    chunks = (4, 2, 8, 128, 128)
    if rotated:
        out_specs = [pl.BlockSpec(memory_space=pltpu.VMEM)] * 4
        out_shape = [pltpu.VMEM(chunks[1:], jnp.float32)] * 4
        scratch = []
    else:
        out_specs = pl.BlockSpec(memory_space=pltpu.HBM)
        out_shape = pltpu.HBM(chunks, jnp.float32)
        scratch = [pltpu.VMEM(chunks, jnp.float32)]
    return pl.pallas_call(
        functools.partial(scale_kernel, half, rotated),
        in_specs=[pl.BlockSpec(memory_space=pltpu.SMEM)]
        + [pl.BlockSpec(memory_space=pltpu.HBM)] * 2,
        out_specs=out_specs,
        out_shape=out_shape,
        scratch_shapes=scratch
        + [
            pltpu.VMEM(chunks, jnp.bfloat16),
            pltpu.VMEM((4, 8, 128, 128), jnp.float32),
            pltpu.SemaphoreType.DMA((4, 3)),
        ],
        compiler_params=params(VMEM),
        cost_estimate=cost(1 << 20, 8 * MIB),
        name="scale_b" if rotated else "scale_a",
    )(
        place,
        pltpu.with_memory_space_constraint(normals.reshape(2, 8, 8, 128, 128), pltpu.HBM),
        pltpu.with_memory_space_constraint(spectrum.reshape(8, 8, 128, 128), pltpu.HBM),
    )


def term_of(piece, table_ref, g):
    return product(rows_z(piece), (table_ref[0, g], table_ref[1, g]))


def transform_y(pairs, table_ref):
    even = odd = None
    for first, second, g in pairs:
        base = lax.rem(g, 2)
        sign = jnp.where(g < 2, 1.0, -1.0).astype(jnp.float32)
        term = product((table_ref[0, base, 0], table_ref[1, base, 0]), columns_y(first + second))
        even = term if even is None else even + term
        term = product(
            (table_ref[0, base, 1], table_ref[1, base, 1]), columns_y((first - second) * sign)
        )
        odd = term if odd is None else odd + term
    return even, odd


def in_vmem(kernel, name, multiplies, out_shape, scalars, operands, scratch=(), hbm=False):
    space = pltpu.HBM if hbm else pltpu.VMEM
    several = isinstance(out_shape, list)
    shapes = out_shape if several else [out_shape]
    specs = [pl.BlockSpec(memory_space=space) for _ in shapes]
    results = [space(shape, jnp.float32) for shape in shapes]
    return pl.pallas_call(
        kernel,
        in_specs=[pl.BlockSpec(memory_space=pltpu.SMEM)] * len(scalars)
        + [pl.BlockSpec(memory_space=pltpu.VMEM)] * len(operands),
        out_specs=specs if several else specs[0],
        out_shape=results if several else results[0],
        scratch_shapes=list(scratch),
        compiler_params=params(VMEM),
        cost_estimate=cost(multiplies, 4 * MIB),
        name=name,
    )(*scalars, *[pltpu.with_memory_space_constraint(x, pltpu.VMEM) for x in operands])


def first_z_kernel(in_ref, table_ref, out_ref, held, semaphores):
    def put(pair):
        return pltpu.make_async_copy(held.at[pair], out_ref.at[pair], semaphores.at[pair])

    table = tuple(table_ref[i].reshape(1024, 512) for i in range(2))
    for pair in range(4):
        rows = jnp.concatenate(
            [
                in_ref[g, plane, 2 * pair : 2 * pair + 2].reshape(256, 128)
                for g in range(4)
                for plane in range(2)
            ],
            axis=1,
        )
        total = product(halves(rows), table)
        for plane in range(2):
            held[pair, plane] = total[:, plane * KEPT : (plane + 1) * KEPT].reshape(2, 128, KEPT)
        put(pair).start()
    for pair in range(4):
        put(pair).wait()


def first_z(arrived, table):
    shape = (4, 2, 2, 128, KEPT)
    scratch = [pltpu.VMEM(shape, jnp.float32), pltpu.SemaphoreType.DMA((4,))]
    return in_vmem(
        first_z_kernel,
        "first_z",
        1024 * 1024 * 512,
        shape,
        [],
        [arrived, table],
        scratch,
        hbm=True,
    )


def first_y_kernel(shifts, place_ref, to_ref, p0, p1, p2, p3, table_ref, *out_refs):
    g = place_ref[0]
    for shift, out_ref in zip(shifts, out_refs):
        cells = pl.ds(2 * lax.rem(to_ref[0] + shift, 4), 2)
        parts = transform_y(
            [(p0[:, cells], p2[:, cells], g), (p1[:, cells], p3[:, cells], lax.rem(g + 3, 4))],
            table_ref,
        )
        for parity, values in enumerate(parts):
            for plane in range(2):
                for x in range(2):
                    out_ref[plane, x, parity * 128 : (parity + 1) * 128] = values[
                        plane * 128 : (plane + 1) * 128, x * 128 : (x + 1) * 128
                    ]


def first_y(shifts, place, to, pieces, table):
    return in_vmem(
        functools.partial(first_y_kernel, shifts),
        "first_y",
        512 * 512 * 512,
        [(2, 2, KEPT, 128)] * 2,
        [place, to],
        [*pieces, table],
    )


def part_z_kernel(place_ref, p0, p1, p3, table_ref, out_ref):
    total = None
    for shift, piece in ((0, p0), (1, p1), (3, p3)):
        term = term_of(piece[...], table_ref, lax.rem(place_ref[0] + (4 - shift), 4))
        total = term if total is None else total + term
    out_ref[...] = total.reshape(2, KEPT, 512)


def part_z(place, pieces, table):
    return in_vmem(
        part_z_kernel, "part_z", 512 * 512 * 768, (2, KEPT, 512), [place], [*pieces, table]
    )


def second_y_kernel(in_ref, table_ref, out_ref):
    parts = transform_y([(in_ref[0], in_ref[2], 0), (in_ref[1], in_ref[3], 1)], table_ref)
    for parity, values in enumerate(parts):
        for x in range(2):
            for plane in range(2):
                out_ref[x, plane, parity * 128 : (parity + 1) * 128] = values[
                    plane * 128 : (plane + 1) * 128, x * KEPT : (x + 1) * KEPT
                ]


def second_y(arrived, table):
    return in_vmem(
        second_y_kernel, "second_y", 512 * 512 * 512, (2, 2, KEPT, KEPT), [], [arrived, table]
    )


def second_kernel(gz_ref, done_y, part_ref, last_z, table_ref, out_ref):
    def put(values, parity, row):
        for half in range(2):
            out_ref[pl.ds(parity * 16 + half * 8 + row, 128, stride=32), :] = values[
                :, half * 128 : (half + 1) * 128
            ]

    total = part_ref[...].reshape(512, 512) + term_of(
        last_z[...], table_ref, lax.rem(gz_ref[0] + 2, 4)
    )
    for parity in range(2):
        for x in range(2):
            start = x * KEPT + parity * 128
            for plane in range(2):
                put(
                    done_y[x, plane, parity * 128 : (parity + 1) * 128], parity, plane * 4 + x
                )
                put(
                    total[start : start + 128, plane * KEPT : (plane + 1) * KEPT],
                    parity,
                    plane * 4 + 2 + x,
                )


def second(gz, done_y, part, last_z, table):
    return in_vmem(
        second_kernel,
        "second",
        512 * 512 * 256,
        (4096, 128),
        [gz],
        [done_y, part, last_z, table],
    )


def third_kernel(slot_ref, in_ref, table_ref, out_ref, held):
    out_ref[...] = jnp.zeros_like(out_ref)
    for parity in range(2):
        columns = jnp.concatenate(
            [in_ref[:, parity, half].reshape(1024, 128) for half in range(2)], axis=1
        )
        first, last = columns[:512], columns[512:]
        for odd, sides in enumerate((first + last, first - last)):
            values = jnp.exp(product((table_ref[0, odd], table_ref[1, odd]), halves(sides)))
            for plane in range(2):
                for half in range(2):
                    held[parity, plane, half, odd * 128 : (odd + 1) * 128] = values[
                        plane * 128 : (plane + 1) * 128, half * 128 : (half + 1) * 128
                    ]

    def place_rows(group, carry):
        for offset in range(4):
            x = group * 4 + offset
            row = group * 2 + offset // 2 + 128 * (offset % 2)
            for parity in range(2):
                for half in range(2):
                    slot = slot_ref[x * 4 + parity * 2 + half]
                    for plane in range(2):
                        out_ref[pl.ds(slot * 2 + plane, 1), :] = held[
                            parity, plane, half, pl.ds(row, 1), :
                        ]
        return carry

    lax.fori_loop(0, KEPT // 4, place_rows, 0)


def third(slots, arrived, table_x):
    scratch = [pltpu.VMEM((2, 2, 2, KEPT, 128), jnp.float32)]
    return in_vmem(
        third_kernel,
        "third",
        512 * 512 * 512,
        (4096, 128),
        [slots],
        [arrived, table_x],
        scratch,
    )


def shifted(piece, axis, shift):
    size = lax.axis_size(axis)
    return lax.ppermute(piece, axis, [(i, (i + shift) % size) for i in range(size)])


def slots_of(block_owner):
    destination = block_owner[:, 0]
    one_hot = (destination[:, None] == jnp.arange(128, dtype=jnp.int32)[None, :]).astype(jnp.int32)
    earlier = jnp.cumsum(one_hot, axis=0) - one_hot
    return destination * CAP + jnp.sum(earlier * one_hot, axis=1)


def per_device(normals, spectrum, block_owner):
    table_x, table_y, table_z = (jnp.asarray(table) for table in tables())
    gy = lax.axis_index("gy").astype(jnp.int32).reshape(1)
    gz = lax.axis_index("gz").astype(jnp.int32).reshape(1)

    a = scale(0, False, gz, normals, spectrum)
    a, place = lax.optimization_barrier((a, gy))
    a = lax.all_to_all(a, "gz", split_axis=0, concat_axis=0, tiled=True)
    b0, b1, b2, b3 = scale(1, True, place, normals, spectrum)
    b1, b3, b2 = shifted(b1, "gy", 1), shifted(b3, "gy", 3), shifted(b2, "gy", 2)

    a, slots = lax.optimization_barrier((a, slots_of(block_owner)))
    a = first_z(a, table_z)
    b0, b1, b2, b3, _ = lax.optimization_barrier((b0, b1, b2, b3, a))
    a = lax.all_to_all(a, "gy", split_axis=0, concat_axis=0, tiled=True)
    pieces = b0, b1, b2, b3
    b1, b3 = first_y((1, 3), gy, gz, pieces, table_y)
    b1, b3 = shifted(b1, "gz", 1), shifted(b3, "gz", 3)
    b2, b0 = first_y((2, 0), gy, gz, pieces, table_y)
    b2 = shifted(b2, "gz", 2)

    a = second_y(a, table_y)
    a, b1, b3 = lax.optimization_barrier((a, b1, b3))
    part_b = part_z(gz, (b0, b1, b3), table_z)
    part_b, b2 = lax.optimization_barrier((part_b, b2))
    planes = second(gz, a, part_b, b2, table_z)
    lines = lax.all_to_all(
        planes.reshape(128, 2, 2, 8, 128), ALL, split_axis=0, concat_axis=0, tiled=True)
    outgoing = third(slots, lines, table_x)
    return lax.all_to_all(
        outgoing.reshape(128, 1, CAP, 2, BW), ALL, split_axis=0, concat_axis=1, tiled=True
    )


def solution(mesh):
    placed = (P(None, "gx", "gy", "gz"), P("gx", "gy", "gz"), P(ALL, None))
    return jax.shard_map(
        per_device,
        mesh=mesh,
        in_specs=placed,
        out_specs=P(ALL, None, None, None, None),
        check_vma=False,
    )
```

```python
import functools

import jax
import jax.numpy as jnp
import ml_dtypes
import numpy as np
from jax import lax
from jax.experimental import pallas as pl
from jax.experimental.pallas import tpu as pltpu
from jax.sharding import PartitionSpec as P

N = 512
KEPT = 256
BW = 128
CAP = 16
ALL = ("gx", "gy", "gz")
MIB = 1 << 20
VMEM = 24


def split_table(table):
    high = table.astype(np.float32).astype(ml_dtypes.bfloat16)
    low = (table - high.astype(np.float64)).astype(np.float32).astype(ml_dtypes.bfloat16)
    return np.stack([high, low])


def cos_sin(positions, kept):
    angles = (positions[:, None] * kept[None, :] % N) * (2.0 * np.pi / N)
    return np.cos(angles), np.sin(angles)


@functools.cache
def tables():
    order = np.arange(KEPT).reshape(KEPT // 2, 2).T.reshape(-1)
    cosine, sine = cos_sin(np.arange(N // 2), order)
    cosine, sine = (t.reshape(2, 128, 2, 128).transpose(0, 2, 1, 3) for t in (cosine, sine))
    real_rows = np.concatenate([cosine, -sine], 3)
    imag_rows = np.concatenate([sine, cosine], 3)
    table_z = np.concatenate([real_rows, imag_rows], 2)
    cosine, sine = cos_sin(np.arange(N // 2), order)
    cosine, sine = (t.T.reshape(2, 128, 2, 128).transpose(2, 0, 1, 3) for t in (cosine, sine))
    top = np.concatenate([cosine, sine], 3)
    bottom = np.concatenate([-sine, cosine], 3)
    table_y = np.concatenate([top, bottom], 2)
    gx, gy, gz = np.meshgrid(np.arange(8), np.arange(4), np.arange(4), indexing="ij")
    first = 64 * gx + 8 * gz + 2 * gy
    second = 64 * gx + 32 + 8 * gy + 2 * gz
    cells = np.stack([first, first + 1, second, second + 1], -1).reshape(128, 4)
    cosine, sine = cos_sin(cells[:64].reshape(-1), order)
    cosine, sine = (
        t.T.reshape(2, KEPT // 2, 64, 1, 4) for t in (cosine, sine)
    )
    top = np.concatenate([cosine, sine], 3).reshape(2, KEPT // 2, 512)
    bottom = np.concatenate([-sine, cosine], 3).reshape(2, KEPT // 2, 512)
    table_x = np.concatenate([top, bottom], 1)
    ordering = np.zeros((KEPT, KEPT), ml_dtypes.bfloat16)
    ordering[np.arange(KEPT), order] = 1
    return split_table(table_x), split_table(table_y), split_table(table_z), ordering


def halves(values):
    high = values.astype(jnp.bfloat16)
    low = (values - high.astype(jnp.float32)).astype(jnp.bfloat16)
    return high, low


def product(left, right):
    def dot(a, b):
        return jnp.dot(a, b, preferred_element_type=jnp.float32)

    return dot(left[0], right[0]) + (dot(left[0], right[1]) + dot(left[1], right[0]))


def params(mib):
    return pltpu.CompilerParams(vmem_limit_bytes=mib * MIB)


def cost(multiplies, moved):
    return pl.CostEstimate(flops=6 * multiplies, bytes_accessed=moved, transcendentals=0)


def rows_z(piece):
    return halves(jnp.concatenate([piece[plane].reshape(-1, 128) for plane in range(2)], axis=1))


def columns_y(piece):
    planes, cells = piece.shape[:2]
    return halves(
        jnp.concatenate([piece[:, x].reshape(256, piece.shape[3]) for x in range(cells)], axis=1)
    )


def in_hbm(*arrays):
    return [pltpu.with_memory_space_constraint(x, pltpu.HBM) for x in arrays]


def scale_kernel(half, shifts, rotated, place_ref, normals_ref, spectrum_ref, *refs):
    *out_refs, held_out, held_n, held_s, semaphores = refs

    def gets(i):
        chunk = 4 * half + (lax.rem(place_ref[0] + shifts[i], 4) if rotated else shifts[i])
        return (
            pltpu.make_async_copy(normals_ref.at[:, chunk], held_n.at[i], semaphores.at[i, 0]),
            pltpu.make_async_copy(spectrum_ref.at[chunk], held_s.at[i], semaphores.at[i, 1]),
        )

    def put(i):
        target = out_refs[i] if rotated else out_refs[0].at[shifts[i]]
        return pltpu.make_async_copy(held_out.at[i], target, semaphores.at[i, 2])

    steps = range(len(shifts))
    for i in steps:
        for copy in gets(i):
            copy.start()
    for i in steps:
        for copy in gets(i):
            copy.wait()
        for plane in range(2):
            held_out[i, plane] = held_n[i, plane].astype(jnp.float32) * held_s[i]
        put(i).start()
    for i in steps:
        put(i).wait()


def scale(half, shifts, rotated, place, normals, spectrum):
    chunk = (2, 8, 128, 128)
    count = len(shifts)
    shapes = [chunk] * count if rotated else [(count,) + chunk]
    hbm = pl.BlockSpec(memory_space=pltpu.HBM)
    return pl.pallas_call(
        functools.partial(scale_kernel, half, shifts, rotated),
        in_specs=[pl.BlockSpec(memory_space=pltpu.SMEM)] + [hbm] * 2,
        out_specs=[hbm] * len(shapes),
        out_shape=[pltpu.HBM(shape, jnp.float32) for shape in shapes],
        scratch_shapes=[
            pltpu.VMEM((count,) + chunk, jnp.float32),
            pltpu.VMEM((count,) + chunk, jnp.bfloat16),
            pltpu.VMEM((count,) + chunk[1:], jnp.float32),
            pltpu.SemaphoreType.DMA((count, 3)),
        ],
        compiler_params=params(VMEM),
        cost_estimate=cost(count << 18, 2 * count * MIB),
        name="scale_b" if rotated else "scale_a",
    )(place, *in_hbm(normals.reshape(2, 8, 8, 128, 128), spectrum.reshape(8, 8, 128, 128)))


def transform(along_z, pairs, table_ref):
    parts = []
    for odd in range(2):
        total = None
        for first, second, g in pairs:
            base = lax.rem(g, 2)
            table = (table_ref[0, base, odd], table_ref[1, base, odd])
            if odd:
                sides = (first - second) * jnp.where(g < 2, 1.0, -1.0).astype(jnp.float32)
            else:
                sides = first + second
            if along_z:
                term = product(rows_z(sides), table)
            else:
                term = product(table, columns_y(sides))
            total = term if total is None else total + term
        parts.append(total)
    return parts


def first_kernel(along_z, shifts, dynamic, place_ref, to_ref, *refs):
    in_refs, refs = (refs[:4], refs[4:]) if dynamic else (refs[:1], refs[1:])
    table_ref, *out_refs, pieces, held_out, semaphores = refs

    def gets(i):
        cells = pl.ds(2 * lax.rem(to_ref[0] + shifts[i], 4), 2)
        if not dynamic:
            source = in_refs[0].at[:, :, cells]
            return [pltpu.make_async_copy(source, pieces.at[i], semaphores.at[i, 0])]
        return [
            pltpu.make_async_copy(ref.at[:, cells], pieces.at[i, s], semaphores.at[i, s])
            for s, ref in enumerate(in_refs)
        ]

    def put(i):
        return pltpu.make_async_copy(held_out.at[i], out_refs[i], semaphores.at[i, 4])

    steps = range(len(shifts))
    for i in steps:
        for copy in gets(i):
            copy.start()
    for i in steps:
        for copy in gets(i):
            copy.wait()
        if dynamic:
            g, h = place_ref[0], lax.rem(place_ref[0] + 3, 4)
        else:
            g, h = 0, 1
        pairs = [(pieces[i, 0], pieces[i, 2], g), (pieces[i, 1], pieces[i, 3], h)]
        for odd, values in enumerate(transform(along_z, pairs, table_ref)):
            half = slice(odd * 128, (odd + 1) * 128)
            for plane in range(2):
                part = slice(plane * 128, (plane + 1) * 128)
                for x in range(2):
                    cell = slice(x * 128, (x + 1) * 128)
                    if along_z:
                        held_out[i, plane, x, :, half] = values[cell, part]
                    else:
                        held_out[i, plane, x, half] = values[part, cell]
        put(i).start()
    for i in steps:
        put(i).wait()


def first(along_z, shifts, place, to, arrived, table):
    dynamic = isinstance(arrived, list)
    operands = arrived if dynamic else [arrived]
    shape = (2, 2, 128, KEPT) if along_z else (2, 2, KEPT, 128)
    hbm = pl.BlockSpec(memory_space=pltpu.HBM)
    count = len(shifts)
    return pl.pallas_call(
        functools.partial(first_kernel, along_z, shifts, dynamic),
        in_specs=[pl.BlockSpec(memory_space=pltpu.SMEM)] * 2
        + [hbm] * len(operands)
        + [pl.BlockSpec(memory_space=pltpu.VMEM)],
        out_specs=[hbm] * count,
        out_shape=[pltpu.HBM(shape, jnp.float32)] * count,
        scratch_shapes=[
            pltpu.VMEM((count, 4, 2, 2, 128, 128), jnp.float32),
            pltpu.VMEM((count,) + shape, jnp.float32),
            pltpu.SemaphoreType.DMA((count, 5)),
        ],
        compiler_params=params(VMEM),
        cost_estimate=cost(count * 256 * 512 * 512, 2 * count * MIB),
        name="first_z" if along_z else "first_y",
    )(place, to, *in_hbm(*operands), table)


def second_y_kernel(place_ref, p0, p1, p2, p3, table_ref, out_ref):
    g, h = place_ref[0], lax.rem(place_ref[0] + 3, 4)
    pairs = [(p0[...], p2[...], g), (p1[...], p3[...], h)]
    for odd, values in enumerate(transform(False, pairs, table_ref)):
        for plane in range(2):
            out_ref[0, plane, odd * 128 : (odd + 1) * 128] = values[
                plane * 128 : (plane + 1) * 128
            ]


def second_y(place, pieces, table):
    return pl.pallas_call(
        second_y_kernel,
        grid_spec=pltpu.PrefetchScalarGridSpec(
            num_scalar_prefetch=1,
            grid=(2,),
            in_specs=[pl.BlockSpec((2, 1, 128, KEPT), lambda i, place: (0, i, 0, 0))] * 4
            + [pl.BlockSpec(table.shape, lambda i, place: (0, 0, 0, 0, 0))],
            out_specs=pl.BlockSpec((1, 2, KEPT, KEPT), lambda i, place: (i, 0, 0, 0)),
        ),
        out_shape=jax.ShapeDtypeStruct((2, 2, KEPT, KEPT), jnp.float32),
        compiler_params=params(VMEM),
        cost_estimate=cost(512 * 512 * 512, 5 * MIB),
        name="second_y",
    )(place, *pieces, table)


def part_z_kernel(place_ref, p1, p3, table_ref, out_ref):
    pairs = [(p1[...], p3[...], lax.rem(place_ref[0] + 3, 4))]
    for odd, values in enumerate(transform(True, pairs, table_ref)):
        out_ref[0, :, odd * 256 : (odd + 1) * 256] = values


def part_z(place, pieces, table):
    return pl.pallas_call(
        part_z_kernel,
        grid_spec=pltpu.PrefetchScalarGridSpec(
            num_scalar_prefetch=1,
            grid=(2,),
            in_specs=[pl.BlockSpec((2, 1, KEPT, 128), lambda i, place: (0, i, 0, 0))] * 2
            + [pl.BlockSpec(table.shape, lambda i, place: (0, 0, 0, 0, 0))],
            out_specs=pl.BlockSpec((1, KEPT, 512), lambda i, place: (i, 0, 0)),
        ),
        out_shape=jax.ShapeDtypeStruct((2, KEPT, 512), jnp.float32),
        compiler_params=params(VMEM),
        cost_estimate=cost(512 * 512 * 256, 4 * MIB),
        name="part_z",
    )(place, *pieces, table)


def second_kernel(place_ref, done_y, part_ref, p0, p2, table_ref, out_ref, held):
    def put(values, half, row):
        held[pl.ds(half * 8 + row, 128, stride=16), :] = values

    parts = transform(True, [(p0[...], p2[...], place_ref[0])], table_ref)
    for half, values in enumerate(parts):
        values = values + part_ref[:, :, half * 256 : (half + 1) * 256].reshape(256, 256)
        for x in range(2):
            for plane in range(2):
                put(done_y[x, plane, :, half * 128 : (half + 1) * 128], half, plane * 4 + x)
                put(
                    values[x * 128 : (x + 1) * 128, plane * 128 : (plane + 1) * 128],
                    half,
                    plane * 4 + 2 + x,
                )
    out_ref[...] = held[...].reshape(128, 1, 2, 8, 128)


def second(place, done_y, part, pieces, table):
    return pl.pallas_call(
        second_kernel,
        grid_spec=pltpu.PrefetchScalarGridSpec(
            num_scalar_prefetch=1,
            grid=(2,),
            in_specs=[
                pl.BlockSpec((2, 2, 128, KEPT), lambda i, place: (0, 0, i, 0)),
                pl.BlockSpec((2, 128, 512), lambda i, place: (0, i, 0)),
            ]
            + [pl.BlockSpec((2, 2, 128, 128), lambda i, place: (0, 0, i, 0))] * 2
            + [pl.BlockSpec(table.shape, lambda i, place: (0, 0, 0, 0, 0))],
            out_specs=pl.BlockSpec((128, 1, 2, 8, 128), lambda i, place: (0, i, 0, 0, 0)),
            scratch_shapes=[pltpu.VMEM((2048, 128), jnp.float32)],
        ),
        out_shape=jax.ShapeDtypeStruct((128, 2, 2, 8, 128), jnp.float32),
        compiler_params=params(VMEM),
        cost_estimate=cost(512 * 512 * 256, 6 * MIB),
        name="second",
    )(place, done_y, part, *pieces, table)


def third_kernel(slot_ref, in_ref, table_ref, ordering_ref, out_ref, held):
    out_ref[...] = jnp.zeros_like(out_ref)
    for parity in range(2):
        columns = jnp.concatenate(
            [in_ref[:, parity, half].reshape(1024, 128) for half in range(2)], axis=1
        )
        first, last = columns[:512], columns[512:]
        for odd, sides in enumerate((first + last, first - last)):
            sides = tuple(
                jnp.dot(
                    part, ordering_ref[...], preferred_element_type=jnp.float32
                ).astype(jnp.bfloat16)
                for part in halves(sides)
            )
            values = jnp.exp(product((table_ref[0, odd], table_ref[1, odd]), sides))
            for plane in range(2):
                for half in range(2):
                    held[parity, plane, half, odd * 128 : (odd + 1) * 128] = values[
                        plane * 128 : (plane + 1) * 128, half * 128 : (half + 1) * 128
                    ]

    def place_rows(group, carry):
        for offset in range(4):
            x = group * 4 + offset
            row = group * 2 + offset // 2 + 128 * (offset % 2)
            for parity in range(2):
                for half in range(2):
                    slot = slot_ref[x * 4 + parity * 2 + half]
                    for plane in range(2):
                        out_ref[pl.ds(slot * 2 + plane, 1), :] = held[
                            parity, plane, half, pl.ds(row, 1), :
                        ]
        return carry

    lax.fori_loop(0, KEPT // 4, place_rows, 0)


def third(slots, arrived, table_x, ordering):
    vmem = pl.BlockSpec(memory_space=pltpu.VMEM)
    return pl.pallas_call(
        third_kernel,
        in_specs=[pl.BlockSpec(memory_space=pltpu.SMEM)] + [vmem] * 3,
        out_specs=vmem,
        out_shape=jax.ShapeDtypeStruct((4096, 128), jnp.float32),
        scratch_shapes=[pltpu.VMEM((2, 2, 2, KEPT, 128), jnp.float32)],
        compiler_params=params(VMEM),
        cost_estimate=cost(768 * 512 * 512, 6 * MIB),
        name="third",
    )(slots, arrived, table_x, ordering)


def shifted(piece, axis, shift):
    size = lax.axis_size(axis)
    return lax.ppermute(piece, axis, [(i, (i + shift) % size) for i in range(size)])


def slots_of(block_owner):
    destination = block_owner[:, 0]
    one_hot = (destination[:, None] == jnp.arange(128, dtype=jnp.int32)[None, :]).astype(jnp.int32)
    earlier = jnp.cumsum(one_hot, axis=0) - one_hot
    return destination * CAP + jnp.sum(earlier * one_hot, axis=1)


def per_device(normals, spectrum, block_owner):
    table_x, table_y, table_z, ordering = (jnp.asarray(table) for table in tables())
    gy = lax.axis_index("gy").astype(jnp.int32).reshape(1)
    gz = lax.axis_index("gz").astype(jnp.int32).reshape(1)

    (a,) = scale(0, (0, 1, 2, 3), False, gz, normals, spectrum)
    a, place = lax.optimization_barrier((a, gy))
    a = lax.all_to_all(a, "gz", split_axis=0, concat_axis=0, tiled=True)
    b1, b3, b2 = scale(1, (1, 3, 2), True, place, normals, spectrum)
    place, b1, b3, b2 = lax.optimization_barrier((place, b1, b3, b2))
    b1, b3, b2 = shifted(b1, "gy", 1), shifted(b3, "gy", 3), shifted(b2, "gy", 2)
    (b0,) = scale(1, (0,), True, place, normals, spectrum)

    a, slots, b0 = lax.optimization_barrier((a, slots_of(block_owner), b0))
    a1, a3, a2, a0 = first(True, (1, 3, 2, 0), gz, gy, a, table_z)
    b1, b2, b3, _ = lax.optimization_barrier((b1, b2, b3, a1))
    pieces = [b0, b1, b2, b3]
    a1, a3 = shifted(a1, "gy", 1), shifted(a3, "gy", 3)
    b1, b3 = first(False, (1, 3), gy, gz, pieces, table_y)
    a2, b1, b3 = lax.optimization_barrier((a2, b1, b3))
    b1, b3, a2 = shifted(b1, "gz", 1), shifted(b3, "gz", 3), shifted(a2, "gy", 2)
    b2, b0 = first(False, (2, 0), gy, gz, pieces, table_y)
    b2 = shifted(b2, "gz", 2)

    part_b = part_z(gz, (b1, b3), table_z)
    done_a = second_y(gy, (a0, a1, a2, a3), table_y)
    done_a, part_b, b2 = lax.optimization_barrier((done_a, part_b, b2))
    planes = second(gz, done_a, part_b, (b0, b2), table_z)
    lines = lax.all_to_all(planes, ALL, split_axis=0, concat_axis=0, tiled=True)
    outgoing = third(slots, lines, table_x, ordering)
    return lax.all_to_all(
        outgoing.reshape(128, 1, CAP, 2, BW), ALL, split_axis=0, concat_axis=1, tiled=True
    )


def solution(mesh):
    placed = (P(None, "gx", "gy", "gz"), P("gx", "gy", "gz"), P(ALL, None))
    return jax.shard_map(
        per_device,
        mesh=mesh,
        in_specs=placed,
        out_specs=P(ALL, None, None, None, None),
        check_vma=False,
    )
```

```python
import functools

import jax
import jax.numpy as jnp
import ml_dtypes
import numpy as np
from jax import lax
from jax.experimental import pallas as pl
from jax.experimental.pallas import tpu as pltpu
from jax.sharding import PartitionSpec as P

N = 512
KEPT = 256
BW = 128
CAP = 16
ALL = ("gx", "gy", "gz")
MIB = 1 << 20
VMEM = 24


def split_table(table):
    high = table.astype(np.float32).astype(ml_dtypes.bfloat16)
    low = (table - high.astype(np.float64)).astype(np.float32).astype(ml_dtypes.bfloat16)
    return np.stack([high, low])


def cos_sin(positions, kept):
    angles = (positions[:, None] * kept[None, :] % N) * (2.0 * np.pi / N)
    return np.cos(angles), np.sin(angles)


@functools.cache
def tables():
    order = np.arange(KEPT).reshape(KEPT // 2, 2).T.reshape(-1)
    cosine, sine = cos_sin(np.arange(N // 2), order)
    cosine, sine = (t.reshape(2, 128, 2, 128).transpose(0, 2, 1, 3) for t in (cosine, sine))
    real_rows = np.concatenate([cosine, -sine], 3)
    imag_rows = np.concatenate([sine, cosine], 3)
    table_z = np.concatenate([real_rows, imag_rows], 2)
    cosine, sine = cos_sin(np.arange(N // 2), order)
    cosine, sine = (t.T.reshape(2, 128, 2, 128).transpose(2, 0, 1, 3) for t in (cosine, sine))
    top = np.concatenate([cosine, sine], 3)
    bottom = np.concatenate([-sine, cosine], 3)
    table_y = np.concatenate([top, bottom], 2)
    gx, gy, gz = np.meshgrid(np.arange(8), np.arange(4), np.arange(4), indexing="ij")
    first = 64 * gx + 8 * gz + 2 * gy
    second = 64 * gx + 32 + 8 * gy + 2 * gz
    cells = np.stack([first, first + 1, second, second + 1], -1).reshape(128, 4)
    cosine, sine = cos_sin(cells[:64].reshape(-1), order)
    cosine, sine = (
        t.T.reshape(2, KEPT // 2, 64, 1, 4) for t in (cosine, sine)
    )
    top = np.concatenate([cosine, sine], 3).reshape(2, KEPT // 2, 512)
    bottom = np.concatenate([-sine, cosine], 3).reshape(2, KEPT // 2, 512)
    table_x = np.concatenate([top, bottom], 1)
    ordering = np.zeros((KEPT, KEPT), ml_dtypes.bfloat16)
    ordering[np.arange(KEPT), order] = 1
    return split_table(table_x), split_table(table_y), split_table(table_z), ordering


def halves(values):
    high = values.astype(jnp.bfloat16)
    low = (values - high.astype(jnp.float32)).astype(jnp.bfloat16)
    return high, low


def product(left, right):
    def dot(a, b):
        return jnp.dot(a, b, preferred_element_type=jnp.float32)

    return dot(left[0], right[0]) + (dot(left[0], right[1]) + dot(left[1], right[0]))


def params(mib):
    return pltpu.CompilerParams(vmem_limit_bytes=mib * MIB)


def cost(multiplies, moved):
    return pl.CostEstimate(
        flops=multiplies >> 16, bytes_accessed=moved >> 16, transcendentals=0
    )


def rows_z(piece):
    return halves(jnp.concatenate([piece[plane].reshape(-1, 128) for plane in range(2)], axis=1))


def columns_y(piece):
    planes, cells = piece.shape[:2]
    return halves(
        jnp.concatenate([piece[:, x].reshape(256, piece.shape[3]) for x in range(cells)], axis=1)
    )


def in_hbm(*arrays):
    return [pltpu.with_memory_space_constraint(x, pltpu.HBM) for x in arrays]


def scale_kernel(whole, shifts, place_ref, normals_ref, spectrum_ref, *refs):
    *out_refs, held_out, held_n, held_s, semaphores = refs
    work = [(i, out_refs[0].at[i]) for i in range(4)] if whole else []
    for shift, out_ref in zip(shifts, out_refs[1:] if whole else out_refs):
        work.append((4 + lax.rem(place_ref[0] + shift, 4), out_ref))

    def gets(i):
        chunk = work[i][0]
        return (
            pltpu.make_async_copy(normals_ref.at[:, chunk], held_n.at[i], semaphores.at[i, 0]),
            pltpu.make_async_copy(spectrum_ref.at[chunk], held_s.at[i], semaphores.at[i, 1]),
        )

    def put(i):
        return pltpu.make_async_copy(held_out.at[i], work[i][1], semaphores.at[i, 2])

    steps = range(len(work))
    for i in steps:
        for copy in gets(i):
            copy.start()
    for i in steps:
        for copy in gets(i):
            copy.wait()
        for plane in range(2):
            held_out[i, plane] = held_n[i, plane].astype(jnp.float32) * held_s[i]
        put(i).start()
    for i in steps:
        put(i).wait()


def scale(whole, shifts, place, normals, spectrum):
    chunk = (2, 8, 128, 128)
    shapes = ([(4,) + chunk] if whole else []) + [chunk] * len(shifts)
    count = 4 * whole + len(shifts)
    hbm = pl.BlockSpec(memory_space=pltpu.HBM)
    return pl.pallas_call(
        functools.partial(scale_kernel, whole, shifts),
        in_specs=[pl.BlockSpec(memory_space=pltpu.SMEM)] + [hbm] * 2,
        out_specs=[hbm] * len(shapes),
        out_shape=[pltpu.HBM(shape, jnp.float32) for shape in shapes],
        scratch_shapes=[
            pltpu.VMEM((count,) + chunk, jnp.float32),
            pltpu.VMEM((count,) + chunk, jnp.bfloat16),
            pltpu.VMEM((count,) + chunk[1:], jnp.float32),
            pltpu.SemaphoreType.DMA((count, 3)),
        ],
        compiler_params=params(VMEM),
        cost_estimate=cost(count << 18, 2 * count * MIB),
        name="scale" if whole else "scale_own",
    )(place, *in_hbm(normals.reshape(2, 8, 8, 128, 128), spectrum.reshape(8, 8, 128, 128)))


def transform(along_z, pairs, table_ref):
    parts = []
    for odd in range(2):
        total = None
        for first, second, g in pairs:
            base = lax.rem(g, 2)
            table = (table_ref[0, base, odd], table_ref[1, base, odd])
            if odd:
                sides = (first - second) * jnp.where(g < 2, 1.0, -1.0).astype(jnp.float32)
            else:
                sides = first + second
            if along_z:
                term = product(rows_z(sides), table)
            else:
                term = product(table, columns_y(sides))
            total = term if total is None else total + term
        parts.append(total)
    return parts


def first_kernel(along_z, shifts, dynamic, place_ref, to_ref, *refs):
    in_refs, refs = (refs[:4], refs[4:]) if dynamic else (refs[:1], refs[1:])
    table_ref, *out_refs, pieces, held_out, semaphores = refs

    def gets(i):
        cells = pl.ds(2 * lax.rem(to_ref[0] + shifts[i], 4), 2)
        if not dynamic:
            source = in_refs[0].at[:, :, cells]
            return [pltpu.make_async_copy(source, pieces.at[i], semaphores.at[i, 0])]
        return [
            pltpu.make_async_copy(ref.at[:, cells], pieces.at[i, s], semaphores.at[i, s])
            for s, ref in enumerate(in_refs)
        ]

    def put(i):
        return pltpu.make_async_copy(held_out.at[i], out_refs[i], semaphores.at[i, 4])

    steps = range(len(shifts))
    for i in steps:
        for copy in gets(i):
            copy.start()
    for i in steps:
        for copy in gets(i):
            copy.wait()
        if dynamic:
            g, h = place_ref[0], lax.rem(place_ref[0] + 3, 4)
        else:
            g, h = 0, 1
        pairs = [(pieces[i, 0], pieces[i, 2], g), (pieces[i, 1], pieces[i, 3], h)]
        for odd, values in enumerate(transform(along_z, pairs, table_ref)):
            half = slice(odd * 128, (odd + 1) * 128)
            for plane in range(2):
                part = slice(plane * 128, (plane + 1) * 128)
                for x in range(2):
                    cell = slice(x * 128, (x + 1) * 128)
                    if along_z:
                        held_out[i, plane, x, :, half] = values[cell, part]
                    else:
                        held_out[i, plane, x, half] = values[part, cell]
        put(i).start()
    for i in steps:
        put(i).wait()


def first(along_z, shifts, place, to, arrived, table):
    dynamic = isinstance(arrived, list)
    operands = arrived if dynamic else [arrived]
    shape = (2, 2, 128, KEPT) if along_z else (2, 2, KEPT, 128)
    hbm = pl.BlockSpec(memory_space=pltpu.HBM)
    count = len(shifts)
    return pl.pallas_call(
        functools.partial(first_kernel, along_z, shifts, dynamic),
        in_specs=[pl.BlockSpec(memory_space=pltpu.SMEM)] * 2
        + [hbm] * len(operands)
        + [pl.BlockSpec(memory_space=pltpu.VMEM)],
        out_specs=[hbm] * count,
        out_shape=[pltpu.HBM(shape, jnp.float32)] * count,
        scratch_shapes=[
            pltpu.VMEM((count, 4, 2, 2, 128, 128), jnp.float32),
            pltpu.VMEM((count,) + shape, jnp.float32),
            pltpu.SemaphoreType.DMA((count, 5)),
        ],
        compiler_params=params(VMEM),
        cost_estimate=cost(count * 256 * 512 * 512, 2 * count * MIB),
        name="first_z" if along_z else "first_y",
    )(place, to, *in_hbm(*operands), table)


def second_y_kernel(place_ref, p0, p1, p2, p3, table_ref, out_ref):
    g, h = place_ref[0], lax.rem(place_ref[0] + 3, 4)
    pairs = [(p0[...], p2[...], g), (p1[...], p3[...], h)]
    for odd, values in enumerate(transform(False, pairs, table_ref)):
        for plane in range(2):
            out_ref[0, plane, odd * 128 : (odd + 1) * 128] = values[
                plane * 128 : (plane + 1) * 128
            ]


def second_y(place, pieces, table):
    return pl.pallas_call(
        second_y_kernel,
        grid_spec=pltpu.PrefetchScalarGridSpec(
            num_scalar_prefetch=1,
            grid=(2,),
            in_specs=[pl.BlockSpec((2, 1, 128, KEPT), lambda i, place: (0, i, 0, 0))] * 4
            + [pl.BlockSpec(table.shape, lambda i, place: (0, 0, 0, 0, 0))],
            out_specs=pl.BlockSpec((1, 2, KEPT, KEPT), lambda i, place: (i, 0, 0, 0)),
        ),
        out_shape=jax.ShapeDtypeStruct((2, 2, KEPT, KEPT), jnp.float32),
        compiler_params=params(VMEM),
        cost_estimate=cost(512 * 512 * 512, 5 * MIB),
        name="second_y",
    )(place, *pieces, table)


def part_z_kernel(place_ref, p1, p3, table_ref, out_ref):
    pairs = [(p1[...], p3[...], lax.rem(place_ref[0] + 3, 4))]
    for odd, values in enumerate(transform(True, pairs, table_ref)):
        out_ref[0, :, odd * 256 : (odd + 1) * 256] = values


def part_z(place, pieces, table):
    return pl.pallas_call(
        part_z_kernel,
        grid_spec=pltpu.PrefetchScalarGridSpec(
            num_scalar_prefetch=1,
            grid=(2,),
            in_specs=[pl.BlockSpec((2, 1, KEPT, 128), lambda i, place: (0, i, 0, 0))] * 2
            + [pl.BlockSpec(table.shape, lambda i, place: (0, 0, 0, 0, 0))],
            out_specs=pl.BlockSpec((1, KEPT, 512), lambda i, place: (i, 0, 0)),
        ),
        out_shape=jax.ShapeDtypeStruct((2, KEPT, 512), jnp.float32),
        compiler_params=params(VMEM),
        cost_estimate=cost(512 * 512 * 256, 4 * MIB),
        name="part_z",
    )(place, *pieces, table)


def second_kernel(place_ref, done_y, part_ref, p0, p2, table_ref, out_ref, held):
    def put(values, half, row):
        held[pl.ds(half * 8 + row, 128, stride=16), :] = values

    parts = transform(True, [(p0[...], p2[...], place_ref[0])], table_ref)
    for half, values in enumerate(parts):
        values = values + part_ref[:, :, half * 256 : (half + 1) * 256].reshape(256, 256)
        for x in range(2):
            for plane in range(2):
                put(done_y[x, plane, :, half * 128 : (half + 1) * 128], half, plane * 4 + x)
                put(
                    values[x * 128 : (x + 1) * 128, plane * 128 : (plane + 1) * 128],
                    half,
                    plane * 4 + 2 + x,
                )
    out_ref[...] = held[...].reshape(128, 1, 2, 8, 128)


def second(place, done_y, part, pieces, table):
    return pl.pallas_call(
        second_kernel,
        grid_spec=pltpu.PrefetchScalarGridSpec(
            num_scalar_prefetch=1,
            grid=(2,),
            in_specs=[
                pl.BlockSpec((2, 2, 128, KEPT), lambda i, place: (0, 0, i, 0)),
                pl.BlockSpec((2, 128, 512), lambda i, place: (0, i, 0)),
            ]
            + [pl.BlockSpec((2, 2, 128, 128), lambda i, place: (0, 0, i, 0))] * 2
            + [pl.BlockSpec(table.shape, lambda i, place: (0, 0, 0, 0, 0))],
            out_specs=pl.BlockSpec((128, 1, 2, 8, 128), lambda i, place: (0, i, 0, 0, 0)),
            scratch_shapes=[pltpu.VMEM((2048, 128), jnp.float32)],
        ),
        out_shape=jax.ShapeDtypeStruct((128, 2, 2, 8, 128), jnp.float32),
        compiler_params=params(VMEM),
        cost_estimate=cost(512 * 512 * 256, 6 * MIB),
        name="second",
    )(place, done_y, part, *pieces, table)


def third_kernel(slot_ref, in_ref, table_ref, ordering_ref, out_ref, held):
    out_ref[...] = jnp.zeros_like(out_ref)
    for parity in range(2):
        columns = jnp.concatenate(
            [in_ref[:, parity, half].reshape(1024, 128) for half in range(2)], axis=1
        )
        first, last = columns[:512], columns[512:]
        for odd, sides in enumerate((first + last, first - last)):
            sides = tuple(
                jnp.dot(
                    part, ordering_ref[...], preferred_element_type=jnp.float32
                ).astype(jnp.bfloat16)
                for part in halves(sides)
            )
            values = jnp.exp(product((table_ref[0, odd], table_ref[1, odd]), sides))
            for plane in range(2):
                for half in range(2):
                    held[parity, plane, half, odd * 128 : (odd + 1) * 128] = values[
                        plane * 128 : (plane + 1) * 128, half * 128 : (half + 1) * 128
                    ]

    def place_rows(group, carry):
        for offset in range(4):
            x = group * 4 + offset
            row = group * 2 + offset // 2 + 128 * (offset % 2)
            for parity in range(2):
                for half in range(2):
                    slot = slot_ref[x * 4 + parity * 2 + half]
                    for plane in range(2):
                        out_ref[pl.ds(slot * 2 + plane, 1), :] = held[
                            parity, plane, half, pl.ds(row, 1), :
                        ]
        return carry

    lax.fori_loop(0, KEPT // 4, place_rows, 0)


def third(slots, arrived, table_x, ordering):
    vmem = pl.BlockSpec(memory_space=pltpu.VMEM)
    return pl.pallas_call(
        third_kernel,
        in_specs=[pl.BlockSpec(memory_space=pltpu.SMEM)] + [vmem] * 3,
        out_specs=vmem,
        out_shape=jax.ShapeDtypeStruct((4096, 128), jnp.float32),
        scratch_shapes=[pltpu.VMEM((2, 2, 2, KEPT, 128), jnp.float32)],
        compiler_params=params(VMEM),
        cost_estimate=cost(768 * 512 * 512, 6 * MIB),
        name="third",
    )(slots, arrived, table_x, ordering)


def shifted(piece, axis, shift):
    size = lax.axis_size(axis)
    return lax.ppermute(piece, axis, [(i, (i + shift) % size) for i in range(size)])


def slots_of(block_owner):
    destination = block_owner[:, 0]
    one_hot = (destination[:, None] == jnp.arange(128, dtype=jnp.int32)[None, :]).astype(jnp.int32)
    earlier = jnp.cumsum(one_hot, axis=0) - one_hot
    return destination * CAP + jnp.sum(earlier * one_hot, axis=1)


def per_device(normals, spectrum, block_owner):
    table_x, table_y, table_z, ordering = (jnp.asarray(table) for table in tables())
    gy = lax.axis_index("gy").astype(jnp.int32).reshape(1)
    gz = lax.axis_index("gz").astype(jnp.int32).reshape(1)

    a, b1, b3, b2 = scale(True, (1, 3, 2), gy, normals, spectrum)
    place, a = lax.optimization_barrier((gy, a))
    a = lax.all_to_all(a, "gz", split_axis=0, concat_axis=0, tiled=True)
    b1, b3, b2 = shifted(b1, "gy", 1), shifted(b3, "gy", 3), shifted(b2, "gy", 2)
    (b0,) = scale(False, (0,), place, normals, spectrum)

    a, slots, b0 = lax.optimization_barrier((a, slots_of(block_owner), b0))
    a1, a3, a2, a0 = first(True, (1, 3, 2, 0), gz, gy, a, table_z)
    b1, b2, b3, _ = lax.optimization_barrier((b1, b2, b3, a1))
    pieces = [b0, b1, b2, b3]
    a1, a3 = shifted(a1, "gy", 1), shifted(a3, "gy", 3)
    b1, b3 = first(False, (1, 3), gy, gz, pieces, table_y)
    a2, b1, b3 = lax.optimization_barrier((a2, b1, b3))
    b1, b3, a2 = shifted(b1, "gz", 1), shifted(b3, "gz", 3), shifted(a2, "gy", 2)
    b2, b0 = first(False, (2, 0), gy, gz, pieces, table_y)
    b2 = shifted(b2, "gz", 2)

    part_b = part_z(gz, (b1, b3), table_z)
    done_a = second_y(gy, (a0, a1, a2, a3), table_y)
    done_a, part_b, b2 = lax.optimization_barrier((done_a, part_b, b2))
    planes = second(gz, done_a, part_b, (b0, b2), table_z)
    lines = lax.all_to_all(planes, ALL, split_axis=0, concat_axis=0, tiled=True)
    outgoing = third(slots, lines, table_x, ordering)
    return lax.all_to_all(
        outgoing.reshape(128, 1, CAP, 2, BW), ALL, split_axis=0, concat_axis=1, tiled=True
    )


def solution(mesh):
    placed = (P(None, "gx", "gy", "gz"), P("gx", "gy", "gz"), P(ALL, None))
    return jax.shard_map(
        per_device,
        mesh=mesh,
        in_specs=placed,
        out_specs=P(ALL, None, None, None, None),
        check_vma=False,
    )
```

```python
import functools

import jax
import jax.numpy as jnp
import ml_dtypes
import numpy as np
from jax import lax
from jax.experimental import pallas as pl
from jax.experimental.pallas import tpu as pltpu
from jax.sharding import PartitionSpec as P

N = 512
KEPT = 256
BW = 128
CAP = 16
ALL = ("gx", "gy", "gz")
MIB = 1 << 20
VMEM = 24


def split_table(table):
    high = table.astype(np.float32).astype(ml_dtypes.bfloat16)
    low = (table - high.astype(np.float64)).astype(np.float32).astype(ml_dtypes.bfloat16)
    return np.stack([high, low])


def cos_sin(positions, kept):
    angles = (positions[:, None] * kept[None, :] % N) * (2.0 * np.pi / N)
    return np.cos(angles), np.sin(angles)


@functools.cache
def tables():
    order = np.arange(KEPT).reshape(KEPT // 2, 2).T.reshape(-1)
    cosine, sine = cos_sin(np.arange(N // 2), order)
    cosine, sine = (t.reshape(2, 128, 2, 128).transpose(0, 2, 1, 3) for t in (cosine, sine))
    real_rows = np.concatenate([cosine, -sine], 3)
    imag_rows = np.concatenate([sine, cosine], 3)
    table_z = np.concatenate([real_rows, imag_rows], 2)
    cosine, sine = cos_sin(np.arange(N // 2), order)
    cosine, sine = (t.T.reshape(2, 128, 2, 128).transpose(2, 0, 1, 3) for t in (cosine, sine))
    top = np.concatenate([cosine, sine], 3)
    bottom = np.concatenate([-sine, cosine], 3)
    table_y = np.concatenate([top, bottom], 2)
    gx, gy, gz = np.meshgrid(np.arange(8), np.arange(4), np.arange(4), indexing="ij")
    first = 64 * gx + 8 * gz + 2 * gy
    second = 64 * gx + 32 + 8 * gy + 2 * gz
    cells = np.stack([first, first + 1, second, second + 1], -1).reshape(128, 4)
    cosine, sine = cos_sin(cells[:64].reshape(-1), order)
    cosine, sine = (
        t.T.reshape(2, KEPT // 2, 64, 1, 4) for t in (cosine, sine)
    )
    top = np.concatenate([cosine, sine], 3).reshape(2, KEPT // 2, 512)
    bottom = np.concatenate([-sine, cosine], 3).reshape(2, KEPT // 2, 512)
    table_x = np.concatenate([top, bottom], 1)
    ordering = np.zeros((KEPT, KEPT), ml_dtypes.bfloat16)
    ordering[np.arange(KEPT), order] = 1
    return split_table(table_x), split_table(table_y), split_table(table_z), ordering


def halves(values):
    high = values.astype(jnp.bfloat16)
    low = (values - high.astype(jnp.float32)).astype(jnp.bfloat16)
    return high, low


def product(left, right):
    def dot(a, b):
        return jnp.dot(a, b, preferred_element_type=jnp.float32)

    return dot(left[0], right[0]) + (dot(left[0], right[1]) + dot(left[1], right[0]))


def params(mib):
    return pltpu.CompilerParams(vmem_limit_bytes=mib * MIB)


def cost(multiplies, moved):
    return pl.CostEstimate(
        flops=multiplies >> 16, bytes_accessed=moved >> 16, transcendentals=0
    )


def rows_z(piece):
    return halves(jnp.concatenate([piece[plane].reshape(-1, 128) for plane in range(2)], axis=1))


def columns_y(piece):
    planes, cells = piece.shape[:2]
    return halves(
        jnp.concatenate([piece[:, x].reshape(256, piece.shape[3]) for x in range(cells)], axis=1)
    )


def in_hbm(*arrays):
    return [pltpu.with_memory_space_constraint(x, pltpu.HBM) for x in arrays]


def scale_kernel(half, shifts, rotated, place_ref, normals_ref, spectrum_ref, *refs):
    *out_refs, held_out, held_n, held_s, semaphores = refs

    def gets(i):
        chunk = 4 * half + (lax.rem(place_ref[0] + shifts[i], 4) if rotated else shifts[i])
        return (
            pltpu.make_async_copy(normals_ref.at[:, chunk], held_n.at[i], semaphores.at[i, 0]),
            pltpu.make_async_copy(spectrum_ref.at[chunk], held_s.at[i], semaphores.at[i, 1]),
        )

    def put(i):
        target = out_refs[i] if rotated else out_refs[0].at[shifts[i]]
        return pltpu.make_async_copy(held_out.at[i], target, semaphores.at[i, 2])

    steps = range(len(shifts))
    for i in steps:
        for copy in gets(i):
            copy.start()
    for i in steps:
        for copy in gets(i):
            copy.wait()
        for plane in range(2):
            held_out[i, plane] = held_n[i, plane].astype(jnp.float32) * held_s[i]
        put(i).start()
    for i in steps:
        put(i).wait()


def scale(half, shifts, rotated, place, normals, spectrum):
    chunk = (2, 8, 128, 128)
    count = len(shifts)
    shapes = [chunk] * count if rotated else [(count,) + chunk]
    hbm = pl.BlockSpec(memory_space=pltpu.HBM)
    return pl.pallas_call(
        functools.partial(scale_kernel, half, shifts, rotated),
        in_specs=[pl.BlockSpec(memory_space=pltpu.SMEM)] + [hbm] * 2,
        out_specs=[hbm] * len(shapes),
        out_shape=[pltpu.HBM(shape, jnp.float32) for shape in shapes],
        scratch_shapes=[
            pltpu.VMEM((count,) + chunk, jnp.float32),
            pltpu.VMEM((count,) + chunk, jnp.bfloat16),
            pltpu.VMEM((count,) + chunk[1:], jnp.float32),
            pltpu.SemaphoreType.DMA((count, 3)),
        ],
        compiler_params=params(VMEM),
        cost_estimate=cost(count << 18, 2 * count * MIB),
        name="scale_b" if rotated else "scale_a",
    )(place, *in_hbm(normals.reshape(2, 8, 8, 128, 128), spectrum.reshape(8, 8, 128, 128)))


def transform(along_z, pairs, table_ref):
    parts = []
    for odd in range(2):
        total = None
        for first, second, g in pairs:
            base = lax.rem(g, 2)
            table = (table_ref[0, base, odd], table_ref[1, base, odd])
            if odd:
                sides = (first - second) * jnp.where(g < 2, 1.0, -1.0).astype(jnp.float32)
            else:
                sides = first + second
            if along_z:
                term = product(rows_z(sides), table)
            else:
                term = product(table, columns_y(sides))
            total = term if total is None else total + term
        parts.append(total)
    return parts


def first_kernel(along_z, shifts, dynamic, place_ref, to_ref, *refs):
    in_refs, refs = (refs[:4], refs[4:]) if dynamic else (refs[:1], refs[1:])
    table_ref, *out_refs, pieces, held_out, semaphores = refs

    def gets(i):
        cells = pl.ds(2 * lax.rem(to_ref[0] + shifts[i], 4), 2)
        if not dynamic:
            source = in_refs[0].at[:, :, cells]
            return [pltpu.make_async_copy(source, pieces.at[i], semaphores.at[i, 0])]
        return [
            pltpu.make_async_copy(ref.at[:, cells], pieces.at[i, s], semaphores.at[i, s])
            for s, ref in enumerate(in_refs)
        ]

    def put(i):
        return pltpu.make_async_copy(held_out.at[i], out_refs[i], semaphores.at[i, 4])

    steps = range(len(shifts))
    for copy in gets(0):
        copy.start()
    for i in steps:
        for copy in gets(i):
            copy.wait()
        if i + 1 < len(shifts):
            for copy in gets(i + 1):
                copy.start()
        if dynamic:
            g, h = place_ref[0], lax.rem(place_ref[0] + 3, 4)
        else:
            g, h = 0, 1
        pairs = [(pieces[i, 0], pieces[i, 2], g), (pieces[i, 1], pieces[i, 3], h)]
        for odd, values in enumerate(transform(along_z, pairs, table_ref)):
            half = slice(odd * 128, (odd + 1) * 128)
            for plane in range(2):
                part = slice(plane * 128, (plane + 1) * 128)
                for x in range(2):
                    cell = slice(x * 128, (x + 1) * 128)
                    if along_z:
                        held_out[i, plane, x, :, half] = values[cell, part]
                    else:
                        held_out[i, plane, x, half] = values[part, cell]
        put(i).start()
    for i in steps:
        put(i).wait()


def first(along_z, shifts, place, to, arrived, table):
    dynamic = isinstance(arrived, list)
    operands = arrived if dynamic else [arrived]
    shape = (2, 2, 128, KEPT) if along_z else (2, 2, KEPT, 128)
    hbm = pl.BlockSpec(memory_space=pltpu.HBM)
    count = len(shifts)
    return pl.pallas_call(
        functools.partial(first_kernel, along_z, shifts, dynamic),
        in_specs=[pl.BlockSpec(memory_space=pltpu.SMEM)] * 2
        + [hbm] * len(operands)
        + [pl.BlockSpec(memory_space=pltpu.VMEM)],
        out_specs=[hbm] * count,
        out_shape=[pltpu.HBM(shape, jnp.float32)] * count,
        scratch_shapes=[
            pltpu.VMEM((count, 4, 2, 2, 128, 128), jnp.float32),
            pltpu.VMEM((count,) + shape, jnp.float32),
            pltpu.SemaphoreType.DMA((count, 5)),
        ],
        compiler_params=params(VMEM),
        cost_estimate=cost(count * 256 * 512 * 512, 2 * count * MIB),
        name="first_z" if along_z else "first_y",
    )(place, to, *in_hbm(*operands), table)


def part_y_kernel(place_ref, p1, p3, table_ref, out_ref):
    pairs = [(p1[...], p3[...], lax.rem(place_ref[0] + 3, 4))]
    for odd, values in enumerate(transform(False, pairs, table_ref)):
        out_ref[odd] = values


def part_y(place, pieces, table):
    return pl.pallas_call(
        part_y_kernel,
        grid_spec=pltpu.PrefetchScalarGridSpec(
            num_scalar_prefetch=1,
            grid=(2,),
            in_specs=[pl.BlockSpec((2, 1, 128, KEPT), lambda i, place: (0, i, 0, 0))] * 2
            + [pl.BlockSpec(table.shape, lambda i, place: (0, 0, 0, 0, 0))],
            out_specs=pl.BlockSpec((2, KEPT, KEPT), lambda i, place: (0, 0, i)),
        ),
        out_shape=jax.ShapeDtypeStruct((2, KEPT, 512), jnp.float32),
        compiler_params=params(VMEM),
        cost_estimate=cost(512 * 512 * 256, 4 * MIB),
        name="part_y",
    )(place, *pieces, table)


def part_z_kernel(place_ref, p1, p3, table_ref, out_ref):
    pairs = [(p1[...], p3[...], lax.rem(place_ref[0] + 3, 4))]
    for odd, values in enumerate(transform(True, pairs, table_ref)):
        out_ref[0, :, odd * 256 : (odd + 1) * 256] = values


def part_z(place, pieces, table):
    return pl.pallas_call(
        part_z_kernel,
        grid_spec=pltpu.PrefetchScalarGridSpec(
            num_scalar_prefetch=1,
            grid=(2,),
            in_specs=[pl.BlockSpec((2, 1, KEPT, 128), lambda i, place: (0, i, 0, 0))] * 2
            + [pl.BlockSpec(table.shape, lambda i, place: (0, 0, 0, 0, 0))],
            out_specs=pl.BlockSpec((1, KEPT, 512), lambda i, place: (i, 0, 0)),
        ),
        out_shape=jax.ShapeDtypeStruct((2, KEPT, 512), jnp.float32),
        compiler_params=params(VMEM),
        cost_estimate=cost(512 * 512 * 256, 4 * MIB),
        name="part_z",
    )(place, *pieces, table)


def second_kernel(
    y_ref, z_ref, part_a, a0, a2, table_y_ref, part_b, b0, b2, table_z_ref, out_ref, held
):
    odd = pl.program_id(0)

    def put(values, half, row):
        held[pl.ds(half * 8 + row, 128, stride=16), :] = values

    base = lax.rem(y_ref[0], 2)
    flip = jnp.where(odd == 0, 1.0, -1.0).astype(jnp.float32)
    sign = jnp.where((odd == 0) | (y_ref[0] < 2), 1.0, -1.0).astype(jnp.float32)
    table = (table_y_ref[0, base, 0], table_y_ref[1, base, 0])
    values = part_a[0] + product(table, columns_y((a0[...] + flip * a2[...]) * sign))
    for plane in range(2):
        for x in range(2):
            for half in range(2):
                start = x * KEPT + half * 128
                put(
                    values[plane * 128 : (plane + 1) * 128, start : start + 128],
                    half,
                    plane * 4 + x,
                )
    parts = transform(True, [(b0[...], b2[...], z_ref[0])], table_z_ref)
    for half, values in enumerate(parts):
        values = values + part_b[:, :, half * 256 : (half + 1) * 256].reshape(256, 256)
        for x in range(2):
            for plane in range(2):
                put(
                    values[x * 128 : (x + 1) * 128, plane * 128 : (plane + 1) * 128],
                    half,
                    plane * 4 + 2 + x,
                )
    out_ref[...] = held[...].reshape(128, 1, 2, 8, 128)


def second(gy, gz, part_a, pieces_a, table_y, part_b, pieces_b, table_z):
    return pl.pallas_call(
        second_kernel,
        grid_spec=pltpu.PrefetchScalarGridSpec(
            num_scalar_prefetch=2,
            grid=(2,),
            in_specs=[pl.BlockSpec((1, KEPT, 512), lambda i, gy, gz: (i, 0, 0))]
            + [pl.BlockSpec((2, 2, 128, KEPT), lambda i, gy, gz: (0, 0, 0, 0))] * 2
            + [
                pl.BlockSpec((2, 2, 1, KEPT, KEPT), lambda i, gy, gz: (0, 0, i, 0, 0)),
                pl.BlockSpec((2, 128, 512), lambda i, gy, gz: (0, i, 0)),
            ]
            + [pl.BlockSpec((2, 2, 128, 128), lambda i, gy, gz: (0, 0, i, 0))] * 2
            + [pl.BlockSpec(table_z.shape, lambda i, gy, gz: (0, 0, 0, 0, 0))],
            out_specs=pl.BlockSpec((128, 1, 2, 8, 128), lambda i, gy, gz: (0, i, 0, 0, 0)),
            scratch_shapes=[pltpu.VMEM((2048, 128), jnp.float32)],
        ),
        out_shape=jax.ShapeDtypeStruct((128, 2, 2, 8, 128), jnp.float32),
        compiler_params=params(VMEM),
        cost_estimate=cost(512 * 512 * 512, 8 * MIB),
        name="second",
    )(gy, gz, part_a, *pieces_a, table_y, part_b, *pieces_b, table_z)


def third_kernel(slot_ref, in_ref, table_ref, ordering_ref, out_ref, held):
    out_ref[...] = jnp.zeros_like(out_ref)
    for parity in range(2):
        columns = jnp.concatenate(
            [in_ref[:, parity, half].reshape(1024, 128) for half in range(2)], axis=1
        )
        first, last = columns[:512], columns[512:]
        for odd, sides in enumerate((first + last, first - last)):
            sides = tuple(
                jnp.dot(
                    part, ordering_ref[...], preferred_element_type=jnp.float32
                ).astype(jnp.bfloat16)
                for part in halves(sides)
            )
            values = jnp.exp(product((table_ref[0, odd], table_ref[1, odd]), sides))
            for plane in range(2):
                for half in range(2):
                    held[parity, plane, half, odd * 128 : (odd + 1) * 128] = values[
                        plane * 128 : (plane + 1) * 128, half * 128 : (half + 1) * 128
                    ]

    def place_rows(group, carry):
        for offset in range(4):
            x = group * 4 + offset
            row = group * 2 + offset // 2 + 128 * (offset % 2)
            for parity in range(2):
                for half in range(2):
                    slot = slot_ref[x * 4 + parity * 2 + half]
                    for plane in range(2):
                        out_ref[pl.ds(slot * 2 + plane, 1), :] = held[
                            parity, plane, half, pl.ds(row, 1), :
                        ]
        return carry

    lax.fori_loop(0, KEPT // 4, place_rows, 0)


def third(slots, arrived, table_x, ordering):
    vmem = pl.BlockSpec(memory_space=pltpu.VMEM)
    return pl.pallas_call(
        third_kernel,
        in_specs=[pl.BlockSpec(memory_space=pltpu.SMEM)] + [vmem] * 3,
        out_specs=vmem,
        out_shape=jax.ShapeDtypeStruct((4096, 128), jnp.float32),
        scratch_shapes=[pltpu.VMEM((2, 2, 2, KEPT, 128), jnp.float32)],
        compiler_params=params(VMEM),
        cost_estimate=cost(768 * 512 * 512, 6 * MIB),
        name="third",
    )(slots, arrived, table_x, ordering)


def shifted(piece, axis, shift):
    size = lax.axis_size(axis)
    return lax.ppermute(piece, axis, [(i, (i + shift) % size) for i in range(size)])


def slots_of(block_owner):
    destination = block_owner[:, 0]
    one_hot = (destination[:, None] == jnp.arange(128, dtype=jnp.int32)[None, :]).astype(jnp.int32)
    earlier = jnp.cumsum(one_hot, axis=0) - one_hot
    return destination * CAP + jnp.sum(earlier * one_hot, axis=1)


def per_device(normals, spectrum, block_owner):
    table_x, table_y, table_z, ordering = (jnp.asarray(table) for table in tables())
    gy = lax.axis_index("gy").astype(jnp.int32).reshape(1)
    gz = lax.axis_index("gz").astype(jnp.int32).reshape(1)

    (a,) = scale(0, (0, 1, 2, 3), False, gz, normals, spectrum)
    a, place = lax.optimization_barrier((a, gy))
    a = lax.all_to_all(a, "gz", split_axis=0, concat_axis=0, tiled=True)
    b1, b3, b2 = scale(1, (1, 3, 2), True, place, normals, spectrum)
    place, b1, b3, b2 = lax.optimization_barrier((place, b1, b3, b2))
    b1, b3, b2 = shifted(b1, "gy", 1), shifted(b3, "gy", 3), shifted(b2, "gy", 2)
    (b0,) = scale(1, (0,), True, place, normals, spectrum)

    a, slots, b0 = lax.optimization_barrier((a, slots_of(block_owner), b0))
    a1, a3, a2, a0 = first(True, (1, 3, 2, 0), gz, gy, a, table_z)
    b1, b2, b3, _ = lax.optimization_barrier((b1, b2, b3, a1))
    pieces = [b0, b1, b2, b3]
    a1, a3 = shifted(a1, "gy", 1), shifted(a3, "gy", 3)
    b1, b3 = first(False, (1, 3), gy, gz, pieces, table_y)
    a2, b1, b3 = lax.optimization_barrier((a2, b1, b3))
    b1, b3, a2 = shifted(b1, "gz", 1), shifted(b3, "gz", 3), shifted(a2, "gy", 2)
    b2, b0 = first(False, (2, 0), gy, gz, pieces, table_y)
    b2 = shifted(b2, "gz", 2)

    part_a = part_y(gy, (a1, a3), table_y)
    part_a, b1, b3 = lax.optimization_barrier((part_a, b1, b3))
    part_b = part_z(gz, (b1, b3), table_z)
    part_b, a2, b2 = lax.optimization_barrier((part_b, a2, b2))
    planes = second(gy, gz, part_a, (a0, a2), table_y, part_b, (b0, b2), table_z)
    lines = lax.all_to_all(planes, ALL, split_axis=0, concat_axis=0, tiled=True)
    outgoing = third(slots, lines, table_x, ordering)
    return lax.all_to_all(
        outgoing.reshape(128, 1, CAP, 2, BW), ALL, split_axis=0, concat_axis=1, tiled=True
    )


def solution(mesh):
    placed = (P(None, "gx", "gy", "gz"), P("gx", "gy", "gz"), P(ALL, None))
    return jax.shard_map(
        per_device,
        mesh=mesh,
        in_specs=placed,
        out_specs=P(ALL, None, None, None, None),
        check_vma=False,
    )
```

```python
import functools

import jax
import jax.numpy as jnp
import ml_dtypes
import numpy as np
from jax import lax
from jax.experimental import pallas as pl
from jax.experimental.pallas import tpu as pltpu
from jax.sharding import PartitionSpec as P

N = 512
KEPT = 256
BW = 128
CAP = 16
ALL = ("gx", "gy", "gz")
MIB = 1 << 20
VMEM = 24


def split_table(table):
    high = table.astype(np.float32).astype(ml_dtypes.bfloat16)
    low = (table - high.astype(np.float64)).astype(np.float32).astype(ml_dtypes.bfloat16)
    return np.stack([high, low])


def cos_sin(positions, kept):
    angles = (positions[:, None] * kept[None, :] % N) * (2.0 * np.pi / N)
    return np.cos(angles), np.sin(angles)


@functools.cache
def tables():
    order = np.arange(KEPT).reshape(KEPT // 2, 2).T.reshape(-1)
    cosine, sine = cos_sin(np.arange(N // 2), order)
    cosine, sine = (t.reshape(2, 128, 2, 128).transpose(0, 2, 1, 3) for t in (cosine, sine))
    real_rows = np.concatenate([cosine, -sine], 3)
    imag_rows = np.concatenate([sine, cosine], 3)
    table_z = np.concatenate([real_rows, imag_rows], 2)
    cosine, sine = cos_sin(np.arange(N // 2), order)
    cosine, sine = (t.T.reshape(2, 128, 2, 128).transpose(2, 0, 1, 3) for t in (cosine, sine))
    top = np.concatenate([cosine, sine], 3)
    bottom = np.concatenate([-sine, cosine], 3)
    table_y = np.concatenate([top, bottom], 2)
    gx, gy, gz = np.meshgrid(np.arange(8), np.arange(4), np.arange(4), indexing="ij")
    first = 64 * gx + 8 * gz + 2 * gy
    second = 64 * gx + 32 + 8 * gy + 2 * gz
    cells = np.stack([first, first + 1, second, second + 1], -1).reshape(128, 4)
    cosine, sine = cos_sin(cells[:64].reshape(-1), order)
    cosine, sine = (
        t.T.reshape(2, KEPT // 2, 64, 1, 4) for t in (cosine, sine)
    )
    top = np.concatenate([cosine, sine], 3).reshape(2, KEPT // 2, 512)
    bottom = np.concatenate([-sine, cosine], 3).reshape(2, KEPT // 2, 512)
    table_x = np.concatenate([top, bottom], 1)
    ordering = np.zeros((KEPT, KEPT), ml_dtypes.bfloat16)
    ordering[np.arange(KEPT), order] = 1
    return split_table(table_x), split_table(table_y), split_table(table_z), ordering


def halves(values):
    high = values.astype(jnp.bfloat16)
    low = (values - high.astype(jnp.float32)).astype(jnp.bfloat16)
    return high, low


def product(left, right):
    def dot(a, b):
        return jnp.dot(a, b, preferred_element_type=jnp.float32)

    return dot(left[0], right[0]) + (dot(left[0], right[1]) + dot(left[1], right[0]))


def params(mib):
    return pltpu.CompilerParams(vmem_limit_bytes=mib * MIB)


def cost(multiplies, moved):
    return pl.CostEstimate(
        flops=multiplies >> 16, bytes_accessed=moved >> 16, transcendentals=0
    )


def rows_z(piece):
    return halves(jnp.concatenate([piece[plane].reshape(-1, 128) for plane in range(2)], axis=1))


def columns_y(piece):
    planes, cells = piece.shape[:2]
    return halves(
        jnp.concatenate([piece[:, x].reshape(256, piece.shape[3]) for x in range(cells)], axis=1)
    )


def in_hbm(*arrays):
    return [pltpu.with_memory_space_constraint(x, pltpu.HBM) for x in arrays]


def scale_kernel(half, shifts, rotated, place_ref, normals_ref, spectrum_ref, *refs):
    *out_refs, held_out, held_n, held_s, semaphores = refs

    def gets(i):
        chunk = 4 * half + (lax.rem(place_ref[0] + shifts[i], 4) if rotated else shifts[i])
        return (
            pltpu.make_async_copy(normals_ref.at[:, chunk], held_n.at[i], semaphores.at[i, 0]),
            pltpu.make_async_copy(spectrum_ref.at[chunk], held_s.at[i], semaphores.at[i, 1]),
        )

    def put(i):
        target = out_refs[i] if rotated else out_refs[0].at[shifts[i]]
        return pltpu.make_async_copy(held_out.at[i], target, semaphores.at[i, 2])

    steps = range(len(shifts))
    for i in steps:
        for copy in gets(i):
            copy.start()
    for i in steps:
        for copy in gets(i):
            copy.wait()
        for plane in range(2):
            held_out[i, plane] = held_n[i, plane].astype(jnp.float32) * held_s[i]
        put(i).start()
    for i in steps:
        put(i).wait()


def scale(half, shifts, rotated, place, normals, spectrum):
    chunk = (2, 8, 128, 128)
    count = len(shifts)
    shapes = [chunk] * count if rotated else [(count,) + chunk]
    hbm = pl.BlockSpec(memory_space=pltpu.HBM)
    return pl.pallas_call(
        functools.partial(scale_kernel, half, shifts, rotated),
        in_specs=[pl.BlockSpec(memory_space=pltpu.SMEM)] + [hbm] * 2,
        out_specs=[hbm] * len(shapes),
        out_shape=[pltpu.HBM(shape, jnp.float32) for shape in shapes],
        scratch_shapes=[
            pltpu.VMEM((count,) + chunk, jnp.float32),
            pltpu.VMEM((count,) + chunk, jnp.bfloat16),
            pltpu.VMEM((count,) + chunk[1:], jnp.float32),
            pltpu.SemaphoreType.DMA((count, 3)),
        ],
        compiler_params=params(VMEM),
        cost_estimate=cost(count << 18, 2 * count * MIB),
        name="scale_b" if rotated else "scale_a",
    )(place, *in_hbm(normals.reshape(2, 8, 8, 128, 128), spectrum.reshape(8, 8, 128, 128)))


def transform(along_z, pairs, table_ref):
    parts = []
    for odd in range(2):
        total = None
        for first, second, g in pairs:
            base = lax.rem(g, 2)
            table = (table_ref[0, base, odd], table_ref[1, base, odd])
            if odd:
                sides = (first - second) * jnp.where(g < 2, 1.0, -1.0).astype(jnp.float32)
            else:
                sides = first + second
            if along_z:
                term = product(rows_z(sides), table)
            else:
                term = product(table, columns_y(sides))
            total = term if total is None else total + term
        parts.append(total)
    return parts


def first_kernel(along_z, shifts, dynamic, place_ref, to_ref, *refs):
    in_refs, refs = (refs[:4], refs[4:]) if dynamic else (refs[:1], refs[1:])
    table_ref, *out_refs, pieces, held_out, semaphores = refs

    def gets(i):
        cells = pl.ds(2 * lax.rem(to_ref[0] + shifts[i], 4), 2)
        if not dynamic:
            source = in_refs[0].at[:, :, cells]
            return [pltpu.make_async_copy(source, pieces.at[i], semaphores.at[i, 0])]
        return [
            pltpu.make_async_copy(ref.at[:, cells], pieces.at[i, s], semaphores.at[i, s])
            for s, ref in enumerate(in_refs)
        ]

    def put(i):
        return pltpu.make_async_copy(held_out.at[i], out_refs[i], semaphores.at[i, 4])

    steps = range(len(shifts))
    for i in steps:
        for copy in gets(i):
            copy.start()
    for i in steps:
        for copy in gets(i):
            copy.wait()
        if dynamic:
            g, h = place_ref[0], lax.rem(place_ref[0] + 3, 4)
        else:
            g, h = 0, 1
        pairs = [(pieces[i, 0], pieces[i, 2], g), (pieces[i, 1], pieces[i, 3], h)]
        for odd, values in enumerate(transform(along_z, pairs, table_ref)):
            half = slice(odd * 128, (odd + 1) * 128)
            for plane in range(2):
                part = slice(plane * 128, (plane + 1) * 128)
                for x in range(2):
                    cell = slice(x * 128, (x + 1) * 128)
                    if along_z:
                        held_out[i, plane, x, :, half] = values[cell, part]
                    else:
                        held_out[i, plane, x, half] = values[part, cell]
        put(i).start()
    for i in steps:
        put(i).wait()


def first(along_z, shifts, place, to, arrived, table):
    dynamic = isinstance(arrived, list)
    operands = arrived if dynamic else [arrived]
    shape = (2, 2, 128, KEPT) if along_z else (2, 2, KEPT, 128)
    hbm = pl.BlockSpec(memory_space=pltpu.HBM)
    count = len(shifts)
    return pl.pallas_call(
        functools.partial(first_kernel, along_z, shifts, dynamic),
        in_specs=[pl.BlockSpec(memory_space=pltpu.SMEM)] * 2
        + [hbm] * len(operands)
        + [pl.BlockSpec(memory_space=pltpu.VMEM)],
        out_specs=[hbm] * count,
        out_shape=[pltpu.HBM(shape, jnp.float32)] * count,
        scratch_shapes=[
            pltpu.VMEM((count, 4, 2, 2, 128, 128), jnp.float32),
            pltpu.VMEM((count,) + shape, jnp.float32),
            pltpu.SemaphoreType.DMA((count, 5)),
        ],
        compiler_params=params(VMEM),
        cost_estimate=cost(count * 256 * 512 * 512, 2 * count * MIB),
        name="first_z" if along_z else "first_y",
    )(place, to, *in_hbm(*operands), table)


def part_y_kernel(place_ref, p1, p3, table_ref, out_ref):
    pairs = [(p1[...], p3[...], lax.rem(place_ref[0] + 3, 4))]
    for odd, values in enumerate(transform(False, pairs, table_ref)):
        out_ref[odd] = values


def part_y(place, pieces, table):
    return pl.pallas_call(
        part_y_kernel,
        grid_spec=pltpu.PrefetchScalarGridSpec(
            num_scalar_prefetch=1,
            grid=(2,),
            in_specs=[pl.BlockSpec((2, 1, 128, KEPT), lambda i, place: (0, i, 0, 0))] * 2
            + [pl.BlockSpec(table.shape, lambda i, place: (0, 0, 0, 0, 0))],
            out_specs=pl.BlockSpec((2, KEPT, KEPT), lambda i, place: (0, 0, i)),
        ),
        out_shape=jax.ShapeDtypeStruct((2, KEPT, 512), jnp.float32),
        compiler_params=params(VMEM),
        cost_estimate=cost(512 * 512 * 256, 4 * MIB),
        name="part_y",
    )(place, *pieces, table)


def part_z_kernel(place_ref, p0, p2, table_ref, out_ref):
    pairs = [(p0[...], p2[...], place_ref[0])]
    for odd, values in enumerate(transform(True, pairs, table_ref)):
        out_ref[0, :, odd * 256 : (odd + 1) * 256] = values


def part_z(place, pieces, table):
    return pl.pallas_call(
        part_z_kernel,
        grid_spec=pltpu.PrefetchScalarGridSpec(
            num_scalar_prefetch=1,
            grid=(2,),
            in_specs=[pl.BlockSpec((2, 1, KEPT, 128), lambda i, place: (0, i, 0, 0))] * 2
            + [pl.BlockSpec(table.shape, lambda i, place: (0, 0, 0, 0, 0))],
            out_specs=pl.BlockSpec((1, KEPT, 512), lambda i, place: (i, 0, 0)),
        ),
        out_shape=jax.ShapeDtypeStruct((2, KEPT, 512), jnp.float32),
        compiler_params=params(VMEM),
        cost_estimate=cost(512 * 512 * 256, 4 * MIB),
        name="part_z",
    )(place, *pieces, table)


def second_kernel(
    y_ref, z_ref, part_a, a0, a2, table_y_ref, part_b, b1, b3, table_z_ref, out_ref, held
):
    odd = pl.program_id(0)

    def put(values, half, row):
        held[pl.ds(half * 8 + row, 128, stride=16), :] = values

    base = lax.rem(y_ref[0], 2)
    flip = jnp.where(odd == 0, 1.0, -1.0).astype(jnp.float32)
    sign = jnp.where((odd == 0) | (y_ref[0] < 2), 1.0, -1.0).astype(jnp.float32)
    table = (table_y_ref[0, base, 0], table_y_ref[1, base, 0])
    values = part_a[0] + product(table, columns_y((a0[...] + flip * a2[...]) * sign))
    for plane in range(2):
        for x in range(2):
            for half in range(2):
                start = x * KEPT + half * 128
                put(
                    values[plane * 128 : (plane + 1) * 128, start : start + 128],
                    half,
                    plane * 4 + x,
                )
    parts = transform(True, [(b1[...], b3[...], lax.rem(z_ref[0] + 3, 4))], table_z_ref)
    for half, values in enumerate(parts):
        values = values + part_b[:, :, half * 256 : (half + 1) * 256].reshape(256, 256)
        for x in range(2):
            for plane in range(2):
                put(
                    values[x * 128 : (x + 1) * 128, plane * 128 : (plane + 1) * 128],
                    half,
                    plane * 4 + 2 + x,
                )
    out_ref[...] = held[...].reshape(128, 1, 2, 8, 128)


def second(gy, gz, part_a, pieces_a, table_y, part_b, pieces_b, table_z):
    return pl.pallas_call(
        second_kernel,
        grid_spec=pltpu.PrefetchScalarGridSpec(
            num_scalar_prefetch=2,
            grid=(2,),
            in_specs=[pl.BlockSpec((1, KEPT, 512), lambda i, gy, gz: (i, 0, 0))]
            + [pl.BlockSpec((2, 2, 128, KEPT), lambda i, gy, gz: (0, 0, 0, 0))] * 2
            + [
                pl.BlockSpec((2, 2, 1, KEPT, KEPT), lambda i, gy, gz: (0, 0, i, 0, 0)),
                pl.BlockSpec((2, 128, 512), lambda i, gy, gz: (0, i, 0)),
            ]
            + [pl.BlockSpec((2, 2, 128, 128), lambda i, gy, gz: (0, 0, i, 0))] * 2
            + [pl.BlockSpec(table_z.shape, lambda i, gy, gz: (0, 0, 0, 0, 0))],
            out_specs=pl.BlockSpec((128, 1, 2, 8, 128), lambda i, gy, gz: (0, i, 0, 0, 0)),
            scratch_shapes=[pltpu.VMEM((2048, 128), jnp.float32)],
        ),
        out_shape=jax.ShapeDtypeStruct((128, 2, 2, 8, 128), jnp.float32),
        compiler_params=params(VMEM),
        cost_estimate=cost(512 * 512 * 512, 8 * MIB),
        name="second",
    )(gy, gz, part_a, *pieces_a, table_y, part_b, *pieces_b, table_z)


def third_kernel(slot_ref, in_ref, table_ref, ordering_ref, out_ref, held):
    out_ref[...] = jnp.zeros_like(out_ref)
    for parity in range(2):
        columns = jnp.concatenate(
            [in_ref[:, parity, half].reshape(1024, 128) for half in range(2)], axis=1
        )
        first, last = columns[:512], columns[512:]
        for odd, sides in enumerate((first + last, first - last)):
            sides = tuple(
                jnp.dot(
                    part, ordering_ref[...], preferred_element_type=jnp.float32
                ).astype(jnp.bfloat16)
                for part in halves(sides)
            )
            values = jnp.exp(product((table_ref[0, odd], table_ref[1, odd]), sides))
            for plane in range(2):
                for half in range(2):
                    held[parity, plane, half, odd * 128 : (odd + 1) * 128] = values[
                        plane * 128 : (plane + 1) * 128, half * 128 : (half + 1) * 128
                    ]

    def place_rows(group, carry):
        for offset in range(4):
            x = group * 4 + offset
            row = group * 2 + offset // 2 + 128 * (offset % 2)
            for parity in range(2):
                for half in range(2):
                    slot = slot_ref[x * 4 + parity * 2 + half]
                    for plane in range(2):
                        out_ref[pl.ds(slot * 2 + plane, 1), :] = held[
                            parity, plane, half, pl.ds(row, 1), :
                        ]
        return carry

    lax.fori_loop(0, KEPT // 4, place_rows, 0)


def third(slots, arrived, table_x, ordering):
    vmem = pl.BlockSpec(memory_space=pltpu.VMEM)
    return pl.pallas_call(
        third_kernel,
        in_specs=[pl.BlockSpec(memory_space=pltpu.SMEM)] + [vmem] * 3,
        out_specs=vmem,
        out_shape=jax.ShapeDtypeStruct((4096, 128), jnp.float32),
        scratch_shapes=[pltpu.VMEM((2, 2, 2, KEPT, 128), jnp.float32)],
        compiler_params=params(VMEM),
        cost_estimate=cost(768 * 512 * 512, 6 * MIB),
        name="third",
    )(slots, arrived, table_x, ordering)


def shifted(piece, axis, shift):
    size = lax.axis_size(axis)
    return lax.ppermute(piece, axis, [(i, (i + shift) % size) for i in range(size)])


def slots_of(block_owner):
    destination = block_owner[:, 0]
    one_hot = (destination[:, None] == jnp.arange(128, dtype=jnp.int32)[None, :]).astype(jnp.int32)
    earlier = jnp.cumsum(one_hot, axis=0) - one_hot
    return destination * CAP + jnp.sum(earlier * one_hot, axis=1)


def per_device(normals, spectrum, block_owner):
    table_x, table_y, table_z, ordering = (jnp.asarray(table) for table in tables())
    gy = lax.axis_index("gy").astype(jnp.int32).reshape(1)
    gz = lax.axis_index("gz").astype(jnp.int32).reshape(1)

    (a,) = scale(0, (0, 1, 2, 3), False, gz, normals, spectrum)
    a, place = lax.optimization_barrier((a, gy))
    a = lax.all_to_all(a, "gz", split_axis=0, concat_axis=0, tiled=True)
    b1, b3, b2 = scale(1, (1, 3, 2), True, place, normals, spectrum)
    place, b1, b3, b2 = lax.optimization_barrier((place, b1, b3, b2))
    b1, b3, b2 = shifted(b1, "gy", 1), shifted(b3, "gy", 3), shifted(b2, "gy", 2)
    (b0,) = scale(1, (0,), True, place, normals, spectrum)

    a, slots, b0 = lax.optimization_barrier((a, slots_of(block_owner), b0))
    a1, a3, a2, a0 = first(True, (1, 3, 2, 0), gz, gy, a, table_z)
    b1, b2, b3, _ = lax.optimization_barrier((b1, b2, b3, a1))
    pieces = [b0, b1, b2, b3]
    a1, a3 = shifted(a1, "gy", 1), shifted(a3, "gy", 3)
    b2, b1 = first(False, (2, 1), gy, gz, pieces, table_y)
    a2, b2, b1 = lax.optimization_barrier((a2, b2, b1))
    b2, b1, a2 = shifted(b2, "gz", 2), shifted(b1, "gz", 1), shifted(a2, "gy", 2)
    b3, b0 = first(False, (3, 0), gy, gz, pieces, table_y)
    b3 = shifted(b3, "gz", 3)

    part_a = part_y(gy, (a1, a3), table_y)
    part_a, b2 = lax.optimization_barrier((part_a, b2))
    part_b = part_z(gz, (b0, b2), table_z)
    part_b, a2, b1, b3 = lax.optimization_barrier((part_b, a2, b1, b3))
    planes = second(gy, gz, part_a, (a0, a2), table_y, part_b, (b1, b3), table_z)
    lines = lax.all_to_all(planes, ALL, split_axis=0, concat_axis=0, tiled=True)
    outgoing = third(slots, lines, table_x, ordering)
    return lax.all_to_all(
        outgoing.reshape(128, 1, CAP, 2, BW), ALL, split_axis=0, concat_axis=1, tiled=True
    )


def solution(mesh):
    placed = (P(None, "gx", "gy", "gz"), P("gx", "gy", "gz"), P(ALL, None))
    return jax.shard_map(
        per_device,
        mesh=mesh,
        in_specs=placed,
        out_specs=P(ALL, None, None, None, None),
        check_vma=False,
    )
```

```python
import functools

import jax
import jax.numpy as jnp
import ml_dtypes
import numpy as np
from jax import lax
from jax.experimental import pallas as pl
from jax.experimental.pallas import tpu as pltpu
from jax.sharding import PartitionSpec as P

N = 512
KEPT = 256
BW = 128
CAP = 16
ALL = ("gx", "gy", "gz")
MIB = 1 << 20
VMEM = 24


def split_table(table):
    high = table.astype(np.float32).astype(ml_dtypes.bfloat16)
    low = (table - high.astype(np.float64)).astype(np.float32).astype(ml_dtypes.bfloat16)
    return np.stack([high, low])


def cos_sin(positions, kept):
    angles = (positions[:, None] * kept[None, :] % N) * (2.0 * np.pi / N)
    return np.cos(angles), np.sin(angles)


@functools.cache
def tables():
    order = np.arange(KEPT).reshape(KEPT // 2, 2).T.reshape(-1)
    cosine, sine = cos_sin(np.arange(N // 2), order)
    cosine, sine = (t.reshape(2, 128, 2, 128).transpose(0, 2, 1, 3) for t in (cosine, sine))
    real_rows = np.concatenate([cosine, -sine], 3)
    imag_rows = np.concatenate([sine, cosine], 3)
    table_z = np.concatenate([real_rows, imag_rows], 2)
    cosine, sine = cos_sin(np.arange(N // 2), order)
    cosine, sine = (t.T.reshape(2, 128, 2, 128).transpose(2, 0, 1, 3) for t in (cosine, sine))
    top = np.concatenate([cosine, sine], 3)
    bottom = np.concatenate([-sine, cosine], 3)
    table_y = np.concatenate([top, bottom], 2)
    gx, gy, gz = np.meshgrid(np.arange(8), np.arange(4), np.arange(4), indexing="ij")
    first = 64 * gx + 8 * gz + 2 * gy
    second = 64 * gx + 32 + 8 * gy + gz
    cells = np.stack([first, first + 1, second, second + 4], -1).reshape(128, 4)
    cosine, sine = cos_sin(cells[:64].reshape(-1), order)
    cosine, sine = (
        t.T.reshape(2, KEPT // 2, 64, 1, 4) for t in (cosine, sine)
    )
    top = np.concatenate([cosine, sine], 3).reshape(2, KEPT // 2, 512)
    bottom = np.concatenate([-sine, cosine], 3).reshape(2, KEPT // 2, 512)
    table_x = np.concatenate([top, bottom], 1)
    ordering = np.zeros((KEPT, KEPT), ml_dtypes.bfloat16)
    ordering[np.arange(KEPT), order] = 1
    return split_table(table_x), split_table(table_y), split_table(table_z), ordering


def halves(values):
    high = values.astype(jnp.bfloat16)
    low = (values - high.astype(jnp.float32)).astype(jnp.bfloat16)
    return high, low


def product(left, right):
    def dot(a, b):
        return jnp.dot(a, b, preferred_element_type=jnp.float32)

    return dot(left[0], right[0]) + (dot(left[0], right[1]) + dot(left[1], right[0]))


def params(mib):
    return pltpu.CompilerParams(vmem_limit_bytes=mib * MIB)


def cost(multiplies, moved):
    return pl.CostEstimate(
        flops=multiplies >> 16, bytes_accessed=moved >> 16, transcendentals=0
    )


def rows_z(piece):
    return halves(jnp.concatenate([piece[plane].reshape(-1, 128) for plane in range(2)], axis=1))


def columns_y(piece):
    planes, cells = piece.shape[:2]
    return halves(
        jnp.concatenate([piece[:, x].reshape(256, piece.shape[3]) for x in range(cells)], axis=1)
    )


def in_hbm(*arrays):
    return [pltpu.with_memory_space_constraint(x, pltpu.HBM) for x in arrays]


def scale_kernel(part, shifts, place_ref, normals_ref, spectrum_ref, *refs):
    *out_refs, held_out, held_n, held_s, semaphores = refs

    def gets(i):
        if part is None:
            source_n, source_s = normals_ref.at[:, i], spectrum_ref.at[i]
        else:
            chunk = 4 + lax.rem(place_ref[0] + shifts[i], 4)
            source_n, source_s = normals_ref.at[:, chunk, part], spectrum_ref.at[chunk, part]
        return (
            pltpu.make_async_copy(source_n, held_n.at[i], semaphores.at[i, 0]),
            pltpu.make_async_copy(source_s, held_s.at[i], semaphores.at[i, 1]),
        )

    def put(i):
        target = out_refs[0].at[i] if part is None else out_refs[i]
        return pltpu.make_async_copy(held_out.at[i], target, semaphores.at[i, 2])

    steps = range(len(shifts))
    for i in steps:
        for copy in gets(i):
            copy.start()
    for i in steps:
        for copy in gets(i):
            copy.wait()
        for plane in range(2):
            held_out[i, plane] = held_n[i, plane].astype(jnp.float32) * held_s[i]
        put(i).start()
    for i in steps:
        put(i).wait()


def scale(part, shifts, place, normals, spectrum):
    count = len(shifts)
    chunk = (2, 8 if part is None else 4, 128, 128)
    shapes = [(count,) + chunk] if part is None else [chunk] * count
    view = (8, 8, 128, 128) if part is None else (8, 2, 4, 128, 128)
    hbm = pl.BlockSpec(memory_space=pltpu.HBM)
    return pl.pallas_call(
        functools.partial(scale_kernel, part, shifts),
        in_specs=[pl.BlockSpec(memory_space=pltpu.SMEM)] + [hbm] * 2,
        out_specs=[hbm] * len(shapes),
        out_shape=[pltpu.HBM(shape, jnp.float32) for shape in shapes],
        scratch_shapes=[
            pltpu.VMEM((count,) + chunk, jnp.float32),
            pltpu.VMEM((count,) + chunk, jnp.bfloat16),
            pltpu.VMEM((count,) + chunk[1:], jnp.float32),
            pltpu.SemaphoreType.DMA((count, 3)),
        ],
        compiler_params=params(VMEM),
        cost_estimate=cost(count << 18, 2 * count * MIB),
        name="scale_a" if part is None else "scale_b",
    )(place, *in_hbm(normals.reshape((2,) + view), spectrum.reshape(view)))


def transform(along_z, pairs, table_ref):
    parts = []
    for odd in range(2):
        total = None
        for first, second, g in pairs:
            base = lax.rem(g, 2)
            table = (table_ref[0, base, odd], table_ref[1, base, odd])
            if odd:
                sides = (first - second) * jnp.where(g < 2, 1.0, -1.0).astype(jnp.float32)
            else:
                sides = first + second
            if along_z:
                term = product(rows_z(sides), table)
            else:
                term = product(table, columns_y(sides))
            total = term if total is None else total + term
        parts.append(total)
    return parts


def first_z_kernel(shifts, to_ref, in_ref, table_ref, *refs):
    *out_refs, pieces, held_out, semaphores = refs

    def get(i):
        cells = pl.ds(2 * lax.rem(to_ref[0] + shifts[i], 4), 2)
        return pltpu.make_async_copy(in_ref.at[:, :, cells], pieces.at[i], semaphores.at[i, 0])

    def put(i):
        return pltpu.make_async_copy(held_out.at[i], out_refs[i], semaphores.at[i, 1])

    steps = range(len(shifts))
    for i in steps:
        get(i).start()
    for i in steps:
        get(i).wait()
        pairs = [(pieces[i, 0], pieces[i, 2], 0), (pieces[i, 1], pieces[i, 3], 1)]
        for odd, values in enumerate(transform(True, pairs, table_ref)):
            half = slice(odd * 128, (odd + 1) * 128)
            for plane in range(2):
                part = slice(plane * 128, (plane + 1) * 128)
                for x in range(2):
                    held_out[i, plane, x, :, half] = values[x * 128 : (x + 1) * 128, part]
        put(i).start()
    for i in steps:
        put(i).wait()


def first_z(shifts, to, arrived, table):
    shape = (2, 2, 128, KEPT)
    hbm = pl.BlockSpec(memory_space=pltpu.HBM)
    count = len(shifts)
    return pl.pallas_call(
        functools.partial(first_z_kernel, shifts),
        in_specs=[
            pl.BlockSpec(memory_space=pltpu.SMEM),
            hbm,
            pl.BlockSpec(memory_space=pltpu.VMEM),
        ],
        out_specs=[hbm] * count,
        out_shape=[pltpu.HBM(shape, jnp.float32)] * count,
        scratch_shapes=[
            pltpu.VMEM((count, 4, 2, 2, 128, 128), jnp.float32),
            pltpu.VMEM((count,) + shape, jnp.float32),
            pltpu.SemaphoreType.DMA((count, 2)),
        ],
        compiler_params=params(VMEM),
        cost_estimate=cost(count * 256 * 512 * 512, 2 * count * MIB),
        name="first_z",
    )(to, *in_hbm(arrived), table)


def first_y_kernel(merge, place_ref, to_ref, *refs):
    in_refs, refs = refs[:4], refs[4:]
    before, refs = (refs[:2], refs[2:]) if merge else ((), refs)
    table_ref, *out_refs, pieces, held_out, semaphores = refs
    gets = [
        pltpu.make_async_copy(ref, pieces.at[s], semaphores.at[0, s])
        for s, ref in enumerate(in_refs)
    ]
    puts = []
    for i, shift in enumerate((1, 3, 2, 0)):
        whole = merge and i >= 2
        source = held_out.at[lax.rem(to_ref[0] + shift, 4)]
        target = out_refs[i].at[:, 1 if whole else 0]
        puts.append(pltpu.make_async_copy(source, target, semaphores.at[1, i]))
    moves = [
        pltpu.make_async_copy(ref.at[:, 0], out_refs[2 + i].at[:, 0], semaphores.at[2, i])
        for i, ref in enumerate(before)
    ]
    for copy in gets + moves:
        copy.start()
    for copy in gets:
        copy.wait()
    g, h = place_ref[0], lax.rem(place_ref[0] + 3, 4)
    pairs = [(pieces[0], pieces[2], g), (pieces[1], pieces[3], h)]
    for odd, values in enumerate(transform(False, pairs, table_ref)):
        for plane in range(2):
            for x in range(4):
                held_out[x, plane, odd * 128 : (odd + 1) * 128] = values[
                    plane * 128 : (plane + 1) * 128, x * 128 : (x + 1) * 128
                ]
    for copy in puts:
        copy.start()
    for copy in puts + moves:
        copy.wait()


def first_y(place, to, pieces, table, before=()):
    merge = bool(before)
    shape = (2, 1, KEPT, 128)
    whole = (2, 2, KEPT, 128) if merge else shape
    hbm = pl.BlockSpec(memory_space=pltpu.HBM)
    operands = in_hbm(*pieces, *before)
    return pl.pallas_call(
        functools.partial(first_y_kernel, merge),
        in_specs=[pl.BlockSpec(memory_space=pltpu.SMEM)] * 2
        + [hbm] * len(operands)
        + [pl.BlockSpec(memory_space=pltpu.VMEM)],
        out_specs=[hbm] * 4,
        out_shape=[pltpu.HBM(shape, jnp.float32)] * 2 + [pltpu.HBM(whole, jnp.float32)] * 2,
        scratch_shapes=[
            pltpu.VMEM((4, 2, 4, 128, 128), jnp.float32),
            pltpu.VMEM((4, 2, KEPT, 128), jnp.float32),
            pltpu.SemaphoreType.DMA((3, 4)),
        ],
        compiler_params=params(VMEM),
        cost_estimate=cost(512 * 512 * 512, 4 * MIB),
        name="first_y",
    )(place, to, *operands, table)


def part_y_kernel(place_ref, p1, p3, table_ref, out_ref):
    pairs = [(p1[...], p3[...], lax.rem(place_ref[0] + 3, 4))]
    for odd, values in enumerate(transform(False, pairs, table_ref)):
        out_ref[odd] = values


def part_y(place, pieces, table):
    return pl.pallas_call(
        part_y_kernel,
        grid_spec=pltpu.PrefetchScalarGridSpec(
            num_scalar_prefetch=1,
            grid=(2,),
            in_specs=[pl.BlockSpec((2, 1, 128, KEPT), lambda i, place: (0, i, 0, 0))] * 2
            + [pl.BlockSpec(table.shape, lambda i, place: (0, 0, 0, 0, 0))],
            out_specs=pl.BlockSpec((2, KEPT, KEPT), lambda i, place: (0, 0, i)),
        ),
        out_shape=jax.ShapeDtypeStruct((2, KEPT, 512), jnp.float32),
        compiler_params=params(VMEM),
        cost_estimate=cost(512 * 512 * 256, 4 * MIB),
        name="part_y",
    )(place, *pieces, table)


def second_z_kernel(place_ref, b0, b2, c1, c3, d1, d3, table_ref, out_ref):
    g, h = place_ref[0], lax.rem(place_ref[0] + 3, 4)
    for x, (p1, p3) in enumerate(((c1, c3), (d1, d3))):
        cell = slice(x, x + 1)
        pairs = [(b0[:, cell], b2[:, cell], g), (p1[...], p3[...], h)]
        for odd, values in enumerate(transform(True, pairs, table_ref)):
            out_ref[x, :, odd * 256 : (odd + 1) * 256] = values


def second_z(place, pieces, table):
    vmem = pl.BlockSpec(memory_space=pltpu.VMEM)
    return pl.pallas_call(
        second_z_kernel,
        in_specs=[pl.BlockSpec(memory_space=pltpu.SMEM)] + [vmem] * 7,
        out_specs=vmem,
        out_shape=jax.ShapeDtypeStruct((2, KEPT, 512), jnp.float32),
        compiler_params=params(VMEM),
        cost_estimate=cost(512 * 512 * 512, 4 * MIB),
        name="second_z",
    )(place, *pieces, table)


def second_kernel(
    y_ref, part_a, a0, a2, table_y_ref, done_b, out_ref, held
):
    odd = pl.program_id(0)

    def put(values, half, row):
        held[pl.ds(half * 8 + row, 128, stride=16), :] = values

    base = lax.rem(y_ref[0], 2)
    flip = jnp.where(odd == 0, 1.0, -1.0).astype(jnp.float32)
    sign = jnp.where((odd == 0) | (y_ref[0] < 2), 1.0, -1.0).astype(jnp.float32)
    table = (table_y_ref[0, base, 0], table_y_ref[1, base, 0])
    values = part_a[0] + product(table, columns_y((a0[...] + flip * a2[...]) * sign))
    for plane in range(2):
        for x in range(2):
            for half in range(2):
                start = x * KEPT + half * 128
                put(
                    values[plane * 128 : (plane + 1) * 128, start : start + 128],
                    half,
                    plane * 4 + x,
                )
    for half in range(2):
        values = done_b[:, :, half * 256 : (half + 1) * 256].reshape(256, 256)
        for x in range(2):
            for plane in range(2):
                put(
                    values[x * 128 : (x + 1) * 128, plane * 128 : (plane + 1) * 128],
                    half,
                    plane * 4 + 2 + x,
                )
    out_ref[...] = held[...].reshape(128, 1, 2, 8, 128)


def second(gy, part_a, pieces_a, table_y, done_b):
    return pl.pallas_call(
        second_kernel,
        grid_spec=pltpu.PrefetchScalarGridSpec(
            num_scalar_prefetch=1,
            grid=(2,),
            in_specs=[pl.BlockSpec((1, KEPT, 512), lambda i, gy: (i, 0, 0))]
            + [pl.BlockSpec((2, 2, 128, KEPT), lambda i, gy: (0, 0, 0, 0))] * 2
            + [
                pl.BlockSpec((2, 2, 1, KEPT, KEPT), lambda i, gy: (0, 0, i, 0, 0)),
                pl.BlockSpec((2, 128, 512), lambda i, gy: (0, i, 0)),
            ],
            out_specs=pl.BlockSpec((128, 1, 2, 8, 128), lambda i, gy: (0, i, 0, 0, 0)),
            scratch_shapes=[pltpu.VMEM((2048, 128), jnp.float32)],
        ),
        out_shape=jax.ShapeDtypeStruct((128, 2, 2, 8, 128), jnp.float32),
        compiler_params=params(VMEM),
        cost_estimate=cost(512 * 512 * 256, 8 * MIB),
        name="second",
    )(gy, part_a, *pieces_a, table_y, done_b)


def third_kernel(slot_ref, in_ref, table_ref, ordering_ref, out_ref, held):
    out_ref[...] = jnp.zeros_like(out_ref)
    for parity in range(2):
        columns = jnp.concatenate(
            [in_ref[:, parity, half].reshape(1024, 128) for half in range(2)], axis=1
        )
        first, last = columns[:512], columns[512:]
        for odd, sides in enumerate((first + last, first - last)):
            sides = tuple(
                jnp.dot(
                    part, ordering_ref[...], preferred_element_type=jnp.float32
                ).astype(jnp.bfloat16)
                for part in halves(sides)
            )
            values = jnp.exp(product((table_ref[0, odd], table_ref[1, odd]), sides))
            for plane in range(2):
                for half in range(2):
                    held[parity, plane, half, odd * 128 : (odd + 1) * 128] = values[
                        plane * 128 : (plane + 1) * 128, half * 128 : (half + 1) * 128
                    ]

    def place_rows(group, carry):
        for offset in range(4):
            x = group * 4 + offset
            row = group * 2 + offset // 2 + 128 * (offset % 2)
            for parity in range(2):
                for half in range(2):
                    slot = slot_ref[x * 4 + parity * 2 + half]
                    for plane in range(2):
                        out_ref[pl.ds(slot * 2 + plane, 1), :] = held[
                            parity, plane, half, pl.ds(row, 1), :
                        ]
        return carry

    lax.fori_loop(0, KEPT // 4, place_rows, 0)


def third(slots, arrived, table_x, ordering):
    vmem = pl.BlockSpec(memory_space=pltpu.VMEM)
    return pl.pallas_call(
        third_kernel,
        in_specs=[pl.BlockSpec(memory_space=pltpu.SMEM)] + [vmem] * 3,
        out_specs=vmem,
        out_shape=jax.ShapeDtypeStruct((4096, 128), jnp.float32),
        scratch_shapes=[pltpu.VMEM((2, 2, 2, KEPT, 128), jnp.float32)],
        compiler_params=params(VMEM),
        cost_estimate=cost(768 * 512 * 512, 6 * MIB),
        name="third",
    )(slots, arrived, table_x, ordering)


def shifted(piece, axis, shift):
    size = lax.axis_size(axis)
    return lax.ppermute(piece, axis, [(i, (i + shift) % size) for i in range(size)])


def slots_of(block_owner):
    destination = block_owner[:, 0]
    one_hot = (destination[:, None] == jnp.arange(128, dtype=jnp.int32)[None, :]).astype(jnp.int32)
    earlier = jnp.cumsum(one_hot, axis=0) - one_hot
    return destination * CAP + jnp.sum(earlier * one_hot, axis=1)


def per_device(normals, spectrum, block_owner):
    table_x, table_y, table_z, ordering = (jnp.asarray(table) for table in tables())
    gy = lax.axis_index("gy").astype(jnp.int32).reshape(1)
    gz = lax.axis_index("gz").astype(jnp.int32).reshape(1)

    (a,) = scale(None, (0, 1, 2, 3), gz, normals, spectrum)
    a, place = lax.optimization_barrier((a, gy))
    a = lax.all_to_all(a, "gz", split_axis=0, concat_axis=0, tiled=True)
    c1, c3, c2 = scale(0, (1, 3, 2), place, normals, spectrum)
    place, c1, c3, c2 = lax.optimization_barrier((place, c1, c3, c2))
    c1, c3, c2 = shifted(c1, "gy", 1), shifted(c3, "gy", 3), shifted(c2, "gy", 2)
    d1, d3, d2 = scale(1, (1, 3, 2), place, normals, spectrum)
    place, d1, d3, d2 = lax.optimization_barrier((place, d1, d3, d2))
    d1, d3, d2 = shifted(d1, "gy", 1), shifted(d3, "gy", 3), shifted(d2, "gy", 2)
    (c0,) = scale(0, (0,), place, normals, spectrum)
    (d0,) = scale(1, (0,), place, normals, spectrum)

    c1, c3, c2, c0 = first_y(gy, gz, (c0, c1, c2, c3), table_y)
    a, slots, _, d0 = lax.optimization_barrier((a, slots_of(block_owner), c1, d0))
    c1, c3 = shifted(c1, "gz", 1), shifted(c3, "gz", 3)
    a1, a3, a2, a0 = first_z((1, 3, 2, 0), gy, a, table_z)
    d1, d2, d3, _ = lax.optimization_barrier((d1, d2, d3, a1))
    a1, a3, a2 = shifted(a1, "gy", 1), shifted(a3, "gy", 3), shifted(a2, "gy", 2)
    d1, d3, b2, b0 = first_y(gy, gz, (d0, d1, d2, d3), table_y, (c2, c0))
    d1, d3, b2 = shifted(d1, "gz", 1), shifted(d3, "gz", 3), shifted(b2, "gz", 2)

    part_a = part_y(gy, (a1, a3), table_y)
    done_b = second_z(gz, (b0, b2, c1, c3, d1, d3), table_z)
    part_a, done_b, a2 = lax.optimization_barrier((part_a, done_b, a2))
    planes = second(gy, part_a, (a0, a2), table_y, done_b)
    lines = lax.all_to_all(planes, ALL, split_axis=0, concat_axis=0, tiled=True)
    outgoing = third(slots, lines, table_x, ordering)
    return lax.all_to_all(
        outgoing.reshape(128, 1, CAP, 2, BW), ALL, split_axis=0, concat_axis=1, tiled=True
    )


def solution(mesh):
    placed = (P(None, "gx", "gy", "gz"), P("gx", "gy", "gz"), P(ALL, None))
    return jax.shard_map(
        per_device,
        mesh=mesh,
        in_specs=placed,
        out_specs=P(ALL, None, None, None, None),
        check_vma=False,
    )
```

```python
import functools

import jax
import jax.numpy as jnp
import ml_dtypes
import numpy as np
from jax import lax
from jax.experimental import pallas as pl
from jax.experimental.pallas import tpu as pltpu
from jax.sharding import PartitionSpec as P

N = 512
KEPT = 256
BW = 128
CAP = 16
ALL = ("gx", "gy", "gz")
MIB = 1 << 20
VMEM = 24


def split_table(table):
    high = table.astype(np.float32).astype(ml_dtypes.bfloat16)
    low = (table - high.astype(np.float64)).astype(np.float32).astype(ml_dtypes.bfloat16)
    return np.stack([high, low])


def cos_sin(positions, kept):
    angles = (positions[:, None] * kept[None, :] % N) * (2.0 * np.pi / N)
    return np.cos(angles), np.sin(angles)


@functools.cache
def tables():
    order = np.arange(KEPT).reshape(KEPT // 2, 2).T.reshape(-1)
    cosine, sine = cos_sin(np.arange(N // 2), order)
    cosine, sine = (t.reshape(2, 128, 2, 128).transpose(0, 2, 1, 3) for t in (cosine, sine))
    real_rows = np.concatenate([cosine, -sine], 3)
    imag_rows = np.concatenate([sine, cosine], 3)
    table_z = np.concatenate([real_rows, imag_rows], 2)
    cosine, sine = cos_sin(np.arange(N // 2), order)
    cosine, sine = (t.T.reshape(2, 128, 2, 128).transpose(2, 0, 1, 3) for t in (cosine, sine))
    top = np.concatenate([cosine, sine], 3)
    bottom = np.concatenate([-sine, cosine], 3)
    table_y = np.concatenate([top, bottom], 2)
    gx, gy, gz = np.meshgrid(np.arange(8), np.arange(4), np.arange(4), indexing="ij")
    first = 64 * gx + 8 * gz + 2 * gy
    second = 64 * gx + 32 + 8 * gy + gz
    cells = np.stack([first, first + 1, second, second + 4], -1).reshape(128, 4)
    cosine, sine = cos_sin(cells[:64].reshape(-1), order)
    cosine, sine = (
        t.T.reshape(2, KEPT // 2, 64, 1, 4) for t in (cosine, sine)
    )
    top = np.concatenate([cosine, sine], 3).reshape(2, KEPT // 2, 512)
    bottom = np.concatenate([-sine, cosine], 3).reshape(2, KEPT // 2, 512)
    table_x = np.concatenate([top, bottom], 1)
    ordering = np.zeros((KEPT, KEPT), ml_dtypes.bfloat16)
    ordering[np.arange(KEPT), order] = 1
    return split_table(table_x), split_table(table_y), split_table(table_z), ordering


def halves(values):
    high = values.astype(jnp.bfloat16)
    low = (values - high.astype(jnp.float32)).astype(jnp.bfloat16)
    return high, low


def product(left, right):
    def dot(a, b):
        return jnp.dot(a, b, preferred_element_type=jnp.float32)

    return dot(left[0], right[0]) + (dot(left[0], right[1]) + dot(left[1], right[0]))


def params(mib):
    return pltpu.CompilerParams(vmem_limit_bytes=mib * MIB)


def cost(multiplies, moved):
    return pl.CostEstimate(
        flops=multiplies >> 16, bytes_accessed=moved >> 16, transcendentals=0
    )


def rows_z(piece):
    return halves(jnp.concatenate([piece[plane].reshape(-1, 128) for plane in range(2)], axis=1))


def columns_y(piece):
    planes, cells = piece.shape[:2]
    return halves(
        jnp.concatenate([piece[:, x].reshape(256, piece.shape[3]) for x in range(cells)], axis=1)
    )


def in_hbm(*arrays):
    return [pltpu.with_memory_space_constraint(x, pltpu.HBM) for x in arrays]


def scale_kernel(part, shifts, place_ref, normals_ref, spectrum_ref, *refs):
    *out_refs, held_out, held_n, held_s, semaphores = refs

    def gets(i):
        if part is None:
            source_n, source_s = normals_ref.at[:, i], spectrum_ref.at[i]
        else:
            chunk = 4 + lax.rem(place_ref[0] + shifts[i], 4)
            source_n, source_s = normals_ref.at[:, chunk, part], spectrum_ref.at[chunk, part]
        return (
            pltpu.make_async_copy(source_n, held_n.at[i], semaphores.at[i, 0]),
            pltpu.make_async_copy(source_s, held_s.at[i], semaphores.at[i, 1]),
        )

    def put(i):
        target = out_refs[0].at[i] if part is None else out_refs[i]
        return pltpu.make_async_copy(held_out.at[i], target, semaphores.at[i, 2])

    steps = range(len(shifts))
    for i in steps:
        for copy in gets(i):
            copy.start()
    for i in steps:
        for copy in gets(i):
            copy.wait()
        for plane in range(2):
            held_out[i, plane] = held_n[i, plane].astype(jnp.float32) * held_s[i]
        put(i).start()
    for i in steps:
        put(i).wait()


def scale(part, shifts, place, normals, spectrum):
    count = len(shifts)
    chunk = (2, 8 if part is None else 4, 128, 128)
    shapes = [(count,) + chunk] if part is None else [chunk] * count
    view = (8, 8, 128, 128) if part is None else (8, 2, 4, 128, 128)
    hbm = pl.BlockSpec(memory_space=pltpu.HBM)
    return pl.pallas_call(
        functools.partial(scale_kernel, part, shifts),
        in_specs=[pl.BlockSpec(memory_space=pltpu.SMEM)] + [hbm] * 2,
        out_specs=[hbm] * len(shapes),
        out_shape=[pltpu.HBM(shape, jnp.float32) for shape in shapes],
        scratch_shapes=[
            pltpu.VMEM((count,) + chunk, jnp.float32),
            pltpu.VMEM((count,) + chunk, jnp.bfloat16),
            pltpu.VMEM((count,) + chunk[1:], jnp.float32),
            pltpu.SemaphoreType.DMA((count, 3)),
        ],
        compiler_params=params(VMEM),
        cost_estimate=cost(count << 18, 2 * count * MIB),
        name="scale_a" if part is None else "scale_b",
    )(place, *in_hbm(normals.reshape((2,) + view), spectrum.reshape(view)))


def transform(along_z, pairs, table_ref):
    parts = []
    for odd in range(2):
        total = None
        for first, second, g in pairs:
            base = lax.rem(g, 2)
            table = (table_ref[0, base, odd], table_ref[1, base, odd])
            if odd:
                sides = (first - second) * jnp.where(g < 2, 1.0, -1.0).astype(jnp.float32)
            else:
                sides = first + second
            if along_z:
                term = product(rows_z(sides), table)
            else:
                term = product(table, columns_y(sides))
            total = term if total is None else total + term
        parts.append(total)
    return parts


def first_z_kernel(shifts, to_ref, in_ref, table_ref, *refs):
    *out_refs, pieces, held_out, semaphores = refs

    def get(i):
        cells = pl.ds(2 * lax.rem(to_ref[0] + shifts[i], 4), 2)
        return pltpu.make_async_copy(in_ref.at[:, :, cells], pieces.at[i], semaphores.at[i, 0])

    def put(i):
        return pltpu.make_async_copy(held_out.at[i], out_refs[i], semaphores.at[i, 1])

    steps = range(len(shifts))
    for i in steps:
        get(i).start()
    for i in steps:
        get(i).wait()
        pairs = [(pieces[i, 0], pieces[i, 2], 0), (pieces[i, 1], pieces[i, 3], 1)]
        for odd, values in enumerate(transform(True, pairs, table_ref)):
            half = slice(odd * 128, (odd + 1) * 128)
            for plane in range(2):
                part = slice(plane * 128, (plane + 1) * 128)
                for x in range(2):
                    held_out[i, plane, x, :, half] = values[x * 128 : (x + 1) * 128, part]
        put(i).start()
    for i in steps:
        put(i).wait()


def first_z(shifts, to, arrived, table):
    shape = (2, 2, 128, KEPT)
    hbm = pl.BlockSpec(memory_space=pltpu.HBM)
    count = len(shifts)
    return pl.pallas_call(
        functools.partial(first_z_kernel, shifts),
        in_specs=[
            pl.BlockSpec(memory_space=pltpu.SMEM),
            hbm,
            pl.BlockSpec(memory_space=pltpu.VMEM),
        ],
        out_specs=[hbm] * count,
        out_shape=[pltpu.HBM(shape, jnp.float32)] * count,
        scratch_shapes=[
            pltpu.VMEM((count, 4, 2, 2, 128, 128), jnp.float32),
            pltpu.VMEM((count,) + shape, jnp.float32),
            pltpu.SemaphoreType.DMA((count, 2)),
        ],
        compiler_params=params(VMEM),
        cost_estimate=cost(count * 256 * 512 * 512, 2 * count * MIB),
        name="first_z",
    )(to, *in_hbm(arrived), table)


def first_y_kernel(merge, place_ref, to_ref, *refs):
    in_refs, refs = refs[:4], refs[4:]
    before, refs = (refs[:2], refs[2:]) if merge else ((), refs)
    table_ref, *out_refs, pieces, held_out, held_before, semaphores = refs
    gets = [
        pltpu.make_async_copy(ref, pieces.at[s], semaphores.at[0, s])
        for s, ref in enumerate(in_refs)
    ]
    puts = []
    for i, shift in enumerate((1, 3, 2, 0)):
        whole = merge and i >= 2
        source = held_out.at[lax.rem(to_ref[0] + shift, 4)]
        target = out_refs[i].at[:, 1 if whole else 0]
        puts.append(pltpu.make_async_copy(source, target, semaphores.at[1, i]))
    gets_before = [
        pltpu.make_async_copy(ref, held_before.at[i], semaphores.at[2, i])
        for i, ref in enumerate(before)
    ]
    puts_before = [
        pltpu.make_async_copy(
            held_before.at[i], out_refs[2 + i].at[:, 0:1], semaphores.at[2, 2 + i]
        )
        for i in range(len(before))
    ]
    for copy in gets + gets_before:
        copy.start()
    for copy in gets_before:
        copy.wait()
    for copy in puts_before:
        copy.start()
    for copy in gets:
        copy.wait()
    g, h = place_ref[0], lax.rem(place_ref[0] + 3, 4)
    pairs = [(pieces[0], pieces[2], g), (pieces[1], pieces[3], h)]
    for odd, values in enumerate(transform(False, pairs, table_ref)):
        for plane in range(2):
            for x in range(4):
                held_out[x, plane, odd * 128 : (odd + 1) * 128] = values[
                    plane * 128 : (plane + 1) * 128, x * 128 : (x + 1) * 128
                ]
    for copy in puts:
        copy.start()
    for copy in puts + puts_before:
        copy.wait()


def first_y(place, to, pieces, table, before=()):
    merge = bool(before)
    shape = (2, 1, KEPT, 128)
    whole = (2, 2, KEPT, 128) if merge else shape
    hbm = pl.BlockSpec(memory_space=pltpu.HBM)
    operands = in_hbm(*pieces, *before)
    return pl.pallas_call(
        functools.partial(first_y_kernel, merge),
        in_specs=[pl.BlockSpec(memory_space=pltpu.SMEM)] * 2
        + [hbm] * len(operands)
        + [pl.BlockSpec(memory_space=pltpu.VMEM)],
        out_specs=[hbm] * 4,
        out_shape=[pltpu.HBM(shape, jnp.float32)] * 2 + [pltpu.HBM(whole, jnp.float32)] * 2,
        scratch_shapes=[
            pltpu.VMEM((4, 2, 4, 128, 128), jnp.float32),
            pltpu.VMEM((4, 2, KEPT, 128), jnp.float32),
            pltpu.VMEM((2,) + shape, jnp.float32),
            pltpu.SemaphoreType.DMA((3, 4)),
        ],
        compiler_params=params(VMEM),
        cost_estimate=cost(512 * 512 * 512, 4 * MIB),
        name="first_y",
    )(place, to, *operands, table)


def part_y_kernel(place_ref, p1, p3, table_ref, out_ref):
    pairs = [(p1[...], p3[...], lax.rem(place_ref[0] + 3, 4))]
    for odd, values in enumerate(transform(False, pairs, table_ref)):
        out_ref[odd] = values


def part_y(place, pieces, table):
    return pl.pallas_call(
        part_y_kernel,
        grid_spec=pltpu.PrefetchScalarGridSpec(
            num_scalar_prefetch=1,
            grid=(2,),
            in_specs=[pl.BlockSpec((2, 1, 128, KEPT), lambda i, place: (0, i, 0, 0))] * 2
            + [pl.BlockSpec(table.shape, lambda i, place: (0, 0, 0, 0, 0))],
            out_specs=pl.BlockSpec((2, KEPT, KEPT), lambda i, place: (0, 0, i)),
        ),
        out_shape=jax.ShapeDtypeStruct((2, KEPT, 512), jnp.float32),
        compiler_params=params(VMEM),
        cost_estimate=cost(512 * 512 * 256, 4 * MIB),
        name="part_y",
    )(place, *pieces, table)


def second_z_kernel(place_ref, b0, b2, c1, c3, d1, d3, table_ref, out_ref):
    g, h = place_ref[0], lax.rem(place_ref[0] + 3, 4)
    for x, (p1, p3) in enumerate(((c1, c3), (d1, d3))):
        cell = slice(x, x + 1)
        pairs = [(b0[:, cell], b2[:, cell], g), (p1[...], p3[...], h)]
        for odd, values in enumerate(transform(True, pairs, table_ref)):
            out_ref[x, :, odd * 256 : (odd + 1) * 256] = values


def second_z(place, pieces, table):
    vmem = pl.BlockSpec(memory_space=pltpu.VMEM)
    return pl.pallas_call(
        second_z_kernel,
        in_specs=[pl.BlockSpec(memory_space=pltpu.SMEM)] + [vmem] * 7,
        out_specs=vmem,
        out_shape=jax.ShapeDtypeStruct((2, KEPT, 512), jnp.float32),
        compiler_params=params(VMEM),
        cost_estimate=cost(512 * 512 * 512, 4 * MIB),
        name="second_z",
    )(place, *pieces, table)


def second_kernel(
    y_ref, part_a, a0, a2, table_y_ref, done_b, out_ref, held
):
    odd = pl.program_id(0)

    def put(values, half, row):
        held[pl.ds(half * 8 + row, 128, stride=16), :] = values

    base = lax.rem(y_ref[0], 2)
    flip = jnp.where(odd == 0, 1.0, -1.0).astype(jnp.float32)
    sign = jnp.where((odd == 0) | (y_ref[0] < 2), 1.0, -1.0).astype(jnp.float32)
    table = (table_y_ref[0, base, 0], table_y_ref[1, base, 0])
    values = part_a[0] + product(table, columns_y((a0[...] + flip * a2[...]) * sign))
    for plane in range(2):
        for x in range(2):
            for half in range(2):
                start = x * KEPT + half * 128
                put(
                    values[plane * 128 : (plane + 1) * 128, start : start + 128],
                    half,
                    plane * 4 + x,
                )
    for half in range(2):
        values = done_b[:, :, half * 256 : (half + 1) * 256].reshape(256, 256)
        for x in range(2):
            for plane in range(2):
                put(
                    values[x * 128 : (x + 1) * 128, plane * 128 : (plane + 1) * 128],
                    half,
                    plane * 4 + 2 + x,
                )
    out_ref[...] = held[...].reshape(128, 1, 2, 8, 128)


def second(gy, part_a, pieces_a, table_y, done_b):
    return pl.pallas_call(
        second_kernel,
        grid_spec=pltpu.PrefetchScalarGridSpec(
            num_scalar_prefetch=1,
            grid=(2,),
            in_specs=[pl.BlockSpec((1, KEPT, 512), lambda i, gy: (i, 0, 0))]
            + [pl.BlockSpec((2, 2, 128, KEPT), lambda i, gy: (0, 0, 0, 0))] * 2
            + [
                pl.BlockSpec((2, 2, 1, KEPT, KEPT), lambda i, gy: (0, 0, i, 0, 0)),
                pl.BlockSpec((2, 128, 512), lambda i, gy: (0, i, 0)),
            ],
            out_specs=pl.BlockSpec((128, 1, 2, 8, 128), lambda i, gy: (0, i, 0, 0, 0)),
            scratch_shapes=[pltpu.VMEM((2048, 128), jnp.float32)],
        ),
        out_shape=jax.ShapeDtypeStruct((128, 2, 2, 8, 128), jnp.float32),
        compiler_params=params(VMEM),
        cost_estimate=cost(512 * 512 * 256, 8 * MIB),
        name="second",
    )(gy, part_a, *pieces_a, table_y, done_b)


def third_kernel(slot_ref, in_ref, table_ref, ordering_ref, out_ref, held):
    out_ref[...] = jnp.zeros_like(out_ref)
    for parity in range(2):
        columns = jnp.concatenate(
            [in_ref[:, parity, half].reshape(1024, 128) for half in range(2)], axis=1
        )
        first, last = columns[:512], columns[512:]
        for odd, sides in enumerate((first + last, first - last)):
            sides = tuple(
                jnp.dot(
                    part, ordering_ref[...], preferred_element_type=jnp.float32
                ).astype(jnp.bfloat16)
                for part in halves(sides)
            )
            values = jnp.exp(product((table_ref[0, odd], table_ref[1, odd]), sides))
            for plane in range(2):
                for half in range(2):
                    held[parity, plane, half, odd * 128 : (odd + 1) * 128] = values[
                        plane * 128 : (plane + 1) * 128, half * 128 : (half + 1) * 128
                    ]

    def place_rows(group, carry):
        for offset in range(4):
            x = group * 4 + offset
            row = group * 2 + offset // 2 + 128 * (offset % 2)
            for parity in range(2):
                for half in range(2):
                    slot = slot_ref[x * 4 + parity * 2 + half]
                    for plane in range(2):
                        out_ref[pl.ds(slot * 2 + plane, 1), :] = held[
                            parity, plane, half, pl.ds(row, 1), :
                        ]
        return carry

    lax.fori_loop(0, KEPT // 4, place_rows, 0)


def third(slots, arrived, table_x, ordering):
    vmem = pl.BlockSpec(memory_space=pltpu.VMEM)
    return pl.pallas_call(
        third_kernel,
        in_specs=[pl.BlockSpec(memory_space=pltpu.SMEM)] + [vmem] * 3,
        out_specs=vmem,
        out_shape=jax.ShapeDtypeStruct((4096, 128), jnp.float32),
        scratch_shapes=[pltpu.VMEM((2, 2, 2, KEPT, 128), jnp.float32)],
        compiler_params=params(VMEM),
        cost_estimate=cost(768 * 512 * 512, 6 * MIB),
        name="third",
    )(slots, arrived, table_x, ordering)


def shifted(piece, axis, shift):
    size = lax.axis_size(axis)
    return lax.ppermute(piece, axis, [(i, (i + shift) % size) for i in range(size)])


def slots_of(block_owner):
    destination = block_owner[:, 0]
    one_hot = (destination[:, None] == jnp.arange(128, dtype=jnp.int32)[None, :]).astype(jnp.int32)
    earlier = jnp.cumsum(one_hot, axis=0) - one_hot
    return destination * CAP + jnp.sum(earlier * one_hot, axis=1)


def per_device(normals, spectrum, block_owner):
    table_x, table_y, table_z, ordering = (jnp.asarray(table) for table in tables())
    gy = lax.axis_index("gy").astype(jnp.int32).reshape(1)
    gz = lax.axis_index("gz").astype(jnp.int32).reshape(1)

    (a,) = scale(None, (0, 1, 2, 3), gz, normals, spectrum)
    a, place = lax.optimization_barrier((a, gy))
    a = lax.all_to_all(a, "gz", split_axis=0, concat_axis=0, tiled=True)
    c1, c3, c2 = scale(0, (1, 3, 2), place, normals, spectrum)
    place, c1, c3, c2 = lax.optimization_barrier((place, c1, c3, c2))
    c1, c3, c2 = shifted(c1, "gy", 1), shifted(c3, "gy", 3), shifted(c2, "gy", 2)
    d1, d3, d2 = scale(1, (1, 3, 2), place, normals, spectrum)
    place, d1, d3, d2 = lax.optimization_barrier((place, d1, d3, d2))
    d1, d3, d2 = shifted(d1, "gy", 1), shifted(d3, "gy", 3), shifted(d2, "gy", 2)
    (c0,) = scale(0, (0,), place, normals, spectrum)
    (d0,) = scale(1, (0,), place, normals, spectrum)

    c1, c3, c2, c0 = first_y(gy, gz, (c0, c1, c2, c3), table_y)
    a, slots, _, d0 = lax.optimization_barrier((a, slots_of(block_owner), c1, d0))
    c1, c3 = shifted(c1, "gz", 1), shifted(c3, "gz", 3)
    a1, a3, a2, a0 = first_z((1, 3, 2, 0), gy, a, table_z)
    d1, d2, d3, c1, c3, _ = lax.optimization_barrier((d1, d2, d3, c1, c3, a1))
    a1, a3, a2 = shifted(a1, "gy", 1), shifted(a3, "gy", 3), shifted(a2, "gy", 2)
    d1, d3, b2, b0 = first_y(gy, gz, (d0, d1, d2, d3), table_y, (c2, c0))
    d1, d3, b2 = shifted(d1, "gz", 1), shifted(d3, "gz", 3), shifted(b2, "gz", 2)

    part_a = part_y(gy, (a1, a3), table_y)
    done_b = second_z(gz, (b0, b2, c1, c3, d1, d3), table_z)
    part_a, done_b, a2 = lax.optimization_barrier((part_a, done_b, a2))
    planes = second(gy, part_a, (a0, a2), table_y, done_b)
    lines = lax.all_to_all(planes, ALL, split_axis=0, concat_axis=0, tiled=True)
    outgoing = third(slots, lines, table_x, ordering)
    return lax.all_to_all(
        outgoing.reshape(128, 1, CAP, 2, BW), ALL, split_axis=0, concat_axis=1, tiled=True
    )


def solution(mesh):
    placed = (P(None, "gx", "gy", "gz"), P("gx", "gy", "gz"), P(ALL, None))
    return jax.shard_map(
        per_device,
        mesh=mesh,
        in_specs=placed,
        out_specs=P(ALL, None, None, None, None),
        check_vma=False,
    )
```

```python
import functools

import jax
import jax.numpy as jnp
import ml_dtypes
import numpy as np
from jax import lax
from jax.experimental import pallas as pl
from jax.experimental.pallas import tpu as pltpu
from jax.sharding import PartitionSpec as P

N = 512
KEPT = 256
BW = 128
CAP = 16
ALL = ("gx", "gy", "gz")
MIB = 1 << 20
VMEM = 24


def split_table(table):
    high = table.astype(np.float32).astype(ml_dtypes.bfloat16)
    low = (table - high.astype(np.float64)).astype(np.float32).astype(ml_dtypes.bfloat16)
    return np.stack([high, low])


def cos_sin(positions, kept):
    angles = (positions[:, None] * kept[None, :] % N) * (2.0 * np.pi / N)
    return np.cos(angles), np.sin(angles)


@functools.cache
def tables():
    order = np.arange(KEPT).reshape(KEPT // 2, 2).T.reshape(-1)
    cosine, sine = cos_sin(np.arange(N // 2), order)
    cosine, sine = (t.reshape(2, 128, 2, 128).transpose(0, 2, 1, 3) for t in (cosine, sine))
    real_rows = np.concatenate([cosine, -sine], 3)
    imag_rows = np.concatenate([sine, cosine], 3)
    table_z = np.concatenate([real_rows, imag_rows], 2)
    cosine, sine = cos_sin(np.arange(N // 2), order)
    cosine, sine = (t.T.reshape(2, 128, 2, 128).transpose(2, 0, 1, 3) for t in (cosine, sine))
    top = np.concatenate([cosine, sine], 3)
    bottom = np.concatenate([-sine, cosine], 3)
    table_y = np.concatenate([top, bottom], 2)
    gx, gy, gz = np.meshgrid(np.arange(8), np.arange(4), np.arange(4), indexing="ij")
    first = 64 * gx + 8 * gz + 2 * gy
    second = 64 * gx + 32 + 8 * gy + gz
    cells = np.stack([first, first + 1, second, second + 4], -1).reshape(128, 4)
    cosine, sine = cos_sin(cells[:64].reshape(-1), order)
    cosine, sine = (
        t.T.reshape(2, KEPT // 2, 64, 1, 4) for t in (cosine, sine)
    )
    top = np.concatenate([cosine, sine], 3).reshape(2, KEPT // 2, 512)
    bottom = np.concatenate([-sine, cosine], 3).reshape(2, KEPT // 2, 512)
    table_x = np.concatenate([top, bottom], 1)
    ordering = np.zeros((KEPT, KEPT), ml_dtypes.bfloat16)
    ordering[np.arange(KEPT), order] = 1
    return split_table(table_x), split_table(table_y), split_table(table_z), ordering


def halves(values):
    high = values.astype(jnp.bfloat16)
    low = (values - high.astype(jnp.float32)).astype(jnp.bfloat16)
    return high, low


def product(left, right):
    def dot(a, b):
        return jnp.dot(a, b, preferred_element_type=jnp.float32)

    return dot(left[0], right[0]) + (dot(left[0], right[1]) + dot(left[1], right[0]))


def params(mib):
    return pltpu.CompilerParams(vmem_limit_bytes=mib * MIB)


def cost(multiplies, moved):
    return pl.CostEstimate(
        flops=multiplies >> 16, bytes_accessed=moved >> 16, transcendentals=0
    )


def rows_z(piece):
    return halves(jnp.concatenate([piece[plane].reshape(-1, 128) for plane in range(2)], axis=1))


def columns_y(piece):
    planes, cells = piece.shape[:2]
    return halves(
        jnp.concatenate([piece[:, x].reshape(256, piece.shape[3]) for x in range(cells)], axis=1)
    )


def in_hbm(*arrays):
    return [pltpu.with_memory_space_constraint(x, pltpu.HBM) for x in arrays]


def scale_kernel(part, shifts, place_ref, normals_ref, spectrum_ref, *refs):
    *out_refs, held_out, held_n, held_s, semaphores = refs

    def gets(i):
        if part is None:
            source_n, source_s = normals_ref.at[:, i], spectrum_ref.at[i]
        else:
            chunk = 4 + lax.rem(place_ref[0] + shifts[i], 4)
            source_n, source_s = normals_ref.at[:, chunk, part], spectrum_ref.at[chunk, part]
        return (
            pltpu.make_async_copy(source_n, held_n.at[i], semaphores.at[i, 0]),
            pltpu.make_async_copy(source_s, held_s.at[i], semaphores.at[i, 1]),
        )

    def put(i):
        target = out_refs[0].at[i] if part is None else out_refs[i]
        return pltpu.make_async_copy(held_out.at[i], target, semaphores.at[i, 2])

    steps = range(len(shifts))
    for i in steps:
        for copy in gets(i):
            copy.start()
    for i in steps:
        for copy in gets(i):
            copy.wait()
        for plane in range(2):
            held_out[i, plane] = held_n[i, plane].astype(jnp.float32) * held_s[i]
        put(i).start()
    for i in steps:
        put(i).wait()


def scale(part, shifts, place, normals, spectrum):
    count = len(shifts)
    chunk = (2, 8 if part is None else 4, 128, 128)
    shapes = [(count,) + chunk] if part is None else [chunk] * count
    view = (8, 8, 128, 128) if part is None else (8, 2, 4, 128, 128)
    hbm = pl.BlockSpec(memory_space=pltpu.HBM)
    return pl.pallas_call(
        functools.partial(scale_kernel, part, shifts),
        in_specs=[pl.BlockSpec(memory_space=pltpu.SMEM)] + [hbm] * 2,
        out_specs=[hbm] * len(shapes),
        out_shape=[pltpu.HBM(shape, jnp.float32) for shape in shapes],
        scratch_shapes=[
            pltpu.VMEM((count,) + chunk, jnp.float32),
            pltpu.VMEM((count,) + chunk, jnp.bfloat16),
            pltpu.VMEM((count,) + chunk[1:], jnp.float32),
            pltpu.SemaphoreType.DMA((count, 3)),
        ],
        compiler_params=params(VMEM),
        cost_estimate=cost(count << 18, 2 * count * MIB),
        name="scale_a" if part is None else "scale_b",
    )(place, *in_hbm(normals.reshape((2,) + view), spectrum.reshape(view)))


def transform(along_z, pairs, table_ref):
    parts = []
    for odd in range(2):
        total = None
        for first, second, g in pairs:
            base = lax.rem(g, 2)
            table = (table_ref[0, base, odd], table_ref[1, base, odd])
            if odd:
                sides = (first - second) * jnp.where(g < 2, 1.0, -1.0).astype(jnp.float32)
            else:
                sides = first + second
            if along_z:
                term = product(rows_z(sides), table)
            else:
                term = product(table, columns_y(sides))
            total = term if total is None else total + term
        parts.append(total)
    return parts


def first_z_kernel(in_ref, table_ref, out_ref, pieces, held_out, semaphores):
    def get(i):
        cells = pl.ds(2 * i, 2)
        return pltpu.make_async_copy(in_ref.at[:, :, cells], pieces.at[i], semaphores.at[i, 0])

    def put(i):
        return pltpu.make_async_copy(held_out.at[i], out_ref.at[i], semaphores.at[i, 1])

    for i in range(4):
        get(i).start()
    for i in range(4):
        get(i).wait()
        pairs = [(pieces[i, 0], pieces[i, 2], 0), (pieces[i, 1], pieces[i, 3], 1)]
        for odd, values in enumerate(transform(True, pairs, table_ref)):
            half = slice(odd * 128, (odd + 1) * 128)
            for plane in range(2):
                part = slice(plane * 128, (plane + 1) * 128)
                for x in range(2):
                    held_out[i, plane, x, :, half] = values[x * 128 : (x + 1) * 128, part]
        put(i).start()
    for i in range(4):
        put(i).wait()


def first_z(arrived, table):
    shape = (4, 2, 2, 128, KEPT)
    hbm = pl.BlockSpec(memory_space=pltpu.HBM)
    return pl.pallas_call(
        first_z_kernel,
        in_specs=[hbm, pl.BlockSpec(memory_space=pltpu.VMEM)],
        out_specs=hbm,
        out_shape=pltpu.HBM(shape, jnp.float32),
        scratch_shapes=[
            pltpu.VMEM((4, 4, 2, 2, 128, 128), jnp.float32),
            pltpu.VMEM(shape, jnp.float32),
            pltpu.SemaphoreType.DMA((4, 2)),
        ],
        compiler_params=params(VMEM),
        cost_estimate=cost(4 * 256 * 512 * 512, 8 * MIB),
        name="first_z",
    )(*in_hbm(arrived), table)


def first_y_kernel(merge, place_ref, to_ref, *refs):
    in_refs, refs = refs[:4], refs[4:]
    before, refs = (refs[:2], refs[2:]) if merge else ((), refs)
    table_ref, *out_refs, pieces, held_out, held_before, semaphores = refs
    gets = [
        pltpu.make_async_copy(ref, pieces.at[s], semaphores.at[0, s])
        for s, ref in enumerate(in_refs)
    ]
    puts = []
    for i, shift in enumerate((1, 3, 2, 0)):
        whole = merge and i >= 2
        source = held_out.at[lax.rem(to_ref[0] + shift, 4)]
        target = out_refs[i].at[:, 1 if whole else 0]
        puts.append(pltpu.make_async_copy(source, target, semaphores.at[1, i]))
    gets_before = [
        pltpu.make_async_copy(ref, held_before.at[i], semaphores.at[2, i])
        for i, ref in enumerate(before)
    ]
    puts_before = [
        pltpu.make_async_copy(
            held_before.at[i], out_refs[2 + i].at[:, 0:1], semaphores.at[2, 2 + i]
        )
        for i in range(len(before))
    ]
    for copy in gets + gets_before:
        copy.start()
    for copy in gets_before:
        copy.wait()
    for copy in puts_before:
        copy.start()
    for copy in gets:
        copy.wait()
    g, h = place_ref[0], lax.rem(place_ref[0] + 3, 4)
    pairs = [(pieces[0], pieces[2], g), (pieces[1], pieces[3], h)]
    for odd, values in enumerate(transform(False, pairs, table_ref)):
        for plane in range(2):
            for x in range(4):
                held_out[x, plane, odd * 128 : (odd + 1) * 128] = values[
                    plane * 128 : (plane + 1) * 128, x * 128 : (x + 1) * 128
                ]
    for copy in puts:
        copy.start()
    for copy in puts + puts_before:
        copy.wait()


def first_y(place, to, pieces, table, before=()):
    merge = bool(before)
    shape = (2, 1, KEPT, 128)
    whole = (2, 2, KEPT, 128) if merge else shape
    hbm = pl.BlockSpec(memory_space=pltpu.HBM)
    operands = in_hbm(*pieces, *before)
    return pl.pallas_call(
        functools.partial(first_y_kernel, merge),
        in_specs=[pl.BlockSpec(memory_space=pltpu.SMEM)] * 2
        + [hbm] * len(operands)
        + [pl.BlockSpec(memory_space=pltpu.VMEM)],
        out_specs=[hbm] * 4,
        out_shape=[pltpu.HBM(shape, jnp.float32)] * 2 + [pltpu.HBM(whole, jnp.float32)] * 2,
        scratch_shapes=[
            pltpu.VMEM((4, 2, 4, 128, 128), jnp.float32),
            pltpu.VMEM((4, 2, KEPT, 128), jnp.float32),
            pltpu.VMEM((2,) + shape, jnp.float32),
            pltpu.SemaphoreType.DMA((3, 4)),
        ],
        compiler_params=params(VMEM),
        cost_estimate=cost(512 * 512 * 512, 4 * MIB),
        name="first_y",
    )(place, to, *operands, table)


def second_y_kernel(p0, p1, p2, p3, table_ref, out_ref):
    pairs = [(p0[0], p2[0], 0), (p1[0], p3[0], 1)]
    for odd, values in enumerate(transform(False, pairs, table_ref)):
        out_ref[odd] = values


def second_y(arrived, table):
    def from_device(g):
        return pl.BlockSpec((1, 2, 1, 128, KEPT), lambda i: (g, 0, i, 0, 0))

    return pl.pallas_call(
        second_y_kernel,
        grid=(2,),
        in_specs=[from_device(g) for g in range(4)]
        + [pl.BlockSpec(table.shape, lambda i: (0, 0, 0, 0, 0))],
        out_specs=pl.BlockSpec((2, KEPT, KEPT), lambda i: (0, 0, i)),
        out_shape=jax.ShapeDtypeStruct((2, KEPT, 512), jnp.float32),
        compiler_params=params(VMEM),
        cost_estimate=cost(512 * 512 * 512, 5 * MIB),
        name="second_y",
    )(arrived, arrived, arrived, arrived, table)


def second_z_kernel(place_ref, b0, b2, c1, c3, d1, d3, table_ref, out_ref):
    g, h = place_ref[0], lax.rem(place_ref[0] + 3, 4)
    for x, (p1, p3) in enumerate(((c1, c3), (d1, d3))):
        cell = slice(x, x + 1)
        pairs = [(b0[:, cell], b2[:, cell], g), (p1[...], p3[...], h)]
        for odd, values in enumerate(transform(True, pairs, table_ref)):
            out_ref[x, :, odd * 256 : (odd + 1) * 256] = values


def second_z(place, pieces, table):
    vmem = pl.BlockSpec(memory_space=pltpu.VMEM)
    return pl.pallas_call(
        second_z_kernel,
        in_specs=[pl.BlockSpec(memory_space=pltpu.SMEM)] + [vmem] * 7,
        out_specs=vmem,
        out_shape=jax.ShapeDtypeStruct((2, KEPT, 512), jnp.float32),
        compiler_params=params(VMEM),
        cost_estimate=cost(512 * 512 * 512, 4 * MIB),
        name="second_z",
    )(place, *pieces, table)


def second_kernel(done_a, done_b, out_ref, held):
    def put(values, half, row):
        held[pl.ds(half * 8 + row, 128, stride=16), :] = values

    for plane in range(2):
        pairs = slice(plane * 128, (plane + 1) * 128)
        for x in range(2):
            for half in range(2):
                start = x * KEPT + half * 128
                put(done_a[0, pairs, start : start + 128], half, plane * 4 + x)
                start = half * KEPT + plane * 128
                put(done_b[x, :, start : start + 128], half, plane * 4 + 2 + x)
    out_ref[...] = held[...].reshape(128, 1, 2, 8, 128)


def second(done_a, done_b):
    return pl.pallas_call(
        second_kernel,
        grid=(2,),
        in_specs=[
            pl.BlockSpec((1, KEPT, 512), lambda i: (i, 0, 0)),
            pl.BlockSpec((2, 128, 512), lambda i: (0, i, 0)),
        ],
        out_specs=pl.BlockSpec((128, 1, 2, 8, 128), lambda i: (0, i, 0, 0, 0)),
        out_shape=jax.ShapeDtypeStruct((128, 2, 2, 8, 128), jnp.float32),
        scratch_shapes=[pltpu.VMEM((2048, 128), jnp.float32)],
        compiler_params=params(VMEM),
        cost_estimate=cost(1 << 20, 4 * MIB),
        name="second",
    )(done_a, done_b)


def third_kernel(slot_ref, in_ref, table_ref, ordering_ref, out_ref, held):
    out_ref[...] = jnp.zeros_like(out_ref)
    for parity in range(2):
        columns = jnp.concatenate(
            [in_ref[:, parity, half].reshape(1024, 128) for half in range(2)], axis=1
        )
        first, last = columns[:512], columns[512:]
        for odd, sides in enumerate((first + last, first - last)):
            sides = tuple(
                jnp.dot(
                    part, ordering_ref[...], preferred_element_type=jnp.float32
                ).astype(jnp.bfloat16)
                for part in halves(sides)
            )
            values = jnp.exp(product((table_ref[0, odd], table_ref[1, odd]), sides))
            for plane in range(2):
                for half in range(2):
                    held[parity, plane, half, odd * 128 : (odd + 1) * 128] = values[
                        plane * 128 : (plane + 1) * 128, half * 128 : (half + 1) * 128
                    ]

    def place_rows(group, carry):
        for offset in range(4):
            x = group * 4 + offset
            row = group * 2 + offset // 2 + 128 * (offset % 2)
            for parity in range(2):
                for half in range(2):
                    slot = slot_ref[x * 4 + parity * 2 + half]
                    for plane in range(2):
                        out_ref[pl.ds(slot * 2 + plane, 1), :] = held[
                            parity, plane, half, pl.ds(row, 1), :
                        ]
        return carry

    lax.fori_loop(0, KEPT // 4, place_rows, 0)


def third(slots, arrived, table_x, ordering):
    vmem = pl.BlockSpec(memory_space=pltpu.VMEM)
    return pl.pallas_call(
        third_kernel,
        in_specs=[pl.BlockSpec(memory_space=pltpu.SMEM)] + [vmem] * 3,
        out_specs=vmem,
        out_shape=jax.ShapeDtypeStruct((4096, 128), jnp.float32),
        scratch_shapes=[pltpu.VMEM((2, 2, 2, KEPT, 128), jnp.float32)],
        compiler_params=params(VMEM),
        cost_estimate=cost(768 * 512 * 512, 6 * MIB),
        name="third",
    )(slots, arrived, table_x, ordering)


def shifted(piece, axis, shift):
    size = lax.axis_size(axis)
    return lax.ppermute(piece, axis, [(i, (i + shift) % size) for i in range(size)])


def slots_of(block_owner):
    destination = block_owner[:, 0]
    one_hot = (destination[:, None] == jnp.arange(128, dtype=jnp.int32)[None, :]).astype(jnp.int32)
    earlier = jnp.cumsum(one_hot, axis=0) - one_hot
    return destination * CAP + jnp.sum(earlier * one_hot, axis=1)


def per_device(normals, spectrum, block_owner):
    table_x, table_y, table_z, ordering = (jnp.asarray(table) for table in tables())
    gy = lax.axis_index("gy").astype(jnp.int32).reshape(1)
    gz = lax.axis_index("gz").astype(jnp.int32).reshape(1)

    (a,) = scale(None, (0, 1, 2, 3), gz, normals, spectrum)
    a, place = lax.optimization_barrier((a, gy))
    a = lax.all_to_all(a, "gz", split_axis=0, concat_axis=0, tiled=True)
    c1, c3, c2 = scale(0, (1, 3, 2), place, normals, spectrum)
    place, c1, c3, c2 = lax.optimization_barrier((place, c1, c3, c2))
    c1, c3, c2 = shifted(c1, "gy", 1), shifted(c3, "gy", 3), shifted(c2, "gy", 2)
    d1, d3, d2 = scale(1, (1, 3, 2), place, normals, spectrum)
    place, d1, d3, d2 = lax.optimization_barrier((place, d1, d3, d2))
    d1, d3, d2 = shifted(d1, "gy", 1), shifted(d3, "gy", 3), shifted(d2, "gy", 2)
    (c0,) = scale(0, (0,), place, normals, spectrum)
    (d0,) = scale(1, (0,), place, normals, spectrum)

    c1, c3, c2, c0 = first_y(gy, gz, (c0, c1, c2, c3), table_y)
    a, slots, _, d0 = lax.optimization_barrier((a, slots_of(block_owner), c1, d0))
    c1, c3 = shifted(c1, "gz", 1), shifted(c3, "gz", 3)
    a = first_z(a, table_z)
    d1, d2, d3, c1, c3, _ = lax.optimization_barrier((d1, d2, d3, c1, c3, a))
    a = lax.all_to_all(a, "gy", split_axis=0, concat_axis=0, tiled=True)
    d1, d3, b2, b0 = first_y(gy, gz, (d0, d1, d2, d3), table_y, (c2, c0))
    d1, d3, b2 = shifted(d1, "gz", 1), shifted(d3, "gz", 3), shifted(b2, "gz", 2)

    a = second_y(a, table_y)
    a, d1, d3, b2 = lax.optimization_barrier((a, d1, d3, b2))
    planes = second(a, second_z(gz, (b0, b2, c1, c3, d1, d3), table_z))
    lines = lax.all_to_all(planes, ALL, split_axis=0, concat_axis=0, tiled=True)
    outgoing = third(slots, lines, table_x, ordering)
    return lax.all_to_all(
        outgoing.reshape(128, 1, CAP, 2, BW), ALL, split_axis=0, concat_axis=1, tiled=True
    )


def solution(mesh):
    placed = (P(None, "gx", "gy", "gz"), P("gx", "gy", "gz"), P(ALL, None))
    return jax.shard_map(
        per_device,
        mesh=mesh,
        in_specs=placed,
        out_specs=P(ALL, None, None, None, None),
        check_vma=False,
    )
```

```python
import functools

import jax
import jax.numpy as jnp
import ml_dtypes
import numpy as np
from jax import lax
from jax.experimental import pallas as pl
from jax.experimental.pallas import tpu as pltpu
from jax.sharding import PartitionSpec as P

N = 512
KEPT = 256
BW = 128
CAP = 16
ALL = ("gx", "gy", "gz")
MIB = 1 << 20
VMEM = 24


def split_table(table):
    high = table.astype(np.float32).astype(ml_dtypes.bfloat16)
    low = (table - high.astype(np.float64)).astype(np.float32).astype(ml_dtypes.bfloat16)
    return np.stack([high, low])


def cos_sin(positions, kept):
    angles = (positions[:, None] * kept[None, :] % N) * (2.0 * np.pi / N)
    return np.cos(angles), np.sin(angles)


@functools.cache
def tables():
    order = np.arange(KEPT).reshape(KEPT // 2, 2).T.reshape(-1)
    cosine, sine = cos_sin(np.arange(N // 2), order)
    cosine, sine = (t.reshape(2, 128, 2, 128).transpose(0, 2, 1, 3) for t in (cosine, sine))
    real_rows = np.concatenate([cosine, -sine], 3)
    imag_rows = np.concatenate([sine, cosine], 3)
    table_z = np.concatenate([real_rows, imag_rows], 2)
    cosine, sine = cos_sin(np.arange(N // 2), order)
    cosine, sine = (t.T.reshape(2, 128, 2, 128).transpose(2, 0, 1, 3) for t in (cosine, sine))
    top = np.concatenate([cosine, sine], 3)
    bottom = np.concatenate([-sine, cosine], 3)
    table_y = np.concatenate([top, bottom], 2)
    gx, gy, gz = np.meshgrid(np.arange(8), np.arange(4), np.arange(4), indexing="ij")
    first = 64 * gx + 8 * gz + 2 * gy
    second = 64 * gx + 32 + 8 * gy + gz
    cells = np.stack([first, first + 1, second, second + 4], -1).reshape(128, 4)
    cosine, sine = cos_sin(cells[:64].reshape(-1), order)
    cosine, sine = (
        t.T.reshape(2, KEPT // 2, 64, 1, 4) for t in (cosine, sine)
    )
    top = np.concatenate([cosine, sine], 3).reshape(2, KEPT // 2, 512)
    bottom = np.concatenate([-sine, cosine], 3).reshape(2, KEPT // 2, 512)
    table_x = np.concatenate([top, bottom], 1)
    ordering = np.zeros((KEPT, KEPT), ml_dtypes.bfloat16)
    ordering[np.arange(KEPT), order] = 1
    return split_table(table_x), split_table(table_y), split_table(table_z), ordering


def halves(values):
    high = values.astype(jnp.bfloat16)
    low = (values - high.astype(jnp.float32)).astype(jnp.bfloat16)
    return high, low


def product(left, right):
    def dot(a, b):
        return jnp.dot(a, b, preferred_element_type=jnp.float32)

    return dot(left[0], right[0]) + (dot(left[0], right[1]) + dot(left[1], right[0]))


def params(mib):
    return pltpu.CompilerParams(vmem_limit_bytes=mib * MIB)


def cost(multiplies, moved):
    return pl.CostEstimate(
        flops=multiplies >> 16, bytes_accessed=moved >> 16, transcendentals=0
    )


def rows_z(piece):
    return halves(jnp.concatenate([piece[plane].reshape(-1, 128) for plane in range(2)], axis=1))


def columns_y(piece):
    planes, cells = piece.shape[:2]
    return halves(
        jnp.concatenate([piece[:, x].reshape(256, piece.shape[3]) for x in range(cells)], axis=1)
    )


def in_hbm(*arrays):
    return [pltpu.with_memory_space_constraint(x, pltpu.HBM) for x in arrays]


def scale_kernel(part, shifts, place_ref, normals_ref, spectrum_ref, *refs):
    *out_refs, held_out, held_n, held_s, semaphores = refs

    def gets(i):
        if part is None:
            source_n, source_s = normals_ref.at[:, i], spectrum_ref.at[i]
        else:
            chunk = 4 + lax.rem(place_ref[0] + shifts[i], 4)
            source_n, source_s = normals_ref.at[:, chunk, part], spectrum_ref.at[chunk, part]
        return (
            pltpu.make_async_copy(source_n, held_n.at[i], semaphores.at[i, 0]),
            pltpu.make_async_copy(source_s, held_s.at[i], semaphores.at[i, 1]),
        )

    def put(i):
        target = out_refs[0].at[i] if part is None else out_refs[i]
        return pltpu.make_async_copy(held_out.at[i], target, semaphores.at[i, 2])

    steps = range(len(shifts))
    for i in steps:
        for copy in gets(i):
            copy.start()
    for i in steps:
        for copy in gets(i):
            copy.wait()
        for plane in range(2):
            held_out[i, plane] = held_n[i, plane].astype(jnp.float32) * held_s[i]
        put(i).start()
    for i in steps:
        put(i).wait()


def scale(part, shifts, place, normals, spectrum):
    count = len(shifts)
    chunk = (2, 8 if part is None else 4, 128, 128)
    shapes = [(count,) + chunk] if part is None else [chunk] * count
    view = (8, 8, 128, 128) if part is None else (8, 2, 4, 128, 128)
    hbm = pl.BlockSpec(memory_space=pltpu.HBM)
    return pl.pallas_call(
        functools.partial(scale_kernel, part, shifts),
        in_specs=[pl.BlockSpec(memory_space=pltpu.SMEM)] + [hbm] * 2,
        out_specs=[hbm] * len(shapes),
        out_shape=[pltpu.HBM(shape, jnp.float32) for shape in shapes],
        scratch_shapes=[
            pltpu.VMEM((count,) + chunk, jnp.float32),
            pltpu.VMEM((count,) + chunk, jnp.bfloat16),
            pltpu.VMEM((count,) + chunk[1:], jnp.float32),
            pltpu.SemaphoreType.DMA((count, 3)),
        ],
        compiler_params=params(VMEM),
        cost_estimate=cost(count << 18, 2 * count * MIB),
        name="scale_a" if part is None else "scale_b",
    )(place, *in_hbm(normals.reshape((2,) + view), spectrum.reshape(view)))


def transform(along_z, pairs, table_ref):
    parts = []
    for odd in range(2):
        total = None
        for first, second, g in pairs:
            base = lax.rem(g, 2)
            table = (table_ref[0, base, odd], table_ref[1, base, odd])
            if odd:
                sides = (first - second) * jnp.where(g < 2, 1.0, -1.0).astype(jnp.float32)
            else:
                sides = first + second
            if along_z:
                term = product(rows_z(sides), table)
            else:
                term = product(table, columns_y(sides))
            total = term if total is None else total + term
        parts.append(total)
    return parts


def first_z_kernel(shifts, to_ref, in_ref, table_ref, *refs):
    *out_refs, pieces, held_out, semaphores = refs

    def get(i):
        cells = pl.ds(2 * lax.rem(to_ref[0] + shifts[i], 4), 2)
        return pltpu.make_async_copy(in_ref.at[:, :, cells], pieces.at[i], semaphores.at[i, 0])

    def put(i):
        return pltpu.make_async_copy(held_out.at[i], out_refs[i], semaphores.at[i, 1])

    steps = range(len(shifts))
    for i in steps:
        get(i).start()
    for i in steps:
        get(i).wait()
        pairs = [(pieces[i, 0], pieces[i, 2], 0), (pieces[i, 1], pieces[i, 3], 1)]
        for odd, values in enumerate(transform(True, pairs, table_ref)):
            half = slice(odd * 128, (odd + 1) * 128)
            for plane in range(2):
                part = slice(plane * 128, (plane + 1) * 128)
                for x in range(2):
                    held_out[i, plane, x, :, half] = values[x * 128 : (x + 1) * 128, part]
        put(i).start()
    for i in steps:
        put(i).wait()


def first_z(shifts, to, arrived, table):
    shape = (2, 2, 128, KEPT)
    hbm = pl.BlockSpec(memory_space=pltpu.HBM)
    count = len(shifts)
    return pl.pallas_call(
        functools.partial(first_z_kernel, shifts),
        in_specs=[
            pl.BlockSpec(memory_space=pltpu.SMEM),
            hbm,
            pl.BlockSpec(memory_space=pltpu.VMEM),
        ],
        out_specs=[hbm] * count,
        out_shape=[pltpu.HBM(shape, jnp.float32)] * count,
        scratch_shapes=[
            pltpu.VMEM((count, 4, 2, 2, 128, 128), jnp.float32),
            pltpu.VMEM((count,) + shape, jnp.float32),
            pltpu.SemaphoreType.DMA((count, 2)),
        ],
        compiler_params=params(VMEM),
        cost_estimate=cost(count * 256 * 512 * 512, 2 * count * MIB),
        name="first_z",
    )(to, *in_hbm(arrived), table)


def first_y_kernel(merge, place_ref, to_ref, *refs):
    in_refs, refs = refs[:4], refs[4:]
    before, refs = (refs[:2], refs[2:]) if merge else ((), refs)
    table_ref, *out_refs, pieces, held_out, held_before, semaphores = refs
    gets = [
        pltpu.make_async_copy(ref, pieces.at[s], semaphores.at[0, s])
        for s, ref in enumerate(in_refs)
    ]
    puts = []
    for i, shift in enumerate((1, 3, 2, 0)):
        whole = merge and i >= 2
        source = held_out.at[lax.rem(to_ref[0] + shift, 4)]
        target = out_refs[i].at[:, 1 if whole else 0]
        puts.append(pltpu.make_async_copy(source, target, semaphores.at[1, i]))
    gets_before = [
        pltpu.make_async_copy(ref, held_before.at[i], semaphores.at[2, i])
        for i, ref in enumerate(before)
    ]
    puts_before = [
        pltpu.make_async_copy(
            held_before.at[i], out_refs[2 + i].at[:, 0:1], semaphores.at[2, 2 + i]
        )
        for i in range(len(before))
    ]
    for copy in gets + gets_before:
        copy.start()
    for copy in gets_before:
        copy.wait()
    for copy in puts_before:
        copy.start()
    for copy in gets:
        copy.wait()
    g, h = place_ref[0], lax.rem(place_ref[0] + 3, 4)
    pairs = [(pieces[0], pieces[2], g), (pieces[1], pieces[3], h)]
    for odd, values in enumerate(transform(False, pairs, table_ref)):
        for plane in range(2):
            for x in range(4):
                held_out[x, plane, odd * 128 : (odd + 1) * 128] = values[
                    plane * 128 : (plane + 1) * 128, x * 128 : (x + 1) * 128
                ]
    for copy in puts:
        copy.start()
    for copy in puts + puts_before:
        copy.wait()


def first_y(place, to, pieces, table, before=()):
    merge = bool(before)
    shape = (2, 1, KEPT, 128)
    whole = (2, 2, KEPT, 128) if merge else shape
    hbm = pl.BlockSpec(memory_space=pltpu.HBM)
    operands = in_hbm(*pieces, *before)
    return pl.pallas_call(
        functools.partial(first_y_kernel, merge),
        in_specs=[pl.BlockSpec(memory_space=pltpu.SMEM)] * 2
        + [hbm] * len(operands)
        + [pl.BlockSpec(memory_space=pltpu.VMEM)],
        out_specs=[hbm] * 4,
        out_shape=[pltpu.HBM(shape, jnp.float32)] * 2 + [pltpu.HBM(whole, jnp.float32)] * 2,
        scratch_shapes=[
            pltpu.VMEM((4, 2, 4, 128, 128), jnp.float32),
            pltpu.VMEM((4, 2, KEPT, 128), jnp.float32),
            pltpu.VMEM((2,) + shape, jnp.float32),
            pltpu.SemaphoreType.DMA((3, 4)),
        ],
        compiler_params=params(VMEM),
        cost_estimate=cost(512 * 512 * 512, 4 * MIB),
        name="first_y",
    )(place, to, *operands, table)


def part_y_kernel(place_ref, p1, p3, table_ref, out_ref):
    pairs = [(p1[...], p3[...], lax.rem(place_ref[0] + 3, 4))]
    for odd, values in enumerate(transform(False, pairs, table_ref)):
        out_ref[odd] = values


def part_y(place, pieces, table):
    return pl.pallas_call(
        part_y_kernel,
        grid_spec=pltpu.PrefetchScalarGridSpec(
            num_scalar_prefetch=1,
            grid=(2,),
            in_specs=[pl.BlockSpec((2, 1, 128, KEPT), lambda i, place: (0, i, 0, 0))] * 2
            + [pl.BlockSpec(table.shape, lambda i, place: (0, 0, 0, 0, 0))],
            out_specs=pl.BlockSpec((2, KEPT, KEPT), lambda i, place: (0, 0, i)),
        ),
        out_shape=jax.ShapeDtypeStruct((2, KEPT, 512), jnp.float32),
        compiler_params=params(VMEM),
        cost_estimate=cost(512 * 512 * 256, 4 * MIB),
        name="part_y",
    )(place, *pieces, table)


def second_z_kernel(place_ref, b0, b2, c1, c3, d1, d3, table_ref, out_ref):
    g, h = place_ref[0], lax.rem(place_ref[0] + 3, 4)
    for x, (p1, p3) in enumerate(((c1, c3), (d1, d3))):
        cell = slice(x, x + 1)
        pairs = [(b0[:, cell], b2[:, cell], g), (p1[...], p3[...], h)]
        for odd, values in enumerate(transform(True, pairs, table_ref)):
            out_ref[x, :, odd * 256 : (odd + 1) * 256] = values


def second_z(place, pieces, table):
    vmem = pl.BlockSpec(memory_space=pltpu.VMEM)
    return pl.pallas_call(
        second_z_kernel,
        in_specs=[pl.BlockSpec(memory_space=pltpu.SMEM)] + [vmem] * 7,
        out_specs=vmem,
        out_shape=jax.ShapeDtypeStruct((2, KEPT, 512), jnp.float32),
        compiler_params=params(VMEM),
        cost_estimate=cost(512 * 512 * 512, 4 * MIB),
        name="second_z",
    )(place, *pieces, table)


def second_kernel(
    y_ref, part_a, a0, a2, table_y_ref, done_b, out_ref, held
):
    odd = pl.program_id(0)

    def put(values, half, row):
        held[pl.ds(half * 8 + row, 128, stride=16), :] = values

    base = lax.rem(y_ref[0], 2)
    flip = jnp.where(odd == 0, 1.0, -1.0).astype(jnp.float32)
    sign = jnp.where((odd == 0) | (y_ref[0] < 2), 1.0, -1.0).astype(jnp.float32)
    table = (table_y_ref[0, base, 0], table_y_ref[1, base, 0])
    values = part_a[0] + product(table, columns_y((a0[...] + flip * a2[...]) * sign))
    for plane in range(2):
        for x in range(2):
            for half in range(2):
                start = x * KEPT + half * 128
                put(
                    values[plane * 128 : (plane + 1) * 128, start : start + 128],
                    half,
                    plane * 4 + x,
                )
    for half in range(2):
        values = done_b[:, :, half * 256 : (half + 1) * 256].reshape(256, 256)
        for x in range(2):
            for plane in range(2):
                put(
                    values[x * 128 : (x + 1) * 128, plane * 128 : (plane + 1) * 128],
                    half,
                    plane * 4 + 2 + x,
                )
    out_ref[...] = held[...].reshape(128, 1, 2, 8, 128)


def second(gy, part_a, pieces_a, table_y, done_b):
    return pl.pallas_call(
        second_kernel,
        grid_spec=pltpu.PrefetchScalarGridSpec(
            num_scalar_prefetch=1,
            grid=(2,),
            in_specs=[pl.BlockSpec((1, KEPT, 512), lambda i, gy: (i, 0, 0))]
            + [pl.BlockSpec((2, 2, 128, KEPT), lambda i, gy: (0, 0, 0, 0))] * 2
            + [
                pl.BlockSpec((2, 2, 1, KEPT, KEPT), lambda i, gy: (0, 0, i, 0, 0)),
                pl.BlockSpec((2, 128, 512), lambda i, gy: (0, i, 0)),
            ],
            out_specs=pl.BlockSpec((128, 1, 2, 8, 128), lambda i, gy: (0, i, 0, 0, 0)),
            scratch_shapes=[pltpu.VMEM((2048, 128), jnp.float32)],
        ),
        out_shape=jax.ShapeDtypeStruct((128, 2, 2, 8, 128), jnp.float32),
        compiler_params=params(VMEM),
        cost_estimate=cost(512 * 512 * 256, 8 * MIB),
        name="second",
    )(gy, part_a, *pieces_a, table_y, done_b)


def third_kernel(slot_ref, in_ref, table_ref, ordering_ref, out_ref, held):
    out_ref[...] = jnp.zeros_like(out_ref)
    for parity in range(2):
        columns = jnp.concatenate(
            [in_ref[:, parity, half].reshape(1024, 128) for half in range(2)], axis=1
        )
        first, last = columns[:512], columns[512:]
        for odd, sides in enumerate((first + last, first - last)):
            sides = tuple(
                jnp.dot(
                    part, ordering_ref[...], preferred_element_type=jnp.float32
                ).astype(jnp.bfloat16)
                for part in halves(sides)
            )
            values = jnp.exp(product((table_ref[0, odd], table_ref[1, odd]), sides))
            for plane in range(2):
                for half in range(2):
                    held[parity, plane, half, odd * 128 : (odd + 1) * 128] = values[
                        plane * 128 : (plane + 1) * 128, half * 128 : (half + 1) * 128
                    ]

    def place_rows(group, carry):
        for offset in range(4):
            x = group * 4 + offset
            row = group * 2 + offset // 2 + 128 * (offset % 2)
            for parity in range(2):
                for half in range(2):
                    slot = slot_ref[x * 4 + parity * 2 + half]
                    for plane in range(2):
                        out_ref[pl.ds(slot * 2 + plane, 1), :] = held[
                            parity, plane, half, pl.ds(row, 1), :
                        ]
        return carry

    lax.fori_loop(0, KEPT // 4, place_rows, 0)


def third(slots, arrived, table_x, ordering):
    vmem = pl.BlockSpec(memory_space=pltpu.VMEM)
    return pl.pallas_call(
        third_kernel,
        in_specs=[pl.BlockSpec(memory_space=pltpu.SMEM)] + [vmem] * 3,
        out_specs=vmem,
        out_shape=jax.ShapeDtypeStruct((4096, 128), jnp.float32),
        scratch_shapes=[pltpu.VMEM((2, 2, 2, KEPT, 128), jnp.float32)],
        compiler_params=params(VMEM),
        cost_estimate=cost(768 * 512 * 512, 6 * MIB),
        name="third",
    )(slots, arrived, table_x, ordering)


def shifted(piece, axis, shift):
    size = lax.axis_size(axis)
    return lax.ppermute(piece, axis, [(i, (i + shift) % size) for i in range(size)])


def slots_of(block_owner):
    destination = block_owner[:, 0]
    one_hot = (destination[:, None] == jnp.arange(128, dtype=jnp.int32)[None, :]).astype(jnp.int32)
    earlier = jnp.cumsum(one_hot, axis=0) - one_hot
    return destination * CAP + jnp.sum(earlier * one_hot, axis=1)


def per_device(normals, spectrum, block_owner):
    table_x, table_y, table_z, ordering = (jnp.asarray(table) for table in tables())
    gy = lax.axis_index("gy").astype(jnp.int32).reshape(1)
    gz = lax.axis_index("gz").astype(jnp.int32).reshape(1)

    (a,) = scale(None, (0, 1, 2, 3), gz, normals, spectrum)
    a, place = lax.optimization_barrier((a, gy))
    a = lax.all_to_all(a, "gz", split_axis=0, concat_axis=0, tiled=True)
    c1, c3, c2 = scale(0, (1, 3, 2), place, normals, spectrum)
    place, c1, c3, c2 = lax.optimization_barrier((place, c1, c3, c2))
    c1, c3, c2 = shifted(c1, "gy", 1), shifted(c3, "gy", 3), shifted(c2, "gy", 2)
    d1, d3, d2 = scale(1, (1, 3, 2), place, normals, spectrum)
    place, d1, d3, d2 = lax.optimization_barrier((place, d1, d3, d2))
    d1, d3, d2 = shifted(d1, "gy", 1), shifted(d3, "gy", 3), shifted(d2, "gy", 2)
    (c0,) = scale(0, (0,), place, normals, spectrum)
    (d0,) = scale(1, (0,), place, normals, spectrum)

    c1, c3, c2, c0 = first_y(gy, gz, (c0, c1, c2, c3), table_y)
    a, slots, _, d0 = lax.optimization_barrier((a, slots_of(block_owner), c1, d0))
    c1, c3 = shifted(c1, "gz", 1), shifted(c3, "gz", 3)
    a1, a3, a2, a0 = first_z((1, 3, 2, 0), gy, a, table_z)
    d1, d2, d3, c1, c3, _ = lax.optimization_barrier((d1, d2, d3, c1, c3, a1))
    a1, a3, a2 = shifted(a1, "gy", 1), shifted(a3, "gy", 3), shifted(a2, "gy", 2)
    d1, d3, b2, b0 = first_y(gy, gz, (d0, d1, d2, d3), table_y, (c2, c0))
    d1, b2 = shifted(d1, "gz", 1), shifted(b2, "gz", 2)
    d3, d1 = lax.optimization_barrier((d3, d1))
    d3 = shifted(d3, "gz", 3)

    part_a = part_y(gy, (a1, a3), table_y)
    done_b = second_z(gz, (b0, b2, c1, c3, d1, d3), table_z)
    part_a, done_b, a2 = lax.optimization_barrier((part_a, done_b, a2))
    planes = second(gy, part_a, (a0, a2), table_y, done_b)
    lines = lax.all_to_all(planes, ALL, split_axis=0, concat_axis=0, tiled=True)
    outgoing = third(slots, lines, table_x, ordering)
    return lax.all_to_all(
        outgoing.reshape(128, 1, CAP, 2, BW), ALL, split_axis=0, concat_axis=1, tiled=True
    )


def solution(mesh):
    placed = (P(None, "gx", "gy", "gz"), P("gx", "gy", "gz"), P(ALL, None))
    return jax.shard_map(
        per_device,
        mesh=mesh,
        in_specs=placed,
        out_specs=P(ALL, None, None, None, None),
        check_vma=False,
    )
```

```python
import functools

import jax
import jax.numpy as jnp
import ml_dtypes
import numpy as np
from jax import lax
from jax.experimental import pallas as pl
from jax.experimental.pallas import tpu as pltpu
from jax.sharding import PartitionSpec as P

N = 512
KEPT = 256
BW = 128
CAP = 16
ALL = ("gx", "gy", "gz")
MIB = 1 << 20
VMEM = 24


def split_table(table):
    high = table.astype(np.float32).astype(ml_dtypes.bfloat16)
    low = (table - high.astype(np.float64)).astype(np.float32).astype(ml_dtypes.bfloat16)
    return np.stack([high, low])


def cos_sin(positions, kept):
    angles = (positions[:, None] * kept[None, :] % N) * (2.0 * np.pi / N)
    return np.cos(angles), np.sin(angles)


@functools.cache
def tables():
    order = np.arange(KEPT).reshape(KEPT // 2, 2).T.reshape(-1)
    cosine, sine = cos_sin(np.arange(N // 2), order)
    cosine, sine = (t.reshape(2, 128, 2, 128).transpose(0, 2, 1, 3) for t in (cosine, sine))
    real_rows = np.concatenate([cosine, -sine], 3)
    imag_rows = np.concatenate([sine, cosine], 3)
    table_z = np.concatenate([real_rows, imag_rows], 2)
    cosine, sine = cos_sin(np.arange(N // 2), order)
    cosine, sine = (t.T.reshape(2, 128, 2, 128).transpose(2, 0, 1, 3) for t in (cosine, sine))
    top = np.concatenate([cosine, sine], 3)
    bottom = np.concatenate([-sine, cosine], 3)
    table_y = np.concatenate([top, bottom], 2)
    gx, gy, gz = np.meshgrid(np.arange(8), np.arange(4), np.arange(4), indexing="ij")
    first = 64 * gx + 8 * gz + 2 * gy
    second = 64 * gx + 32 + 8 * gy + gz
    cells = np.stack([first, first + 1, second, second + 4], -1).reshape(128, 4)
    cosine, sine = cos_sin(cells[:64].reshape(-1), order)
    cosine, sine = (
        t.T.reshape(2, KEPT // 2, 64, 1, 4) for t in (cosine, sine)
    )
    top = np.concatenate([cosine, sine], 3).reshape(2, KEPT // 2, 512)
    bottom = np.concatenate([-sine, cosine], 3).reshape(2, KEPT // 2, 512)
    table_x = np.concatenate([top, bottom], 1)
    ordering = np.zeros((KEPT, KEPT), ml_dtypes.bfloat16)
    ordering[np.arange(KEPT), order] = 1
    return split_table(table_x), split_table(table_y), split_table(table_z), ordering


def halves(values):
    high = values.astype(jnp.bfloat16)
    low = (values - high.astype(jnp.float32)).astype(jnp.bfloat16)
    return high, low


def product(left, right):
    def dot(a, b):
        return jnp.dot(a, b, preferred_element_type=jnp.float32)

    return dot(left[0], right[0]) + (dot(left[0], right[1]) + dot(left[1], right[0]))


def params(mib):
    return pltpu.CompilerParams(vmem_limit_bytes=mib * MIB)


def cost(multiplies, moved):
    return pl.CostEstimate(
        flops=multiplies >> 16, bytes_accessed=moved >> 16, transcendentals=0
    )


def rows_z(piece):
    return halves(jnp.concatenate([piece[plane].reshape(-1, 128) for plane in range(2)], axis=1))


def columns_y(piece):
    planes, cells = piece.shape[:2]
    return halves(
        jnp.concatenate([piece[:, x].reshape(256, piece.shape[3]) for x in range(cells)], axis=1)
    )


def in_hbm(*arrays):
    return [pltpu.with_memory_space_constraint(x, pltpu.HBM) for x in arrays]


def scale_kernel(part, shifts, place_ref, normals_ref, spectrum_ref, *refs):
    *out_refs, held_out, held_n, held_s, semaphores = refs

    def gets(i):
        if part is None:
            source_n, source_s = normals_ref.at[:, i], spectrum_ref.at[i]
        else:
            chunk = 4 + lax.rem(place_ref[0] + shifts[i], 4)
            source_n, source_s = normals_ref.at[:, chunk, part], spectrum_ref.at[chunk, part]
        return (
            pltpu.make_async_copy(source_n, held_n.at[i], semaphores.at[i, 0]),
            pltpu.make_async_copy(source_s, held_s.at[i], semaphores.at[i, 1]),
        )

    def put(i):
        target = out_refs[0].at[i] if part is None else out_refs[i]
        return pltpu.make_async_copy(held_out.at[i], target, semaphores.at[i, 2])

    steps = range(len(shifts))
    for i in steps:
        for copy in gets(i):
            copy.start()
    for i in steps:
        for copy in gets(i):
            copy.wait()
        for plane in range(2):
            held_out[i, plane] = held_n[i, plane].astype(jnp.float32) * held_s[i]
        put(i).start()
    for i in steps:
        put(i).wait()


def scale(part, shifts, place, normals, spectrum):
    count = len(shifts)
    chunk = (2, 8 if part is None else 4, 128, 128)
    shapes = [(count,) + chunk] if part is None else [chunk] * count
    view = (8, 8, 128, 128) if part is None else (8, 2, 4, 128, 128)
    hbm = pl.BlockSpec(memory_space=pltpu.HBM)
    return pl.pallas_call(
        functools.partial(scale_kernel, part, shifts),
        in_specs=[pl.BlockSpec(memory_space=pltpu.SMEM)] + [hbm] * 2,
        out_specs=[hbm] * len(shapes),
        out_shape=[pltpu.HBM(shape, jnp.float32) for shape in shapes],
        scratch_shapes=[
            pltpu.VMEM((count,) + chunk, jnp.float32),
            pltpu.VMEM((count,) + chunk, jnp.bfloat16),
            pltpu.VMEM((count,) + chunk[1:], jnp.float32),
            pltpu.SemaphoreType.DMA((count, 3)),
        ],
        compiler_params=params(VMEM),
        cost_estimate=cost(count << 18, 2 * count * MIB),
        name="scale_a" if part is None else "scale_b",
    )(place, *in_hbm(normals.reshape((2,) + view), spectrum.reshape(view)))


def transform(along_z, pairs, table_ref):
    parts = []
    for odd in range(2):
        total = None
        for first, second, g in pairs:
            base = lax.rem(g, 2)
            table = (table_ref[0, base, odd], table_ref[1, base, odd])
            if odd:
                sides = (first - second) * jnp.where(g < 2, 1.0, -1.0).astype(jnp.float32)
            else:
                sides = first + second
            if along_z:
                term = product(rows_z(sides), table)
            else:
                term = product(table, columns_y(sides))
            total = term if total is None else total + term
        parts.append(total)
    return parts


def first_z_kernel(shifts, to_ref, in_ref, table_ref, *refs):
    *out_refs, pieces, held_out, semaphores = refs

    def get(i):
        cells = pl.ds(2 * lax.rem(to_ref[0] + shifts[i], 4), 2)
        return pltpu.make_async_copy(in_ref.at[:, :, cells], pieces.at[i], semaphores.at[i, 0])

    def put(i):
        return pltpu.make_async_copy(held_out.at[i], out_refs[i], semaphores.at[i, 1])

    steps = range(len(shifts))
    for i in steps:
        get(i).start()
    for i in steps:
        get(i).wait()
        pairs = [(pieces[i, 0], pieces[i, 2], 0), (pieces[i, 1], pieces[i, 3], 1)]
        for odd, values in enumerate(transform(True, pairs, table_ref)):
            half = slice(odd * 128, (odd + 1) * 128)
            for plane in range(2):
                part = slice(plane * 128, (plane + 1) * 128)
                for x in range(2):
                    held_out[i, plane, x, :, half] = values[x * 128 : (x + 1) * 128, part]
        put(i).start()
    for i in steps:
        put(i).wait()


def first_z(shifts, to, arrived, table):
    shape = (2, 2, 128, KEPT)
    hbm = pl.BlockSpec(memory_space=pltpu.HBM)
    count = len(shifts)
    return pl.pallas_call(
        functools.partial(first_z_kernel, shifts),
        in_specs=[
            pl.BlockSpec(memory_space=pltpu.SMEM),
            hbm,
            pl.BlockSpec(memory_space=pltpu.VMEM),
        ],
        out_specs=[hbm] * count,
        out_shape=[pltpu.HBM(shape, jnp.float32)] * count,
        scratch_shapes=[
            pltpu.VMEM((count, 4, 2, 2, 128, 128), jnp.float32),
            pltpu.VMEM((count,) + shape, jnp.float32),
            pltpu.SemaphoreType.DMA((count, 2)),
        ],
        compiler_params=params(VMEM),
        cost_estimate=cost(count * 256 * 512 * 512, 2 * count * MIB),
        name="first_z",
    )(to, *in_hbm(arrived), table)


def first_y_kernel(merge, place_ref, to_ref, *refs):
    in_refs, refs = refs[:4], refs[4:]
    before, refs = (refs[:2], refs[2:]) if merge else ((), refs)
    table_ref, *out_refs, pieces, held_out, held_before, semaphores = refs
    gets = [
        pltpu.make_async_copy(ref, pieces.at[s], semaphores.at[0, s])
        for s, ref in enumerate(in_refs)
    ]
    puts = []
    for i, shift in enumerate((1, 3, 2, 0)):
        whole = merge and i >= 2
        source = held_out.at[lax.rem(to_ref[0] + shift, 4)]
        target = out_refs[i].at[:, 1 if whole else 0]
        puts.append(pltpu.make_async_copy(source, target, semaphores.at[1, i]))
    gets_before = [
        pltpu.make_async_copy(ref, held_before.at[i], semaphores.at[2, i])
        for i, ref in enumerate(before)
    ]
    puts_before = [
        pltpu.make_async_copy(
            held_before.at[i], out_refs[2 + i].at[:, 0:1], semaphores.at[2, 2 + i]
        )
        for i in range(len(before))
    ]
    for copy in gets + gets_before:
        copy.start()
    for copy in gets_before:
        copy.wait()
    for copy in puts_before:
        copy.start()
    for copy in gets:
        copy.wait()
    g, h = place_ref[0], lax.rem(place_ref[0] + 3, 4)
    pairs = [(pieces[0], pieces[2], g), (pieces[1], pieces[3], h)]
    for odd, values in enumerate(transform(False, pairs, table_ref)):
        for plane in range(2):
            for x in range(4):
                held_out[x, plane, odd * 128 : (odd + 1) * 128] = values[
                    plane * 128 : (plane + 1) * 128, x * 128 : (x + 1) * 128
                ]
    for copy in puts:
        copy.start()
    for copy in puts + puts_before:
        copy.wait()


def first_y(place, to, pieces, table, before=()):
    merge = bool(before)
    shape = (2, 1, KEPT, 128)
    whole = (2, 2, KEPT, 128) if merge else shape
    hbm = pl.BlockSpec(memory_space=pltpu.HBM)
    operands = in_hbm(*pieces, *before)
    return pl.pallas_call(
        functools.partial(first_y_kernel, merge),
        in_specs=[pl.BlockSpec(memory_space=pltpu.SMEM)] * 2
        + [hbm] * len(operands)
        + [pl.BlockSpec(memory_space=pltpu.VMEM)],
        out_specs=[hbm] * 4,
        out_shape=[pltpu.HBM(shape, jnp.float32)] * 2 + [pltpu.HBM(whole, jnp.float32)] * 2,
        scratch_shapes=[
            pltpu.VMEM((4, 2, 4, 128, 128), jnp.float32),
            pltpu.VMEM((4, 2, KEPT, 128), jnp.float32),
            pltpu.VMEM((2,) + shape, jnp.float32),
            pltpu.SemaphoreType.DMA((3, 4)),
        ],
        compiler_params=params(VMEM),
        cost_estimate=cost(512 * 512 * 512, 4 * MIB),
        name="first_y",
    )(place, to, *operands, table)


def part_y_kernel(place_ref, p0, p2, table_ref, out_ref):
    pairs = [(p0[...], p2[...], place_ref[0])]
    for odd, values in enumerate(transform(False, pairs, table_ref)):
        out_ref[odd] = values


def part_y(place, pieces, table):
    return pl.pallas_call(
        part_y_kernel,
        grid_spec=pltpu.PrefetchScalarGridSpec(
            num_scalar_prefetch=1,
            grid=(2,),
            in_specs=[pl.BlockSpec((2, 1, 128, KEPT), lambda i, place: (0, i, 0, 0))] * 2
            + [pl.BlockSpec(table.shape, lambda i, place: (0, 0, 0, 0, 0))],
            out_specs=pl.BlockSpec((2, KEPT, KEPT), lambda i, place: (0, 0, i)),
        ),
        out_shape=jax.ShapeDtypeStruct((2, KEPT, 512), jnp.float32),
        compiler_params=params(VMEM),
        cost_estimate=cost(512 * 512 * 256, 4 * MIB),
        name="part_y",
    )(place, *pieces, table)


def second_z_kernel(place_ref, b0, b2, c1, c3, d1, d3, table_ref, out_ref):
    g, h = place_ref[0], lax.rem(place_ref[0] + 3, 4)
    for x, (p1, p3) in enumerate(((c1, c3), (d1, d3))):
        cell = slice(x, x + 1)
        pairs = [(b0[:, cell], b2[:, cell], g), (p1[...], p3[...], h)]
        for odd, values in enumerate(transform(True, pairs, table_ref)):
            out_ref[x, :, odd * 256 : (odd + 1) * 256] = values


def second_z(place, pieces, table):
    vmem = pl.BlockSpec(memory_space=pltpu.VMEM)
    return pl.pallas_call(
        second_z_kernel,
        in_specs=[pl.BlockSpec(memory_space=pltpu.SMEM)] + [vmem] * 7,
        out_specs=vmem,
        out_shape=jax.ShapeDtypeStruct((2, KEPT, 512), jnp.float32),
        compiler_params=params(VMEM),
        cost_estimate=cost(512 * 512 * 512, 4 * MIB),
        name="second_z",
    )(place, *pieces, table)


def second_kernel(
    y_ref, part_a, a1, a3, table_y_ref, done_b, out_ref, held
):
    odd = pl.program_id(0)

    def put(values, half, row):
        held[pl.ds(half * 8 + row, 128, stride=16), :] = values

    g = lax.rem(y_ref[0] + 3, 4)
    base = lax.rem(g, 2)
    flip = jnp.where(odd == 0, 1.0, -1.0).astype(jnp.float32)
    sign = jnp.where((odd == 0) | (g < 2), 1.0, -1.0).astype(jnp.float32)
    table = (table_y_ref[0, base, 0], table_y_ref[1, base, 0])
    values = part_a[0] + product(table, columns_y((a1[...] + flip * a3[...]) * sign))
    for plane in range(2):
        for x in range(2):
            for half in range(2):
                start = x * KEPT + half * 128
                put(
                    values[plane * 128 : (plane + 1) * 128, start : start + 128],
                    half,
                    plane * 4 + x,
                )
    for half in range(2):
        values = done_b[:, :, half * 256 : (half + 1) * 256].reshape(256, 256)
        for x in range(2):
            for plane in range(2):
                put(
                    values[x * 128 : (x + 1) * 128, plane * 128 : (plane + 1) * 128],
                    half,
                    plane * 4 + 2 + x,
                )
    out_ref[...] = held[...].reshape(128, 1, 2, 8, 128)


def second(gy, part_a, pieces_a, table_y, done_b):
    return pl.pallas_call(
        second_kernel,
        grid_spec=pltpu.PrefetchScalarGridSpec(
            num_scalar_prefetch=1,
            grid=(2,),
            in_specs=[pl.BlockSpec((1, KEPT, 512), lambda i, gy: (i, 0, 0))]
            + [pl.BlockSpec((2, 2, 128, KEPT), lambda i, gy: (0, 0, 0, 0))] * 2
            + [
                pl.BlockSpec((2, 2, 1, KEPT, KEPT), lambda i, gy: (0, 0, i, 0, 0)),
                pl.BlockSpec((2, 128, 512), lambda i, gy: (0, i, 0)),
            ],
            out_specs=pl.BlockSpec((128, 1, 2, 8, 128), lambda i, gy: (0, i, 0, 0, 0)),
            scratch_shapes=[pltpu.VMEM((2048, 128), jnp.float32)],
        ),
        out_shape=jax.ShapeDtypeStruct((128, 2, 2, 8, 128), jnp.float32),
        compiler_params=params(VMEM),
        cost_estimate=cost(512 * 512 * 256, 8 * MIB),
        name="second",
    )(gy, part_a, *pieces_a, table_y, done_b)


def third_kernel(slot_ref, in_ref, table_ref, ordering_ref, out_ref, held):
    out_ref[...] = jnp.zeros_like(out_ref)
    for parity in range(2):
        columns = jnp.concatenate(
            [in_ref[:, parity, half].reshape(1024, 128) for half in range(2)], axis=1
        )
        first, last = columns[:512], columns[512:]
        for odd, sides in enumerate((first + last, first - last)):
            sides = tuple(
                jnp.dot(
                    part, ordering_ref[...], preferred_element_type=jnp.float32
                ).astype(jnp.bfloat16)
                for part in halves(sides)
            )
            values = jnp.exp(product((table_ref[0, odd], table_ref[1, odd]), sides))
            for plane in range(2):
                for half in range(2):
                    held[parity, plane, half, odd * 128 : (odd + 1) * 128] = values[
                        plane * 128 : (plane + 1) * 128, half * 128 : (half + 1) * 128
                    ]

    def place_rows(group, carry):
        for offset in range(4):
            x = group * 4 + offset
            row = group * 2 + offset // 2 + 128 * (offset % 2)
            for parity in range(2):
                for half in range(2):
                    slot = slot_ref[x * 4 + parity * 2 + half]
                    for plane in range(2):
                        out_ref[pl.ds(slot * 2 + plane, 1), :] = held[
                            parity, plane, half, pl.ds(row, 1), :
                        ]
        return carry

    lax.fori_loop(0, KEPT // 4, place_rows, 0)


def third(slots, arrived, table_x, ordering):
    vmem = pl.BlockSpec(memory_space=pltpu.VMEM)
    return pl.pallas_call(
        third_kernel,
        in_specs=[pl.BlockSpec(memory_space=pltpu.SMEM)] + [vmem] * 3,
        out_specs=vmem,
        out_shape=jax.ShapeDtypeStruct((4096, 128), jnp.float32),
        scratch_shapes=[pltpu.VMEM((2, 2, 2, KEPT, 128), jnp.float32)],
        compiler_params=params(VMEM),
        cost_estimate=cost(768 * 512 * 512, 6 * MIB),
        name="third",
    )(slots, arrived, table_x, ordering)


def shifted(piece, axis, shift):
    size = lax.axis_size(axis)
    return lax.ppermute(piece, axis, [(i, (i + shift) % size) for i in range(size)])


def slots_of(block_owner):
    destination = block_owner[:, 0]
    one_hot = (destination[:, None] == jnp.arange(128, dtype=jnp.int32)[None, :]).astype(jnp.int32)
    earlier = jnp.cumsum(one_hot, axis=0) - one_hot
    return destination * CAP + jnp.sum(earlier * one_hot, axis=1)


def per_device(normals, spectrum, block_owner):
    table_x, table_y, table_z, ordering = (jnp.asarray(table) for table in tables())
    gy = lax.axis_index("gy").astype(jnp.int32).reshape(1)
    gz = lax.axis_index("gz").astype(jnp.int32).reshape(1)

    (a,) = scale(None, (0, 1, 2, 3), gz, normals, spectrum)
    a, place = lax.optimization_barrier((a, gy))
    a = lax.all_to_all(a, "gz", split_axis=0, concat_axis=0, tiled=True)
    c1, c3, c2 = scale(0, (1, 3, 2), place, normals, spectrum)
    place, c1, c3, c2 = lax.optimization_barrier((place, c1, c3, c2))
    c1, c3, c2 = shifted(c1, "gy", 1), shifted(c3, "gy", 3), shifted(c2, "gy", 2)
    d1, d3, d2 = scale(1, (1, 3, 2), place, normals, spectrum)
    place, d1, d3, d2 = lax.optimization_barrier((place, d1, d3, d2))
    d1, d3, d2 = shifted(d1, "gy", 1), shifted(d3, "gy", 3), shifted(d2, "gy", 2)
    (c0,) = scale(0, (0,), place, normals, spectrum)
    (d0,) = scale(1, (0,), place, normals, spectrum)

    c1, c3, c2, c0 = first_y(gy, gz, (c0, c1, c2, c3), table_y)
    a, slots, _, d0 = lax.optimization_barrier((a, slots_of(block_owner), c1, d0))
    c1, c3 = shifted(c1, "gz", 1), shifted(c3, "gz", 3)
    a2, a1, a3, a0 = first_z((2, 1, 3, 0), gy, a, table_z)
    d1, d2, d3, c1, c3, _ = lax.optimization_barrier((d1, d2, d3, c1, c3, a2))
    a1, a3, a2 = shifted(a1, "gy", 1), shifted(a3, "gy", 3), shifted(a2, "gy", 2)
    d1, d3, b2, b0 = first_y(gy, gz, (d0, d1, d2, d3), table_y, (c2, c0))
    d1, d3, b2 = shifted(d1, "gz", 1), shifted(d3, "gz", 3), shifted(b2, "gz", 2)

    part_a = part_y(gy, (a0, a2), table_y)
    part_a, b2 = lax.optimization_barrier((part_a, b2))
    done_b = second_z(gz, (b0, b2, c1, c3, d1, d3), table_z)
    part_a, done_b, a1, a3 = lax.optimization_barrier((part_a, done_b, a1, a3))
    planes = second(gy, part_a, (a1, a3), table_y, done_b)
    lines = lax.all_to_all(planes, ALL, split_axis=0, concat_axis=0, tiled=True)
    outgoing = third(slots, lines, table_x, ordering)
    return lax.all_to_all(
        outgoing.reshape(128, 1, CAP, 2, BW), ALL, split_axis=0, concat_axis=1, tiled=True
    )


def solution(mesh):
    placed = (P(None, "gx", "gy", "gz"), P("gx", "gy", "gz"), P(ALL, None))
    return jax.shard_map(
        per_device,
        mesh=mesh,
        in_specs=placed,
        out_specs=P(ALL, None, None, None, None),
        check_vma=False,
    )
```

```python
import functools

import jax
import jax.numpy as jnp
import ml_dtypes
import numpy as np
from jax import lax
from jax.experimental import pallas as pl
from jax.experimental.pallas import tpu as pltpu
from jax.sharding import PartitionSpec as P

N = 512
KEPT = 256
BW = 128
CAP = 16
ALL = ("gx", "gy", "gz")
MIB = 1 << 20
VMEM = 24


def split_table(table):
    high = table.astype(np.float32).astype(ml_dtypes.bfloat16)
    low = (table - high.astype(np.float64)).astype(np.float32).astype(ml_dtypes.bfloat16)
    return np.stack([high, low])


def cos_sin(positions, kept):
    angles = (positions[:, None] * kept[None, :] % N) * (2.0 * np.pi / N)
    return np.cos(angles), np.sin(angles)


@functools.cache
def tables():
    order = np.arange(KEPT).reshape(KEPT // 2, 2).T.reshape(-1)
    cosine, sine = cos_sin(np.arange(N // 2), order)
    cosine, sine = (t.reshape(2, 128, 2, 128).transpose(0, 2, 1, 3) for t in (cosine, sine))
    real_rows = np.concatenate([cosine, -sine], 3)
    imag_rows = np.concatenate([sine, cosine], 3)
    table_z = np.concatenate([real_rows, imag_rows], 2)
    cosine, sine = cos_sin(np.arange(N // 2), order)
    cosine, sine = (t.T.reshape(2, 128, 2, 128).transpose(2, 0, 1, 3) for t in (cosine, sine))
    top = np.concatenate([cosine, sine], 3)
    bottom = np.concatenate([-sine, cosine], 3)
    table_y = np.concatenate([top, bottom], 2)
    gx, gy, gz = np.meshgrid(np.arange(8), np.arange(4), np.arange(4), indexing="ij")
    first = 64 * gx + 8 * gz + 2 * gy
    second = 64 * gx + 32 + 8 * gy + gz
    cells = np.stack([first, first + 1, second, second + 4], -1).reshape(128, 4)
    cosine, sine = cos_sin(cells[:64].reshape(-1), order)
    cosine, sine = (
        t.T.reshape(2, KEPT // 2, 64, 1, 4) for t in (cosine, sine)
    )
    top = np.concatenate([cosine, sine], 3).reshape(2, KEPT // 2, 512)
    bottom = np.concatenate([-sine, cosine], 3).reshape(2, KEPT // 2, 512)
    table_x = np.concatenate([top, bottom], 1)
    ordering = np.zeros((KEPT, KEPT), ml_dtypes.bfloat16)
    ordering[np.arange(KEPT), order] = 1
    return split_table(table_x), split_table(table_y), split_table(table_z), ordering


def halves(values):
    high = values.astype(jnp.bfloat16)
    low = (values - high.astype(jnp.float32)).astype(jnp.bfloat16)
    return high, low


def product(left, right):
    def dot(a, b):
        return jnp.dot(a, b, preferred_element_type=jnp.float32)

    return dot(left[0], right[0]) + (dot(left[0], right[1]) + dot(left[1], right[0]))


def params(mib):
    return pltpu.CompilerParams(vmem_limit_bytes=mib * MIB)


def cost(multiplies, moved):
    return pl.CostEstimate(
        flops=multiplies >> 16, bytes_accessed=moved >> 16, transcendentals=0
    )


def rows_z(piece):
    return halves(jnp.concatenate([piece[plane].reshape(-1, 128) for plane in range(2)], axis=1))


def columns_y(piece):
    planes, cells = piece.shape[:2]
    return halves(
        jnp.concatenate([piece[:, x].reshape(256, piece.shape[3]) for x in range(cells)], axis=1)
    )


def in_hbm(*arrays):
    return [pltpu.with_memory_space_constraint(x, pltpu.HBM) for x in arrays]


def scale_kernel(part, shifts, place_ref, normals_ref, spectrum_ref, *refs):
    *out_refs, held_out, held_n, held_s, semaphores = refs

    def gets(i):
        if part is None:
            source_n, source_s = normals_ref.at[:, i], spectrum_ref.at[i]
        else:
            chunk = 4 + lax.rem(place_ref[0] + shifts[i], 4)
            source_n, source_s = normals_ref.at[:, chunk, part], spectrum_ref.at[chunk, part]
        return (
            pltpu.make_async_copy(source_n, held_n.at[i], semaphores.at[i, 0]),
            pltpu.make_async_copy(source_s, held_s.at[i], semaphores.at[i, 1]),
        )

    def put(i):
        target = out_refs[0].at[i] if part is None else out_refs[i]
        return pltpu.make_async_copy(held_out.at[i], target, semaphores.at[i, 2])

    steps = range(len(shifts))
    for i in steps:
        for copy in gets(i):
            copy.start()
    for i in steps:
        for copy in gets(i):
            copy.wait()
        for plane in range(2):
            held_out[i, plane] = held_n[i, plane].astype(jnp.float32) * held_s[i]
        put(i).start()
    for i in steps:
        put(i).wait()


def scale(part, shifts, place, normals, spectrum):
    count = len(shifts)
    chunk = (2, 8 if part is None else 4, 128, 128)
    shapes = [(count,) + chunk] if part is None else [chunk] * count
    view = (8, 8, 128, 128) if part is None else (8, 2, 4, 128, 128)
    hbm = pl.BlockSpec(memory_space=pltpu.HBM)
    return pl.pallas_call(
        functools.partial(scale_kernel, part, shifts),
        in_specs=[pl.BlockSpec(memory_space=pltpu.SMEM)] + [hbm] * 2,
        out_specs=[hbm] * len(shapes),
        out_shape=[pltpu.HBM(shape, jnp.float32) for shape in shapes],
        scratch_shapes=[
            pltpu.VMEM((count,) + chunk, jnp.float32),
            pltpu.VMEM((count,) + chunk, jnp.bfloat16),
            pltpu.VMEM((count,) + chunk[1:], jnp.float32),
            pltpu.SemaphoreType.DMA((count, 3)),
        ],
        compiler_params=params(VMEM),
        cost_estimate=cost(count << 18, 2 * count * MIB),
        name="scale_a" if part is None else "scale_b",
    )(place, *in_hbm(normals.reshape((2,) + view), spectrum.reshape(view)))


def transform(along_z, pairs, table_ref):
    parts = []
    for odd in range(2):
        total = None
        for first, second, g in pairs:
            base = lax.rem(g, 2)
            table = (table_ref[0, base, odd], table_ref[1, base, odd])
            if odd:
                sides = (first - second) * jnp.where(g < 2, 1.0, -1.0).astype(jnp.float32)
            else:
                sides = first + second
            if along_z:
                term = product(rows_z(sides), table)
            else:
                term = product(table, columns_y(sides))
            total = term if total is None else total + term
        parts.append(total)
    return parts


def first_z_kernel(shifts, to_ref, in_ref, table_ref, *refs):
    *out_refs, pieces, held_out, semaphores = refs

    def get(i):
        cells = pl.ds(2 * lax.rem(to_ref[0] + shifts[i], 4), 2)
        return pltpu.make_async_copy(in_ref.at[:, :, cells], pieces.at[i], semaphores.at[i, 0])

    def put(i):
        return pltpu.make_async_copy(held_out.at[i], out_refs[i], semaphores.at[i, 1])

    steps = range(len(shifts))
    for i in steps[:2]:
        get(i).start()
    for i in steps:
        get(i).wait()
        if i + 2 < len(shifts):
            get(i + 2).start()
        pairs = [(pieces[i, 0], pieces[i, 2], 0), (pieces[i, 1], pieces[i, 3], 1)]
        for odd, values in enumerate(transform(True, pairs, table_ref)):
            half = slice(odd * 128, (odd + 1) * 128)
            for plane in range(2):
                part = slice(plane * 128, (plane + 1) * 128)
                for x in range(2):
                    held_out[i, plane, x, :, half] = values[x * 128 : (x + 1) * 128, part]
        put(i).start()
    for i in steps:
        put(i).wait()


def first_z(shifts, to, arrived, table):
    shape = (2, 2, 128, KEPT)
    hbm = pl.BlockSpec(memory_space=pltpu.HBM)
    count = len(shifts)
    return pl.pallas_call(
        functools.partial(first_z_kernel, shifts),
        in_specs=[
            pl.BlockSpec(memory_space=pltpu.SMEM),
            hbm,
            pl.BlockSpec(memory_space=pltpu.VMEM),
        ],
        out_specs=[hbm] * count,
        out_shape=[pltpu.HBM(shape, jnp.float32)] * count,
        scratch_shapes=[
            pltpu.VMEM((count, 4, 2, 2, 128, 128), jnp.float32),
            pltpu.VMEM((count,) + shape, jnp.float32),
            pltpu.SemaphoreType.DMA((count, 2)),
        ],
        compiler_params=params(VMEM),
        cost_estimate=cost(count * 256 * 512 * 512, 2 * count * MIB),
        name="first_z",
    )(to, *in_hbm(arrived), table)


def first_y_kernel(merge, place_ref, to_ref, *refs):
    in_refs, refs = refs[:4], refs[4:]
    before, refs = (refs[:2], refs[2:]) if merge else ((), refs)
    table_ref, *out_refs, pieces, held_out, held_before, semaphores = refs
    gets = [
        pltpu.make_async_copy(ref, pieces.at[s], semaphores.at[0, s])
        for s, ref in enumerate(in_refs)
    ]
    puts = []
    for i, shift in enumerate((1, 3, 2, 0)):
        whole = merge and i >= 2
        source = held_out.at[lax.rem(to_ref[0] + shift, 4)]
        target = out_refs[i].at[:, 1 if whole else 0]
        puts.append(pltpu.make_async_copy(source, target, semaphores.at[1, i]))
    gets_before = [
        pltpu.make_async_copy(ref, held_before.at[i], semaphores.at[2, i])
        for i, ref in enumerate(before)
    ]
    puts_before = [
        pltpu.make_async_copy(
            held_before.at[i], out_refs[2 + i].at[:, 0:1], semaphores.at[2, 2 + i]
        )
        for i in range(len(before))
    ]
    for copy in gets + gets_before:
        copy.start()
    for copy in gets_before:
        copy.wait()
    for copy in puts_before:
        copy.start()
    for copy in gets:
        copy.wait()
    g, h = place_ref[0], lax.rem(place_ref[0] + 3, 4)
    pairs = [(pieces[0], pieces[2], g), (pieces[1], pieces[3], h)]
    for odd, values in enumerate(transform(False, pairs, table_ref)):
        for plane in range(2):
            for x in range(4):
                held_out[x, plane, odd * 128 : (odd + 1) * 128] = values[
                    plane * 128 : (plane + 1) * 128, x * 128 : (x + 1) * 128
                ]
    for copy in puts:
        copy.start()
    for copy in puts + puts_before:
        copy.wait()


def first_y(place, to, pieces, table, before=()):
    merge = bool(before)
    shape = (2, 1, KEPT, 128)
    whole = (2, 2, KEPT, 128) if merge else shape
    hbm = pl.BlockSpec(memory_space=pltpu.HBM)
    operands = in_hbm(*pieces, *before)
    return pl.pallas_call(
        functools.partial(first_y_kernel, merge),
        in_specs=[pl.BlockSpec(memory_space=pltpu.SMEM)] * 2
        + [hbm] * len(operands)
        + [pl.BlockSpec(memory_space=pltpu.VMEM)],
        out_specs=[hbm] * 4,
        out_shape=[pltpu.HBM(shape, jnp.float32)] * 2 + [pltpu.HBM(whole, jnp.float32)] * 2,
        scratch_shapes=[
            pltpu.VMEM((4, 2, 4, 128, 128), jnp.float32),
            pltpu.VMEM((4, 2, KEPT, 128), jnp.float32),
            pltpu.VMEM((2,) + shape, jnp.float32),
            pltpu.SemaphoreType.DMA((3, 4)),
        ],
        compiler_params=params(VMEM),
        cost_estimate=cost(512 * 512 * 512, 4 * MIB),
        name="first_y",
    )(place, to, *operands, table)


def part_y_kernel(place_ref, p0, p2, table_ref, out_ref):
    pairs = [(p0[...], p2[...], place_ref[0])]
    for odd, values in enumerate(transform(False, pairs, table_ref)):
        out_ref[odd] = values


def part_y(place, pieces, table):
    return pl.pallas_call(
        part_y_kernel,
        grid_spec=pltpu.PrefetchScalarGridSpec(
            num_scalar_prefetch=1,
            grid=(2,),
            in_specs=[pl.BlockSpec((2, 1, 128, KEPT), lambda i, place: (0, i, 0, 0))] * 2
            + [pl.BlockSpec(table.shape, lambda i, place: (0, 0, 0, 0, 0))],
            out_specs=pl.BlockSpec((2, KEPT, KEPT), lambda i, place: (0, 0, i)),
        ),
        out_shape=jax.ShapeDtypeStruct((2, KEPT, 512), jnp.float32),
        compiler_params=params(VMEM),
        cost_estimate=cost(512 * 512 * 256, 4 * MIB),
        name="part_y",
    )(place, *pieces, table)


def second_z_kernel(place_ref, b0, b2, c1, c3, d1, d3, table_ref, out_ref):
    g, h = place_ref[0], lax.rem(place_ref[0] + 3, 4)
    for x, (p1, p3) in enumerate(((c1, c3), (d1, d3))):
        cell = slice(x, x + 1)
        pairs = [(b0[:, cell], b2[:, cell], g), (p1[...], p3[...], h)]
        for odd, values in enumerate(transform(True, pairs, table_ref)):
            out_ref[x, :, odd * 256 : (odd + 1) * 256] = values


def second_z(place, pieces, table):
    vmem = pl.BlockSpec(memory_space=pltpu.VMEM)
    return pl.pallas_call(
        second_z_kernel,
        in_specs=[pl.BlockSpec(memory_space=pltpu.SMEM)] + [vmem] * 7,
        out_specs=vmem,
        out_shape=jax.ShapeDtypeStruct((2, KEPT, 512), jnp.float32),
        compiler_params=params(VMEM),
        cost_estimate=cost(512 * 512 * 512, 4 * MIB),
        name="second_z",
    )(place, *pieces, table)


def second_kernel(
    y_ref, part_a, a1, a3, table_y_ref, done_b, out_ref, held
):
    odd = pl.program_id(0)

    def put(values, half, row):
        held[pl.ds(half * 8 + row, 128, stride=16), :] = values

    g = lax.rem(y_ref[0] + 3, 4)
    base = lax.rem(g, 2)
    flip = jnp.where(odd == 0, 1.0, -1.0).astype(jnp.float32)
    sign = jnp.where((odd == 0) | (g < 2), 1.0, -1.0).astype(jnp.float32)
    table = (table_y_ref[0, base, 0], table_y_ref[1, base, 0])
    values = part_a[0] + product(table, columns_y((a1[...] + flip * a3[...]) * sign))
    for plane in range(2):
        for x in range(2):
            for half in range(2):
                start = x * KEPT + half * 128
                put(
                    values[plane * 128 : (plane + 1) * 128, start : start + 128],
                    half,
                    plane * 4 + x,
                )
    for half in range(2):
        values = done_b[:, :, half * 256 : (half + 1) * 256].reshape(256, 256)
        for x in range(2):
            for plane in range(2):
                put(
                    values[x * 128 : (x + 1) * 128, plane * 128 : (plane + 1) * 128],
                    half,
                    plane * 4 + 2 + x,
                )
    out_ref[...] = held[...].reshape(128, 1, 2, 8, 128)


def second(gy, part_a, pieces_a, table_y, done_b):
    return pl.pallas_call(
        second_kernel,
        grid_spec=pltpu.PrefetchScalarGridSpec(
            num_scalar_prefetch=1,
            grid=(2,),
            in_specs=[pl.BlockSpec((1, KEPT, 512), lambda i, gy: (i, 0, 0))]
            + [pl.BlockSpec((2, 2, 128, KEPT), lambda i, gy: (0, 0, 0, 0))] * 2
            + [
                pl.BlockSpec((2, 2, 1, KEPT, KEPT), lambda i, gy: (0, 0, i, 0, 0)),
                pl.BlockSpec((2, 128, 512), lambda i, gy: (0, i, 0)),
            ],
            out_specs=pl.BlockSpec((128, 1, 2, 8, 128), lambda i, gy: (0, i, 0, 0, 0)),
            scratch_shapes=[pltpu.VMEM((2048, 128), jnp.float32)],
        ),
        out_shape=jax.ShapeDtypeStruct((128, 2, 2, 8, 128), jnp.float32),
        compiler_params=params(VMEM),
        cost_estimate=cost(512 * 512 * 256, 8 * MIB),
        name="second",
    )(gy, part_a, *pieces_a, table_y, done_b)


def third_kernel(slot_ref, in_ref, table_ref, ordering_ref, out_ref, held):
    out_ref[...] = jnp.zeros_like(out_ref)
    for parity in range(2):
        columns = jnp.concatenate(
            [in_ref[:, parity, half].reshape(1024, 128) for half in range(2)], axis=1
        )
        first, last = columns[:512], columns[512:]
        for odd, sides in enumerate((first + last, first - last)):
            sides = tuple(
                jnp.dot(
                    part, ordering_ref[...], preferred_element_type=jnp.float32
                ).astype(jnp.bfloat16)
                for part in halves(sides)
            )
            values = jnp.exp(product((table_ref[0, odd], table_ref[1, odd]), sides))
            for plane in range(2):
                for half in range(2):
                    held[parity, plane, half, odd * 128 : (odd + 1) * 128] = values[
                        plane * 128 : (plane + 1) * 128, half * 128 : (half + 1) * 128
                    ]

    def place_rows(group, carry):
        for offset in range(4):
            x = group * 4 + offset
            row = group * 2 + offset // 2 + 128 * (offset % 2)
            for parity in range(2):
                for half in range(2):
                    slot = slot_ref[x * 4 + parity * 2 + half]
                    for plane in range(2):
                        out_ref[pl.ds(slot * 2 + plane, 1), :] = held[
                            parity, plane, half, pl.ds(row, 1), :
                        ]
        return carry

    lax.fori_loop(0, KEPT // 4, place_rows, 0)


def third(slots, arrived, table_x, ordering):
    vmem = pl.BlockSpec(memory_space=pltpu.VMEM)
    return pl.pallas_call(
        third_kernel,
        in_specs=[pl.BlockSpec(memory_space=pltpu.SMEM)] + [vmem] * 3,
        out_specs=vmem,
        out_shape=jax.ShapeDtypeStruct((4096, 128), jnp.float32),
        scratch_shapes=[pltpu.VMEM((2, 2, 2, KEPT, 128), jnp.float32)],
        compiler_params=params(VMEM),
        cost_estimate=cost(768 * 512 * 512, 6 * MIB),
        name="third",
    )(slots, arrived, table_x, ordering)


def shifted(piece, axis, shift):
    size = lax.axis_size(axis)
    return lax.ppermute(piece, axis, [(i, (i + shift) % size) for i in range(size)])


def slots_of(block_owner):
    destination = block_owner[:, 0]
    one_hot = (destination[:, None] == jnp.arange(128, dtype=jnp.int32)[None, :]).astype(jnp.int32)
    earlier = jnp.cumsum(one_hot, axis=0) - one_hot
    return destination * CAP + jnp.sum(earlier * one_hot, axis=1)


def per_device(normals, spectrum, block_owner):
    table_x, table_y, table_z, ordering = (jnp.asarray(table) for table in tables())
    gy = lax.axis_index("gy").astype(jnp.int32).reshape(1)
    gz = lax.axis_index("gz").astype(jnp.int32).reshape(1)

    (a,) = scale(None, (0, 1, 2, 3), gz, normals, spectrum)
    a, place = lax.optimization_barrier((a, gy))
    a = lax.all_to_all(a, "gz", split_axis=0, concat_axis=0, tiled=True)
    c1, c3, c2 = scale(0, (1, 3, 2), place, normals, spectrum)
    place, c1, c3, c2 = lax.optimization_barrier((place, c1, c3, c2))
    c1, c3, c2 = shifted(c1, "gy", 1), shifted(c3, "gy", 3), shifted(c2, "gy", 2)
    d1, d3, d2 = scale(1, (1, 3, 2), place, normals, spectrum)
    place, d1, d3, d2 = lax.optimization_barrier((place, d1, d3, d2))
    d1, d3, d2 = shifted(d1, "gy", 1), shifted(d3, "gy", 3), shifted(d2, "gy", 2)
    (c0,) = scale(0, (0,), place, normals, spectrum)
    (d0,) = scale(1, (0,), place, normals, spectrum)

    c1, c3, c2, c0 = first_y(gy, gz, (c0, c1, c2, c3), table_y)
    a, slots, c1, c3, d0 = lax.optimization_barrier((a, slots_of(block_owner), c1, c3, d0))
    c1, c3 = shifted(c1, "gz", 1), shifted(c3, "gz", 3)
    a2, a1, a3, a0 = first_z((2, 1, 3, 0), gy, a, table_z)
    d1, d2, d3, c1, c3, _ = lax.optimization_barrier((d1, d2, d3, c1, c3, a2))
    a1, a3, a2 = shifted(a1, "gy", 1), shifted(a3, "gy", 3), shifted(a2, "gy", 2)
    d1, d3, b2, b0 = first_y(gy, gz, (d0, d1, d2, d3), table_y, (c2, c0))
    d1, d3, b2 = shifted(d1, "gz", 1), shifted(d3, "gz", 3), shifted(b2, "gz", 2)

    part_a = part_y(gy, (a0, a2), table_y)
    part_a, b2 = lax.optimization_barrier((part_a, b2))
    done_b = second_z(gz, (b0, b2, c1, c3, d1, d3), table_z)
    part_a, done_b, a1, a3 = lax.optimization_barrier((part_a, done_b, a1, a3))
    planes = second(gy, part_a, (a1, a3), table_y, done_b)
    lines = lax.all_to_all(planes, ALL, split_axis=0, concat_axis=0, tiled=True)
    outgoing = third(slots, lines, table_x, ordering)
    return lax.all_to_all(
        outgoing.reshape(128, 1, CAP, 2, BW), ALL, split_axis=0, concat_axis=1, tiled=True
    )


def solution(mesh):
    placed = (P(None, "gx", "gy", "gz"), P("gx", "gy", "gz"), P(ALL, None))
    return jax.shard_map(
        per_device,
        mesh=mesh,
        in_specs=placed,
        out_specs=P(ALL, None, None, None, None),
        check_vma=False,
    )
```

```python
import functools

import jax
import jax.numpy as jnp
import ml_dtypes
import numpy as np
from jax import lax
from jax.experimental import pallas as pl
from jax.experimental.pallas import tpu as pltpu
from jax.sharding import PartitionSpec as P

N = 512
KEPT = 256
BW = 128
CAP = 16
ALL = ("gx", "gy", "gz")
MIB = 1 << 20
VMEM = 24


def split_table(table):
    high = table.astype(np.float32).astype(ml_dtypes.bfloat16)
    low = (table - high.astype(np.float64)).astype(np.float32).astype(ml_dtypes.bfloat16)
    return np.stack([high, low])


def cos_sin(positions, kept):
    angles = (positions[:, None] * kept[None, :] % N) * (2.0 * np.pi / N)
    return np.cos(angles), np.sin(angles)


@functools.cache
def tables():
    order = np.arange(KEPT).reshape(KEPT // 2, 2).T.reshape(-1)
    cosine, sine = cos_sin(np.arange(N // 2), order)
    cosine, sine = (t.reshape(2, 128, 2, 128).transpose(0, 2, 1, 3) for t in (cosine, sine))
    real_rows = np.concatenate([cosine, -sine], 3)
    imag_rows = np.concatenate([sine, cosine], 3)
    table_z = np.concatenate([real_rows, imag_rows], 2)
    cosine, sine = cos_sin(np.arange(N // 2), order)
    cosine, sine = (t.T.reshape(2, 128, 2, 128).transpose(2, 0, 1, 3) for t in (cosine, sine))
    top = np.concatenate([cosine, sine], 3)
    bottom = np.concatenate([-sine, cosine], 3)
    table_y = np.concatenate([top, bottom], 2)
    gx, gy, gz = np.meshgrid(np.arange(8), np.arange(4), np.arange(4), indexing="ij")
    first = 64 * gx + 8 * gz + 2 * gy
    second = 64 * gx + 32 + 8 * gy + gz
    cells = np.stack([first, first + 1, second, second + 4], -1).reshape(128, 4)
    cosine, sine = cos_sin(cells[:64].reshape(-1), order)
    cosine, sine = (
        t.T.reshape(2, KEPT // 2, 64, 1, 4) for t in (cosine, sine)
    )
    top = np.concatenate([cosine, sine], 3).reshape(2, KEPT // 2, 512)
    bottom = np.concatenate([-sine, cosine], 3).reshape(2, KEPT // 2, 512)
    table_x = np.concatenate([top, bottom], 1)
    ordering = np.zeros((KEPT, KEPT), ml_dtypes.bfloat16)
    ordering[np.arange(KEPT), order] = 1
    return split_table(table_x), split_table(table_y), split_table(table_z), ordering


def halves(values):
    high = values.astype(jnp.bfloat16)
    low = (values - high.astype(jnp.float32)).astype(jnp.bfloat16)
    return high, low


def product(left, right):
    def dot(a, b):
        return jnp.dot(a, b, preferred_element_type=jnp.float32)

    return dot(left[0], right[0]) + (dot(left[0], right[1]) + dot(left[1], right[0]))


def params(mib):
    return pltpu.CompilerParams(vmem_limit_bytes=mib * MIB)


def cost(multiplies, moved):
    return pl.CostEstimate(
        flops=multiplies >> 16, bytes_accessed=moved >> 16, transcendentals=0
    )


def rows_z(piece):
    return halves(jnp.concatenate([piece[plane].reshape(-1, 128) for plane in range(2)], axis=1))


def columns_y(piece):
    planes, cells = piece.shape[:2]
    return halves(
        jnp.concatenate([piece[:, x].reshape(256, piece.shape[3]) for x in range(cells)], axis=1)
    )


def in_hbm(*arrays):
    return [pltpu.with_memory_space_constraint(x, pltpu.HBM) for x in arrays]


def scale_kernel(part, shifts, place_ref, normals_ref, spectrum_ref, *refs):
    *out_refs, held_out, held_n, held_s, semaphores = refs

    def gets(i):
        if part is None:
            source_n, source_s = normals_ref.at[:, i], spectrum_ref.at[i]
        else:
            chunk = 4 + lax.rem(place_ref[0] + shifts[i], 4)
            source_n, source_s = normals_ref.at[:, chunk, part], spectrum_ref.at[chunk, part]
        return (
            pltpu.make_async_copy(source_n, held_n.at[i], semaphores.at[i, 0]),
            pltpu.make_async_copy(source_s, held_s.at[i], semaphores.at[i, 1]),
        )

    def put(i):
        target = out_refs[0].at[i] if part is None else out_refs[i]
        return pltpu.make_async_copy(held_out.at[i], target, semaphores.at[i, 2])

    steps = range(len(shifts))
    for i in steps:
        for copy in gets(i):
            copy.start()
    for i in steps:
        for copy in gets(i):
            copy.wait()
        for plane in range(2):
            held_out[i, plane] = held_n[i, plane].astype(jnp.float32) * held_s[i]
        put(i).start()
    for i in steps:
        put(i).wait()


def scale(part, shifts, place, normals, spectrum):
    count = len(shifts)
    chunk = (2, 8 if part is None else 4, 128, 128)
    shapes = [(count,) + chunk] if part is None else [chunk] * count
    view = (8, 8, 128, 128) if part is None else (8, 2, 4, 128, 128)
    hbm = pl.BlockSpec(memory_space=pltpu.HBM)
    return pl.pallas_call(
        functools.partial(scale_kernel, part, shifts),
        in_specs=[pl.BlockSpec(memory_space=pltpu.SMEM)] + [hbm] * 2,
        out_specs=[hbm] * len(shapes),
        out_shape=[pltpu.HBM(shape, jnp.float32) for shape in shapes],
        scratch_shapes=[
            pltpu.VMEM((count,) + chunk, jnp.float32),
            pltpu.VMEM((count,) + chunk, jnp.bfloat16),
            pltpu.VMEM((count,) + chunk[1:], jnp.float32),
            pltpu.SemaphoreType.DMA((count, 3)),
        ],
        compiler_params=params(VMEM),
        cost_estimate=cost(count << 18, 2 * count * MIB),
        name="scale_a" if part is None else "scale_b",
    )(place, *in_hbm(normals.reshape((2,) + view), spectrum.reshape(view)))


def transform(along_z, pairs, table_ref):
    parts = []
    for odd in range(2):
        total = None
        for first, second, g in pairs:
            base = lax.rem(g, 2)
            table = (table_ref[0, base, odd], table_ref[1, base, odd])
            if odd:
                sides = (first - second) * jnp.where(g < 2, 1.0, -1.0).astype(jnp.float32)
            else:
                sides = first + second
            if along_z:
                term = product(rows_z(sides), table)
            else:
                term = product(table, columns_y(sides))
            total = term if total is None else total + term
        parts.append(total)
    return parts


def first_z_kernel(shifts, to_ref, in_ref, table_ref, *refs):
    *out_refs, pieces, held_out, semaphores = refs

    def get(i):
        cells = pl.ds(2 * lax.rem(to_ref[0] + shifts[i], 4), 2)
        return pltpu.make_async_copy(in_ref.at[:, :, cells], pieces.at[i], semaphores.at[i, 0])

    def put(i):
        return pltpu.make_async_copy(held_out.at[i], out_refs[i], semaphores.at[i, 1])

    steps = range(len(shifts))
    for i in steps:
        get(i).start()
    for i in steps:
        get(i).wait()
        pairs = [(pieces[i, 0], pieces[i, 2], 0), (pieces[i, 1], pieces[i, 3], 1)]
        for odd, values in enumerate(transform(True, pairs, table_ref)):
            half = slice(odd * 128, (odd + 1) * 128)
            for plane in range(2):
                part = slice(plane * 128, (plane + 1) * 128)
                for x in range(2):
                    held_out[i, plane, x, :, half] = values[x * 128 : (x + 1) * 128, part]
        put(i).start()
    for i in steps:
        put(i).wait()


def first_z(shifts, to, arrived, table):
    shape = (2, 2, 128, KEPT)
    hbm = pl.BlockSpec(memory_space=pltpu.HBM)
    count = len(shifts)
    return pl.pallas_call(
        functools.partial(first_z_kernel, shifts),
        in_specs=[
            pl.BlockSpec(memory_space=pltpu.SMEM),
            hbm,
            pl.BlockSpec(memory_space=pltpu.VMEM),
        ],
        out_specs=[hbm] * count,
        out_shape=[pltpu.HBM(shape, jnp.float32)] * count,
        scratch_shapes=[
            pltpu.VMEM((count, 4, 2, 2, 128, 128), jnp.float32),
            pltpu.VMEM((count,) + shape, jnp.float32),
            pltpu.SemaphoreType.DMA((count, 2)),
        ],
        compiler_params=params(VMEM),
        cost_estimate=cost(count * 256 * 512 * 512, 2 * count * MIB),
        name="first_z",
    )(to, *in_hbm(arrived), table)


def first_y_kernel(merge, place_ref, to_ref, *refs):
    in_refs, refs = refs[:4], refs[6 if merge else 4 :]
    table_ref, *out_refs, pieces, held_out, semaphores = refs

    def gets(i):
        x = pl.ds(lax.rem(to_ref[0] + (1, 3, 2, 0)[i], 4), 1)
        return [
            pltpu.make_async_copy(ref.at[:, x], pieces.at[i, s], semaphores.at[i, s])
            for s, ref in enumerate(in_refs)
        ]

    def put(i):
        target = out_refs[i].at[:, 1:2] if merge and i >= 2 else out_refs[i].at[:, 0:1]
        return pltpu.make_async_copy(held_out.at[i], target, semaphores.at[i, 4])

    for i in range(4):
        for copy in gets(i):
            copy.start()
    g, h = place_ref[0], lax.rem(place_ref[0] + 3, 4)
    for group in ((0, 1), (2, 3)):
        for i in group:
            for copy in gets(i):
                copy.wait()
        p0, p1, p2, p3 = (
            jnp.concatenate([pieces[i, s] for i in group], axis=1) for s in range(4)
        )
        for odd, values in enumerate(transform(False, [(p0, p2, g), (p1, p3, h)], table_ref)):
            for plane in range(2):
                for x, i in enumerate(group):
                    held_out[i, plane, 0, odd * 128 : (odd + 1) * 128] = values[
                        plane * 128 : (plane + 1) * 128, x * 128 : (x + 1) * 128
                    ]
        for i in group:
            put(i).start()
    for i in range(4):
        put(i).wait()


def first_y(place, to, pieces, table, before=()):
    merge = bool(before)
    shape, whole = (2, 1, KEPT, 128), (2, 2, KEPT, 128)
    hbm = pl.BlockSpec(memory_space=pltpu.HBM)
    operands = in_hbm(*pieces, *before)
    return pl.pallas_call(
        functools.partial(first_y_kernel, merge),
        in_specs=[pl.BlockSpec(memory_space=pltpu.SMEM)] * 2
        + [hbm] * len(operands)
        + [pl.BlockSpec(memory_space=pltpu.VMEM)],
        out_specs=[hbm] * 4,
        out_shape=[pltpu.HBM(shape, jnp.float32)] * 2 + [pltpu.HBM(whole, jnp.float32)] * 2,
        scratch_shapes=[
            pltpu.VMEM((4, 4, 2, 1, 128, 128), jnp.float32),
            pltpu.VMEM((4,) + shape, jnp.float32),
            pltpu.SemaphoreType.DMA((4, 5)),
        ],
        input_output_aliases={6: 2, 7: 3} if merge else {},
        compiler_params=params(VMEM),
        cost_estimate=cost(512 * 512 * 512, 4 * MIB),
        name="first_y",
    )(place, to, *operands, table)


def part_y_kernel(place_ref, p0, p2, table_ref, out_ref):
    pairs = [(p0[...], p2[...], place_ref[0])]
    for odd, values in enumerate(transform(False, pairs, table_ref)):
        out_ref[odd] = values


def part_y(place, pieces, table):
    return pl.pallas_call(
        part_y_kernel,
        grid_spec=pltpu.PrefetchScalarGridSpec(
            num_scalar_prefetch=1,
            grid=(2,),
            in_specs=[pl.BlockSpec((2, 1, 128, KEPT), lambda i, place: (0, i, 0, 0))] * 2
            + [pl.BlockSpec(table.shape, lambda i, place: (0, 0, 0, 0, 0))],
            out_specs=pl.BlockSpec((2, KEPT, KEPT), lambda i, place: (0, 0, i)),
        ),
        out_shape=jax.ShapeDtypeStruct((2, KEPT, 512), jnp.float32),
        compiler_params=params(VMEM),
        cost_estimate=cost(512 * 512 * 256, 4 * MIB),
        name="part_y",
    )(place, *pieces, table)


def second_z_kernel(place_ref, b0, b2, c1, c3, d1, d3, table_ref, out_ref):
    g, h = place_ref[0], lax.rem(place_ref[0] + 3, 4)
    for x, (p1, p3) in enumerate(((c1, c3), (d1, d3))):
        cell = slice(x, x + 1)
        pairs = [(b0[:, cell], b2[:, cell], g), (p1[...], p3[...], h)]
        for odd, values in enumerate(transform(True, pairs, table_ref)):
            out_ref[x, :, odd * 256 : (odd + 1) * 256] = values


def second_z(place, pieces, table):
    vmem = pl.BlockSpec(memory_space=pltpu.VMEM)
    return pl.pallas_call(
        second_z_kernel,
        in_specs=[pl.BlockSpec(memory_space=pltpu.SMEM)] + [vmem] * 7,
        out_specs=vmem,
        out_shape=jax.ShapeDtypeStruct((2, KEPT, 512), jnp.float32),
        compiler_params=params(VMEM),
        cost_estimate=cost(512 * 512 * 512, 4 * MIB),
        name="second_z",
    )(place, *pieces, table)


def second_kernel(
    y_ref, part_a, a1, a3, table_y_ref, done_b, out_ref, held
):
    odd = pl.program_id(0)

    def put(values, half, row):
        held[pl.ds(half * 8 + row, 128, stride=16), :] = values

    g = lax.rem(y_ref[0] + 3, 4)
    base = lax.rem(g, 2)
    flip = jnp.where(odd == 0, 1.0, -1.0).astype(jnp.float32)
    sign = jnp.where((odd == 0) | (g < 2), 1.0, -1.0).astype(jnp.float32)
    table = (table_y_ref[0, base, 0], table_y_ref[1, base, 0])
    values = part_a[0] + product(table, columns_y((a1[...] + flip * a3[...]) * sign))
    for plane in range(2):
        for x in range(2):
            for half in range(2):
                start = x * KEPT + half * 128
                put(
                    values[plane * 128 : (plane + 1) * 128, start : start + 128],
                    half,
                    plane * 4 + x,
                )
    for half in range(2):
        values = done_b[:, :, half * 256 : (half + 1) * 256].reshape(256, 256)
        for x in range(2):
            for plane in range(2):
                put(
                    values[x * 128 : (x + 1) * 128, plane * 128 : (plane + 1) * 128],
                    half,
                    plane * 4 + 2 + x,
                )
    out_ref[...] = held[...].reshape(128, 1, 2, 8, 128)


def second(gy, part_a, pieces_a, table_y, done_b):
    return pl.pallas_call(
        second_kernel,
        grid_spec=pltpu.PrefetchScalarGridSpec(
            num_scalar_prefetch=1,
            grid=(2,),
            in_specs=[pl.BlockSpec((1, KEPT, 512), lambda i, gy: (i, 0, 0))]
            + [pl.BlockSpec((2, 2, 128, KEPT), lambda i, gy: (0, 0, 0, 0))] * 2
            + [
                pl.BlockSpec((2, 2, 1, KEPT, KEPT), lambda i, gy: (0, 0, i, 0, 0)),
                pl.BlockSpec((2, 128, 512), lambda i, gy: (0, i, 0)),
            ],
            out_specs=pl.BlockSpec((128, 1, 2, 8, 128), lambda i, gy: (0, i, 0, 0, 0)),
            scratch_shapes=[pltpu.VMEM((2048, 128), jnp.float32)],
        ),
        out_shape=jax.ShapeDtypeStruct((128, 2, 2, 8, 128), jnp.float32),
        compiler_params=params(VMEM),
        cost_estimate=cost(512 * 512 * 256, 8 * MIB),
        name="second",
    )(gy, part_a, *pieces_a, table_y, done_b)


def third_kernel(slot_ref, in_ref, table_ref, ordering_ref, out_ref, held):
    out_ref[...] = jnp.zeros_like(out_ref)
    for parity in range(2):
        columns = jnp.concatenate(
            [in_ref[:, parity, half].reshape(1024, 128) for half in range(2)], axis=1
        )
        first, last = columns[:512], columns[512:]
        for odd, sides in enumerate((first + last, first - last)):
            sides = tuple(
                jnp.dot(
                    part, ordering_ref[...], preferred_element_type=jnp.float32
                ).astype(jnp.bfloat16)
                for part in halves(sides)
            )
            values = jnp.exp(product((table_ref[0, odd], table_ref[1, odd]), sides))
            for plane in range(2):
                for half in range(2):
                    held[parity, plane, half, odd * 128 : (odd + 1) * 128] = values[
                        plane * 128 : (plane + 1) * 128, half * 128 : (half + 1) * 128
                    ]

    def place_rows(group, carry):
        for offset in range(8):
            x = group * 8 + offset
            row = group * 4 + offset // 2 + 128 * (offset % 2)
            for parity in range(2):
                for half in range(2):
                    slot = slot_ref[x * 4 + parity * 2 + half]
                    for plane in range(2):
                        out_ref[pl.ds(slot * 2 + plane, 1), :] = held[
                            parity, plane, half, pl.ds(row, 1), :
                        ]
        return carry

    lax.fori_loop(0, KEPT // 8, place_rows, 0)


def third(slots, arrived, table_x, ordering):
    vmem = pl.BlockSpec(memory_space=pltpu.VMEM)
    return pl.pallas_call(
        third_kernel,
        in_specs=[pl.BlockSpec(memory_space=pltpu.SMEM)] + [vmem] * 3,
        out_specs=vmem,
        out_shape=jax.ShapeDtypeStruct((4096, 128), jnp.float32),
        scratch_shapes=[pltpu.VMEM((2, 2, 2, KEPT, 128), jnp.float32)],
        compiler_params=params(VMEM),
        cost_estimate=cost(768 * 512 * 512, 6 * MIB),
        name="third",
    )(slots, arrived, table_x, ordering)


def shifted(piece, axis, shift):
    size = lax.axis_size(axis)
    return lax.ppermute(piece, axis, [(i, (i + shift) % size) for i in range(size)])


def slots_of(block_owner):
    destination = block_owner[:, 0]
    one_hot = (destination[:, None] == jnp.arange(128, dtype=jnp.int32)[None, :]).astype(jnp.int32)
    earlier = jnp.cumsum(one_hot, axis=0) - one_hot
    return destination * CAP + jnp.sum(earlier * one_hot, axis=1)


def per_device(normals, spectrum, block_owner):
    table_x, table_y, table_z, ordering = (jnp.asarray(table) for table in tables())
    gy = lax.axis_index("gy").astype(jnp.int32).reshape(1)
    gz = lax.axis_index("gz").astype(jnp.int32).reshape(1)

    (a,) = scale(None, (0, 1, 2, 3), gz, normals, spectrum)
    a, place = lax.optimization_barrier((a, gy))
    a = lax.all_to_all(a, "gz", split_axis=0, concat_axis=0, tiled=True)
    c1, c3, c2 = scale(0, (1, 3, 2), place, normals, spectrum)
    place, c1, c3, c2 = lax.optimization_barrier((place, c1, c3, c2))
    c1, c3, c2 = shifted(c1, "gy", 1), shifted(c3, "gy", 3), shifted(c2, "gy", 2)
    d1, d3, d2 = scale(1, (1, 3, 2), place, normals, spectrum)
    place, d1, d3, d2 = lax.optimization_barrier((place, d1, d3, d2))
    d1, d3, d2 = shifted(d1, "gy", 1), shifted(d3, "gy", 3), shifted(d2, "gy", 2)
    (c0,) = scale(0, (0,), place, normals, spectrum)
    (d0,) = scale(1, (0,), place, normals, spectrum)

    c1, c3, c2, c0 = first_y(gy, gz, (c0, c1, c2, c3), table_y)
    a, slots, _, d0 = lax.optimization_barrier((a, slots_of(block_owner), c1, d0))
    c1, c3 = shifted(c1, "gz", 1), shifted(c3, "gz", 3)
    a2, a1, a3, a0 = first_z((2, 1, 3, 0), gy, a, table_z)
    d1, d2, d3, c1, c3, _ = lax.optimization_barrier((d1, d2, d3, c1, c3, a2))
    a1, a3, a2 = shifted(a1, "gy", 1), shifted(a3, "gy", 3), shifted(a2, "gy", 2)
    d1, d3, b2, b0 = first_y(gy, gz, (d0, d1, d2, d3), table_y, (c2, c0))
    d1, d3, b2 = shifted(d1, "gz", 1), shifted(d3, "gz", 3), shifted(b2, "gz", 2)

    part_a = part_y(gy, (a0, a2), table_y)
    part_a, b2 = lax.optimization_barrier((part_a, b2))
    done_b = second_z(gz, (b0, b2, c1, c3, d1, d3), table_z)
    part_a, done_b, a1, a3 = lax.optimization_barrier((part_a, done_b, a1, a3))
    planes = second(gy, part_a, (a1, a3), table_y, done_b)
    lines = lax.all_to_all(planes, ALL, split_axis=0, concat_axis=0, tiled=True)
    outgoing = third(slots, lines, table_x, ordering)
    return lax.all_to_all(
        outgoing.reshape(128, 1, CAP, 2, BW), ALL, split_axis=0, concat_axis=1, tiled=True
    )


def solution(mesh):
    placed = (P(None, "gx", "gy", "gz"), P("gx", "gy", "gz"), P(ALL, None))
    return jax.shard_map(
        per_device,
        mesh=mesh,
        in_specs=placed,
        out_specs=P(ALL, None, None, None, None),
        check_vma=False,
    )
```

```python
import functools

import jax
import jax.numpy as jnp
import ml_dtypes
import numpy as np
from jax import lax
from jax.experimental import pallas as pl
from jax.experimental.pallas import tpu as pltpu
from jax.sharding import PartitionSpec as P

N = 512
KEPT = 256
BW = 128
CAP = 16
ALL = ("gx", "gy", "gz")
MIB = 1 << 20
VMEM = 24


def split_table(table):
    high = table.astype(np.float32).astype(ml_dtypes.bfloat16)
    low = (table - high.astype(np.float64)).astype(np.float32).astype(ml_dtypes.bfloat16)
    return np.stack([high, low])


def cos_sin(positions, kept):
    angles = (positions[:, None] * kept[None, :] % N) * (2.0 * np.pi / N)
    return np.cos(angles), np.sin(angles)


@functools.cache
def tables():
    order = np.arange(KEPT).reshape(KEPT // 2, 2).T.reshape(-1)
    cosine, sine = cos_sin(np.arange(N // 2), order)
    cosine, sine = (t.reshape(2, 128, 2, 128).transpose(0, 2, 1, 3) for t in (cosine, sine))
    real_rows = np.concatenate([cosine, -sine], 3)
    imag_rows = np.concatenate([sine, cosine], 3)
    table_z = np.concatenate([real_rows, imag_rows], 2)
    cosine, sine = cos_sin(np.arange(N // 2), order)
    cosine, sine = (t.T.reshape(2, 128, 2, 128).transpose(2, 0, 1, 3) for t in (cosine, sine))
    top = np.concatenate([cosine, sine], 3)
    bottom = np.concatenate([-sine, cosine], 3)
    table_y = np.concatenate([top, bottom], 2)
    gx, gy, gz = np.meshgrid(np.arange(8), np.arange(4), np.arange(4), indexing="ij")
    first = 64 * gx + 8 * gz + 2 * gy
    second = 64 * gx + 32 + 8 * gy + gz
    cells = np.stack([first, first + 1, second, second + 4], -1).reshape(128, 4)
    cosine, sine = cos_sin(cells[:64].reshape(-1), order)
    cosine, sine = (
        t.T.reshape(2, KEPT // 2, 64, 1, 4) for t in (cosine, sine)
    )
    top = np.concatenate([cosine, sine], 3).reshape(2, KEPT // 2, 512)
    bottom = np.concatenate([-sine, cosine], 3).reshape(2, KEPT // 2, 512)
    table_x = np.concatenate([top, bottom], 1)
    ordering = np.zeros((KEPT, KEPT), ml_dtypes.bfloat16)
    ordering[np.arange(KEPT), order] = 1
    return split_table(table_x), split_table(table_y), split_table(table_z), ordering


def halves(values):
    high = values.astype(jnp.bfloat16)
    low = (values - high.astype(jnp.float32)).astype(jnp.bfloat16)
    return high, low


def product(left, right):
    def dot(a, b):
        return jnp.dot(a, b, preferred_element_type=jnp.float32)

    return dot(left[0], right[0]) + (dot(left[0], right[1]) + dot(left[1], right[0]))


def params(mib):
    return pltpu.CompilerParams(vmem_limit_bytes=mib * MIB)


def cost(multiplies, moved):
    return pl.CostEstimate(
        flops=multiplies >> 16, bytes_accessed=moved >> 16, transcendentals=0
    )


def rows_z(piece):
    return halves(jnp.concatenate([piece[plane].reshape(-1, 128) for plane in range(2)], axis=1))


def columns_y(piece):
    planes, cells = piece.shape[:2]
    return halves(
        jnp.concatenate([piece[:, x].reshape(256, piece.shape[3]) for x in range(cells)], axis=1)
    )


def in_hbm(*arrays):
    return [pltpu.with_memory_space_constraint(x, pltpu.HBM) for x in arrays]


def scale_kernel(part, shifts, place_ref, normals_ref, spectrum_ref, *refs):
    *out_refs, held_out, held_n, held_s, semaphores = refs

    def gets(i):
        if part is None:
            source_n, source_s = normals_ref.at[:, i], spectrum_ref.at[i]
        else:
            chunk = 4 + lax.rem(place_ref[0] + shifts[i], 4)
            source_n, source_s = normals_ref.at[:, chunk, part], spectrum_ref.at[chunk, part]
        return (
            pltpu.make_async_copy(source_n, held_n.at[i], semaphores.at[i, 0]),
            pltpu.make_async_copy(source_s, held_s.at[i], semaphores.at[i, 1]),
        )

    def put(i):
        target = out_refs[0].at[i] if part is None else out_refs[i]
        return pltpu.make_async_copy(held_out.at[i], target, semaphores.at[i, 2])

    steps = range(len(shifts))
    for i in steps:
        for copy in gets(i):
            copy.start()
    for i in steps:
        for copy in gets(i):
            copy.wait()
        for plane in range(2):
            held_out[i, plane] = held_n[i, plane].astype(jnp.float32) * held_s[i]
        put(i).start()
    for i in steps:
        put(i).wait()


def scale(part, shifts, place, normals, spectrum):
    count = len(shifts)
    chunk = (2, 8 if part is None else 4, 128, 128)
    shapes = [(count,) + chunk] if part is None else [chunk] * count
    view = (8, 8, 128, 128) if part is None else (8, 2, 4, 128, 128)
    hbm = pl.BlockSpec(memory_space=pltpu.HBM)
    return pl.pallas_call(
        functools.partial(scale_kernel, part, shifts),
        in_specs=[pl.BlockSpec(memory_space=pltpu.SMEM)] + [hbm] * 2,
        out_specs=[hbm] * len(shapes),
        out_shape=[pltpu.HBM(shape, jnp.float32) for shape in shapes],
        scratch_shapes=[
            pltpu.VMEM((count,) + chunk, jnp.float32),
            pltpu.VMEM((count,) + chunk, jnp.bfloat16),
            pltpu.VMEM((count,) + chunk[1:], jnp.float32),
            pltpu.SemaphoreType.DMA((count, 3)),
        ],
        compiler_params=params(VMEM),
        cost_estimate=cost(count << 18, 2 * count * MIB),
        name="scale_a" if part is None else "scale_b",
    )(place, *in_hbm(normals.reshape((2,) + view), spectrum.reshape(view)))


def transform(along_z, pairs, table_ref):
    parts = []
    for odd in range(2):
        total = None
        for first, second, g in pairs:
            base = lax.rem(g, 2)
            table = (table_ref[0, base, odd], table_ref[1, base, odd])
            if odd:
                sides = (first - second) * jnp.where(g < 2, 1.0, -1.0).astype(jnp.float32)
            else:
                sides = first + second
            if along_z:
                term = product(rows_z(sides), table)
            else:
                term = product(table, columns_y(sides))
            total = term if total is None else total + term
        parts.append(total)
    return parts


def first_z_kernel(shifts, to_ref, in_ref, table_ref, *refs):
    *out_refs, pieces, held_out, semaphores = refs

    def get(i):
        cells = pl.ds(2 * lax.rem(to_ref[0] + shifts[i], 4), 2)
        return pltpu.make_async_copy(in_ref.at[:, :, cells], pieces.at[i], semaphores.at[i, 0])

    def put(i):
        return pltpu.make_async_copy(held_out.at[i], out_refs[i], semaphores.at[i, 1])

    steps = range(len(shifts))
    for i in steps:
        get(i).start()
    for i in steps:
        get(i).wait()
        pairs = [(pieces[i, 0], pieces[i, 2], 0), (pieces[i, 1], pieces[i, 3], 1)]
        for odd, values in enumerate(transform(True, pairs, table_ref)):
            half = slice(odd * 128, (odd + 1) * 128)
            for plane in range(2):
                part = slice(plane * 128, (plane + 1) * 128)
                for x in range(2):
                    held_out[i, plane, x, :, half] = values[x * 128 : (x + 1) * 128, part]
        put(i).start()
    for i in steps:
        put(i).wait()


def first_z(shifts, to, arrived, table):
    shape = (2, 2, 128, KEPT)
    hbm = pl.BlockSpec(memory_space=pltpu.HBM)
    count = len(shifts)
    return pl.pallas_call(
        functools.partial(first_z_kernel, shifts),
        in_specs=[
            pl.BlockSpec(memory_space=pltpu.SMEM),
            hbm,
            pl.BlockSpec(memory_space=pltpu.VMEM),
        ],
        out_specs=[hbm] * count,
        out_shape=[pltpu.HBM(shape, jnp.float32)] * count,
        scratch_shapes=[
            pltpu.VMEM((count, 4, 2, 2, 128, 128), jnp.float32),
            pltpu.VMEM((count,) + shape, jnp.float32),
            pltpu.SemaphoreType.DMA((count, 2)),
        ],
        compiler_params=params(VMEM),
        cost_estimate=cost(count * 256 * 512 * 512, 2 * count * MIB),
        name="first_z",
    )(to, *in_hbm(arrived), table)


def first_y_kernel(merge, place_ref, to_ref, *refs):
    in_refs, refs = refs[:4], refs[6 if merge else 4 :]
    table_ref, *out_refs, pieces, held_out, semaphores = refs

    def gets(i):
        x = pl.ds(lax.rem(to_ref[0] + (1, 3, 2, 0)[i], 4), 1)
        return [
            pltpu.make_async_copy(ref.at[:, x], pieces.at[i, s], semaphores.at[i, s])
            for s, ref in enumerate(in_refs)
        ]

    def put(i):
        target = out_refs[i].at[:, 1:2] if merge and i >= 2 else out_refs[i].at[:, 0:1]
        return pltpu.make_async_copy(held_out.at[i], target, semaphores.at[i, 4])

    for i in range(4):
        for copy in gets(i):
            copy.start()
    g, h = place_ref[0], lax.rem(place_ref[0] + 3, 4)
    for group in ((0, 1), (2, 3)):
        for i in group:
            for copy in gets(i):
                copy.wait()
        p0, p1, p2, p3 = (
            jnp.concatenate([pieces[i, s] for i in group], axis=1) for s in range(4)
        )
        for odd, values in enumerate(transform(False, [(p0, p2, g), (p1, p3, h)], table_ref)):
            for plane in range(2):
                for x, i in enumerate(group):
                    held_out[i, plane, 0, odd * 128 : (odd + 1) * 128] = values[
                        plane * 128 : (plane + 1) * 128, x * 128 : (x + 1) * 128
                    ]
        for i in group:
            put(i).start()
    for i in range(4):
        put(i).wait()


def first_y(place, to, pieces, table, before=()):
    merge = bool(before)
    shape, whole = (2, 1, KEPT, 128), (2, 2, KEPT, 128)
    hbm = pl.BlockSpec(memory_space=pltpu.HBM)
    operands = in_hbm(*pieces, *before)
    return pl.pallas_call(
        functools.partial(first_y_kernel, merge),
        in_specs=[pl.BlockSpec(memory_space=pltpu.SMEM)] * 2
        + [hbm] * len(operands)
        + [pl.BlockSpec(memory_space=pltpu.VMEM)],
        out_specs=[hbm] * 4,
        out_shape=[pltpu.HBM(shape, jnp.float32)] * 2 + [pltpu.HBM(whole, jnp.float32)] * 2,
        scratch_shapes=[
            pltpu.VMEM((4, 4, 2, 1, 128, 128), jnp.float32),
            pltpu.VMEM((4,) + shape, jnp.float32),
            pltpu.SemaphoreType.DMA((4, 5)),
        ],
        input_output_aliases={6: 2, 7: 3} if merge else {},
        compiler_params=params(VMEM),
        cost_estimate=cost(512 * 512 * 512, 4 * MIB),
        name="first_y",
    )(place, to, *operands, table)


def part_y_kernel(place_ref, p0, p2, table_ref, out_ref):
    pairs = [(p0[...], p2[...], place_ref[0])]
    for odd, values in enumerate(transform(False, pairs, table_ref)):
        out_ref[odd] = values


def part_y(place, pieces, table):
    return pl.pallas_call(
        part_y_kernel,
        grid_spec=pltpu.PrefetchScalarGridSpec(
            num_scalar_prefetch=1,
            grid=(2,),
            in_specs=[pl.BlockSpec((2, 1, 128, KEPT), lambda i, place: (0, i, 0, 0))] * 2
            + [pl.BlockSpec(table.shape, lambda i, place: (0, 0, 0, 0, 0))],
            out_specs=pl.BlockSpec((2, KEPT, KEPT), lambda i, place: (0, 0, i)),
        ),
        out_shape=jax.ShapeDtypeStruct((2, KEPT, 512), jnp.float32),
        compiler_params=params(VMEM),
        cost_estimate=cost(512 * 512 * 256, 4 * MIB),
        name="part_y",
    )(place, *pieces, table)


def second_kernel(
    y_ref,
    z_ref,
    part_a,
    a1,
    a3,
    table_y_ref,
    b0,
    b2,
    c1,
    c3,
    d1,
    d3,
    table_z_ref,
    out_ref,
    held,
):
    odd = pl.program_id(0)

    def put(values, half, row):
        held[pl.ds(half * 8 + row, 128, stride=16), :] = values

    g = lax.rem(y_ref[0] + 3, 4)
    base = lax.rem(g, 2)
    flip = jnp.where(odd == 0, 1.0, -1.0).astype(jnp.float32)
    sign = jnp.where((odd == 0) | (g < 2), 1.0, -1.0).astype(jnp.float32)
    table = (table_y_ref[0, base, 0], table_y_ref[1, base, 0])
    values = part_a[0] + product(table, columns_y((a1[...] + flip * a3[...]) * sign))
    for plane in range(2):
        for x in range(2):
            for half in range(2):
                start = x * KEPT + half * 128
                put(
                    values[plane * 128 : (plane + 1) * 128, start : start + 128],
                    half,
                    plane * 4 + x,
                )
    near, far = (
        jnp.concatenate([c[...], d[...]], axis=1) for c, d in ((c1, d1), (c3, d3))
    )
    pairs = [(b0[...], b2[...], z_ref[0]), (near, far, lax.rem(z_ref[0] + 3, 4))]
    for half, values in enumerate(transform(True, pairs, table_z_ref)):
        for x in range(2):
            for plane in range(2):
                put(
                    values[x * 128 : (x + 1) * 128, plane * 128 : (plane + 1) * 128],
                    half,
                    plane * 4 + 2 + x,
                )
    out_ref[...] = held[...].reshape(128, 1, 2, 8, 128)


def second(gy, gz, part_a, pieces_a, table_y, pieces_b, table_z):
    def rows(cells):
        return pl.BlockSpec((2, cells, 128, 128), lambda i, gy, gz: (0, 0, i, 0))

    return pl.pallas_call(
        second_kernel,
        grid_spec=pltpu.PrefetchScalarGridSpec(
            num_scalar_prefetch=2,
            grid=(2,),
            in_specs=[pl.BlockSpec((1, KEPT, 512), lambda i, gy, gz: (i, 0, 0))]
            + [pl.BlockSpec((2, 2, 128, KEPT), lambda i, gy, gz: (0, 0, 0, 0))] * 2
            + [pl.BlockSpec((2, 2, 1, KEPT, KEPT), lambda i, gy, gz: (0, 0, i, 0, 0))]
            + [rows(2)] * 2
            + [rows(1)] * 4
            + [pl.BlockSpec(table_z.shape, lambda i, gy, gz: (0, 0, 0, 0, 0))],
            out_specs=pl.BlockSpec((128, 1, 2, 8, 128), lambda i, gy, gz: (0, i, 0, 0, 0)),
            scratch_shapes=[pltpu.VMEM((2048, 128), jnp.float32)],
        ),
        out_shape=jax.ShapeDtypeStruct((128, 2, 2, 8, 128), jnp.float32),
        compiler_params=params(VMEM),
        cost_estimate=cost(512 * 512 * 768, 8 * MIB),
        name="second",
    )(gy, gz, part_a, *pieces_a, table_y, *pieces_b, table_z)


def third_kernel(slot_ref, in_ref, table_ref, ordering_ref, out_ref, held):
    out_ref[...] = jnp.zeros_like(out_ref)
    for parity in range(2):
        columns = jnp.concatenate(
            [in_ref[:, parity, half].reshape(1024, 128) for half in range(2)], axis=1
        )
        first, last = columns[:512], columns[512:]
        for odd, sides in enumerate((first + last, first - last)):
            sides = tuple(
                jnp.dot(
                    part, ordering_ref[...], preferred_element_type=jnp.float32
                ).astype(jnp.bfloat16)
                for part in halves(sides)
            )
            values = jnp.exp(product((table_ref[0, odd], table_ref[1, odd]), sides))
            for plane in range(2):
                for half in range(2):
                    held[parity, plane, half, odd * 128 : (odd + 1) * 128] = values[
                        plane * 128 : (plane + 1) * 128, half * 128 : (half + 1) * 128
                    ]

    def place_rows(group, carry):
        for offset in range(8):
            x = group * 8 + offset
            row = group * 4 + offset // 2 + 128 * (offset % 2)
            for parity in range(2):
                for half in range(2):
                    slot = slot_ref[x * 4 + parity * 2 + half]
                    for plane in range(2):
                        out_ref[pl.ds(slot * 2 + plane, 1), :] = held[
                            parity, plane, half, pl.ds(row, 1), :
                        ]
        return carry

    lax.fori_loop(0, KEPT // 8, place_rows, 0)


def third(slots, arrived, table_x, ordering):
    vmem = pl.BlockSpec(memory_space=pltpu.VMEM)
    return pl.pallas_call(
        third_kernel,
        in_specs=[pl.BlockSpec(memory_space=pltpu.SMEM)] + [vmem] * 3,
        out_specs=vmem,
        out_shape=jax.ShapeDtypeStruct((4096, 128), jnp.float32),
        scratch_shapes=[pltpu.VMEM((2, 2, 2, KEPT, 128), jnp.float32)],
        compiler_params=params(VMEM),
        cost_estimate=cost(768 * 512 * 512, 6 * MIB),
        name="third",
    )(slots, arrived, table_x, ordering)


def shifted(piece, axis, shift):
    size = lax.axis_size(axis)
    return lax.ppermute(piece, axis, [(i, (i + shift) % size) for i in range(size)])


def slots_of(block_owner):
    destination = block_owner[:, 0]
    one_hot = (destination[:, None] == jnp.arange(128, dtype=jnp.int32)[None, :]).astype(jnp.int32)
    earlier = jnp.cumsum(one_hot, axis=0) - one_hot
    return destination * CAP + jnp.sum(earlier * one_hot, axis=1)


def per_device(normals, spectrum, block_owner):
    table_x, table_y, table_z, ordering = (jnp.asarray(table) for table in tables())
    gy = lax.axis_index("gy").astype(jnp.int32).reshape(1)
    gz = lax.axis_index("gz").astype(jnp.int32).reshape(1)

    (a,) = scale(None, (0, 1, 2, 3), gz, normals, spectrum)
    a, place = lax.optimization_barrier((a, gy))
    a = lax.all_to_all(a, "gz", split_axis=0, concat_axis=0, tiled=True)
    c1, c3, c2 = scale(0, (1, 3, 2), place, normals, spectrum)
    place, c1, c3, c2 = lax.optimization_barrier((place, c1, c3, c2))
    c1, c3, c2 = shifted(c1, "gy", 1), shifted(c3, "gy", 3), shifted(c2, "gy", 2)
    d1, d3, d2 = scale(1, (1, 3, 2), place, normals, spectrum)
    place, d1, d3, d2 = lax.optimization_barrier((place, d1, d3, d2))
    d1, d3, d2 = shifted(d1, "gy", 1), shifted(d3, "gy", 3), shifted(d2, "gy", 2)
    (c0,) = scale(0, (0,), place, normals, spectrum)
    (d0,) = scale(1, (0,), place, normals, spectrum)

    c1, c3, c2, c0 = first_y(gy, gz, (c0, c1, c2, c3), table_y)
    a, slots, _, d0 = lax.optimization_barrier((a, slots_of(block_owner), c1, d0))
    c1, c3 = shifted(c1, "gz", 1), shifted(c3, "gz", 3)
    a2, a1, a3, a0 = first_z((2, 1, 3, 0), gy, a, table_z)
    d1, d2, d3, c1, c3, _ = lax.optimization_barrier((d1, d2, d3, c1, c3, a2))
    a1, a3, a2 = shifted(a1, "gy", 1), shifted(a3, "gy", 3), shifted(a2, "gy", 2)
    d1, d3, b2, b0 = first_y(gy, gz, (d0, d1, d2, d3), table_y, (c2, c0))
    d1, d3, b2 = shifted(d1, "gz", 1), shifted(d3, "gz", 3), shifted(b2, "gz", 2)

    part_a = part_y(gy, (a0, a2), table_y)
    part_a, b2 = lax.optimization_barrier((part_a, b2))
    b2, d1, d3 = lax.optimization_barrier((b2, d1, d3))
    part_a, a1, a3, d1, d3 = lax.optimization_barrier((part_a, a1, a3, d1, d3))
    planes = second(
        gy, gz, part_a, (a1, a3), table_y, (b0, b2, c1, c3, d1, d3), table_z
    )
    lines = lax.all_to_all(planes, ALL, split_axis=0, concat_axis=0, tiled=True)
    outgoing = third(slots, lines, table_x, ordering)
    return lax.all_to_all(
        outgoing.reshape(128, 1, CAP, 2, BW), ALL, split_axis=0, concat_axis=1, tiled=True
    )


def solution(mesh):
    placed = (P(None, "gx", "gy", "gz"), P("gx", "gy", "gz"), P(ALL, None))
    return jax.shard_map(
        per_device,
        mesh=mesh,
        in_specs=placed,
        out_specs=P(ALL, None, None, None, None),
        check_vma=False,
    )
```

```python
import functools

import jax
import jax.numpy as jnp
import ml_dtypes
import numpy as np
from jax import lax
from jax.experimental import pallas as pl
from jax.experimental.pallas import tpu as pltpu
from jax.sharding import PartitionSpec as P

N = 512
KEPT = 256
BW = 128
CAP = 16
ALL = ("gx", "gy", "gz")
MIB = 1 << 20
VMEM = 24


def split_table(table):
    high = table.astype(np.float32).astype(ml_dtypes.bfloat16)
    low = (table - high.astype(np.float64)).astype(np.float32).astype(ml_dtypes.bfloat16)
    return np.stack([high, low])


def cos_sin(positions, kept):
    angles = (positions[:, None] * kept[None, :] % N) * (2.0 * np.pi / N)
    return np.cos(angles), np.sin(angles)


@functools.cache
def tables():
    order = np.arange(KEPT).reshape(KEPT // 2, 2).T.reshape(-1)
    cosine, sine = cos_sin(np.arange(N // 2), order)
    cosine, sine = (t.reshape(2, 128, 2, 128).transpose(0, 2, 1, 3) for t in (cosine, sine))
    real_rows = np.concatenate([cosine, -sine], 3)
    imag_rows = np.concatenate([sine, cosine], 3)
    table_z = np.concatenate([real_rows, imag_rows], 2)
    cosine, sine = cos_sin(np.arange(N // 2), order)
    cosine, sine = (t.T.reshape(2, 128, 2, 128).transpose(2, 0, 1, 3) for t in (cosine, sine))
    top = np.concatenate([cosine, sine], 3)
    bottom = np.concatenate([-sine, cosine], 3)
    table_y = np.concatenate([top, bottom], 2)
    gx, gy, gz = np.meshgrid(np.arange(8), np.arange(4), np.arange(4), indexing="ij")
    first = 64 * gx + 8 * gz + 2 * gy
    second = 64 * gx + 32 + 8 * gy + gz
    cells = np.stack([first, first + 1, second, second + 4], -1).reshape(128, 4)
    cosine, sine = cos_sin(cells[:64].reshape(-1), order)
    cosine, sine = (
        t.T.reshape(2, KEPT // 2, 64, 1, 4) for t in (cosine, sine)
    )
    top = np.concatenate([cosine, sine], 3).reshape(2, KEPT // 2, 512)
    bottom = np.concatenate([-sine, cosine], 3).reshape(2, KEPT // 2, 512)
    table_x = np.concatenate([top, bottom], 1)
    ordering = np.zeros((KEPT, KEPT), ml_dtypes.bfloat16)
    ordering[np.arange(KEPT), order] = 1
    return split_table(table_x), split_table(table_y), split_table(table_z), ordering


def halves(values):
    high = values.astype(jnp.bfloat16)
    low = (values - high.astype(jnp.float32)).astype(jnp.bfloat16)
    return high, low


def product(left, right):
    def dot(a, b):
        return jnp.dot(a, b, preferred_element_type=jnp.float32)

    return dot(left[0], right[0]) + (dot(left[0], right[1]) + dot(left[1], right[0]))


def params(mib):
    return pltpu.CompilerParams(vmem_limit_bytes=mib * MIB)


def cost(multiplies, moved):
    return pl.CostEstimate(
        flops=multiplies >> 16, bytes_accessed=moved >> 16, transcendentals=0
    )


def rows_z(piece):
    return halves(jnp.concatenate([piece[plane].reshape(-1, 128) for plane in range(2)], axis=1))


def columns_y(piece):
    planes, cells = piece.shape[:2]
    return halves(
        jnp.concatenate([piece[:, x].reshape(256, piece.shape[3]) for x in range(cells)], axis=1)
    )


def in_hbm(*arrays):
    return [pltpu.with_memory_space_constraint(x, pltpu.HBM) for x in arrays]


def scale_kernel(part, shifts, place_ref, normals_ref, spectrum_ref, *refs):
    *out_refs, held_out, held_n, held_s, semaphores = refs
    half = held_n.shape[2] // 2
    steps = [(i, side, pl.ds(side * half, half)) for i in range(len(shifts)) for side in range(2)]

    def gets(i, side, cells):
        if part is None:
            source_n, source_s = normals_ref.at[:, i, cells], spectrum_ref.at[i, cells]
        else:
            chunk = 4 + lax.rem(place_ref[0] + shifts[i], 4)
            source_n = normals_ref.at[:, chunk, part, cells]
            source_s = spectrum_ref.at[chunk, part, cells]
        return (
            pltpu.make_async_copy(source_n, held_n.at[i, :, cells], semaphores.at[i, side, 0]),
            pltpu.make_async_copy(source_s, held_s.at[i, cells], semaphores.at[i, side, 1]),
        )

    def put(i, side, cells):
        target = out_refs[0].at[i, :, cells] if part is None else out_refs[i].at[:, cells]
        return pltpu.make_async_copy(
            held_out.at[i, :, cells], target, semaphores.at[i, side, 2]
        )

    for step in steps:
        for copy in gets(*step):
            copy.start()
    for step in steps:
        for copy in gets(*step):
            copy.wait()
        i, side, cells = step
        for plane in range(2):
            held_out[i, plane, cells] = (
                held_n[i, plane, cells].astype(jnp.float32) * held_s[i, cells]
            )
        put(*step).start()
    for step in steps:
        put(*step).wait()


def scale(part, shifts, place, normals, spectrum):
    count = len(shifts)
    chunk = (2, 8 if part is None else 4, 128, 128)
    shapes = [(count,) + chunk] if part is None else [chunk] * count
    view = (8, 8, 128, 128) if part is None else (8, 2, 4, 128, 128)
    hbm = pl.BlockSpec(memory_space=pltpu.HBM)
    return pl.pallas_call(
        functools.partial(scale_kernel, part, shifts),
        in_specs=[pl.BlockSpec(memory_space=pltpu.SMEM)] + [hbm] * 2,
        out_specs=[hbm] * len(shapes),
        out_shape=[pltpu.HBM(shape, jnp.float32) for shape in shapes],
        scratch_shapes=[
            pltpu.VMEM((count,) + chunk, jnp.float32),
            pltpu.VMEM((count,) + chunk, jnp.bfloat16),
            pltpu.VMEM((count,) + chunk[1:], jnp.float32),
            pltpu.SemaphoreType.DMA((count, 2, 3)),
        ],
        compiler_params=params(VMEM),
        cost_estimate=cost(count << 18, 2 * count * MIB),
        name="scale_a" if part is None else "scale_b",
    )(place, *in_hbm(normals.reshape((2,) + view), spectrum.reshape(view)))


def transform(along_z, pairs, table_ref):
    parts = []
    for odd in range(2):
        total = None
        for first, second, g in pairs:
            base = lax.rem(g, 2)
            table = (table_ref[0, base, odd], table_ref[1, base, odd])
            if odd:
                sides = (first - second) * jnp.where(g < 2, 1.0, -1.0).astype(jnp.float32)
            else:
                sides = first + second
            if along_z:
                term = product(rows_z(sides), table)
            else:
                term = product(table, columns_y(sides))
            total = term if total is None else total + term
        parts.append(total)
    return parts


def first_z_kernel(shifts, to_ref, in_ref, table_ref, *refs):
    *out_refs, pieces, held_out, semaphores = refs

    def get(i):
        cells = pl.ds(2 * lax.rem(to_ref[0] + shifts[i], 4), 2)
        return pltpu.make_async_copy(in_ref.at[:, :, cells], pieces.at[i], semaphores.at[i, 0])

    def put(i):
        return pltpu.make_async_copy(held_out.at[i], out_refs[i], semaphores.at[i, 1])

    steps = range(len(shifts))
    for i in steps:
        get(i).start()
    for i in steps:
        get(i).wait()
        pairs = [(pieces[i, 0], pieces[i, 2], 0), (pieces[i, 1], pieces[i, 3], 1)]
        for odd, values in enumerate(transform(True, pairs, table_ref)):
            half = slice(odd * 128, (odd + 1) * 128)
            for plane in range(2):
                part = slice(plane * 128, (plane + 1) * 128)
                for x in range(2):
                    held_out[i, plane, x, :, half] = values[x * 128 : (x + 1) * 128, part]
        put(i).start()
    for i in steps:
        put(i).wait()


def first_z(shifts, to, arrived, table):
    shape = (2, 2, 128, KEPT)
    hbm = pl.BlockSpec(memory_space=pltpu.HBM)
    count = len(shifts)
    return pl.pallas_call(
        functools.partial(first_z_kernel, shifts),
        in_specs=[
            pl.BlockSpec(memory_space=pltpu.SMEM),
            hbm,
            pl.BlockSpec(memory_space=pltpu.VMEM),
        ],
        out_specs=[hbm] * count,
        out_shape=[pltpu.HBM(shape, jnp.float32)] * count,
        scratch_shapes=[
            pltpu.VMEM((count, 4, 2, 2, 128, 128), jnp.float32),
            pltpu.VMEM((count,) + shape, jnp.float32),
            pltpu.SemaphoreType.DMA((count, 2)),
        ],
        compiler_params=params(VMEM),
        cost_estimate=cost(count * 256 * 512 * 512, 2 * count * MIB),
        name="first_z",
    )(to, *in_hbm(arrived), table)


def first_y_kernel(merge, place_ref, to_ref, *refs):
    in_refs, refs = refs[:4], refs[6 if merge else 4 :]
    table_ref, *out_refs, pieces, held_out, semaphores = refs

    def gets(i):
        x = pl.ds(lax.rem(to_ref[0] + (1, 3, 2, 0)[i], 4), 1)
        return [
            pltpu.make_async_copy(ref.at[:, x], pieces.at[i, s], semaphores.at[i, s])
            for s, ref in enumerate(in_refs)
        ]

    def put(i):
        target = out_refs[i].at[:, 1:2] if merge and i >= 2 else out_refs[i].at[:, 0:1]
        return pltpu.make_async_copy(held_out.at[i], target, semaphores.at[i, 4])

    for i in range(4):
        for copy in gets(i):
            copy.start()
    g, h = place_ref[0], lax.rem(place_ref[0] + 3, 4)
    for group in ((0, 1), (2, 3)):
        for i in group:
            for copy in gets(i):
                copy.wait()
        p0, p1, p2, p3 = (
            jnp.concatenate([pieces[i, s] for i in group], axis=1) for s in range(4)
        )
        for odd, values in enumerate(transform(False, [(p0, p2, g), (p1, p3, h)], table_ref)):
            for plane in range(2):
                for x, i in enumerate(group):
                    held_out[i, plane, 0, odd * 128 : (odd + 1) * 128] = values[
                        plane * 128 : (plane + 1) * 128, x * 128 : (x + 1) * 128
                    ]
        for i in group:
            put(i).start()
    for i in range(4):
        put(i).wait()


def first_y(place, to, pieces, table, before=()):
    merge = bool(before)
    shape, whole = (2, 1, KEPT, 128), (2, 2, KEPT, 128)
    hbm = pl.BlockSpec(memory_space=pltpu.HBM)
    operands = in_hbm(*pieces, *before)
    return pl.pallas_call(
        functools.partial(first_y_kernel, merge),
        in_specs=[pl.BlockSpec(memory_space=pltpu.SMEM)] * 2
        + [hbm] * len(operands)
        + [pl.BlockSpec(memory_space=pltpu.VMEM)],
        out_specs=[hbm] * 4,
        out_shape=[pltpu.HBM(shape, jnp.float32)] * 2 + [pltpu.HBM(whole, jnp.float32)] * 2,
        scratch_shapes=[
            pltpu.VMEM((4, 4, 2, 1, 128, 128), jnp.float32),
            pltpu.VMEM((4,) + shape, jnp.float32),
            pltpu.SemaphoreType.DMA((4, 5)),
        ],
        input_output_aliases={6: 2, 7: 3} if merge else {},
        compiler_params=params(VMEM),
        cost_estimate=cost(512 * 512 * 512, 4 * MIB),
        name="first_y",
    )(place, to, *operands, table)


def part_y_kernel(place_ref, p0, p2, table_ref, out_ref):
    pairs = [(p0[...], p2[...], place_ref[0])]
    for odd, values in enumerate(transform(False, pairs, table_ref)):
        out_ref[odd] = values


def part_y(place, pieces, table):
    return pl.pallas_call(
        part_y_kernel,
        grid_spec=pltpu.PrefetchScalarGridSpec(
            num_scalar_prefetch=1,
            grid=(2,),
            in_specs=[pl.BlockSpec((2, 1, 128, KEPT), lambda i, place: (0, i, 0, 0))] * 2
            + [pl.BlockSpec(table.shape, lambda i, place: (0, 0, 0, 0, 0))],
            out_specs=pl.BlockSpec((2, KEPT, KEPT), lambda i, place: (0, 0, i)),
        ),
        out_shape=jax.ShapeDtypeStruct((2, KEPT, 512), jnp.float32),
        compiler_params=params(VMEM),
        cost_estimate=cost(512 * 512 * 256, 4 * MIB),
        name="part_y",
    )(place, *pieces, table)


def second_kernel(
    y_ref,
    z_ref,
    part_a,
    a1,
    a3,
    table_y_ref,
    b0,
    b2,
    c1,
    c3,
    d1,
    d3,
    table_z_ref,
    out_ref,
    held,
):
    odd = pl.program_id(0)

    def put(values, half, row):
        held[pl.ds(half * 8 + row, 128, stride=16), :] = values

    g = lax.rem(y_ref[0] + 3, 4)
    base = lax.rem(g, 2)
    flip = jnp.where(odd == 0, 1.0, -1.0).astype(jnp.float32)
    sign = jnp.where((odd == 0) | (g < 2), 1.0, -1.0).astype(jnp.float32)
    table = (table_y_ref[0, base, 0], table_y_ref[1, base, 0])
    values = part_a[0] + product(table, columns_y((a1[...] + flip * a3[...]) * sign))
    for plane in range(2):
        for x in range(2):
            for half in range(2):
                start = x * KEPT + half * 128
                put(
                    values[plane * 128 : (plane + 1) * 128, start : start + 128],
                    half,
                    plane * 4 + x,
                )
    near, far = (
        jnp.concatenate([c[...], d[...]], axis=1) for c, d in ((c1, d1), (c3, d3))
    )
    pairs = [(b0[...], b2[...], z_ref[0]), (near, far, lax.rem(z_ref[0] + 3, 4))]
    for half, values in enumerate(transform(True, pairs, table_z_ref)):
        for x in range(2):
            for plane in range(2):
                put(
                    values[x * 128 : (x + 1) * 128, plane * 128 : (plane + 1) * 128],
                    half,
                    plane * 4 + 2 + x,
                )
    out_ref[...] = held[...].reshape(128, 1, 2, 8, 128)


def second(gy, gz, part_a, pieces_a, table_y, pieces_b, table_z):
    def rows(cells):
        return pl.BlockSpec((2, cells, 128, 128), lambda i, gy, gz: (0, 0, i, 0))

    return pl.pallas_call(
        second_kernel,
        grid_spec=pltpu.PrefetchScalarGridSpec(
            num_scalar_prefetch=2,
            grid=(2,),
            in_specs=[pl.BlockSpec((1, KEPT, 512), lambda i, gy, gz: (i, 0, 0))]
            + [pl.BlockSpec((2, 2, 128, KEPT), lambda i, gy, gz: (0, 0, 0, 0))] * 2
            + [pl.BlockSpec((2, 2, 1, KEPT, KEPT), lambda i, gy, gz: (0, 0, i, 0, 0))]
            + [rows(2)] * 2
            + [rows(1)] * 4
            + [pl.BlockSpec(table_z.shape, lambda i, gy, gz: (0, 0, 0, 0, 0))],
            out_specs=pl.BlockSpec((128, 1, 2, 8, 128), lambda i, gy, gz: (0, i, 0, 0, 0)),
            scratch_shapes=[pltpu.VMEM((2048, 128), jnp.float32)],
        ),
        out_shape=jax.ShapeDtypeStruct((128, 2, 2, 8, 128), jnp.float32),
        compiler_params=params(VMEM),
        cost_estimate=cost(512 * 512 * 768, 8 * MIB),
        name="second",
    )(gy, gz, part_a, *pieces_a, table_y, *pieces_b, table_z)


def third_kernel(slot_ref, in_ref, table_ref, ordering_ref, out_ref, held):
    out_ref[...] = jnp.zeros_like(out_ref)
    for parity in range(2):
        columns = jnp.concatenate(
            [in_ref[:, parity, half].reshape(1024, 128) for half in range(2)], axis=1
        )
        first, last = columns[:512], columns[512:]
        for odd, sides in enumerate((first + last, first - last)):
            sides = tuple(
                jnp.dot(
                    part, ordering_ref[...], preferred_element_type=jnp.float32
                ).astype(jnp.bfloat16)
                for part in halves(sides)
            )
            values = jnp.exp(product((table_ref[0, odd], table_ref[1, odd]), sides))
            for plane in range(2):
                for half in range(2):
                    held[parity, plane, half, odd * 128 : (odd + 1) * 128] = values[
                        plane * 128 : (plane + 1) * 128, half * 128 : (half + 1) * 128
                    ]

    def place_rows(group, carry):
        for offset in range(8):
            x = group * 8 + offset
            row = group * 4 + offset // 2 + 128 * (offset % 2)
            for parity in range(2):
                for half in range(2):
                    slot = slot_ref[x * 4 + parity * 2 + half]
                    for plane in range(2):
                        out_ref[pl.ds(slot * 2 + plane, 1), :] = held[
                            parity, plane, half, pl.ds(row, 1), :
                        ]
        return carry

    lax.fori_loop(0, KEPT // 8, place_rows, 0)


def third(slots, arrived, table_x, ordering):
    vmem = pl.BlockSpec(memory_space=pltpu.VMEM)
    return pl.pallas_call(
        third_kernel,
        in_specs=[pl.BlockSpec(memory_space=pltpu.SMEM)] + [vmem] * 3,
        out_specs=vmem,
        out_shape=jax.ShapeDtypeStruct((4096, 128), jnp.float32),
        scratch_shapes=[pltpu.VMEM((2, 2, 2, KEPT, 128), jnp.float32)],
        compiler_params=params(VMEM),
        cost_estimate=cost(768 * 512 * 512, 6 * MIB),
        name="third",
    )(slots, arrived, table_x, ordering)


def shifted(piece, axis, shift):
    size = lax.axis_size(axis)
    return lax.ppermute(piece, axis, [(i, (i + shift) % size) for i in range(size)])


def slots_of(block_owner):
    destination = block_owner[:, 0]
    one_hot = (destination[:, None] == jnp.arange(128, dtype=jnp.int32)[None, :]).astype(jnp.int32)
    earlier = jnp.cumsum(one_hot, axis=0) - one_hot
    return destination * CAP + jnp.sum(earlier * one_hot, axis=1)


def per_device(normals, spectrum, block_owner):
    table_x, table_y, table_z, ordering = (jnp.asarray(table) for table in tables())
    gy = lax.axis_index("gy").astype(jnp.int32).reshape(1)
    gz = lax.axis_index("gz").astype(jnp.int32).reshape(1)

    (a,) = scale(None, (0, 1, 2, 3), gz, normals, spectrum)
    a, place = lax.optimization_barrier((a, gy))
    a = lax.all_to_all(a, "gz", split_axis=0, concat_axis=0, tiled=True)
    c1, c3, c2 = scale(0, (1, 3, 2), place, normals, spectrum)
    place, c1, c3, c2 = lax.optimization_barrier((place, c1, c3, c2))
    c1, c3, c2 = shifted(c1, "gy", 1), shifted(c3, "gy", 3), shifted(c2, "gy", 2)
    d1, d3, d2 = scale(1, (1, 3, 2), place, normals, spectrum)
    place, d1, d3, d2 = lax.optimization_barrier((place, d1, d3, d2))
    d1, d3, d2 = shifted(d1, "gy", 1), shifted(d3, "gy", 3), shifted(d2, "gy", 2)
    (c0,) = scale(0, (0,), place, normals, spectrum)
    (d0,) = scale(1, (0,), place, normals, spectrum)

    c1, c3, c2, c0 = first_y(gy, gz, (c0, c1, c2, c3), table_y)
    a, slots, _, d0 = lax.optimization_barrier((a, slots_of(block_owner), c1, d0))
    c1, c3 = shifted(c1, "gz", 1), shifted(c3, "gz", 3)
    a2, a1, a3, a0 = first_z((2, 1, 3, 0), gy, a, table_z)
    d1, d2, d3, c1, c3, _ = lax.optimization_barrier((d1, d2, d3, c1, c3, a2))
    a1, a3, a2 = shifted(a1, "gy", 1), shifted(a3, "gy", 3), shifted(a2, "gy", 2)
    d1, d3, b2, b0 = first_y(gy, gz, (d0, d1, d2, d3), table_y, (c2, c0))
    d1, d3, b2 = shifted(d1, "gz", 1), shifted(d3, "gz", 3), shifted(b2, "gz", 2)

    part_a = part_y(gy, (a0, a2), table_y)
    part_a, b2 = lax.optimization_barrier((part_a, b2))
    b2, d1, d3 = lax.optimization_barrier((b2, d1, d3))
    part_a, a1, a3, d1, d3 = lax.optimization_barrier((part_a, a1, a3, d1, d3))
    planes = second(
        gy, gz, part_a, (a1, a3), table_y, (b0, b2, c1, c3, d1, d3), table_z
    )
    lines = lax.all_to_all(planes, ALL, split_axis=0, concat_axis=0, tiled=True)
    outgoing = third(slots, lines, table_x, ordering)
    return lax.all_to_all(
        outgoing.reshape(128, 1, CAP, 2, BW), ALL, split_axis=0, concat_axis=1, tiled=True
    )


def solution(mesh):
    placed = (P(None, "gx", "gy", "gz"), P("gx", "gy", "gz"), P(ALL, None))
    return jax.shard_map(
        per_device,
        mesh=mesh,
        in_specs=placed,
        out_specs=P(ALL, None, None, None, None),
        check_vma=False,
    )
```

```python
import functools

import jax
import jax.numpy as jnp
import ml_dtypes
import numpy as np
from jax import lax
from jax.experimental import pallas as pl
from jax.experimental.pallas import tpu as pltpu
from jax.sharding import PartitionSpec as P

N = 512
KEPT = 256
BW = 128
CAP = 16
ALL = ("gx", "gy", "gz")
MIB = 1 << 20
VMEM = 24


def split_table(table):
    high = table.astype(np.float32).astype(ml_dtypes.bfloat16)
    low = (table - high.astype(np.float64)).astype(np.float32).astype(ml_dtypes.bfloat16)
    return np.stack([high, low])


def cos_sin(positions, kept):
    angles = (positions[:, None] * kept[None, :] % N) * (2.0 * np.pi / N)
    return np.cos(angles), np.sin(angles)


@functools.cache
def tables():
    order = np.arange(KEPT).reshape(KEPT // 2, 2).T.reshape(-1)
    cosine, sine = cos_sin(np.arange(N // 2), order)
    cosine, sine = (t.reshape(2, 128, 2, 128).transpose(0, 2, 1, 3) for t in (cosine, sine))
    real_rows = np.concatenate([cosine, -sine], 3)
    imag_rows = np.concatenate([sine, cosine], 3)
    table_z = np.concatenate([real_rows, imag_rows], 2)
    cosine, sine = cos_sin(np.arange(N // 2), order)
    cosine, sine = (t.T.reshape(2, 128, 2, 128).transpose(2, 0, 1, 3) for t in (cosine, sine))
    top = np.concatenate([cosine, sine], 3)
    bottom = np.concatenate([-sine, cosine], 3)
    table_y = np.concatenate([top, bottom], 2)
    gx, gy, gz = np.meshgrid(np.arange(8), np.arange(4), np.arange(4), indexing="ij")
    first = 64 * gx + 8 * gz + 2 * gy
    second = 64 * gx + 32 + 8 * gy + gz
    cells = np.stack([first, first + 1, second, second + 4], -1).reshape(128, 4)
    cosine, sine = cos_sin(cells[:64].reshape(-1), order)
    cosine, sine = (
        t.T.reshape(2, KEPT // 2, 64, 1, 4) for t in (cosine, sine)
    )
    top = np.concatenate([cosine, sine], 3).reshape(2, KEPT // 2, 512)
    bottom = np.concatenate([-sine, cosine], 3).reshape(2, KEPT // 2, 512)
    table_x = np.concatenate([top, bottom], 1)
    ordering = np.zeros((KEPT, KEPT), ml_dtypes.bfloat16)
    ordering[np.arange(KEPT), order] = 1
    return split_table(table_x), split_table(table_y), split_table(table_z), ordering


def halves(values):
    high = values.astype(jnp.bfloat16)
    low = (values - high.astype(jnp.float32)).astype(jnp.bfloat16)
    return high, low


def product(left, right):
    def dot(a, b):
        return jnp.dot(a, b, preferred_element_type=jnp.float32)

    return dot(left[0], right[0]) + (dot(left[0], right[1]) + dot(left[1], right[0]))


def params(mib):
    return pltpu.CompilerParams(vmem_limit_bytes=mib * MIB)


def cost(multiplies, moved):
    return pl.CostEstimate(
        flops=multiplies >> 16, bytes_accessed=moved >> 16, transcendentals=0
    )


def rows_z(piece):
    return halves(jnp.concatenate([piece[plane].reshape(-1, 128) for plane in range(2)], axis=1))


def columns_y(piece):
    planes, cells = piece.shape[:2]
    return halves(
        jnp.concatenate([piece[:, x].reshape(256, piece.shape[3]) for x in range(cells)], axis=1)
    )


def in_hbm(*arrays):
    return [pltpu.with_memory_space_constraint(x, pltpu.HBM) for x in arrays]


def scale_kernel(part, shifts, place_ref, normals_ref, spectrum_ref, *refs):
    *out_refs, held_out, held_n, held_s, semaphores = refs

    def gets(i):
        if part is None:
            source_n, source_s = normals_ref.at[:, i], spectrum_ref.at[i]
        else:
            chunk = 4 + lax.rem(place_ref[0] + shifts[i], 4)
            source_n, source_s = normals_ref.at[:, chunk, part], spectrum_ref.at[chunk, part]
        return (
            pltpu.make_async_copy(source_n, held_n.at[i], semaphores.at[i, 0]),
            pltpu.make_async_copy(source_s, held_s.at[i], semaphores.at[i, 1]),
        )

    def put(i):
        target = out_refs[0].at[i] if part is None else out_refs[i]
        return pltpu.make_async_copy(held_out.at[i], target, semaphores.at[i, 2])

    steps = range(len(shifts))
    for i in steps:
        for copy in gets(i):
            copy.start()
    for i in steps:
        for copy in gets(i):
            copy.wait()
        for plane in range(2):
            held_out[i, plane] = held_n[i, plane].astype(jnp.float32) * held_s[i]
        put(i).start()
    for i in steps:
        put(i).wait()


def scale(part, shifts, place, normals, spectrum):
    count = len(shifts)
    chunk = (2, 8 if part is None else 4, 128, 128)
    shapes = [(count,) + chunk] if part is None else [chunk] * count
    view = (8, 8, 128, 128) if part is None else (8, 2, 4, 128, 128)
    hbm = pl.BlockSpec(memory_space=pltpu.HBM)
    return pl.pallas_call(
        functools.partial(scale_kernel, part, shifts),
        in_specs=[pl.BlockSpec(memory_space=pltpu.SMEM)] + [hbm] * 2,
        out_specs=[hbm] * len(shapes),
        out_shape=[pltpu.HBM(shape, jnp.float32) for shape in shapes],
        scratch_shapes=[
            pltpu.VMEM((count,) + chunk, jnp.float32),
            pltpu.VMEM((count,) + chunk, jnp.bfloat16),
            pltpu.VMEM((count,) + chunk[1:], jnp.float32),
            pltpu.SemaphoreType.DMA((count, 3)),
        ],
        compiler_params=params(VMEM),
        cost_estimate=cost(count << 18, 2 * count * MIB),
        name="scale_a" if part is None else "scale_b",
    )(place, *in_hbm(normals.reshape((2,) + view), spectrum.reshape(view)))


def transform(along_z, pairs, table_ref):
    parts = []
    for odd in range(2):
        total = None
        for first, second, g in pairs:
            base = lax.rem(g, 2)
            table = (table_ref[0, base, odd], table_ref[1, base, odd])
            if odd:
                sides = (first - second) * jnp.where(g < 2, 1.0, -1.0).astype(jnp.float32)
            else:
                sides = first + second
            if along_z:
                term = product(rows_z(sides), table)
            else:
                term = product(table, columns_y(sides))
            total = term if total is None else total + term
        parts.append(total)
    return parts


def first_z_kernel(shifts, to_ref, in_ref, table_ref, *refs):
    *out_refs, pieces, held_out, semaphores = refs

    def get(i):
        cells = pl.ds(2 * lax.rem(to_ref[0] + shifts[i], 4), 2)
        return pltpu.make_async_copy(in_ref.at[:, :, cells], pieces.at[i], semaphores.at[i, 0])

    def put(i):
        return pltpu.make_async_copy(held_out.at[i], out_refs[i], semaphores.at[i, 1])

    steps = range(len(shifts))
    for i in steps:
        get(i).start()
    for i in steps:
        get(i).wait()
        pairs = [(pieces[i, 0], pieces[i, 2], 0), (pieces[i, 1], pieces[i, 3], 1)]
        for odd, values in enumerate(transform(True, pairs, table_ref)):
            half = slice(odd * 128, (odd + 1) * 128)
            for plane in range(2):
                part = slice(plane * 128, (plane + 1) * 128)
                for x in range(2):
                    held_out[i, plane, x, :, half] = values[x * 128 : (x + 1) * 128, part]
        put(i).start()
    for i in steps:
        put(i).wait()


def first_z(shifts, to, arrived, table):
    shape = (2, 2, 128, KEPT)
    hbm = pl.BlockSpec(memory_space=pltpu.HBM)
    count = len(shifts)
    return pl.pallas_call(
        functools.partial(first_z_kernel, shifts),
        in_specs=[
            pl.BlockSpec(memory_space=pltpu.SMEM),
            hbm,
            pl.BlockSpec(memory_space=pltpu.VMEM),
        ],
        out_specs=[hbm] * count,
        out_shape=[pltpu.HBM(shape, jnp.float32)] * count,
        scratch_shapes=[
            pltpu.VMEM((count, 4, 2, 2, 128, 128), jnp.float32),
            pltpu.VMEM((count,) + shape, jnp.float32),
            pltpu.SemaphoreType.DMA((count, 2)),
        ],
        compiler_params=params(VMEM),
        cost_estimate=cost(count * 256 * 512 * 512, 2 * count * MIB),
        name="first_z",
    )(to, *in_hbm(arrived), table)


def first_y_kernel(merge, place_ref, to_ref, *refs):
    in_refs, refs = refs[:4], refs[6 if merge else 4 :]
    table_ref, *out_refs, pieces, held_out, semaphores = refs

    def gets(i):
        x = pl.ds(lax.rem(to_ref[0] + (1, 3, 2, 0)[i], 4), 1)
        return [
            pltpu.make_async_copy(ref.at[:, x], pieces.at[i, s], semaphores.at[i, s])
            for s, ref in enumerate(in_refs)
        ]

    def put(i):
        target = out_refs[i].at[:, 1:2] if merge and i >= 2 else out_refs[i].at[:, 0:1]
        return pltpu.make_async_copy(held_out.at[i], target, semaphores.at[i, 4])

    for i in range(4):
        for copy in gets(i):
            copy.start()
    g, h = place_ref[0], lax.rem(place_ref[0] + 3, 4)
    for group in ((0, 1), (2, 3)):
        for i in group:
            for copy in gets(i):
                copy.wait()
        p0, p1, p2, p3 = (
            jnp.concatenate([pieces[i, s] for i in group], axis=1) for s in range(4)
        )
        for odd, values in enumerate(transform(False, [(p0, p2, g), (p1, p3, h)], table_ref)):
            for plane in range(2):
                for x, i in enumerate(group):
                    held_out[i, plane, 0, odd * 128 : (odd + 1) * 128] = values[
                        plane * 128 : (plane + 1) * 128, x * 128 : (x + 1) * 128
                    ]
        for i in group:
            put(i).start()
    for i in range(4):
        put(i).wait()


def first_y(place, to, pieces, table, before=()):
    merge = bool(before)
    shape, whole = (2, 1, KEPT, 128), (2, 2, KEPT, 128)
    hbm = pl.BlockSpec(memory_space=pltpu.HBM)
    operands = in_hbm(*pieces, *before)
    return pl.pallas_call(
        functools.partial(first_y_kernel, merge),
        in_specs=[pl.BlockSpec(memory_space=pltpu.SMEM)] * 2
        + [hbm] * len(operands)
        + [pl.BlockSpec(memory_space=pltpu.VMEM)],
        out_specs=[hbm] * 4,
        out_shape=[pltpu.HBM(shape, jnp.float32)] * 2 + [pltpu.HBM(whole, jnp.float32)] * 2,
        scratch_shapes=[
            pltpu.VMEM((4, 4, 2, 1, 128, 128), jnp.float32),
            pltpu.VMEM((4,) + shape, jnp.float32),
            pltpu.SemaphoreType.DMA((4, 5)),
        ],
        input_output_aliases={6: 2, 7: 3} if merge else {},
        compiler_params=params(VMEM),
        cost_estimate=cost(512 * 512 * 512, 4 * MIB),
        name="first_y",
    )(place, to, *operands, table)


def part_y_kernel(place_ref, p0, p2, table_ref, out_ref):
    pairs = [(p0[...], p2[...], place_ref[0])]
    for odd, values in enumerate(transform(False, pairs, table_ref)):
        out_ref[odd] = values


def part_y(place, pieces, table):
    return pl.pallas_call(
        part_y_kernel,
        grid_spec=pltpu.PrefetchScalarGridSpec(
            num_scalar_prefetch=1,
            grid=(2,),
            in_specs=[pl.BlockSpec((2, 1, 128, KEPT), lambda i, place: (0, i, 0, 0))] * 2
            + [pl.BlockSpec(table.shape, lambda i, place: (0, 0, 0, 0, 0))],
            out_specs=pl.BlockSpec((2, KEPT, KEPT), lambda i, place: (0, 0, i)),
        ),
        out_shape=jax.ShapeDtypeStruct((2, KEPT, 512), jnp.float32),
        compiler_params=params(VMEM),
        cost_estimate=cost(512 * 512 * 256, 4 * MIB),
        name="part_y",
    )(place, *pieces, table)


def sum_y_kernel(place_ref, part_ref, p1, p3, table_ref, out_ref):
    odd = pl.program_id(0)
    g = lax.rem(place_ref[0] + 3, 4)
    base = lax.rem(g, 2)
    flip = jnp.where(odd == 0, 1.0, -1.0).astype(jnp.float32)
    sign = jnp.where((odd == 0) | (g < 2), 1.0, -1.0).astype(jnp.float32)
    table = (table_ref[0, base, 0], table_ref[1, base, 0])
    sides = (p1[...] + flip * p3[...]) * sign
    out_ref[0] = part_ref[0] + product(table, columns_y(sides))


def sum_y(place, part, pieces, table):
    block = pl.BlockSpec((1, KEPT, 512), lambda i, place: (i, 0, 0))
    return pl.pallas_call(
        sum_y_kernel,
        grid_spec=pltpu.PrefetchScalarGridSpec(
            num_scalar_prefetch=1,
            grid=(2,),
            in_specs=[block]
            + [pl.BlockSpec((2, 2, 128, KEPT), lambda i, place: (0, 0, 0, 0))] * 2
            + [pl.BlockSpec((2, 2, 1, KEPT, KEPT), lambda i, place: (0, 0, i, 0, 0))],
            out_specs=block,
        ),
        out_shape=jax.ShapeDtypeStruct((2, KEPT, 512), jnp.float32),
        compiler_params=params(VMEM),
        cost_estimate=cost(512 * 512 * 256, 4 * MIB),
        name="sum_y",
    )(place, part, *pieces, table)


def second_kernel(place_ref, done_a, b0, b2, c1, c3, d1, d3, table_ref, out_ref, held):
    def put(values, half, row):
        held[pl.ds(half * 8 + row, 128, stride=16), :] = values

    for plane in range(2):
        for x in range(2):
            for half in range(2):
                start = x * KEPT + half * 128
                put(
                    done_a[0, plane * 128 : (plane + 1) * 128, start : start + 128],
                    half,
                    plane * 4 + x,
                )
    near, far = (
        jnp.concatenate([c[...], d[...]], axis=1) for c, d in ((c1, d1), (c3, d3))
    )
    pairs = [(b0[...], b2[...], place_ref[0]), (near, far, lax.rem(place_ref[0] + 3, 4))]
    for half, values in enumerate(transform(True, pairs, table_ref)):
        for x in range(2):
            for plane in range(2):
                put(
                    values[x * 128 : (x + 1) * 128, plane * 128 : (plane + 1) * 128],
                    half,
                    plane * 4 + 2 + x,
                )
    out_ref[...] = held[...].reshape(128, 1, 2, 8, 128)


def second(place, done_a, pieces_b, table_z):
    def rows(cells):
        return pl.BlockSpec((2, cells, 128, 128), lambda i, place: (0, 0, i, 0))

    return pl.pallas_call(
        second_kernel,
        grid_spec=pltpu.PrefetchScalarGridSpec(
            num_scalar_prefetch=1,
            grid=(2,),
            in_specs=[pl.BlockSpec((1, KEPT, 512), lambda i, place: (i, 0, 0))]
            + [rows(2)] * 2
            + [rows(1)] * 4
            + [pl.BlockSpec(table_z.shape, lambda i, place: (0, 0, 0, 0, 0))],
            out_specs=pl.BlockSpec((128, 1, 2, 8, 128), lambda i, place: (0, i, 0, 0, 0)),
            scratch_shapes=[pltpu.VMEM((2048, 128), jnp.float32)],
        ),
        out_shape=jax.ShapeDtypeStruct((128, 2, 2, 8, 128), jnp.float32),
        compiler_params=params(VMEM),
        cost_estimate=cost(512 * 512 * 512, 8 * MIB),
        name="second",
    )(place, done_a, *pieces_b, table_z)


def third_kernel(slot_ref, in_ref, table_ref, ordering_ref, out_ref, held):
    out_ref[...] = jnp.zeros_like(out_ref)
    for parity in range(2):
        columns = jnp.concatenate(
            [in_ref[:, parity, half].reshape(1024, 128) for half in range(2)], axis=1
        )
        first, last = columns[:512], columns[512:]
        for odd, sides in enumerate((first + last, first - last)):
            sides = tuple(
                jnp.dot(
                    part, ordering_ref[...], preferred_element_type=jnp.float32
                ).astype(jnp.bfloat16)
                for part in halves(sides)
            )
            values = jnp.exp(product((table_ref[0, odd], table_ref[1, odd]), sides))
            for plane in range(2):
                for half in range(2):
                    held[parity, plane, half, odd * 128 : (odd + 1) * 128] = values[
                        plane * 128 : (plane + 1) * 128, half * 128 : (half + 1) * 128
                    ]

    def place_rows(group, carry):
        for offset in range(8):
            x = group * 8 + offset
            row = group * 4 + offset // 2 + 128 * (offset % 2)
            for parity in range(2):
                for half in range(2):
                    slot = slot_ref[x * 4 + parity * 2 + half]
                    for plane in range(2):
                        out_ref[pl.ds(slot * 2 + plane, 1), :] = held[
                            parity, plane, half, pl.ds(row, 1), :
                        ]
        return carry

    lax.fori_loop(0, KEPT // 8, place_rows, 0)


def third(slots, arrived, table_x, ordering):
    vmem = pl.BlockSpec(memory_space=pltpu.VMEM)
    return pl.pallas_call(
        third_kernel,
        in_specs=[pl.BlockSpec(memory_space=pltpu.SMEM)] + [vmem] * 3,
        out_specs=vmem,
        out_shape=jax.ShapeDtypeStruct((4096, 128), jnp.float32),
        scratch_shapes=[pltpu.VMEM((2, 2, 2, KEPT, 128), jnp.float32)],
        compiler_params=params(VMEM),
        cost_estimate=cost(768 * 512 * 512, 6 * MIB),
        name="third",
    )(slots, arrived, table_x, ordering)


def shifted(piece, axis, shift):
    size = lax.axis_size(axis)
    return lax.ppermute(piece, axis, [(i, (i + shift) % size) for i in range(size)])


def slots_of(block_owner):
    destination = block_owner[:, 0]
    one_hot = (destination[:, None] == jnp.arange(128, dtype=jnp.int32)[None, :]).astype(jnp.int32)
    earlier = jnp.cumsum(one_hot, axis=0) - one_hot
    return destination * CAP + jnp.sum(earlier * one_hot, axis=1)


def per_device(normals, spectrum, block_owner):
    table_x, table_y, table_z, ordering = (jnp.asarray(table) for table in tables())
    gy = lax.axis_index("gy").astype(jnp.int32).reshape(1)
    gz = lax.axis_index("gz").astype(jnp.int32).reshape(1)

    (a,) = scale(None, (0, 1, 2, 3), gz, normals, spectrum)
    a, place = lax.optimization_barrier((a, gy))
    a = lax.all_to_all(a, "gz", split_axis=0, concat_axis=0, tiled=True)
    c1, c3, c2 = scale(0, (1, 3, 2), place, normals, spectrum)
    place, c1, c3, c2 = lax.optimization_barrier((place, c1, c3, c2))
    c1, c3, c2 = shifted(c1, "gy", 1), shifted(c3, "gy", 3), shifted(c2, "gy", 2)
    d1, d3, d2 = scale(1, (1, 3, 2), place, normals, spectrum)
    place, d1, d3, d2 = lax.optimization_barrier((place, d1, d3, d2))
    d1, d3, d2 = shifted(d1, "gy", 1), shifted(d3, "gy", 3), shifted(d2, "gy", 2)
    (c0,) = scale(0, (0,), place, normals, spectrum)
    (d0,) = scale(1, (0,), place, normals, spectrum)

    c1, c3, c2, c0 = first_y(gy, gz, (c0, c1, c2, c3), table_y)
    a, slots, _, d0 = lax.optimization_barrier((a, slots_of(block_owner), c1, d0))
    c1, c3 = shifted(c1, "gz", 1), shifted(c3, "gz", 3)
    a2, a1, a3, a0 = first_z((2, 1, 3, 0), gy, a, table_z)
    d1, d2, d3, c1, c3, _ = lax.optimization_barrier((d1, d2, d3, c1, c3, a2))
    a1, a3, a2 = shifted(a1, "gy", 1), shifted(a3, "gy", 3), shifted(a2, "gy", 2)
    d1, d3, b2, b0 = first_y(gy, gz, (d0, d1, d2, d3), table_y, (c2, c0))
    d1, d3, b2 = shifted(d1, "gz", 1), shifted(d3, "gz", 3), shifted(b2, "gz", 2)

    part_a = part_y(gy, (a0, a2), table_y)
    part_a, b2 = lax.optimization_barrier((part_a, b2))
    done_a = sum_y(gy, part_a, (a1, a3), table_y)
    done_a, b2, d1, d3 = lax.optimization_barrier((done_a, b2, d1, d3))
    planes = second(gz, done_a, (b0, b2, c1, c3, d1, d3), table_z)
    lines = lax.all_to_all(planes, ALL, split_axis=0, concat_axis=0, tiled=True)
    outgoing = third(slots, lines, table_x, ordering)
    return lax.all_to_all(
        outgoing.reshape(128, 1, CAP, 2, BW), ALL, split_axis=0, concat_axis=1, tiled=True
    )


def solution(mesh):
    placed = (P(None, "gx", "gy", "gz"), P("gx", "gy", "gz"), P(ALL, None))
    return jax.shard_map(
        per_device,
        mesh=mesh,
        in_specs=placed,
        out_specs=P(ALL, None, None, None, None),
        check_vma=False,
    )
```

```python
import functools

import jax
import jax.numpy as jnp
import ml_dtypes
import numpy as np
from jax import lax
from jax.experimental import pallas as pl
from jax.experimental.pallas import tpu as pltpu
from jax.sharding import PartitionSpec as P

N = 512
KEPT = 256
BW = 128
CAP = 16
ALL = ("gx", "gy", "gz")
MIB = 1 << 20
VMEM = 24


def split_table(table):
    high = table.astype(np.float32).astype(ml_dtypes.bfloat16)
    low = (table - high.astype(np.float64)).astype(np.float32).astype(ml_dtypes.bfloat16)
    return np.stack([high, low])


def cos_sin(positions, kept):
    angles = (positions[:, None] * kept[None, :] % N) * (2.0 * np.pi / N)
    return np.cos(angles), np.sin(angles)


@functools.cache
def tables():
    order = np.arange(KEPT).reshape(KEPT // 2, 2).T.reshape(-1)
    cosine, sine = cos_sin(np.arange(N // 2), order)
    cosine, sine = (t.reshape(2, 128, 2, 128).transpose(0, 2, 1, 3) for t in (cosine, sine))
    real_rows = np.concatenate([cosine, -sine], 3)
    imag_rows = np.concatenate([sine, cosine], 3)
    table_z = np.concatenate([real_rows, imag_rows], 2)
    cosine, sine = cos_sin(np.arange(N // 2), order)
    cosine, sine = (t.T.reshape(2, 128, 2, 128).transpose(2, 0, 1, 3) for t in (cosine, sine))
    top = np.concatenate([cosine, sine], 3)
    bottom = np.concatenate([-sine, cosine], 3)
    table_y = np.concatenate([top, bottom], 2)
    gx, gy, gz = np.meshgrid(np.arange(8), np.arange(4), np.arange(4), indexing="ij")
    first = 64 * gx + 8 * gz + 2 * gy
    second = 64 * gx + 32 + 8 * gy + gz
    cells = np.stack([first, first + 1, second, second + 4], -1).reshape(128, 4)
    cosine, sine = cos_sin(cells[:64].reshape(-1), order)
    cosine, sine = (
        t.T.reshape(2, KEPT // 2, 64, 1, 4) for t in (cosine, sine)
    )
    top = np.concatenate([cosine, sine], 3).reshape(2, KEPT // 2, 512)
    bottom = np.concatenate([-sine, cosine], 3).reshape(2, KEPT // 2, 512)
    table_x = np.concatenate([top, bottom], 1)
    ordering = np.zeros((KEPT, KEPT), ml_dtypes.bfloat16)
    ordering[np.arange(KEPT), order] = 1
    return split_table(table_x), split_table(table_y), split_table(table_z), ordering


def halves(values):
    high = values.astype(jnp.bfloat16)
    low = (values - high.astype(jnp.float32)).astype(jnp.bfloat16)
    return high, low


def product(left, right):
    def dot(a, b):
        return jnp.dot(a, b, preferred_element_type=jnp.float32)

    return dot(left[0], right[0]) + (dot(left[0], right[1]) + dot(left[1], right[0]))


def params(mib):
    return pltpu.CompilerParams(vmem_limit_bytes=mib * MIB)


def cost(multiplies, moved):
    return pl.CostEstimate(
        flops=multiplies >> 16, bytes_accessed=moved >> 16, transcendentals=0
    )


def rows_z(piece):
    return halves(jnp.concatenate([piece[plane].reshape(-1, 128) for plane in range(2)], axis=1))


def columns_y(piece):
    planes, cells = piece.shape[:2]
    return halves(
        jnp.concatenate([piece[:, x].reshape(256, piece.shape[3]) for x in range(cells)], axis=1)
    )


def in_hbm(*arrays):
    return [pltpu.with_memory_space_constraint(x, pltpu.HBM) for x in arrays]


def scale_kernel(part, shifts, place_ref, normals_ref, spectrum_ref, *refs):
    *out_refs, held_out, held_n, held_s, semaphores = refs

    def gets(i):
        if part is None:
            source_n, source_s = normals_ref.at[:, i], spectrum_ref.at[i]
        else:
            chunk = 4 + lax.rem(place_ref[0] + shifts[i], 4)
            source_n, source_s = normals_ref.at[:, chunk, part], spectrum_ref.at[chunk, part]
        return (
            pltpu.make_async_copy(source_n, held_n.at[i], semaphores.at[i, 0]),
            pltpu.make_async_copy(source_s, held_s.at[i], semaphores.at[i, 1]),
        )

    def put(i):
        target = out_refs[0].at[i] if part is None else out_refs[i]
        return pltpu.make_async_copy(held_out.at[i], target, semaphores.at[i, 2])

    steps = range(len(shifts))
    for i in steps:
        for copy in gets(i):
            copy.start()
    for i in steps:
        for copy in gets(i):
            copy.wait()
        for plane in range(2):
            held_out[i, plane] = held_n[i, plane].astype(jnp.float32) * held_s[i]
        put(i).start()
    for i in steps:
        put(i).wait()


def scale(part, shifts, place, normals, spectrum):
    count = len(shifts)
    chunk = (2, 8 if part is None else 4, 128, 128)
    shapes = [(count,) + chunk] if part is None else [chunk] * count
    view = (8, 8, 128, 128) if part is None else (8, 2, 4, 128, 128)
    hbm = pl.BlockSpec(memory_space=pltpu.HBM)
    return pl.pallas_call(
        functools.partial(scale_kernel, part, shifts),
        in_specs=[pl.BlockSpec(memory_space=pltpu.SMEM)] + [hbm] * 2,
        out_specs=[hbm] * len(shapes),
        out_shape=[pltpu.HBM(shape, jnp.float32) for shape in shapes],
        scratch_shapes=[
            pltpu.VMEM((count,) + chunk, jnp.float32),
            pltpu.VMEM((count,) + chunk, jnp.bfloat16),
            pltpu.VMEM((count,) + chunk[1:], jnp.float32),
            pltpu.SemaphoreType.DMA((count, 3)),
        ],
        compiler_params=params(VMEM),
        cost_estimate=cost(count << 18, 2 * count * MIB),
        name="scale_a" if part is None else "scale_b",
    )(place, *in_hbm(normals.reshape((2,) + view), spectrum.reshape(view)))


def scale_first_kernel(normals_ref, spectrum_ref, out_ref, held_out, held_n, held_s, semaphores):
    def gets(i):
        chunks = pl.ds(2 * i, 2)
        return (
            pltpu.make_async_copy(normals_ref.at[:, chunks], held_n.at[i], semaphores.at[i, 0]),
            pltpu.make_async_copy(spectrum_ref.at[chunks], held_s.at[i], semaphores.at[i, 1]),
        )

    def put(i):
        chunks = pl.ds(2 * i, 2)
        return pltpu.make_async_copy(
            held_out.at[chunks], out_ref.at[chunks], semaphores.at[i, 2]
        )

    for i in range(2):
        for copy in gets(i):
            copy.start()
    for i in range(2):
        for copy in gets(i):
            copy.wait()
        for chunk in range(2):
            for plane in range(2):
                held_out[2 * i + chunk, plane] = (
                    held_n[i, plane, chunk].astype(jnp.float32) * held_s[i, chunk]
                )
        put(i).start()
    for i in range(2):
        put(i).wait()


def scale_first(normals, spectrum):
    shape = (4, 2, 8, 128, 128)
    view = (8, 8, 128, 128)
    hbm = pl.BlockSpec(memory_space=pltpu.HBM)
    return pl.pallas_call(
        scale_first_kernel,
        in_specs=[hbm] * 2,
        out_specs=hbm,
        out_shape=pltpu.HBM(shape, jnp.float32),
        scratch_shapes=[
            pltpu.VMEM(shape, jnp.float32),
            pltpu.VMEM((2, 2, 2, 8, 128, 128), jnp.bfloat16),
            pltpu.VMEM((2, 2, 8, 128, 128), jnp.float32),
            pltpu.SemaphoreType.DMA((2, 3)),
        ],
        compiler_params=params(VMEM),
        cost_estimate=cost(1 << 20, 8 * MIB),
        name="scale_a",
    )(*in_hbm(normals.reshape((2,) + view), spectrum.reshape(view)))


def transform(along_z, pairs, table_ref):
    parts = []
    for odd in range(2):
        total = None
        for first, second, g in pairs:
            base = lax.rem(g, 2)
            table = (table_ref[0, base, odd], table_ref[1, base, odd])
            if odd:
                sides = (first - second) * jnp.where(g < 2, 1.0, -1.0).astype(jnp.float32)
            else:
                sides = first + second
            if along_z:
                term = product(rows_z(sides), table)
            else:
                term = product(table, columns_y(sides))
            total = term if total is None else total + term
        parts.append(total)
    return parts


def first_z_kernel(shifts, to_ref, in_ref, table_ref, *refs):
    *out_refs, pieces, held_out, semaphores = refs

    def get(i):
        cells = pl.ds(2 * lax.rem(to_ref[0] + shifts[i], 4), 2)
        return pltpu.make_async_copy(in_ref.at[:, :, cells], pieces.at[i], semaphores.at[i, 0])

    def put(i):
        return pltpu.make_async_copy(held_out.at[i], out_refs[i], semaphores.at[i, 1])

    steps = range(len(shifts))
    for i in steps:
        get(i).start()
    for i in steps:
        get(i).wait()
        pairs = [(pieces[i, 0], pieces[i, 2], 0), (pieces[i, 1], pieces[i, 3], 1)]
        for odd, values in enumerate(transform(True, pairs, table_ref)):
            half = slice(odd * 128, (odd + 1) * 128)
            for plane in range(2):
                part = slice(plane * 128, (plane + 1) * 128)
                for x in range(2):
                    held_out[i, plane, x, :, half] = values[x * 128 : (x + 1) * 128, part]
        put(i).start()
    for i in steps:
        put(i).wait()


def first_z(shifts, to, arrived, table):
    shape = (2, 2, 128, KEPT)
    hbm = pl.BlockSpec(memory_space=pltpu.HBM)
    count = len(shifts)
    return pl.pallas_call(
        functools.partial(first_z_kernel, shifts),
        in_specs=[
            pl.BlockSpec(memory_space=pltpu.SMEM),
            hbm,
            pl.BlockSpec(memory_space=pltpu.VMEM),
        ],
        out_specs=[hbm] * count,
        out_shape=[pltpu.HBM(shape, jnp.float32)] * count,
        scratch_shapes=[
            pltpu.VMEM((count, 4, 2, 2, 128, 128), jnp.float32),
            pltpu.VMEM((count,) + shape, jnp.float32),
            pltpu.SemaphoreType.DMA((count, 2)),
        ],
        compiler_params=params(VMEM),
        cost_estimate=cost(count * 256 * 512 * 512, 2 * count * MIB),
        name="first_z",
    )(to, *in_hbm(arrived), table)


def first_y_kernel(merge, place_ref, to_ref, *refs):
    in_refs, refs = refs[:4], refs[6 if merge else 4 :]
    table_ref, *out_refs, pieces, held_out, semaphores = refs

    def gets(i):
        x = pl.ds(lax.rem(to_ref[0] + (1, 3, 2, 0)[i], 4), 1)
        return [
            pltpu.make_async_copy(ref.at[:, x], pieces.at[i, s], semaphores.at[i, s])
            for s, ref in enumerate(in_refs)
        ]

    def put(i):
        target = out_refs[i].at[:, 1:2] if merge and i >= 2 else out_refs[i].at[:, 0:1]
        return pltpu.make_async_copy(held_out.at[i], target, semaphores.at[i, 4])

    for i in range(4):
        for copy in gets(i):
            copy.start()
    g, h = place_ref[0], lax.rem(place_ref[0] + 3, 4)
    for group in ((0, 1), (2, 3)):
        for i in group:
            for copy in gets(i):
                copy.wait()
        p0, p1, p2, p3 = (
            jnp.concatenate([pieces[i, s] for i in group], axis=1) for s in range(4)
        )
        for odd, values in enumerate(transform(False, [(p0, p2, g), (p1, p3, h)], table_ref)):
            for plane in range(2):
                for x, i in enumerate(group):
                    held_out[i, plane, 0, odd * 128 : (odd + 1) * 128] = values[
                        plane * 128 : (plane + 1) * 128, x * 128 : (x + 1) * 128
                    ]
        for i in group:
            put(i).start()
    for i in range(4):
        put(i).wait()


def first_y(place, to, pieces, table, before=()):
    merge = bool(before)
    shape, whole = (2, 1, KEPT, 128), (2, 2, KEPT, 128)
    hbm = pl.BlockSpec(memory_space=pltpu.HBM)
    operands = in_hbm(*pieces, *before)
    return pl.pallas_call(
        functools.partial(first_y_kernel, merge),
        in_specs=[pl.BlockSpec(memory_space=pltpu.SMEM)] * 2
        + [hbm] * len(operands)
        + [pl.BlockSpec(memory_space=pltpu.VMEM)],
        out_specs=[hbm] * 4,
        out_shape=[pltpu.HBM(shape, jnp.float32)] * 2 + [pltpu.HBM(whole, jnp.float32)] * 2,
        scratch_shapes=[
            pltpu.VMEM((4, 4, 2, 1, 128, 128), jnp.float32),
            pltpu.VMEM((4,) + shape, jnp.float32),
            pltpu.SemaphoreType.DMA((4, 5)),
        ],
        input_output_aliases={6: 2, 7: 3} if merge else {},
        compiler_params=params(VMEM),
        cost_estimate=cost(512 * 512 * 512, 4 * MIB),
        name="first_y",
    )(place, to, *operands, table)


def part_y_kernel(place_ref, p0, p2, table_ref, out_ref):
    pairs = [(p0[...], p2[...], place_ref[0])]
    for odd, values in enumerate(transform(False, pairs, table_ref)):
        out_ref[odd] = values


def part_y(place, pieces, table):
    return pl.pallas_call(
        part_y_kernel,
        grid_spec=pltpu.PrefetchScalarGridSpec(
            num_scalar_prefetch=1,
            grid=(2,),
            in_specs=[pl.BlockSpec((2, 1, 128, KEPT), lambda i, place: (0, i, 0, 0))] * 2
            + [pl.BlockSpec(table.shape, lambda i, place: (0, 0, 0, 0, 0))],
            out_specs=pl.BlockSpec((2, KEPT, KEPT), lambda i, place: (0, 0, i)),
        ),
        out_shape=jax.ShapeDtypeStruct((2, KEPT, 512), jnp.float32),
        compiler_params=params(VMEM),
        cost_estimate=cost(512 * 512 * 256, 4 * MIB),
        name="part_y",
    )(place, *pieces, table)


def sum_y_kernel(place_ref, part_ref, p1, p3, table_ref, out_ref):
    odd = pl.program_id(0)
    g = lax.rem(place_ref[0] + 3, 4)
    base = lax.rem(g, 2)
    flip = jnp.where(odd == 0, 1.0, -1.0).astype(jnp.float32)
    sign = jnp.where((odd == 0) | (g < 2), 1.0, -1.0).astype(jnp.float32)
    table = (table_ref[0, base, 0], table_ref[1, base, 0])
    sides = (p1[...] + flip * p3[...]) * sign
    out_ref[0] = part_ref[0] + product(table, columns_y(sides))


def sum_y(place, part, pieces, table):
    block = pl.BlockSpec((1, KEPT, 512), lambda i, place: (i, 0, 0))
    return pl.pallas_call(
        sum_y_kernel,
        grid_spec=pltpu.PrefetchScalarGridSpec(
            num_scalar_prefetch=1,
            grid=(2,),
            in_specs=[block]
            + [pl.BlockSpec((2, 2, 128, KEPT), lambda i, place: (0, 0, 0, 0))] * 2
            + [pl.BlockSpec((2, 2, 1, KEPT, KEPT), lambda i, place: (0, 0, i, 0, 0))],
            out_specs=block,
        ),
        out_shape=jax.ShapeDtypeStruct((2, KEPT, 512), jnp.float32),
        compiler_params=params(VMEM),
        cost_estimate=cost(512 * 512 * 256, 4 * MIB),
        name="sum_y",
    )(place, part, *pieces, table)


def second_kernel(place_ref, done_a, b0, b2, c1, c3, d1, d3, table_ref, out_ref, held):
    def put(values, half, row):
        held[pl.ds(half * 8 + row, 128, stride=16), :] = values

    for plane in range(2):
        for x in range(2):
            for half in range(2):
                start = x * KEPT + half * 128
                put(
                    done_a[0, plane * 128 : (plane + 1) * 128, start : start + 128],
                    half,
                    plane * 4 + x,
                )
    near, far = (
        jnp.concatenate([c[...], d[...]], axis=1) for c, d in ((c1, d1), (c3, d3))
    )
    pairs = [(b0[...], b2[...], place_ref[0]), (near, far, lax.rem(place_ref[0] + 3, 4))]
    for half, values in enumerate(transform(True, pairs, table_ref)):
        for x in range(2):
            for plane in range(2):
                put(
                    values[x * 128 : (x + 1) * 128, plane * 128 : (plane + 1) * 128],
                    half,
                    plane * 4 + 2 + x,
                )
    out_ref[...] = held[...].reshape(128, 1, 2, 8, 128)


def second(place, done_a, pieces_b, table_z):
    def rows(cells):
        return pl.BlockSpec((2, cells, 128, 128), lambda i, place: (0, 0, i, 0))

    return pl.pallas_call(
        second_kernel,
        grid_spec=pltpu.PrefetchScalarGridSpec(
            num_scalar_prefetch=1,
            grid=(2,),
            in_specs=[pl.BlockSpec((1, KEPT, 512), lambda i, place: (i, 0, 0))]
            + [rows(2)] * 2
            + [rows(1)] * 4
            + [pl.BlockSpec(table_z.shape, lambda i, place: (0, 0, 0, 0, 0))],
            out_specs=pl.BlockSpec((128, 1, 2, 8, 128), lambda i, place: (0, i, 0, 0, 0)),
            scratch_shapes=[pltpu.VMEM((2048, 128), jnp.float32)],
        ),
        out_shape=jax.ShapeDtypeStruct((128, 2, 2, 8, 128), jnp.float32),
        compiler_params=params(VMEM),
        cost_estimate=cost(512 * 512 * 512, 8 * MIB),
        name="second",
    )(place, done_a, *pieces_b, table_z)


def third_kernel(slot_ref, in_ref, table_ref, ordering_ref, out_ref, held):
    out_ref[...] = jnp.zeros_like(out_ref)
    for parity in range(2):
        columns = jnp.concatenate(
            [in_ref[:, parity, half].reshape(1024, 128) for half in range(2)], axis=1
        )
        first, last = columns[:512], columns[512:]
        for odd, sides in enumerate((first + last, first - last)):
            sides = tuple(
                jnp.dot(
                    part, ordering_ref[...], preferred_element_type=jnp.float32
                ).astype(jnp.bfloat16)
                for part in halves(sides)
            )
            values = jnp.exp(product((table_ref[0, odd], table_ref[1, odd]), sides))
            for plane in range(2):
                for half in range(2):
                    held[parity, plane, half, odd * 128 : (odd + 1) * 128] = values[
                        plane * 128 : (plane + 1) * 128, half * 128 : (half + 1) * 128
                    ]

    def place_rows(group, carry):
        for offset in range(8):
            x = group * 8 + offset
            row = group * 4 + offset // 2 + 128 * (offset % 2)
            for parity in range(2):
                for half in range(2):
                    slot = slot_ref[x * 4 + parity * 2 + half]
                    for plane in range(2):
                        out_ref[pl.ds(slot * 2 + plane, 1), :] = held[
                            parity, plane, half, pl.ds(row, 1), :
                        ]
        return carry

    lax.fori_loop(0, KEPT // 8, place_rows, 0)


def third(slots, arrived, table_x, ordering):
    vmem = pl.BlockSpec(memory_space=pltpu.VMEM)
    return pl.pallas_call(
        third_kernel,
        in_specs=[pl.BlockSpec(memory_space=pltpu.SMEM)] + [vmem] * 3,
        out_specs=vmem,
        out_shape=jax.ShapeDtypeStruct((4096, 128), jnp.float32),
        scratch_shapes=[pltpu.VMEM((2, 2, 2, KEPT, 128), jnp.float32)],
        compiler_params=params(VMEM),
        cost_estimate=cost(768 * 512 * 512, 6 * MIB),
        name="third",
    )(slots, arrived, table_x, ordering)


def shifted(piece, axis, shift):
    size = lax.axis_size(axis)
    return lax.ppermute(piece, axis, [(i, (i + shift) % size) for i in range(size)])


def slots_of(block_owner):
    destination = block_owner[:, 0]
    one_hot = (destination[:, None] == jnp.arange(128, dtype=jnp.int32)[None, :]).astype(jnp.int32)
    earlier = jnp.cumsum(one_hot, axis=0) - one_hot
    return destination * CAP + jnp.sum(earlier * one_hot, axis=1)


def per_device(normals, spectrum, block_owner):
    table_x, table_y, table_z, ordering = (jnp.asarray(table) for table in tables())
    gy = lax.axis_index("gy").astype(jnp.int32).reshape(1)
    gz = lax.axis_index("gz").astype(jnp.int32).reshape(1)

    a = scale_first(normals, spectrum)
    a, place = lax.optimization_barrier((a, gy))
    a = lax.all_to_all(a, "gz", split_axis=0, concat_axis=0, tiled=True)
    c1, c3, c2 = scale(0, (1, 3, 2), place, normals, spectrum)
    place, c1, c3, c2 = lax.optimization_barrier((place, c1, c3, c2))
    c1, c3, c2 = shifted(c1, "gy", 1), shifted(c3, "gy", 3), shifted(c2, "gy", 2)
    d1, d3, d2 = scale(1, (1, 3, 2), place, normals, spectrum)
    place, d1, d3, d2 = lax.optimization_barrier((place, d1, d3, d2))
    d1, d3, d2 = shifted(d1, "gy", 1), shifted(d3, "gy", 3), shifted(d2, "gy", 2)
    (c0,) = scale(0, (0,), place, normals, spectrum)
    (d0,) = scale(1, (0,), place, normals, spectrum)

    c1, c3, c2, c0 = first_y(gy, gz, (c0, c1, c2, c3), table_y)
    a, slots, _, d0 = lax.optimization_barrier((a, slots_of(block_owner), c1, d0))
    c1, c3 = shifted(c1, "gz", 1), shifted(c3, "gz", 3)
    a2, a1, a3, a0 = first_z((2, 1, 3, 0), gy, a, table_z)
    d1, d2, d3, c1, c3, _ = lax.optimization_barrier((d1, d2, d3, c1, c3, a2))
    a1, a3, a2 = shifted(a1, "gy", 1), shifted(a3, "gy", 3), shifted(a2, "gy", 2)
    d1, d3, b2, b0 = first_y(gy, gz, (d0, d1, d2, d3), table_y, (c2, c0))
    d1, d3, b2 = shifted(d1, "gz", 1), shifted(d3, "gz", 3), shifted(b2, "gz", 2)

    part_a = part_y(gy, (a0, a2), table_y)
    part_a, b2 = lax.optimization_barrier((part_a, b2))
    done_a = sum_y(gy, part_a, (a1, a3), table_y)
    done_a, b2, d1, d3 = lax.optimization_barrier((done_a, b2, d1, d3))
    planes = second(gz, done_a, (b0, b2, c1, c3, d1, d3), table_z)
    lines = lax.all_to_all(planes, ALL, split_axis=0, concat_axis=0, tiled=True)
    outgoing = third(slots, lines, table_x, ordering)
    return lax.all_to_all(
        outgoing.reshape(128, 1, CAP, 2, BW), ALL, split_axis=0, concat_axis=1, tiled=True
    )


def solution(mesh):
    placed = (P(None, "gx", "gy", "gz"), P("gx", "gy", "gz"), P(ALL, None))
    return jax.shard_map(
        per_device,
        mesh=mesh,
        in_specs=placed,
        out_specs=P(ALL, None, None, None, None),
        check_vma=False,
    )
```

```python
import functools

import jax
import jax.numpy as jnp
import ml_dtypes
import numpy as np
from jax import lax
from jax.experimental import pallas as pl
from jax.experimental.pallas import tpu as pltpu
from jax.sharding import PartitionSpec as P

N = 512
KEPT = 256
BW = 128
CAP = 16
ALL = ("gx", "gy", "gz")
MIB = 1 << 20
VMEM = 16


def split_table(table):
    high = table.astype(np.float32).astype(ml_dtypes.bfloat16)
    low = (table - high.astype(np.float64)).astype(np.float32).astype(ml_dtypes.bfloat16)
    return np.stack([high, low])


def cos_sin(positions, kept):
    angles = (positions[:, None] * kept[None, :] % N) * (2.0 * np.pi / N)
    return np.cos(angles), np.sin(angles)


@functools.cache
def tables():
    order = np.arange(KEPT).reshape(KEPT // 2, 2).T.reshape(-1)
    cosine, sine = cos_sin(np.arange(N // 2), order)
    cosine, sine = (t.reshape(2, 128, 2, 128).transpose(0, 2, 1, 3) for t in (cosine, sine))
    real_rows = np.concatenate([cosine, -sine], 3)
    imag_rows = np.concatenate([sine, cosine], 3)
    table_z = np.concatenate([real_rows, imag_rows], 2)
    cosine, sine = cos_sin(np.arange(N // 2), order)
    cosine, sine = (t.T.reshape(2, 128, 2, 128).transpose(2, 0, 1, 3) for t in (cosine, sine))
    top = np.concatenate([cosine, sine], 3)
    bottom = np.concatenate([-sine, cosine], 3)
    table_y = np.concatenate([top, bottom], 2)
    gx, gy, gz = np.meshgrid(np.arange(8), np.arange(4), np.arange(4), indexing="ij")
    first = 64 * gx + 8 * gz + 2 * gy
    second = 64 * gx + 32 + 8 * gy + gz
    cells = np.stack([first, first + 1, second, second + 4], -1).reshape(128, 4)
    cosine, sine = cos_sin(cells[:64].reshape(-1), order)
    cosine, sine = (
        t.T.reshape(2, KEPT // 2, 64, 1, 4) for t in (cosine, sine)
    )
    top = np.concatenate([cosine, sine], 3).reshape(2, KEPT // 2, 512)
    bottom = np.concatenate([-sine, cosine], 3).reshape(2, KEPT // 2, 512)
    table_x = np.concatenate([top, bottom], 1)
    ordering = np.zeros((KEPT, KEPT), ml_dtypes.bfloat16)
    ordering[np.arange(KEPT), order] = 1
    return split_table(table_x), split_table(table_y), split_table(table_z), ordering


def halves(values):
    high = values.astype(jnp.bfloat16)
    low = (values - high.astype(jnp.float32)).astype(jnp.bfloat16)
    return high, low


def product(left, right):
    def dot(a, b):
        return jnp.dot(a, b, preferred_element_type=jnp.float32)

    return dot(left[0], right[0]) + (dot(left[0], right[1]) + dot(left[1], right[0]))


def params(mib):
    return pltpu.CompilerParams(vmem_limit_bytes=mib * MIB)


def cost(multiplies, moved):
    return pl.CostEstimate(
        flops=multiplies >> 16, bytes_accessed=moved >> 16, transcendentals=0
    )


def rows_z(piece):
    return halves(jnp.concatenate([piece[plane].reshape(-1, 128) for plane in range(2)], axis=1))


def columns_y(piece):
    planes, cells = piece.shape[:2]
    return halves(
        jnp.concatenate([piece[:, x].reshape(256, piece.shape[3]) for x in range(cells)], axis=1)
    )


def in_hbm(*arrays):
    return [pltpu.with_memory_space_constraint(x, pltpu.HBM) for x in arrays]


def scale_kernel(part, shifts, place_ref, normals_ref, spectrum_ref, *refs):
    *out_refs, held_out, held_n, held_s, semaphores = refs

    def gets(i):
        if part is None:
            source_n, source_s = normals_ref.at[:, i], spectrum_ref.at[i]
        else:
            chunk = 4 + lax.rem(place_ref[0] + shifts[i], 4)
            source_n, source_s = normals_ref.at[:, chunk, part], spectrum_ref.at[chunk, part]
        return (
            pltpu.make_async_copy(source_n, held_n.at[i], semaphores.at[i, 0]),
            pltpu.make_async_copy(source_s, held_s.at[i], semaphores.at[i, 1]),
        )

    def put(i):
        target = out_refs[0].at[i] if part is None else out_refs[i]
        return pltpu.make_async_copy(held_out.at[i], target, semaphores.at[i, 2])

    steps = range(len(shifts))
    for i in steps:
        for copy in gets(i):
            copy.start()
    for i in steps:
        for copy in gets(i):
            copy.wait()
        for plane in range(2):
            held_out[i, plane] = held_n[i, plane].astype(jnp.float32) * held_s[i]
        put(i).start()
    for i in steps:
        put(i).wait()


def scale(part, shifts, place, normals, spectrum):
    count = len(shifts)
    chunk = (2, 8 if part is None else 4, 128, 128)
    shapes = [(count,) + chunk] if part is None else [chunk] * count
    view = (8, 8, 128, 128) if part is None else (8, 2, 4, 128, 128)
    hbm = pl.BlockSpec(memory_space=pltpu.HBM)
    return pl.pallas_call(
        functools.partial(scale_kernel, part, shifts),
        in_specs=[pl.BlockSpec(memory_space=pltpu.SMEM)] + [hbm] * 2,
        out_specs=[hbm] * len(shapes),
        out_shape=[pltpu.HBM(shape, jnp.float32) for shape in shapes],
        scratch_shapes=[
            pltpu.VMEM((count,) + chunk, jnp.float32),
            pltpu.VMEM((count,) + chunk, jnp.bfloat16),
            pltpu.VMEM((count,) + chunk[1:], jnp.float32),
            pltpu.SemaphoreType.DMA((count, 3)),
        ],
        compiler_params=params(VMEM),
        cost_estimate=cost(count << 18, 2 * count * MIB),
        name="scale_a" if part is None else "scale_b",
    )(place, *in_hbm(normals.reshape((2,) + view), spectrum.reshape(view)))


def transform(along_z, pairs, table_ref):
    parts = []
    for odd in range(2):
        total = None
        for first, second, g in pairs:
            base = lax.rem(g, 2)
            table = (table_ref[0, base, odd], table_ref[1, base, odd])
            if odd:
                sides = (first - second) * jnp.where(g < 2, 1.0, -1.0).astype(jnp.float32)
            else:
                sides = first + second
            if along_z:
                term = product(rows_z(sides), table)
            else:
                term = product(table, columns_y(sides))
            total = term if total is None else total + term
        parts.append(total)
    return parts


def first_z_kernel(shifts, to_ref, in_ref, table_ref, *refs):
    *out_refs, pieces, held_out, semaphores = refs

    def get(i):
        cells = pl.ds(2 * lax.rem(to_ref[0] + shifts[i], 4), 2)
        return pltpu.make_async_copy(in_ref.at[:, :, cells], pieces.at[i], semaphores.at[i, 0])

    def put(i):
        return pltpu.make_async_copy(held_out.at[i], out_refs[i], semaphores.at[i, 1])

    steps = range(len(shifts))
    for i in steps:
        get(i).start()
    for i in steps:
        get(i).wait()
        pairs = [(pieces[i, 0], pieces[i, 2], 0), (pieces[i, 1], pieces[i, 3], 1)]
        for odd, values in enumerate(transform(True, pairs, table_ref)):
            half = slice(odd * 128, (odd + 1) * 128)
            for plane in range(2):
                part = slice(plane * 128, (plane + 1) * 128)
                for x in range(2):
                    held_out[i, plane, x, :, half] = values[x * 128 : (x + 1) * 128, part]
        put(i).start()
    for i in steps:
        put(i).wait()


def first_z(shifts, to, arrived, table):
    shape = (2, 2, 128, KEPT)
    hbm = pl.BlockSpec(memory_space=pltpu.HBM)
    count = len(shifts)
    return pl.pallas_call(
        functools.partial(first_z_kernel, shifts),
        in_specs=[
            pl.BlockSpec(memory_space=pltpu.SMEM),
            hbm,
            pl.BlockSpec(memory_space=pltpu.VMEM),
        ],
        out_specs=[hbm] * count,
        out_shape=[pltpu.HBM(shape, jnp.float32)] * count,
        scratch_shapes=[
            pltpu.VMEM((count, 4, 2, 2, 128, 128), jnp.float32),
            pltpu.VMEM((count,) + shape, jnp.float32),
            pltpu.SemaphoreType.DMA((count, 2)),
        ],
        compiler_params=params(VMEM),
        cost_estimate=cost(count * 256 * 512 * 512, 2 * count * MIB),
        name="first_z",
    )(to, *in_hbm(arrived), table)


def first_y_kernel(merge, place_ref, to_ref, *refs):
    in_refs, refs = refs[:4], refs[6 if merge else 4 :]
    table_ref, *out_refs, pieces, held_out, semaphores = refs

    def gets(i):
        x = pl.ds(lax.rem(to_ref[0] + (1, 3, 2, 0)[i], 4), 1)
        return [
            pltpu.make_async_copy(ref.at[:, x], pieces.at[i, s], semaphores.at[i, s])
            for s, ref in enumerate(in_refs)
        ]

    def put(i):
        target = out_refs[i].at[:, 1:2] if merge and i >= 2 else out_refs[i].at[:, 0:1]
        return pltpu.make_async_copy(held_out.at[i], target, semaphores.at[i, 4])

    for i in range(4):
        for copy in gets(i):
            copy.start()
    g, h = place_ref[0], lax.rem(place_ref[0] + 3, 4)
    for group in ((0, 1), (2, 3)):
        for i in group:
            for copy in gets(i):
                copy.wait()
        p0, p1, p2, p3 = (
            jnp.concatenate([pieces[i, s] for i in group], axis=1) for s in range(4)
        )
        for odd, values in enumerate(transform(False, [(p0, p2, g), (p1, p3, h)], table_ref)):
            for plane in range(2):
                for x, i in enumerate(group):
                    held_out[i, plane, 0, odd * 128 : (odd + 1) * 128] = values[
                        plane * 128 : (plane + 1) * 128, x * 128 : (x + 1) * 128
                    ]
        for i in group:
            put(i).start()
    for i in range(4):
        put(i).wait()


def first_y(place, to, pieces, table, before=()):
    merge = bool(before)
    shape, whole = (2, 1, KEPT, 128), (2, 2, KEPT, 128)
    hbm = pl.BlockSpec(memory_space=pltpu.HBM)
    operands = in_hbm(*pieces, *before)
    return pl.pallas_call(
        functools.partial(first_y_kernel, merge),
        in_specs=[pl.BlockSpec(memory_space=pltpu.SMEM)] * 2
        + [hbm] * len(operands)
        + [pl.BlockSpec(memory_space=pltpu.VMEM)],
        out_specs=[hbm] * 4,
        out_shape=[pltpu.HBM(shape, jnp.float32)] * 2 + [pltpu.HBM(whole, jnp.float32)] * 2,
        scratch_shapes=[
            pltpu.VMEM((4, 4, 2, 1, 128, 128), jnp.float32),
            pltpu.VMEM((4,) + shape, jnp.float32),
            pltpu.SemaphoreType.DMA((4, 5)),
        ],
        input_output_aliases={6: 2, 7: 3} if merge else {},
        compiler_params=params(VMEM),
        cost_estimate=cost(512 * 512 * 512, 4 * MIB),
        name="first_y",
    )(place, to, *operands, table)


def part_y_kernel(place_ref, p0, p2, table_ref, out_ref):
    pairs = [(p0[...], p2[...], place_ref[0])]
    for odd, values in enumerate(transform(False, pairs, table_ref)):
        out_ref[odd] = values


def part_y(place, pieces, table):
    return pl.pallas_call(
        part_y_kernel,
        grid_spec=pltpu.PrefetchScalarGridSpec(
            num_scalar_prefetch=1,
            grid=(2,),
            in_specs=[pl.BlockSpec((2, 1, 128, KEPT), lambda i, place: (0, i, 0, 0))] * 2
            + [pl.BlockSpec(table.shape, lambda i, place: (0, 0, 0, 0, 0))],
            out_specs=pl.BlockSpec((2, KEPT, KEPT), lambda i, place: (0, 0, i)),
        ),
        out_shape=jax.ShapeDtypeStruct((2, KEPT, 512), jnp.float32),
        compiler_params=params(VMEM),
        cost_estimate=cost(512 * 512 * 256, 4 * MIB),
        name="part_y",
    )(place, *pieces, table)


def sum_y_kernel(place_ref, part_ref, p1, p3, table_ref, out_ref):
    odd = pl.program_id(0)
    g = lax.rem(place_ref[0] + 3, 4)
    base = lax.rem(g, 2)
    flip = jnp.where(odd == 0, 1.0, -1.0).astype(jnp.float32)
    sign = jnp.where((odd == 0) | (g < 2), 1.0, -1.0).astype(jnp.float32)
    table = (table_ref[0, base, 0], table_ref[1, base, 0])
    sides = (p1[...] + flip * p3[...]) * sign
    out_ref[0] = part_ref[0] + product(table, columns_y(sides))


def sum_y(place, part, pieces, table):
    block = pl.BlockSpec((1, KEPT, 512), lambda i, place: (i, 0, 0))
    return pl.pallas_call(
        sum_y_kernel,
        grid_spec=pltpu.PrefetchScalarGridSpec(
            num_scalar_prefetch=1,
            grid=(2,),
            in_specs=[block]
            + [pl.BlockSpec((2, 2, 128, KEPT), lambda i, place: (0, 0, 0, 0))] * 2
            + [pl.BlockSpec((2, 2, 1, KEPT, KEPT), lambda i, place: (0, 0, i, 0, 0))],
            out_specs=block,
        ),
        out_shape=jax.ShapeDtypeStruct((2, KEPT, 512), jnp.float32),
        compiler_params=params(VMEM),
        cost_estimate=cost(512 * 512 * 256, 4 * MIB),
        name="sum_y",
    )(place, part, *pieces, table)


def second_kernel(place_ref, done_a, b0, b2, c1, c3, d1, d3, table_ref, out_ref, held):
    def put(values, half, row):
        held[pl.ds(half * 8 + row, 128, stride=16), :] = values

    for plane in range(2):
        for x in range(2):
            for half in range(2):
                start = x * KEPT + half * 128
                put(
                    done_a[0, plane * 128 : (plane + 1) * 128, start : start + 128],
                    half,
                    plane * 4 + x,
                )
    near, far = (
        jnp.concatenate([c[...], d[...]], axis=1) for c, d in ((c1, d1), (c3, d3))
    )
    pairs = [(b0[...], b2[...], place_ref[0]), (near, far, lax.rem(place_ref[0] + 3, 4))]
    for half, values in enumerate(transform(True, pairs, table_ref)):
        for x in range(2):
            for plane in range(2):
                put(
                    values[x * 128 : (x + 1) * 128, plane * 128 : (plane + 1) * 128],
                    half,
                    plane * 4 + 2 + x,
                )
    out_ref[...] = held[...].reshape(128, 1, 2, 8, 128)


def second(place, done_a, pieces_b, table_z):
    def rows(cells):
        return pl.BlockSpec((2, cells, 128, 128), lambda i, place: (0, 0, i, 0))

    return pl.pallas_call(
        second_kernel,
        grid_spec=pltpu.PrefetchScalarGridSpec(
            num_scalar_prefetch=1,
            grid=(2,),
            in_specs=[pl.BlockSpec((1, KEPT, 512), lambda i, place: (i, 0, 0))]
            + [rows(2)] * 2
            + [rows(1)] * 4
            + [pl.BlockSpec(table_z.shape, lambda i, place: (0, 0, 0, 0, 0))],
            out_specs=pl.BlockSpec((128, 1, 2, 8, 128), lambda i, place: (0, i, 0, 0, 0)),
            scratch_shapes=[pltpu.VMEM((2048, 128), jnp.float32)],
        ),
        out_shape=jax.ShapeDtypeStruct((128, 2, 2, 8, 128), jnp.float32),
        compiler_params=params(VMEM),
        cost_estimate=cost(512 * 512 * 512, 8 * MIB),
        name="second",
    )(place, done_a, *pieces_b, table_z)


def third_kernel(slot_ref, in_ref, table_ref, ordering_ref, out_ref, held):
    out_ref[...] = jnp.zeros_like(out_ref)
    for parity in range(2):
        columns = jnp.concatenate(
            [in_ref[:, parity, half].reshape(1024, 128) for half in range(2)], axis=1
        )
        first, last = columns[:512], columns[512:]
        for odd, sides in enumerate((first + last, first - last)):
            sides = tuple(
                jnp.dot(
                    part, ordering_ref[...], preferred_element_type=jnp.float32
                ).astype(jnp.bfloat16)
                for part in halves(sides)
            )
            values = jnp.exp(product((table_ref[0, odd], table_ref[1, odd]), sides))
            for plane in range(2):
                for half in range(2):
                    held[parity, plane, half, odd * 128 : (odd + 1) * 128] = values[
                        plane * 128 : (plane + 1) * 128, half * 128 : (half + 1) * 128
                    ]

    def place_rows(group, carry):
        for offset in range(8):
            x = group * 8 + offset
            row = group * 4 + offset // 2 + 128 * (offset % 2)
            for parity in range(2):
                for half in range(2):
                    slot = slot_ref[x * 4 + parity * 2 + half]
                    for plane in range(2):
                        out_ref[pl.ds(slot * 2 + plane, 1), :] = held[
                            parity, plane, half, pl.ds(row, 1), :
                        ]
        return carry

    lax.fori_loop(0, KEPT // 8, place_rows, 0)


def third(slots, arrived, table_x, ordering):
    vmem = pl.BlockSpec(memory_space=pltpu.VMEM)
    return pl.pallas_call(
        third_kernel,
        in_specs=[pl.BlockSpec(memory_space=pltpu.SMEM)] + [vmem] * 3,
        out_specs=vmem,
        out_shape=jax.ShapeDtypeStruct((4096, 128), jnp.float32),
        scratch_shapes=[pltpu.VMEM((2, 2, 2, KEPT, 128), jnp.float32)],
        compiler_params=params(VMEM),
        cost_estimate=cost(768 * 512 * 512, 6 * MIB),
        name="third",
    )(slots, arrived, table_x, ordering)


def shifted(piece, axis, shift):
    size = lax.axis_size(axis)
    return lax.ppermute(piece, axis, [(i, (i + shift) % size) for i in range(size)])


def slots_of(block_owner):
    destination = block_owner[:, 0]
    one_hot = (destination[:, None] == jnp.arange(128, dtype=jnp.int32)[None, :]).astype(jnp.int32)
    earlier = jnp.cumsum(one_hot, axis=0) - one_hot
    return destination * CAP + jnp.sum(earlier * one_hot, axis=1)


def per_device(normals, spectrum, block_owner):
    table_x, table_y, table_z, ordering = (jnp.asarray(table) for table in tables())
    gy = lax.axis_index("gy").astype(jnp.int32).reshape(1)
    gz = lax.axis_index("gz").astype(jnp.int32).reshape(1)

    (a,) = scale(None, (0, 1, 2, 3), gz, normals, spectrum)
    a, place = lax.optimization_barrier((a, gy))
    a = lax.all_to_all(a, "gz", split_axis=0, concat_axis=0, tiled=True)
    c1, c3, c2 = scale(0, (1, 3, 2), place, normals, spectrum)
    place, c1, c3, c2 = lax.optimization_barrier((place, c1, c3, c2))
    c1, c3, c2 = shifted(c1, "gy", 1), shifted(c3, "gy", 3), shifted(c2, "gy", 2)
    d1, d3, d2 = scale(1, (1, 3, 2), place, normals, spectrum)
    place, d1, d3, d2 = lax.optimization_barrier((place, d1, d3, d2))
    d1, d3, d2 = shifted(d1, "gy", 1), shifted(d3, "gy", 3), shifted(d2, "gy", 2)
    (c0,) = scale(0, (0,), place, normals, spectrum)
    (d0,) = scale(1, (0,), place, normals, spectrum)

    c1, c3, c2, c0 = first_y(gy, gz, (c0, c1, c2, c3), table_y)
    a, slots, _, d0 = lax.optimization_barrier((a, slots_of(block_owner), c1, d0))
    c1, c3 = shifted(c1, "gz", 1), shifted(c3, "gz", 3)
    a2, a1, a3, a0 = first_z((2, 1, 3, 0), gy, a, table_z)
    d1, d2, d3, c1, c3, _ = lax.optimization_barrier((d1, d2, d3, c1, c3, a2))
    a1, a3, a2 = shifted(a1, "gy", 1), shifted(a3, "gy", 3), shifted(a2, "gy", 2)
    d1, d3, b2, b0 = first_y(gy, gz, (d0, d1, d2, d3), table_y, (c2, c0))
    d1, d3, b2 = shifted(d1, "gz", 1), shifted(d3, "gz", 3), shifted(b2, "gz", 2)

    part_a = part_y(gy, (a0, a2), table_y)
    part_a, b2 = lax.optimization_barrier((part_a, b2))
    done_a = sum_y(gy, part_a, (a1, a3), table_y)
    done_a, b2, d1, d3 = lax.optimization_barrier((done_a, b2, d1, d3))
    planes = second(gz, done_a, (b0, b2, c1, c3, d1, d3), table_z)
    lines = lax.all_to_all(planes, ALL, split_axis=0, concat_axis=0, tiled=True)
    outgoing = third(slots, lines, table_x, ordering)
    return lax.all_to_all(
        outgoing.reshape(128, 1, CAP, 2, BW), ALL, split_axis=0, concat_axis=1, tiled=True
    )


def solution(mesh):
    placed = (P(None, "gx", "gy", "gz"), P("gx", "gy", "gz"), P(ALL, None))
    return jax.shard_map(
        per_device,
        mesh=mesh,
        in_specs=placed,
        out_specs=P(ALL, None, None, None, None),
        check_vma=False,
    )
```
